32 devices in a mesh: dp: 16 (over z, x, core), fsdp: 2 (over y).
Axes of the slice: x: 2, y: 2, z: 4, core: 2. Of those that a mesh axis runs over, the one named last changes fastest.
Arguments:
- inputs: bfloat16 [2, 2, 1024, 1024], P(None, 'fsdp', 'dp'), may hold values from -6 to 6
- encoded: bfloat16 [2, 2, 512, 1024], P(None, 'fsdp', 'dp'), may hold values from -6 to 6
- cotangent: bfloat16 [2, 2, 1024, 1024], P(None, 'fsdp', 'dp'), may hold values from -6 to 6
- doc_ids: int32 [2, 2, 16], P(None, 'fsdp'), may hold values from 0 to 2, never falling along the last dimension, each value on 1 to 12 neighbouring positions
- buckets: int32 [1024], replicated, may hold values from 0 to 31, as said below
- gain_self: bfloat16 [1024], P('fsdp'), may hold values from 0.5 to 1.5
- query_self: bfloat16 [1024, 1024], P('fsdp'), may hold values from -0.09375 to 0.09375
- key_self: bfloat16 [1024, 1024], P('fsdp'), may hold values from -0.09375 to 0.09375
- value_self: bfloat16 [1024, 1024], P('fsdp'), may hold values from -0.1875 to 0.1875
- output_self: bfloat16 [1024, 1024], P('fsdp'), may hold values from -0.75 to 0.75
- position_bias: bfloat16 [32, 16], P('fsdp'), may hold values from -4 to 4
- gain_cross: bfloat16 [1024], P('fsdp'), may hold values from 0.5 to 1.5
- query_cross: bfloat16 [1024, 1024], P('fsdp'), may hold values from -0.09375 to 0.09375
- key_cross: bfloat16 [1024, 1024], P('fsdp'), may hold values from -0.09375 to 0.09375
- value_cross: bfloat16 [1024, 1024], P('fsdp'), may hold values from -0.1875 to 0.1875
- output_cross: bfloat16 [1024, 1024], P('fsdp'), may hold values from -0.75 to 0.75
- gain_dense: bfloat16 [1024], P('fsdp'), may hold values from 0.5 to 1.5
- dense_gate: bfloat16 [1024, 2816], P('fsdp'), may hold values from -0.1875 to 0.1875
- dense_up: bfloat16 [1024, 2816], P('fsdp'), may hold values from -0.1875 to 0.1875
- dense_down: bfloat16 [2816, 1024], P('fsdp'), may hold values from -0.15625 to 0.15625
Outputs:
- outputs: bfloat16 [2, 2, 1024, 1024], P(None, 'fsdp', 'dp')
- grad_inputs: float32 [2, 2, 1024, 1024], P(None, 'fsdp', 'dp')
- grad_encoded: float32 [2, 2, 512, 1024], P(None, 'fsdp', 'dp')
- grad_gain_self: float32 [1024], P('fsdp')
- grad_query_self: float32 [1024, 1024], P('fsdp')
- grad_key_self: float32 [1024, 1024], P('fsdp')
- grad_value_self: float32 [1024, 1024], P('fsdp')
- grad_output_self: float32 [1024, 1024], P('fsdp')
- grad_position_bias: float32 [32, 16], P('fsdp')
- grad_gain_cross: float32 [1024], P('fsdp')
- grad_query_cross: float32 [1024, 1024], P('fsdp')
- grad_key_cross: float32 [1024, 1024], P('fsdp')
- grad_value_cross: float32 [1024, 1024], P('fsdp')
- grad_output_cross: float32 [1024, 1024], P('fsdp')
- grad_gain_dense: float32 [1024], P('fsdp')
- grad_dense_gate: float32 [1024, 2816], P('fsdp')
- grad_dense_up: float32 [1024, 2816], P('fsdp')
- grad_dense_down: float32 [2816, 1024], P('fsdp')
The draws below stay inside these ranges and needn't reach their ends.
Inputs may be any that keep to these rules, and one draw needn't show every extreme that they name: Along the last dimension doc_ids never fall; each document covers 1 to 12 blocks, one exactly 12. buckets[d] = d for d < 16; buckets never falls as d grows, and buckets[1023] = 31.
All inputs are finite; a program needn't handle non-finite values.
Results may differ from the reference program's by a relative error of at most 0.03.
The reference program's roundings to bfloat16 on the way count: a program that leaves them out, or rounds other values in their place, can miss the bound.
Values may be sent and summed in bfloat16 or wider, within the bound.
No kernel may reach another device: no remote copies, remote signals or barrier semaphores. Data moves between devices by JAX's collectives and lax.ppermute only.
A program may use at most 256 MiB of HBM per device.

```python
import math
import jax
import jax.numpy as jnp
import numpy as np
from jax import lax

D = 1024
HEADS = 16
FF = 2816
NB = 32
MICRO = 2
SEQ = 1024
ENC = 512
NSEQ = 2
N_DP = 16


def draw_buckets(key, part):
    distance = jnp.arange(SEQ, dtype=jnp.int32)
    exact_part = NB // 2
    ratio_bits = max(1, (SEQ // exact_part).bit_length() - 1)
    climb_rate = max(1, exact_part * 10 // (7 * ratio_bits))
    rolled = jax.random.randint(key, (SEQ,), 0, distance + 1)
    steps_up = ((distance >= exact_part) & (rolled < climb_rate)).astype(jnp.int32)
    climbed = exact_part - 1 + jnp.cumsum(steps_up)
    lookup = jnp.where(distance < exact_part, distance, jnp.minimum(climbed, NB - 1))
    return jnp.where(distance == SEQ - 1, NB - 1, lookup).astype(jnp.int32)


def level_of(key, extent, split, low, high):
    level, own = 1.0, jax.random.fold_in(key, 6)
    for dim, parts in split:
        draws = jnp.exp(jax.random.uniform(jax.random.fold_in(own, dim), (parts,), jnp.float32, low / len(split), high / len(split)))
        level = level * jnp.repeat(draws, extent[dim] // parts).reshape([-1 if axis == dim else 1 for axis in range(len(extent))])
    return level


def profile(count, total, limit, slope):
    portions = [(1 << 20) // math.isqrt(standing ** slope) + 1 for standing in range(2, count + 1)]
    surplus, holding = total - limit - (count - 1), [1] * (count - 1)
    while surplus > 0:
        movable = [i for i in range(count - 1) if holding[i] < limit]
        mass, remaining = sum([portions[i] for i in movable]), surplus
        for i in movable:
            extra = min(limit - holding[i], max(1, remaining * portions[i] // mass), surplus)
            holding[i] = holding[i] + extra
            surplus = surplus - extra
    return np.array([limit] + holding)


def uneven_parts(stream_key, number_of, total, reach, slope):
    if number_of == 2:
        one = jax.random.randint(stream_key, (), max(1, total - reach), min(reach, total - 1) + 1)
        return jnp.stack([one, total - one])
    lengths = jnp.asarray(profile(number_of, total, reach, slope), jnp.int32)
    pairs = (number_of - 1) // 2
    giver, receiver = lengths[1:1 + 2 * pairs:2], lengths[2:2 + 2 * pairs:2]
    margin = jnp.minimum(giver - 1, reach - receiver)
    moved = jax.random.randint(jax.random.fold_in(stream_key, 1), (pairs,), 0, 1 << 20) % (margin + 1)
    lengths = lengths.at[1:1 + 2 * pairs:2].set(giver - moved).at[2:2 + 2 * pairs:2].set(receiver + moved)
    return lengths[jax.random.permutation(jax.random.fold_in(stream_key, 2), number_of)]


def centred(rng, dims, scale, bound, cuts=(), kind=jnp.bfloat16):
    values = jax.random.normal(rng, dims, jnp.float32) * scale
    if len(cuts) > 0:
        values = level_of(rng, dims, cuts, -0.22, 0.18) * values
    return jnp.clip(values, min=-bound, max=bound).astype(kind)


def setup_inputs(seed: int = 0) -> dict:
    arg_keys = jax.random.split(jax.random.key(seed), 21)
    inputs = centred(arg_keys[0], (MICRO, NSEQ, SEQ, D), 1.0, 6.0, ((1, 2), (2, 16)))
    encoded = centred(arg_keys[1], (MICRO, NSEQ, ENC, D), 1.0, 6.0, ((1, 2), (2, 16)))
    cotangent = centred(arg_keys[2], (MICRO, NSEQ, SEQ, D), 1.0, 6.0, ((1, 2), (2, 16)))
    doc_ids = jax.vmap(lambda own: jnp.searchsorted(jnp.cumsum(uneven_parts(own, 3, N_DP, 3 * N_DP // 4, 0)), jnp.arange(N_DP), side="right"))(jax.random.split(arg_keys[3], MICRO * NSEQ)).reshape((MICRO, NSEQ, N_DP)).astype(jnp.int32)
    buckets = draw_buckets(jax.random.fold_in(arg_keys[20], 71), 0)
    gain_self = jnp.clip(1.0 + 0.1 * jax.random.normal(arg_keys[5], (D,), jnp.float32), 0.5, 1.5).astype(jnp.bfloat16)
    query_self = centred(arg_keys[6], (D, D), (4 * D) ** -0.5, 0.09375, ((0, 2),))
    key_self = centred(arg_keys[7], (D, D), (4 * D) ** -0.5, 0.09375, ((0, 2),))
    value_self = centred(arg_keys[8], (D, D), D ** -0.5, 0.1875, ((0, 2),))
    output_self = centred(arg_keys[9], (D, D), (D // 16) ** -0.5, 0.75, ((0, 2),))
    position_bias = centred(arg_keys[10], (NB, HEADS), 1.0, 4.0, ((0, 2),))
    gain_cross = jnp.clip(1.0 + 0.1 * jax.random.normal(arg_keys[11], (D,), jnp.float32), 0.5, 1.5).astype(jnp.bfloat16)
    query_cross = centred(arg_keys[12], (D, D), (4 * D) ** -0.5, 0.09375, ((0, 2),))
    key_cross = centred(arg_keys[13], (D, D), (4 * D) ** -0.5, 0.09375, ((0, 2),))
    value_cross = centred(arg_keys[14], (D, D), D ** -0.5, 0.1875, ((0, 2),))
    output_cross = centred(arg_keys[15], (D, D), (D // 16) ** -0.5, 0.75, ((0, 2),))
    gain_dense = jnp.clip(1.0 + 0.1 * jax.random.normal(arg_keys[16], (D,), jnp.float32), 0.5, 1.5).astype(jnp.bfloat16)
    dense_gate = centred(arg_keys[17], (D, FF), D ** -0.5, 0.1875, ((0, 2),))
    dense_up = centred(arg_keys[18], (D, FF), D ** -0.5, 0.1875, ((0, 2),))
    dense_down = centred(arg_keys[19], (FF, D), (FF // 2) ** -0.5, 0.15625, ((0, 2),))
    return dict(inputs=inputs, encoded=encoded, cotangent=cotangent, doc_ids=doc_ids, buckets=buckets, gain_self=gain_self, query_self=query_self, key_self=key_self, value_self=value_self, output_self=output_self, position_bias=position_bias, gain_cross=gain_cross, query_cross=query_cross, key_cross=key_cross, value_cross=value_cross, output_cross=output_cross, gain_dense=gain_dense, dense_gate=dense_gate, dense_up=dense_up, dense_down=dense_down)


EPS = 1e-06
NEGATIVE = -1e+30
HIGHEST = lax.Precision.HIGHEST

@jax.custom_vjp
def low(v):
    return lax.optimization_barrier(v.astype(jnp.bfloat16)).astype(jnp.float32)

@jax.custom_vjp
def low_back(v):
    return v

def low_keep(v):
    return (low(v), None)

def low_pass(kept, grad):
    return (grad,)

def back_keep(v):
    return (v, None)

def back_low(kept, grad):
    return (low(grad),)
low.defvjp(low_keep, low_pass)
low_back.defvjp(back_keep, back_low)

def norm_rows(values, gain):
    return values * lax.rsqrt(lax.optimization_barrier(jnp.mean(values * values, axis=-1, keepdims=True)) + EPS) * gain

def project(values, weight):
    return jnp.dot(values, weight, precision=HIGHEST)

def split_heads(matrix, head_count):
    return matrix.reshape(matrix.shape[0], head_count, -1)

def attention(queries, key_rows, value_rows, bias, allowed):
    scores = jnp.einsum('qhd,khd->hqk', queries, key_rows, precision=HIGHEST)
    if bias is not None:
        scores = jnp.where(allowed[None], scores + bias, NEGATIVE)
    scores = low_back(scores)
    probability = low(jax.nn.softmax(scores, axis=-1))
    mixed = jnp.einsum('hqk,khd->qhd', probability, value_rows, precision=HIGHEST)
    return low_back(low(mixed.reshape(mixed.shape[0], -1)))

def layer(params, tokens, states, block_docs, buckets):
    gain_self, query_self, key_self, value_self, output_self, position_bias, gain_cross, query_cross, key_cross, value_cross, output_cross, gain_dense, dense_gate, dense_up, dense_down = params
    length = tokens.shape[0]
    head_count = position_bias.shape[1]
    position = jnp.arange(length, dtype=jnp.int32)
    apart = position[:, None] - position[None, :]
    token_docs = jnp.repeat(block_docs, length // block_docs.shape[0])
    allowed = (apart >= 0) & (token_docs[:, None] == token_docs[None, :])
    distance_bias = position_bias[buckets]
    bias = jnp.transpose(distance_bias[jnp.clip(apart, 0, length - 1)], (2, 0, 1))
    normed_one = low(norm_rows(tokens, gain_self))
    queries = low_back(low(project(normed_one, query_self)))
    key_rows = low_back(low(project(normed_one, key_self)))
    value_rows = low_back(low(project(normed_one, value_self)))
    mixed_self = attention(split_heads(queries, head_count), split_heads(key_rows, head_count), split_heads(value_rows, head_count), bias, allowed)
    after_self = tokens + low_back(project(mixed_self, output_self))
    normed_two = low(norm_rows(after_self, gain_cross))
    cross_queries = low_back(low(project(normed_two, query_cross)))
    enc_keys = low_back(low(project(states, key_cross)))
    enc_values = low_back(low(project(states, value_cross)))
    mixed_cross = attention(split_heads(cross_queries, head_count), split_heads(enc_keys, head_count), split_heads(enc_values, head_count), None, None)
    after_cross = after_self + low_back(project(mixed_cross, output_cross))
    normed_three = low(norm_rows(after_cross, gain_dense))
    gate_pre = low_back(project(normed_three, dense_gate))
    upper_pre = low_back(project(normed_three, dense_up))
    hidden = low(jax.nn.gelu(gate_pre, approximate=True) * upper_pre)
    return after_cross + low_back(project(hidden, dense_down))

def reference(inputs, encoded, cotangent, doc_ids, buckets, gain_self, query_self, key_self, value_self, output_self, position_bias, gain_cross, query_cross, key_cross, value_cross, output_cross, gain_dense, dense_gate, dense_up, dense_down):
    params = (gain_self, query_self, key_self, value_self, output_self, position_bias, gain_cross, query_cross, key_cross, value_cross, output_cross, gain_dense, dense_gate, dense_up, dense_down)
    params = tuple((weight.astype(jnp.float32) for weight in params))
    width = inputs.shape[3]
    sequence_count = inputs.shape[0] * inputs.shape[1]
    tokens = inputs.astype(jnp.float32).reshape(sequence_count, -1, width)
    states = encoded.astype(jnp.float32).reshape(sequence_count, -1, width)
    block_docs = doc_ids.reshape(sequence_count, -1)

    def run(all_params, all_tokens, all_states):

        def one_sequence(item):
            return layer(all_params, item[0], item[1], item[2], buckets)
        return lax.map(jax.checkpoint(one_sequence), (all_tokens, all_states, block_docs))
    results, pullback = jax.vjp(run, params, tokens, states)
    grad_params, grad_tokens, grad_states = pullback(cotangent.astype(jnp.float32).reshape(results.shape))
    g_gain_self, g_query_self, g_key_self, g_value_self, g_output_self, g_position_bias, g_gain_cross, g_query_cross, g_key_cross, g_value_cross, g_output_cross, g_gain_dense, g_dense_gate, g_dense_up, g_dense_down = grad_params
    return (results.astype(jnp.bfloat16).reshape(inputs.shape), grad_tokens.reshape(inputs.shape), grad_states.reshape(encoded.shape), g_gain_self, g_query_self, g_key_self, g_value_self, g_output_self, g_position_bias, g_gain_cross, g_query_cross, g_key_cross, g_value_cross, g_output_cross, g_gain_dense, g_dense_gate, g_dense_up, g_dense_down)
```

```python
import functools

import jax
import jax.numpy as jnp
from jax import lax
from jax.experimental import pallas as pl
from jax.experimental.pallas import tpu as pltpu
from jax.sharding import PartitionSpec as P

EPS = 1e-06
NEGATIVE = -1e30
TILE = 256
F32 = jnp.float32
BF16 = jnp.bfloat16
VMEM_LIMIT = 56 * 1024 * 1024


def vmem():
    return pl.BlockSpec(memory_space=pltpu.VMEM)


def smem():
    return pl.BlockSpec(memory_space=pltpu.SMEM)


def params(limit=VMEM_LIMIT):
    return pltpu.CompilerParams(vmem_limit_bytes=limit)


def dot(left, right):
    return jnp.dot(left, right, preferred_element_type=F32)


def dot_t(left, right):
    return lax.dot_general(left, right, (((1,), (1,)), ((), ())), preferred_element_type=F32)


def t_dot(left, right):
    return lax.dot_general(left, right, (((0,), (0,)), ((), ())), preferred_element_type=F32)


def norm_rows(values, gain):
    return values * lax.rsqrt(jnp.mean(values * values, axis=-1, keepdims=True) + EPS) * gain


def norm_back(values, gain, grad):
    r = lax.rsqrt(jnp.mean(values * values, axis=-1, keepdims=True) + EPS)
    scaled = grad * gain
    inner = jnp.mean(scaled * values, axis=-1, keepdims=True)
    back = r * scaled - values * (r * r * r * inner)
    return back, jnp.sum(grad * (values * r), axis=0, keepdims=True)


def low_lanes(rows):
    return lax.broadcasted_iota(jnp.int32, (rows, 128), 1) < 64


def pair_up(first, second):
    lane = low_lanes(first.shape[0])
    low = jnp.where(lane, first, pltpu.roll(second, 64, 1))
    high = jnp.where(lane, pltpu.roll(first, 64, 1), second)
    return low, high


def keep_half(values, half):
    lane = low_lanes(values.shape[0])
    return jnp.where(lane if half == 0 else ~lane, values, jnp.zeros_like(values))


def softmax_rows(scores):
    top = jnp.max(scores, axis=-1, keepdims=True)
    raised = jnp.exp(scores - top)
    return raised * (1.0 / jnp.sum(raised, axis=-1, keepdims=True))


def table_kernel(edge_ref, value_ref, out_ref):
    rows, length = out_ref.shape
    bucket_count = value_ref.shape[0]
    for start in range(0, length, TILE):
        place = (rows, TILE)
        apart = (
            lax.broadcasted_iota(jnp.int32, place, 0)
            - lax.broadcasted_iota(jnp.int32, place, 1)
            + (length - rows - start)
        )
        value = jnp.full(place, value_ref[0], F32)
        for bucket in range(1, bucket_count):
            value = jnp.where(apart >= edge_ref[bucket], value_ref[bucket], value)
        out_ref[:, start : start + TILE] = jnp.where(apart >= 0, value, NEGATIVE)


def bias_table(edges, values, length):
    return pl.pallas_call(
        table_kernel,
        out_shape=jax.ShapeDtypeStruct((TILE, length), F32),
        in_specs=[smem(), smem()],
        out_specs=vmem(),
        name="bias_table",
    )(edges, values)


def bucket_kernel(edge_ref, grad_ref, out_ref):
    rows, length = grad_ref.shape
    bucket_count = out_ref.shape[0]
    above = [jnp.zeros((8, TILE), F32) for _ in range(bucket_count)]
    for start in range(0, length, TILE):
        for row in range(0, rows, 8):
            place = (8, TILE)
            apart = (
                lax.broadcasted_iota(jnp.int32, place, 0)
                - lax.broadcasted_iota(jnp.int32, place, 1)
                + (length - rows - start + row)
            )
            tile = grad_ref[row : row + 8, start : start + TILE]
            for bucket in range(bucket_count):
                above[bucket] = above[bucket] + jnp.where(apart >= edge_ref[bucket], tile, 0.0)
    for bucket in range(bucket_count):
        rest = above[bucket + 1] if bucket + 1 < bucket_count else 0.0
        part = jnp.sum(above[bucket] - rest, axis=0, keepdims=True)
        out_ref[bucket : bucket + 1, :] = part[:, :128] + part[:, 128:]


def bucket_sums(edges, grad, bucket_count):
    return pl.pallas_call(
        bucket_kernel,
        out_shape=jax.ShapeDtypeStruct((bucket_count, 128), F32),
        in_specs=[smem(), vmem()],
        out_specs=vmem(),
        name="bucket_sums",
    )(edges, grad)


def self_scores(q, k, table, doc_col, doc_row):
    scores = dot_t(q, k) + table
    return jnp.where(doc_col == doc_row, scores, NEGATIVE)


def self_forward_kernel(
    pos_ref, x_ref, gain_ref, w_ref, table_ref, doc_row_ref, doc_col_ref, n_ref, qkv_ref, o_ref
):
    blocks, _, rows, width = x_ref.shape
    length = blocks * rows
    group = TILE // rows
    lane = lax.broadcasted_iota(jnp.int32, (TILE, 384), 1) % 128 < 64

    def project(step, carry):
        parts = []
        for inner in range(group):
            own = step * group + inner
            x = x_ref[pos_ref[own]].astype(F32).reshape(2 * rows, width)
            n = norm_rows(x, gain_ref[...]).astype(BF16).reshape(2, rows, width)
            n_ref[own] = n
            parts.append(n)
        first = jnp.concatenate([part[0] for part in parts], axis=0)
        second = jnp.concatenate([part[1] for part in parts], axis=0)
        made = dot(jnp.concatenate([first, second], axis=0), w_ref[...])
        picked = jnp.where(lane, made[:TILE], made[TILE:])
        qkv_ref[pl.ds(pl.multiple_of(step * TILE, TILE), TILE), :] = picked.astype(BF16)
        return carry

    lax.fori_loop(0, blocks // group, project, 0)
    for block in range(length // TILE):
        start, count = block * TILE, (block + 1) * TILE
        table = table_ref[:, length - count :]
        q = qkv_ref[start:count, 0:128]
        k = qkv_ref[:count, 128:256]
        v = qkv_ref[:count, 256:384]
        mixed = []
        for half in range(2):
            scores = self_scores(
                keep_half(q, half),
                k,
                table,
                doc_col_ref[half, start:count, :],
                doc_row_ref[half : half + 1, :count],
            )
            mixed.append(dot(softmax_rows(scores).astype(BF16), v))
        o_ref[start:count, :] = jnp.where(low_lanes(TILE), mixed[0], mixed[1]).astype(BF16)


def self_backward_kernel(
    qkv_ref, do_ref, table_ref, doc_row_ref, doc_col_ref, dqkv_ref, grad_ref, dk_ref, dv_ref
):
    length = qkv_ref.shape[0]
    grad_ref[...] = jnp.zeros_like(grad_ref)
    dk_ref[...] = jnp.zeros_like(dk_ref)
    dv_ref[...] = jnp.zeros_like(dv_ref)
    for block in range(length // TILE):
        start, count = block * TILE, (block + 1) * TILE
        table = table_ref[:, length - count :]
        k = qkv_ref[:count, 128:256]
        v = qkv_ref[:count, 256:384]
        made = []
        for half in range(2):
            q = keep_half(qkv_ref[start:count, 0:128], half)
            do = keep_half(do_ref[start:count, :], half)
            p = softmax_rows(
                self_scores(
                    q,
                    k,
                    table,
                    doc_col_ref[half, start:count, :],
                    doc_row_ref[half : half + 1, :count],
                )
            )
            dp = dot_t(do, v)
            ds = (p * (dp - jnp.sum(p * dp, axis=-1, keepdims=True))).astype(BF16)
            grad_ref[:, length - count :] += ds.astype(F32)
            made.append(dot(ds, k))
            dk_ref[:count, :] += t_dot(ds, q)
            dv_ref[:count, :] += t_dot(p.astype(BF16), do)
        dq = jnp.where(low_lanes(TILE), made[0], made[1])
        dqkv_ref[start:count, 0:128] = dq.astype(BF16)
    dqkv_ref[:, 128:256] = dk_ref[...].astype(BF16)
    dqkv_ref[:, 256:384] = dv_ref[...].astype(BF16)


def head_weight_kernel(n_ref, d_ref, out_ref):
    blocks, _, rows, width = n_ref.shape
    shards = out_ref.shape[0]
    span = width // shards
    lane = lax.broadcasted_iota(jnp.int32, (blocks * rows, 384), 1) % 128 < 64
    d = d_ref[...]
    zero = jnp.zeros_like(d)
    right = [jnp.where(lane, d, zero), jnp.where(lane, zero, d)]
    half = span // 2
    for shard in range(shards):
        total = jnp.zeros((span, 384), F32)
        for micro in range(2):
            left = n_ref[:, micro, :, shard * span : (shard + 1) * span]
            total = total + t_dot(left.reshape(blocks * rows, span), right[micro])
        q, k, v = (
            total[:, at : at + 128] + pltpu.roll(total[:, at : at + 128], 64, 1)
            for at in (0, 128, 256)
        )
        out_ref[shard, :span, :] = jnp.where(low_lanes(span), q, k).astype(BF16)
        out_ref[shard, span:, :] = jnp.where(low_lanes(half), v[:half], v[half:]).astype(BF16)


def mid_forward_kernel(
    o1_ref,
    x_ref,
    wo_ref,
    gain_cross_ref,
    wq_ref,
    ke_ref,
    ve_ref,
    wc_ref,
    gain_dense_ref,
    o1c_ref,
    x1_ref,
    n2_ref,
    q2_ref,
    o2_ref,
    x2_ref,
    n3_ref,
):
    heads, rows, _ = o1_ref.shape
    width = x_ref.shape[-1]
    for pair in range(heads // 2):
        at = pair * 128
        low, high = pair_up(o1_ref[2 * pair].astype(F32), o1_ref[2 * pair + 1].astype(F32))
        o1c_ref[0:rows, at : at + 128] = low.astype(BF16)
        o1c_ref[rows : 2 * rows, at : at + 128] = high.astype(BF16)
    x = x_ref[...].astype(F32).reshape(2 * rows, width)
    x1 = x + dot(o1c_ref[...], wo_ref[...])
    x1_ref[...] = x1
    n2 = norm_rows(x1, gain_cross_ref[...]).astype(BF16)
    n2_ref[...] = n2
    q2_ref[...] = dot(n2, wq_ref[...]).astype(BF16)
    for micro in range(2):
        for pair in range(heads // 2):
            at = pair * 128
            span = slice(micro * rows, (micro + 1) * rows)
            q = q2_ref[span, at : at + 128]
            both = jnp.concatenate([keep_half(q, 0), keep_half(q, 1)], axis=0)
            p = softmax_rows(dot_t(both, ke_ref[micro, :, at : at + 128]))
            o = dot(p.astype(BF16), ve_ref[micro, :, at : at + 128])
            o2_ref[span, at : at + 128] = jnp.where(
                low_lanes(rows), o[:rows], o[rows:]
            ).astype(BF16)
    x2 = x1 + dot(o2_ref[...], wc_ref[...])
    x2_ref[...] = x2
    n3_ref[...] = norm_rows(x2, gain_dense_ref[...]).astype(BF16)


def mid_backward_kernel(
    g_ref,
    dn3_ref,
    dn3_more_ref,
    x2_ref,
    gain_dense_ref,
    wc_ref,
    q2_ref,
    ke_ref,
    ve_ref,
    wq_ref,
    x1_ref,
    gain_cross_ref,
    wo_ref,
    gx2b_ref,
    dq2_ref,
    gx1_ref,
    gx1b_ref,
    do1_ref,
    dkv_ref,
    dc_ref,
    do2_ref,
):
    heads, rows, _ = do1_ref.shape
    blocks, _, part, _ = dkv_ref.shape
    width = x1_ref.shape[-1]
    dn3 = dn3_ref[...] + dn3_more_ref[...].astype(F32)
    back, dc = norm_back(x2_ref[...], gain_dense_ref[...], dn3)
    dc_ref[0:1, :] = dc
    gx2 = g_ref[...].astype(F32).reshape(2 * rows, width) + back
    gx2b = gx2.astype(BF16)
    gx2b_ref[...] = gx2b
    do2_ref[...] = dot_t(gx2b, wc_ref[...]).astype(BF16)
    for micro in range(2):
        for pair in range(heads // 2):
            at = pair * 128
            span = slice(micro * rows, (micro + 1) * rows)
            q = q2_ref[span, at : at + 128]
            do = do2_ref[span, at : at + 128]
            q = jnp.concatenate([keep_half(q, 0), keep_half(q, 1)], axis=0)
            do = jnp.concatenate([keep_half(do, 0), keep_half(do, 1)], axis=0)
            k = ke_ref[micro, :, at : at + 128]
            v = ve_ref[micro, :, at : at + 128]
            p = softmax_rows(dot_t(q, k))
            dp = dot_t(do, v)
            ds = (p * (dp - jnp.sum(p * dp, axis=-1, keepdims=True))).astype(BF16)
            dq = dot(ds, k)
            dq2_ref[span, at : at + 128] = jnp.where(
                low_lanes(rows), dq[:rows], dq[rows:]
            ).astype(BF16)
            dk = t_dot(ds, q).astype(BF16).reshape(blocks, part, 128)
            dv = t_dot(p.astype(BF16), do).astype(BF16).reshape(blocks, part, 128)
            dkv_ref[:, micro, :, at : at + 128] = dk
            dkv_ref[:, micro, :, width + at : width + at + 128] = dv
    dn2 = dot_t(dq2_ref[...], wq_ref[...])
    back, dc = norm_back(x1_ref[...], gain_cross_ref[...], dn2)
    dc_ref[1:2, :] = dc
    gx1 = gx2 + back
    gx1_ref[...] = gx1
    gx1b = gx1.astype(BF16)
    gx1b_ref[...] = gx1b
    do1 = dot_t(gx1b, wo_ref[...]).astype(BF16).astype(F32)
    for pair in range(heads // 2):
        at = pair * 128
        low, high = pair_up(do1[:rows, at : at + 128], do1[rows:, at : at + 128])
        do1_ref[2 * pair] = low.astype(BF16)
        do1_ref[2 * pair + 1] = high.astype(BF16)


def dense_kernel(
    n_ref, g_ref, wg_ref, wu_ref, wd_ref, hid_ref, da_ref, db_ref, y_ref, ylow_ref, d_ref, dlow_ref
):
    n = n_ref[...]
    a = dot(n, wg_ref[...])
    b = dot(n, wu_ref[...])
    scale = 0.7978845608028654
    cubed = 0.044715
    inner = jnp.tanh(scale * (a + cubed * (a * a * a)))
    gelu = 0.5 * a * (1.0 + inner)
    slope = 0.5 * (1.0 + inner) + 0.5 * a * (1.0 - inner * inner) * (
        scale * (1.0 + 3.0 * cubed * (a * a))
    )
    hid = (gelu * b).astype(BF16)
    hid_ref[...] = hid
    dh = dot_t(g_ref[...], wd_ref[...])
    da = (dh * b * slope).astype(BF16)
    db = (dh * gelu).astype(BF16)
    da_ref[...] = da
    db_ref[...] = db
    d = dot_t(da, wg_ref[...]) + dot_t(db, wu_ref[...])
    d_ref[...] = d
    dlow_ref[...] = d.astype(BF16)
    y = dot(hid, wd_ref[...])
    y_ref[...] = y
    ylow_ref[...] = y.astype(BF16)


def dense_layer(n, g, wg, wu, wd, step):
    count, width = n.shape
    hidden = wg.shape[1]
    row = lambda size: pl.BlockSpec((step, size), lambda i: (i, 0))
    whole = lambda array: pl.BlockSpec(array.shape, lambda i: (0, 0))
    made = lambda size, kind: jax.ShapeDtypeStruct((count, size), kind)
    return pl.pallas_call(
        dense_kernel,
        grid=(count // step,),
        in_specs=[row(width), row(width), whole(wg), whole(wu), whole(wd)],
        out_specs=[row(hidden)] * 3 + [row(width)] * 4,
        out_shape=[made(hidden, BF16)] * 3
        + [made(width, F32), made(width, BF16), made(width, F32), made(width, BF16)],
        compiler_params=params(),
        name="dense_layer",
    )(n, g, wg, wu, wd)


def spread_kernel(counts, where_ref, in_ref, *out_refs):
    for place, out_ref in enumerate(out_refs):
        out_ref[...] = in_ref[0, 0, place].astype(F32)


def spread(where, pieces, shapes, index):
    count, halves, kinds, rows, cols = pieces.shape
    return pl.pallas_call(
        functools.partial(spread_kernel, kinds),
        grid_spec=pltpu.PrefetchScalarGridSpec(
            num_scalar_prefetch=1,
            grid=(count, halves),
            in_specs=[
                pl.BlockSpec((1, 1, kinds, rows, cols), lambda t, h, where: (t, h, 0, 0, 0))
            ],
            out_specs=[pl.BlockSpec((rows, cols), index)] * kinds,
        ),
        out_shape=[jax.ShapeDtypeStruct(shape, F32) for shape in shapes],
        compiler_params=params(),
        name="spread",
    )(where, pieces)


def head_spread_kernel(pos_ref, in_ref, q_ref, k_ref, v_ref):
    span, width = q_ref.shape
    half = span // 2
    for pair in range(width // 128):
        at = pair * 128
        first, second = in_ref[pos_ref[2 * pair]], in_ref[pos_ref[2 * pair + 1]]
        low, high = pair_up(first.astype(F32), second.astype(F32))
        q_ref[:, at : at + 128] = low[:span]
        k_ref[:, at : at + 128] = high[:span]
        v_ref[:half, at : at + 128] = low[span:]
        v_ref[half:, at : at + 128] = high[span:]


def per_device(
    inputs,
    encoded,
    cotangent,
    doc_ids,
    buckets,
    gain_self,
    query_self,
    key_self,
    value_self,
    output_self,
    position_bias,
    gain_cross,
    query_cross,
    key_cross,
    value_cross,
    output_cross,
    gain_dense,
    dense_gate,
    dense_up,
    dense_down,
):
    micro_count, _, rows, width = inputs.shape
    part = encoded.shape[2]
    heads = position_bias.shape[1]
    dp, fs = lax.axis_size("dp"), lax.axis_size("fsdp")
    me, shard = lax.axis_index("dp"), lax.axis_index("fsdp")
    core = me % 2
    length = rows * dp
    tokens = micro_count * rows
    copies = dp // heads
    head = me // copies
    span = width // fs
    hidden = dense_down.shape[0]
    bits = [1 << place for place in reversed(range(dp.bit_length() - 1))]

    def swap_dp(values, bit):
        return lax.ppermute(values, "dp", [(j, j ^ bit) for j in range(dp)])

    def swap_fs(values):
        return lax.ppermute(values, "fsdp", [(j, 1 - j) for j in range(2)])

    def two(first, second, which):
        return jnp.where(
            which == 0,
            jnp.concatenate([first, second], axis=-2),
            jnp.concatenate([second, first], axis=-2),
        )

    def other_rows(values):
        half = values.shape[-2] // 2
        sent = lax.dynamic_slice_in_dim(values, core * half, half, axis=values.ndim - 2)
        got = swap_fs(sent)
        return two(got, swap_dp(got, 1), core)

    def whole_rows(values):
        if fs == 2:
            return two(values, other_rows(values), shard)
        return lax.all_gather(values, "fsdp", axis=1, tiled=True)

    def gather_small(values):
        if fs == 2:
            got = swap_fs(values)
            return jnp.where(
                shard == 0,
                jnp.concatenate([values, got], axis=-1),
                jnp.concatenate([got, values], axis=-1),
            )
        return lax.all_gather(values, "fsdp", axis=1, tiled=True)

    def both_tokens(values):
        if fs == 2:
            return jnp.concatenate([values, swap_fs(values)], axis=0)
        return lax.all_gather(values, "fsdp", axis=0, tiled=True)

    def gather_all(values):
        for bit in bits:
            values = jnp.concatenate([values, swap_dp(values, bit)], axis=0)
        return values

    def sum_chips(values):
        chip, size = me // 2, values.shape[0]
        for bit in reversed(bits[:-1]):
            values = values.reshape((size // 2, 2) + values.shape[1:])
            size = size // 2
            mine = (me // bit) % 2
            kept = lax.dynamic_index_in_dim(values, mine, 1, keepdims=False)
            sent = lax.dynamic_index_in_dim(values, 1 - mine, 1, keepdims=False)
            got = swap_dp(sent, bit)
            values = (kept.astype(F32) + got.astype(F32)).astype(BF16)
        return values

    turned = [
        sum(((t >> place) & 1) << (len(bits) - 1 - place) for place in range(len(bits)))
        for t in range(dp)
    ]
    source = me ^ jnp.array(turned, jnp.int32)
    place_of = jnp.zeros((dp,), jnp.int32).at[source].set(jnp.arange(dp, dtype=jnp.int32))

    x = inputs[:, 0]
    g = cotangent[:, 0]
    e = encoded[:, 0]

    pieces = {0: x}
    for bit in bits:
        for known in list(pieces):
            pieces[known | bit] = swap_dp(pieces[known], bit)
    x_all = jnp.stack([pieces[turn] for turn in turned])
    e_all = lax.all_gather(e, "dp", axis=0)

    gains = gather_small(jnp.stack([gain_self, gain_cross, gain_dense])).astype(F32)
    gain_one, gain_two, gain_three = gains[0:1], gains[1:2], gains[2:3]
    bias_all = gather_small(position_bias.T).T.astype(F32)
    own_head = lambda w: lax.dynamic_slice_in_dim(w, head * 64, 64, axis=1)
    head_pack = jnp.concatenate([own_head(query_self), own_head(key_self), own_head(value_self)], axis=1)
    if fs == 2:
        head_whole = two(head_pack, swap_fs(head_pack), shard)
    else:
        picked = jnp.concatenate(
            [w.reshape(span, heads, 64) for w in (query_self, key_self, value_self)], axis=2
        )
        whole = lax.all_gather(picked.reshape(span, heads * 192), "fsdp", axis=0, tiled=True)
        head_whole = lax.dynamic_slice_in_dim(whole, head * 192, 192, axis=1)
    head_w = jnp.concatenate(
        [head_whole[:, at : at + 64] for at in (0, 0, 64, 64, 128, 128)], axis=1
    )

    cross_kv = whole_rows(jnp.stack([key_cross, value_cross]))
    near = whole_rows(jnp.stack([output_self, query_cross, output_cross]))
    wo, wq2, wc = near[0], near[1], near[2]

    slab = jnp.stack([dense_gate, dense_up])
    if fs == 2:
        mine = lax.dynamic_slice_in_dim(slab, shard * hidden, hidden, axis=2)
        theirs = lax.dynamic_slice_in_dim(slab, (1 - shard) * hidden, hidden, axis=2)
        gate_up = two(mine, other_rows(theirs), shard)
    else:
        gate_up = lax.all_to_all(slab, "fsdp", 2, 1, tiled=True)

    g_group = both_tokens(g.reshape(tokens, width))

    marks = jnp.arange(bias_all.shape[0], dtype=jnp.int32)
    edges = jnp.sum((buckets[:, None] < marks[None, :]).astype(jnp.int32), axis=0)
    bias_values = lax.dynamic_slice_in_dim(bias_all, head, 1, axis=1)[:, 0]
    table = bias_table(edges, bias_values, length)
    doc_row = jnp.repeat(doc_ids[:, 0], rows, axis=1, total_repeat_length=length)
    doc_col = doc_row[:, :, None]

    n_all, qkv, mixed = pl.pallas_call(
        self_forward_kernel,
        out_shape=[
            jax.ShapeDtypeStruct((dp, micro_count, rows, width), BF16),
            jax.ShapeDtypeStruct((length, 384), BF16),
            jax.ShapeDtypeStruct((length, 128), BF16),
        ],
        in_specs=[smem()] + [vmem()] * 6,
        out_specs=[vmem()] * 3,
        compiler_params=params(),
        name="self_forward",
    )(place_of, x_all, gain_one, head_w, table, doc_row, doc_col)
    o1_heads = lax.all_to_all(mixed.reshape(dp, rows, 128), "dp", 0, 0, tiled=True)[::copies]

    states = jnp.swapaxes(e_all, 0, 1).reshape(micro_count, dp * part, width)
    ke = dot(states, cross_kv[0]).astype(BF16)
    ve = dot(states, cross_kv[1]).astype(BF16)

    row32 = jax.ShapeDtypeStruct((tokens, width), F32)
    row16 = jax.ShapeDtypeStruct((tokens, width), BF16)
    o1, x1, n2, q2, o2, x2, n3 = pl.pallas_call(
        mid_forward_kernel,
        out_shape=[row16, row32, row16, row16, row16, row32, row16],
        in_specs=[vmem()] * 9,
        out_specs=[vmem()] * 7,
        compiler_params=params(),
        name="mid_forward",
    )(o1_heads, x, wo, gain_two, wq2, ke, ve, wc, gain_three)

    n_group = both_tokens(n3)
    hid, da, db, y32, y16, d32, d16 = dense_layer(
        n_group, g_group, gate_up[0], gate_up[1], dense_down, tokens
    )
    if fs == 2:
        dn3, dn3_more = d32[:tokens], swap_fs(d16[tokens:])
        dense_out = y32[:tokens] + swap_fs(y16[tokens:]).astype(F32)
    else:
        dn3 = jnp.zeros((tokens, width), F32)
        dn3_more = lax.psum_scatter(d16, "fsdp", scatter_dimension=0, tiled=True)
        dense_out = lax.psum_scatter(y16, "fsdp", scatter_dimension=0, tiled=True).astype(F32)
    outputs = (x2 + dense_out).astype(BF16)

    gx2b, dq2, gx1, gx1b, do1_heads, dkv, dc_two = pl.pallas_call(
        mid_backward_kernel,
        out_shape=[
            row16,
            row16,
            row32,
            row16,
            jax.ShapeDtypeStruct((heads, rows, 128), BF16),
            jax.ShapeDtypeStruct((dp, micro_count, part, 2 * width), BF16),
            jax.ShapeDtypeStruct((2, width), F32),
        ],
        in_specs=[vmem()] * 13,
        out_specs=[vmem()] * 7,
        scratch_shapes=[pltpu.VMEM((tokens, width), BF16)],
        compiler_params=params(),
        name="mid_backward",
    )(g, dn3, dn3_more, x2, gain_three, wc, q2, ke, ve, wq2, x1, gain_two, wo)
    do1 = lax.all_to_all(
        jnp.repeat(do1_heads, copies, axis=0) if copies > 1 else do1_heads, "dp", 0, 0, tiled=True
    ).reshape(length, 128)

    dqkv, table_grad = pl.pallas_call(
        self_backward_kernel,
        out_shape=[
            jax.ShapeDtypeStruct((length, 384), BF16),
            jax.ShapeDtypeStruct((TILE, length), F32),
        ],
        in_specs=[vmem()] * 5,
        out_specs=[vmem()] * 2,
        scratch_shapes=[pltpu.VMEM((length, 128), F32), pltpu.VMEM((length, 128), F32)],
        compiler_params=params(),
        name="self_backward",
    )(qkv, do1, table, doc_row, doc_col)
    head_grad = pl.pallas_call(
        head_weight_kernel,
        out_shape=jax.ShapeDtypeStruct((fs, span * 3 // 2, 128), BF16),
        in_specs=[vmem()] * 2,
        out_specs=vmem(),
        compiler_params=params(),
        name="head_weight",
    )(n_all, dqkv)
    if fs == 2:
        kept = lax.dynamic_index_in_dim(head_grad, shard, 0, keepdims=False)
        sent = lax.dynamic_index_in_dim(head_grad, 1 - shard, 0, keepdims=False)
        head_sum = (kept.astype(F32) + swap_fs(sent).astype(F32)).astype(BF16)
    else:
        head_sum = lax.psum_scatter(head_grad, "fsdp", scatter_dimension=0, tiled=False)
    head_pieces = gather_all(head_sum[None])
    head_places = place_of[jnp.arange(heads) * copies]
    grad_query_self, grad_key_self, grad_value_self = pl.pallas_call(
        head_spread_kernel,
        out_shape=[jax.ShapeDtypeStruct((span, width), F32)] * 3,
        in_specs=[smem(), vmem()],
        out_specs=[vmem()] * 3,
        compiler_params=params(),
        name="head_spread",
    )(head_places, head_pieces)

    table_sums = jnp.sum(bucket_sums(edges, table_grad, bias_all.shape[0]), axis=1)

    own_d = lax.all_to_all(dqkv.reshape(dp, rows, 384), "dp", 0, 0, tiled=True)[::copies]
    own_d = own_d.reshape(heads, rows, 3, 2, 64).transpose(2, 3, 1, 0, 4).reshape(3, tokens, width)
    first = whole_rows(jnp.stack([query_self, key_self, value_self]))
    dn1 = sum(dot_t(own_d[at], first[at]) for at in range(3))
    back, dc_one = norm_back(x.astype(F32).reshape(tokens, width), gain_one, dn1)
    grad_inputs = gx1 + back

    own_dkv = lax.psum_scatter(dkv, "dp", scatter_dimension=0, tiled=False)
    own_dkv = own_dkv.reshape(micro_count * part, 2 * width)
    grad_encoded = dot_t(own_dkv[:, :width], cross_kv[0]) + dot_t(own_dkv[:, width:], cross_kv[1])

    chips = dp // 2
    half = span // 2

    def group_left(values):
        if fs == 2:
            kept = lax.dynamic_slice_in_dim(values, shard * span, span, axis=1)
            sent = lax.dynamic_slice_in_dim(values, (1 - shard) * span, span, axis=1)
            return jnp.concatenate([kept, swap_fs(sent)], axis=0)
        return lax.all_to_all(values, "fsdp", 1, 0, tiled=True)

    def chip_left(values, size):
        kept = lax.dynamic_slice_in_dim(values, core * size, size, axis=1)
        sent = lax.dynamic_slice_in_dim(values, (1 - core) * size, size, axis=1)
        return jnp.concatenate([kept, swap_dp(sent, 1)], axis=0)

    def chip_all(values):
        return jnp.concatenate([values, swap_dp(values, 1)], axis=0)

    def in_order(values):
        values = lax.all_gather(values, "dp", axis=0, tiled=True)
        return values.reshape((chips, 2) + values.shape[1:]).astype(F32)

    def row_block(j):
        return (j % 2) * chips + j // 2

    def token_weights(lefts, rights):
        left = jnp.concatenate([group_left(v) for v in lefts], axis=0)
        left = chip_left(left, half)
        right = chip_all(both_tokens(jnp.concatenate(rights, axis=1)))
        group = left.shape[0] // 2 // len(lefts)
        totals = []
        at = 0
        for place, value in enumerate(rights):
            low = left[place * group : (place + 1) * group]
            high = left[(len(lefts) + place) * group : (len(lefts) + place + 1) * group]
            totals.append(
                t_dot(jnp.concatenate([low, high], axis=0), right[:, at : at + value.shape[1]])
            )
            at += value.shape[1]
        made = jnp.stack([total.astype(BF16).reshape(chips, -1, total.shape[1]) for total in totals], axis=1)
        made = sum_chips(made)
        if made.shape[2] % 8:
            pieces = in_order(made).transpose(2, 1, 0, 3, 4)
            return [piece.reshape(span, -1) for piece in pieces]
        pieces = gather_all(made)
        return spread(
            source,
            pieces[:, None],
            [(span, pieces.shape[-1])] * len(lefts),
            lambda t, h, where: (row_block(where[t]), 0),
        )

    grad_query_cross, grad_output_cross, grad_output_self = token_weights(
        [n2, o2, o1], [dq2, gx2b, gx1b]
    )
    (grad_kv_cross,) = token_weights([e.reshape(micro_count * part, width)], [own_dkv])
    grad_key_cross, grad_value_cross = grad_kv_cross[:, :width], grad_kv_cross[:, width:]

    picked = n_group.reshape(n_group.shape[0], fs, 2, half)
    n_mine = lax.dynamic_index_in_dim(picked, core, 2, keepdims=False)
    n_sent = lax.dynamic_index_in_dim(picked, 1 - core, 2, keepdims=False)
    n_chip = jnp.concatenate([n_mine, swap_dp(n_sent, 1)], axis=0)
    back_chip = chip_all(jnp.concatenate([da, db, hid], axis=1))
    g_chip = chip_left(g_group, width // 2)
    n_chip = n_chip.reshape(n_chip.shape[0], fs * half)
    made = t_dot(n_chip, back_chip[:, : 2 * hidden]).astype(BF16)
    made = made.reshape(fs, half, 2, hidden).transpose(0, 2, 1, 3)
    if fs == 2:
        kept = lax.dynamic_index_in_dim(made, shard, 0, keepdims=False)
        sent = lax.dynamic_index_in_dim(made, 1 - shard, 0, keepdims=False)
        halves = jnp.stack([kept, swap_fs(sent)])
    else:
        halves = lax.all_to_all(made, "fsdp", 0, 0, tiled=True)
    halves = halves.reshape(fs, 2, chips, half // chips, hidden).transpose(2, 0, 1, 3, 4)
    halves = sum_chips(halves)
    dense_where = jnp.concatenate([source, jnp.where(fs == 2, shard, 0)[None].astype(jnp.int32)])
    if halves.shape[3] % 8 or hidden % 128:
        ordered = in_order(halves).transpose(3, 1, 0, 4, 2, 5).reshape(2, span, fs * hidden)
        grad_dense_gate, grad_dense_up = ordered[0], ordered[1]
    else:
        grad_dense_gate, grad_dense_up = spread(
            dense_where,
            gather_all(halves),
            [(span, fs * hidden)] * 2,
            lambda t, h, where: (row_block(where[t]), h ^ where[dp]),
        )
    down = t_dot(back_chip[:, 2 * hidden :], g_chip).astype(BF16)
    down = down.reshape(chips, hidden // chips, width // 2)
    down = sum_chips(down)
    if down.shape[1] % 8:
        grad_dense_down = in_order(down).transpose(0, 2, 1, 3).reshape(hidden, width)
    else:
        (grad_dense_down,) = spread(
            source,
            gather_all(down)[:, None, None],
            [(hidden, width)],
            lambda t, h, where: (where[t] // 2, where[t] % 2),
        )

    column = (jnp.arange(heads) == head) & (me % copies == 0)
    bias_row = jnp.where(column[None, :], table_sums[:, None], 0.0).reshape(1, -1)
    bias_row = jnp.pad(bias_row, ((0, 0), (0, width - bias_row.shape[1])))
    sums = lax.psum(jnp.concatenate([dc_one, dc_two, bias_row], axis=0), ("dp", "fsdp"))
    own = lax.dynamic_slice_in_dim(sums[:3], shard * span, span, axis=1)
    grad_bias = sums[3, : bias_all.size].reshape(bias_all.shape)
    grad_bias = lax.dynamic_slice_in_dim(
        grad_bias, shard * position_bias.shape[0], position_bias.shape[0], axis=0
    )
    shape = (micro_count, 1, rows, width)
    return (
        outputs.reshape(shape),
        grad_inputs.reshape(shape),
        grad_encoded.reshape(micro_count, 1, part, width),
        own[0],
        grad_query_self,
        grad_key_self,
        grad_value_self,
        grad_output_self,
        grad_bias,
        own[2],
        grad_query_cross,
        grad_key_cross,
        grad_value_cross,
        grad_output_cross,
        own[1],
        grad_dense_gate,
        grad_dense_up,
        grad_dense_down,
    )


def solution(mesh):
    matrix = P("fsdp", None)
    token = P(None, "fsdp", "dp", None)
    weights = (
        (P("fsdp"),)
        + (matrix,) * 5
        + (P("fsdp"),)
        + (matrix,) * 4
        + (P("fsdp"),)
        + (matrix,) * 3
    )
    return jax.shard_map(
        per_device,
        mesh=mesh,
        in_specs=(token,) * 3 + (P(None, "fsdp", None), P()) + weights,
        out_specs=(token,) * 3 + weights,
        check_vma=False,
    )
```

```python
import functools

import jax
import jax.numpy as jnp
from jax import lax
from jax.experimental import pallas as pl
from jax.experimental.pallas import tpu as pltpu
from jax.sharding import PartitionSpec as P

EPS = 1e-06
NEGATIVE = -1e30
TILE = 256
F32 = jnp.float32
BF16 = jnp.bfloat16
VMEM_LIMIT = 56 * 1024 * 1024


def vmem():
    return pl.BlockSpec(memory_space=pltpu.VMEM)


def smem():
    return pl.BlockSpec(memory_space=pltpu.SMEM)


def params(limit=VMEM_LIMIT):
    return pltpu.CompilerParams(vmem_limit_bytes=limit)


def cost(microseconds):
    return pl.CostEstimate(
        flops=int(microseconds * 1.15e9),
        bytes_accessed=int(microseconds * 3.69e6),
        transcendentals=0,
    )


def aligned(start, size):
    return pl.ds(pl.multiple_of(start, size), size)


def dot(left, right):
    return jnp.dot(left, right, preferred_element_type=F32)


def dot_t(left, right):
    return lax.dot_general(left, right, (((1,), (1,)), ((), ())), preferred_element_type=F32)


def t_dot(left, right):
    return lax.dot_general(left, right, (((0,), (0,)), ((), ())), preferred_element_type=F32)


def norm_rows(values, gain):
    return values * lax.rsqrt(jnp.mean(values * values, axis=-1, keepdims=True) + EPS) * gain


def norm_back(values, gain, grad):
    r = lax.rsqrt(jnp.mean(values * values, axis=-1, keepdims=True) + EPS)
    scaled = grad * gain
    inner = jnp.mean(scaled * values, axis=-1, keepdims=True)
    back = r * scaled - values * (r * r * r * inner)
    return back, jnp.sum(grad * (values * r), axis=0, keepdims=True)


def low_lanes(rows):
    return lax.broadcasted_iota(jnp.int32, (rows, 128), 1) < 64


def pair_up(first, second):
    lane = low_lanes(first.shape[0])
    low = jnp.where(lane, first, pltpu.roll(second, 64, 1))
    high = jnp.where(lane, pltpu.roll(first, 64, 1), second)
    return low, high


def keep_half(values, half):
    lane = low_lanes(values.shape[0])
    return jnp.where(lane if half == 0 else ~lane, values, jnp.zeros_like(values))


def softmax_rows(scores):
    top = jnp.max(scores, axis=-1, keepdims=True)
    raised = jnp.exp(scores - top)
    return raised * (1.0 / jnp.sum(raised, axis=-1, keepdims=True))


def table_kernel(edge_ref, value_ref, out_ref):
    rows, length = out_ref.shape
    bucket_count = value_ref.shape[0]
    for start in range(0, length, TILE):
        place = (rows, TILE)
        apart = (
            lax.broadcasted_iota(jnp.int32, place, 0)
            - lax.broadcasted_iota(jnp.int32, place, 1)
            + (length - rows - start)
        )
        value = jnp.full(place, value_ref[0], F32)
        for bucket in range(1, bucket_count):
            value = jnp.where(apart >= edge_ref[bucket], value_ref[bucket], value)
        out_ref[:, start : start + TILE] = jnp.where(apart >= 0, value, NEGATIVE)


def bias_table(edges, values, length):
    return pl.pallas_call(
        table_kernel,
        out_shape=jax.ShapeDtypeStruct((TILE, length), F32),
        in_specs=[smem(), smem()],
        out_specs=vmem(),
        cost_estimate=cost(4),
        name="bias_table",
    )(edges, values)


def bucket_kernel(edge_ref, grad_ref, out_ref):
    rows, length = grad_ref.shape
    bucket_count = out_ref.shape[0]
    above = [jnp.zeros((8, TILE), F32) for _ in range(bucket_count)]
    for start in range(0, length, TILE):
        for row in range(0, rows, 8):
            place = (8, TILE)
            apart = (
                lax.broadcasted_iota(jnp.int32, place, 0)
                - lax.broadcasted_iota(jnp.int32, place, 1)
                + (length - rows - start + row)
            )
            tile = grad_ref[row : row + 8, start : start + TILE]
            for bucket in range(bucket_count):
                above[bucket] = above[bucket] + jnp.where(apart >= edge_ref[bucket], tile, 0.0)
    for bucket in range(bucket_count):
        rest = above[bucket + 1] if bucket + 1 < bucket_count else 0.0
        part = jnp.sum(above[bucket] - rest, axis=0, keepdims=True)
        out_ref[bucket : bucket + 1, :] = part[:, :128] + part[:, 128:]


def bucket_sums(edges, grad, bucket_count):
    return pl.pallas_call(
        bucket_kernel,
        out_shape=jax.ShapeDtypeStruct((bucket_count, 128), F32),
        in_specs=[smem(), vmem()],
        out_specs=vmem(),
        cost_estimate=cost(7),
        name="bucket_sums",
    )(edges, grad)


def times(x_ref, starts_ref, pieces):
    if len(pieces) == 1:
        return dot(x_ref[...], pieces[0])
    total = None
    for place, piece in enumerate(pieces):
        rows = piece.shape[0]
        part = dot(x_ref[:, aligned(starts_ref[place], rows)], piece)
        total = part if total is None else total + part
    return total


def times_back(out_ref, starts_ref, terms):
    for place in range(len(terms[0][1])):
        total = sum(dot_t(d, pieces[place]) for d, pieces in terms)
        rows = terms[0][1][place].shape[0]
        if len(terms[0][1]) == 1:
            out_ref[...] = total
        else:
            out_ref[:, aligned(starts_ref[place], rows)] = total


def pieces_of(own_ref, more, index):
    return [own_ref[...]] + [ref[index] for ref in more]


def self_scores(q, k, table, doc_col, doc_row):
    scores = dot_t(q, k) + table
    return jnp.where(doc_col == doc_row, scores, NEGATIVE)


def self_forward_kernel(groups, source_ref, *refs):
    x_refs = refs[:groups]
    gain_ref, w_ref, table_ref, doc_row_ref, doc_col_ref, n_ref, qkv_ref, o_ref = refs[groups:]
    count, _, rows, width = x_refs[0].shape
    length = groups * count * rows
    lane = lax.broadcasted_iota(jnp.int32, (rows, 384), 1) % 128 < 64
    together = min(TILE // rows, count)
    for place, x_ref in enumerate(x_refs):
        for first in range(0, count, together):
            parts = []
            for inner in range(first, first + together):
                x = x_ref[inner].astype(F32).reshape(2 * rows, width)
                n = norm_rows(x, gain_ref[...]).astype(BF16)
                n_ref[source_ref[place * count + inner]] = n.reshape(2, rows, width)
                parts.append(n)
            made = dot(jnp.concatenate(parts, axis=0), w_ref[...])
            for inner in range(together):
                at = 2 * rows * inner
                picked = jnp.where(lane, made[at : at + rows], made[at + rows : at + 2 * rows])
                own = source_ref[place * count + first + inner]
                qkv_ref[aligned(own * rows, rows), :] = picked.astype(BF16)
    for block in range(length // TILE):
        start, stop = block * TILE, (block + 1) * TILE
        table = table_ref[:, length - stop :]
        q = qkv_ref[start:stop, 0:128]
        k = qkv_ref[:stop, 128:256]
        v = qkv_ref[:stop, 256:384]
        mixed = []
        for half in range(2):
            scores = self_scores(
                keep_half(q, half),
                k,
                table,
                doc_col_ref[half, start:stop, :],
                doc_row_ref[half : half + 1, :stop],
            )
            mixed.append(dot(softmax_rows(scores).astype(BF16), v))
        o_ref[start:stop, :] = jnp.where(low_lanes(TILE), mixed[0], mixed[1]).astype(BF16)


def self_backward_kernel(
    qkv_ref, do_ref, table_ref, doc_row_ref, doc_col_ref, dqkv_ref, grad_ref, dk_ref, dv_ref
):
    length = qkv_ref.shape[0]
    grad_ref[...] = jnp.zeros_like(grad_ref)
    dk_ref[...] = jnp.zeros_like(dk_ref)
    dv_ref[...] = jnp.zeros_like(dv_ref)
    for block in range(length // TILE):
        start, count = block * TILE, (block + 1) * TILE
        table = table_ref[:, length - count :]
        k = qkv_ref[:count, 128:256]
        v = qkv_ref[:count, 256:384]
        made = []
        for half in range(2):
            q = keep_half(qkv_ref[start:count, 0:128], half)
            do = keep_half(do_ref[start:count, :], half)
            p = softmax_rows(
                self_scores(
                    q,
                    k,
                    table,
                    doc_col_ref[half, start:count, :],
                    doc_row_ref[half : half + 1, :count],
                )
            )
            dp = dot_t(do, v)
            ds = (p * (dp - jnp.sum(p * dp, axis=-1, keepdims=True))).astype(BF16)
            grad_ref[:, length - count :] += ds.astype(F32)
            made.append(dot(ds, k))
            dk_ref[:count, :] += t_dot(ds, q)
            dv_ref[:count, :] += t_dot(p.astype(BF16), do)
        dq = jnp.where(low_lanes(TILE), made[0], made[1])
        dqkv_ref[start:count, 0:128] = dq.astype(BF16)
    dqkv_ref[:, 128:256] = dk_ref[...].astype(BF16)
    dqkv_ref[:, 256:384] = dv_ref[...].astype(BF16)


def head_weight_kernel(n_ref, d_ref, out_ref):
    blocks, _, rows, width = n_ref.shape
    shards = out_ref.shape[0]
    span = width // shards
    lane = lax.broadcasted_iota(jnp.int32, (blocks * rows, 384), 1) % 128 < 64
    d = d_ref[...]
    zero = jnp.zeros_like(d)
    right = [jnp.where(lane, d, zero), jnp.where(lane, zero, d)]
    half = span // 2
    for shard in range(shards):
        total = jnp.zeros((span, 384), F32)
        for micro in range(2):
            left = n_ref[:, micro, :, shard * span : (shard + 1) * span]
            total = total + t_dot(left.reshape(blocks * rows, span), right[micro])
        q, k, v = (
            total[:, at : at + 128] + pltpu.roll(total[:, at : at + 128], 64, 1)
            for at in (0, 128, 256)
        )
        out_ref[shard, :span, :] = jnp.where(low_lanes(span), q, k).astype(BF16)
        out_ref[shard, span:, :] = jnp.where(low_lanes(half), v[:half], v[half:]).astype(BF16)


def cross_kv_kernel(split, starts_ref, e_ref, wk_ref, wv_ref, *refs):
    more, (ke_ref, ve_ref) = refs[:split], refs[split:]
    blocks, _, part, _ = e_ref.shape
    for index, (own_ref, out_ref) in enumerate(((wk_ref, ke_ref), (wv_ref, ve_ref)), 3):
        total = None
        pieces = pieces_of(own_ref, more, index)
        for place, piece in enumerate(pieces):
            rows = piece.shape[0]
            if split:
                left = e_ref[:, 0, :, aligned(starts_ref[place], rows)]
            else:
                left = e_ref[:, 0]
            made = dot(left.reshape(blocks * part, rows), piece)
            total = made if total is None else total + made
        out_ref[0] = total.astype(BF16)


def cross_kv(starts, e_all, wk, wv, more):
    blocks, micro, part, width = e_all.shape
    whole = lambda array: pl.BlockSpec(array.shape, lambda m, s: (0,) * array.ndim)
    out = pl.BlockSpec((1, blocks * part, width), lambda m, s: (m, 0, 0))
    return pl.pallas_call(
        functools.partial(cross_kv_kernel, len(more)),
        grid_spec=pltpu.PrefetchScalarGridSpec(
            num_scalar_prefetch=1,
            grid=(micro,),
            in_specs=[pl.BlockSpec((blocks, 1, part, width), lambda m, s: (0, m, 0, 0))]
            + [whole(array) for array in (wk, wv, *more)],
            out_specs=[out, out],
        ),
        out_shape=[jax.ShapeDtypeStruct((micro, blocks * part, width), BF16)] * 2,
        compiler_params=params(),
        cost_estimate=cost(8),
        name="cross_kv",
    )(starts, e_all, wk, wv, *more)


def mid_forward_kernel(split, starts_ref, o1_ref, x_ref, gain_ref, ke_ref, ve_ref, wo, wq, wc, *refs):
    more = refs[:split]
    left_ref, x1_ref, q2_ref, x2_ref, n3_ref, o1c_ref, n2_ref, o2_ref = refs[split:]
    heads, rows, _ = o1_ref.shape
    width = x_ref.shape[-1]
    for pair in range(heads // 2):
        at = pair * 128
        low, high = pair_up(o1_ref[2 * pair].astype(F32), o1_ref[2 * pair + 1].astype(F32))
        o1c_ref[0:rows, at : at + 128] = low.astype(BF16)
        o1c_ref[rows : 2 * rows, at : at + 128] = high.astype(BF16)
    x = x_ref[...].astype(F32).reshape(2 * rows, width)
    x1 = x + times(o1c_ref, starts_ref, pieces_of(wo, more, 0))
    x1_ref[...] = x1
    n2_ref[...] = norm_rows(x1, gain_ref[1:2]).astype(BF16)
    q2_ref[...] = times(n2_ref, starts_ref, pieces_of(wq, more, 1)).astype(BF16)
    for micro in range(2):
        for pair in range(heads // 2):
            at = pair * 128
            span = slice(micro * rows, (micro + 1) * rows)
            q = q2_ref[span, at : at + 128]
            both = jnp.concatenate([keep_half(q, 0), keep_half(q, 1)], axis=0)
            p = softmax_rows(dot_t(both, ke_ref[micro, :, at : at + 128]))
            o = dot(p.astype(BF16), ve_ref[micro, :, at : at + 128])
            o2_ref[span, at : at + 128] = jnp.where(
                low_lanes(rows), o[:rows], o[rows:]
            ).astype(BF16)
    x2 = x1 + times(o2_ref, starts_ref, pieces_of(wc, more, 2))
    x2_ref[...] = x2
    n3_ref[...] = norm_rows(x2, gain_ref[2:3]).astype(BF16)
    left_ref[0] = o2_ref[...]
    left_ref[1] = n2_ref[...]
    left_ref[2] = o1c_ref[...]


def mid_backward_kernel(
    split, starts_ref, g_ref, dn3_ref, more_ref, x1_ref, x2_ref, gain_ref, q2_ref, ke_ref, ve_ref,
    wo, wq, wc, *refs
):
    more = refs[:split]
    right_ref, gx1_ref, do1_ref, dkv_ref, dc_ref, back_ref, do2_ref, dq2_ref = refs[split:]
    heads, rows, _ = do1_ref.shape
    blocks, micros, part = dkv_ref.shape[1:4]
    width = x1_ref.shape[-1]
    dn3 = dn3_ref[...] + more_ref[...].astype(F32)
    back, dc = norm_back(x2_ref[...], gain_ref[2:3], dn3)
    dc_ref[0:1, :] = dc
    gx2 = g_ref[...].astype(F32).reshape(2 * rows, width) + back
    gx2b = gx2.astype(BF16)
    right_ref[:, 0:width] = gx2b
    times_back(back_ref, starts_ref, [(gx2b, pieces_of(wc, more, 2))])
    do2_ref[...] = back_ref[...].astype(BF16)
    for micro in range(2):
        for pair in range(heads // 2):
            at = pair * 128
            span = slice(micro * rows, (micro + 1) * rows)
            q = q2_ref[span, at : at + 128]
            do = do2_ref[span, at : at + 128]
            q = jnp.concatenate([keep_half(q, 0), keep_half(q, 1)], axis=0)
            do = jnp.concatenate([keep_half(do, 0), keep_half(do, 1)], axis=0)
            k = ke_ref[micro, :, at : at + 128]
            v = ve_ref[micro, :, at : at + 128]
            p = softmax_rows(dot_t(q, k))
            dp = dot_t(do, v)
            ds = (p * (dp - jnp.sum(p * dp, axis=-1, keepdims=True))).astype(BF16)
            dq = dot(ds, k)
            dq2_ref[span, at : at + 128] = jnp.where(
                low_lanes(rows), dq[:rows], dq[rows:]
            ).astype(BF16)
            low, high = pair_up(t_dot(ds, q), t_dot(p.astype(BF16), do))
            dkv_ref[2 * pair, :, micro] = low.astype(BF16).reshape(blocks, part, 128)
            dkv_ref[2 * pair + 1, :, micro] = high.astype(BF16).reshape(blocks, part, 128)
    right_ref[:, width : 2 * width] = dq2_ref[...]
    times_back(back_ref, starts_ref, [(dq2_ref[...], pieces_of(wq, more, 1))])
    back, dc = norm_back(x1_ref[...], gain_ref[1:2], back_ref[...])
    dc_ref[1:2, :] = dc
    gx1 = gx2 + back
    gx1_ref[...] = gx1
    gx1b = gx1.astype(BF16)
    right_ref[:, 2 * width :] = gx1b
    times_back(back_ref, starts_ref, [(gx1b, pieces_of(wo, more, 0))])
    for pair in range(heads // 2):
        at = pair * 128
        do1 = back_ref[:, at : at + 128].astype(BF16).astype(F32)
        low, high = pair_up(do1[:rows], do1[rows:])
        do1_ref[2 * pair] = low.astype(BF16)
        do1_ref[2 * pair + 1] = high.astype(BF16)


def input_grad_kernel(split, starts_ref, d_ref, x_ref, gain_ref, gx1_ref, wq, wk, wv, *refs):
    more = refs[:split]
    out_ref, dc_ref, all_ref, back_ref = refs[split:]
    heads, rows, _ = d_ref.shape
    width = x_ref.shape[-1]
    for kind in range(3):
        for pair in range(heads // 2):
            lanes = slice(kind * 128, (kind + 1) * 128)
            low, high = pair_up(
                d_ref[2 * pair, :, lanes].astype(F32), d_ref[2 * pair + 1, :, lanes].astype(F32)
            )
            at = kind * width + pair * 128
            all_ref[0:rows, at : at + 128] = low.astype(BF16)
            all_ref[rows : 2 * rows, at : at + 128] = high.astype(BF16)
    terms = [
        (all_ref[:, kind * width : (kind + 1) * width], pieces_of(own, more, kind))
        for kind, own in enumerate((wq, wk, wv))
    ]
    times_back(back_ref, starts_ref, terms)
    x = x_ref[...].astype(F32).reshape(2 * rows, width)
    back, dc = norm_back(x, gain_ref[0:1], back_ref[...])
    dc_ref[...] = dc
    out_ref[...] = gx1_ref[...] + back


def encoder_grad_kernel(split, starts_ref, d_ref, wk, wv, *refs):
    more = refs[:split]
    out_ref, k_ref, v_ref = refs[split:]
    for pair in range(d_ref.shape[0] // 2):
        at = pair * 128
        low, high = pair_up(d_ref[2 * pair].astype(F32), d_ref[2 * pair + 1].astype(F32))
        k_ref[:, at : at + 128] = low.astype(BF16)
        v_ref[:, at : at + 128] = high.astype(BF16)
    terms = [(k_ref[...], pieces_of(wk, more, 3)), (v_ref[...], pieces_of(wv, more, 4))]
    times_back(out_ref, starts_ref, terms)


def cross_head_weight_kernel(e_ref, d_ref, out_ref):
    blocks, micro, part, width = e_ref.shape
    shards, span, _ = out_ref.shape
    for shard in range(shards):
        left = e_ref[:, :, :, shard * span : (shard + 1) * span]
        left = left.reshape(blocks * micro * part, span)
        out_ref[shard] = t_dot(left, d_ref[...]).astype(BF16)


def dense_kernel(split, starts_ref, n_ref, g_ref, wg, wu, wd_ref, *refs):
    more = refs[:split]
    back_ref, y_ref, ylow_ref, d_ref, dlow_ref = refs[split:]
    hidden = wd_ref.shape[0]
    gate, up = pieces_of(wg, more, 0), pieces_of(wu, more, 1)
    a = times(n_ref, starts_ref, gate)
    b = times(n_ref, starts_ref, up)
    scale = 0.7978845608028654
    cubed = 0.044715
    inner = jnp.tanh(scale * (a + cubed * (a * a * a)))
    gelu = 0.5 * a * (1.0 + inner)
    slope = 0.5 * (1.0 + inner) + 0.5 * a * (1.0 - inner * inner) * (
        scale * (1.0 + 3.0 * cubed * (a * a))
    )
    hid = (gelu * b).astype(BF16)
    dh = dot_t(g_ref[...], wd_ref[...])
    da = (dh * b * slope).astype(BF16)
    db = (dh * gelu).astype(BF16)
    times_back(d_ref, starts_ref, [(da, gate), (db, up)])
    dlow_ref[...] = d_ref[...].astype(BF16)
    y = dot(hid, wd_ref[...])
    y_ref[...] = y
    ylow_ref[...] = y.astype(BF16)
    back_ref[:, 0:hidden] = da
    back_ref[:, hidden : 2 * hidden] = db
    back_ref[:, 2 * hidden : 3 * hidden] = hid
    if more:
        shard, other = starts_ref[len(more) + 1], 1 - starts_ref[len(more) + 2]
        put_features(back_ref, 3 * hidden, n_ref, g_ref, shard, other)


def put_features(out_ref, at, n_ref, g_ref, shard, core):
    quarter = n_ref.shape[1] // 4
    for side, place in enumerate((2 * shard + core, 2 * (1 - shard) + core)):
        lanes = slice(at + side * quarter, at + (side + 1) * quarter)
        out_ref[:, lanes] = n_ref[:, aligned(place * quarter, quarter)]
    lanes = slice(at + 2 * quarter, at + 4 * quarter)
    out_ref[:, lanes] = g_ref[:, aligned(core * 2 * quarter, 2 * quarter)]


def dense_layer(starts, n, g, wg, wu, wd, more, step):
    count, width = n.shape
    hidden = wd.shape[0]
    which = starts.shape[0] - 2
    back = 3 * hidden + (width if more else 0)
    row = lambda size: pl.BlockSpec((step, size), lambda i, s: (i, 0))
    whole = lambda array: pl.BlockSpec(array.shape, lambda i, s: (0,) * array.ndim)
    column = pl.BlockSpec((wg.shape[0], hidden), lambda i, s: (0, s[which]))
    made = lambda size, kind: jax.ShapeDtypeStruct((count, size), kind)
    return pl.pallas_call(
        functools.partial(dense_kernel, len(more)),
        grid_spec=pltpu.PrefetchScalarGridSpec(
            num_scalar_prefetch=1,
            grid=(count // step,),
            in_specs=[row(width), row(width), column, column, whole(wd)]
            + [whole(array) for array in more],
            out_specs=[row(back)] + [row(width)] * 4,
        ),
        out_shape=[made(back, BF16)]
        + [made(width, F32), made(width, BF16), made(width, F32), made(width, BF16)],
        compiler_params=params(),
        cost_estimate=cost(13),
        name="dense_layer",
    )(starts, n, g, wg, wu, wd, *more)


def put_chunk(ref, slot, at, value):
    rows, width = value.shape
    for block in range(width // 128):
        ref[slot, at + block * rows : at + (block + 1) * rows, :] = value[
            :, block * 128 : (block + 1) * 128
        ].astype(BF16)


def take_chunk(ref, slot, at, rows, width):
    return jnp.concatenate(
        [
            ref[slot, at + block * rows : at + (block + 1) * rows, :].astype(F32)
            for block in range(width // 128)
        ],
        axis=1,
    )


def put_all(scratch_ref, value, chip, chunk_refs, at):
    count = 2 * chunk_refs[0].shape[0]
    rows = value.shape[0] // count
    scratch_ref[: value.shape[0], : value.shape[1]] = value
    for r in range(count):
        chunk = scratch_ref[aligned((chip ^ r) * rows, rows), : value.shape[1]]
        put_chunk(chunk_refs[r // (count // 2)], r % (count // 2), at, chunk)


def dense_weight_kernel(
    where_ref, n0_ref, n1_ref, g0_ref, g1_ref, own0_ref, own1_ref, mate0_ref, mate1_ref, keep_ref,
    send_ref, down_keep_ref, down_send_ref, far_keep_ref, far_send_ref, scratch_ref, left_ref
):
    tokens, width = n0_ref.shape
    hidden = (own0_ref.shape[1] - width) // 3
    quarter = width // 4
    at = keep_ref.shape[1] // 2
    x_chip, core, shard, z_chip = where_ref[0], where_ref[1], where_ref[2], where_ref[3]
    put_features(left_ref.at[:tokens], 0, n0_ref, g0_ref, shard, core)
    put_features(left_ref.at[tokens : 2 * tokens], 0, n1_ref, g1_ref, shard, core)
    left_ref[2 * tokens : 3 * tokens, :] = mate0_ref[:, 3 * hidden :]
    left_ref[3 * tokens :, :] = mate1_ref[:, 3 * hidden :]

    def whole(kind):
        span = slice(kind * hidden, (kind + 1) * hidden)
        refs = (own0_ref, own1_ref, mate0_ref, mate1_ref)
        return jnp.concatenate([ref[:, span] for ref in refs], axis=0)

    for kind in range(2):
        right = whole(kind)
        for side, (chip, refs) in enumerate(
            ((z_chip, (keep_ref, send_ref)), (x_chip, (far_keep_ref, far_send_ref)))
        ):
            value = t_dot(left_ref[:, side * quarter : (side + 1) * quarter], right)
            put_all(scratch_ref, value, chip, refs, kind * at)
    value = t_dot(whole(2), left_ref[:, 2 * quarter :])
    put_all(scratch_ref, value, x_chip, (down_keep_ref, down_send_ref), 0)


def token_weight_kernel(
    where_ref, left_ref, left_mate_ref, r0_ref, r1_ref, r2_ref, r3_ref, keep_ref, send_ref,
    scratch_ref
):
    width = r0_ref.shape[1] // 3
    tokens = r0_ref.shape[0]
    half = left_ref.shape[1] // 3
    rows = half // (2 * keep_ref.shape[0])
    for kind in range(3):
        span = slice(kind * width, (kind + 1) * width)
        lanes = slice(kind * half, (kind + 1) * half)
        value = t_dot(left_ref[:tokens, lanes], r0_ref[:, span])
        value = value + t_dot(left_ref[tokens:, lanes], r1_ref[:, span])
        value = value + t_dot(left_mate_ref[:tokens, lanes], r2_ref[:, span])
        value = value + t_dot(left_mate_ref[tokens:, lanes], r3_ref[:, span])
        put_all(scratch_ref, value, where_ref[0], (keep_ref, send_ref), kind * rows * width // 128)


def chunk_weights(kernel, where, operands, counts, chips, scratches, length, name):
    shapes = []
    for count in counts:
        shapes += [jax.ShapeDtypeStruct((chips // 2, count, 128), BF16)] * 2
    return pl.pallas_call(
        kernel,
        out_shape=shapes,
        in_specs=[smem()] + [vmem()] * len(operands),
        out_specs=[vmem()] * len(shapes),
        scratch_shapes=scratches,
        compiler_params=params(),
        cost_estimate=cost(length),
        name=name,
    )(where, *operands)


def spread_gate_kernel(where_ref, low, high, far_low, far_high, out_ref, other_ref):
    x_chip, core, shard, z_chip = where_ref[0], where_ref[1], where_ref[2], where_ref[3]
    rows = out_ref.shape[2] // low.shape[0]
    hidden = out_ref.shape[3] // 2
    at = rows * hidden // 128
    count = low.shape[0]
    for side, (chip, refs) in enumerate(((z_chip, (low, high)), (x_chip, (far_low, far_high)))):
        for cores, ref in enumerate(refs):
            for r in range(count):
                place = aligned(((chip ^ r) % count) * rows, rows)
                lanes = aligned((shard ^ side) * hidden, hidden)
                out_ref[core ^ cores, 0, place, lanes] = take_chunk(ref, r, 0, rows, hidden)
                other_ref[core ^ cores, 0, place, lanes] = take_chunk(ref, r, at, rows, hidden)


def spread_gate(where, low, high, far_low, far_high, hidden, span):
    chips, total, _ = low.shape
    count = chips // 2
    rows = span // (2 * chips)
    into = lambda at: pl.BlockSpec(
        (count, total, 128), lambda b, where: (b ^ (where[at] // count), 0, 0)
    )
    out = pl.BlockSpec((2, 1, count * rows, 2 * hidden), lambda b, where: (0, b, 0, 0))
    made = pl.pallas_call(
        spread_gate_kernel,
        grid_spec=pltpu.PrefetchScalarGridSpec(
            num_scalar_prefetch=1,
            grid=(2,),
            in_specs=[into(3), into(3), into(0), into(0)],
            out_specs=[out, out],
        ),
        out_shape=[jax.ShapeDtypeStruct((2, 2, count * rows, 2 * hidden), F32)] * 2,
        compiler_params=params(),
        cost_estimate=cost(8),
        name="spread_gate",
    )(where, low, high, far_low, far_high)
    return [array.reshape(span, 2 * hidden) for array in made]


def spread_down_kernel(where_ref, low, high, out_ref):
    chip, core = where_ref[0], where_ref[1]
    count = low.shape[0]
    rows = out_ref.shape[0] // count
    width = out_ref.shape[1] // 2
    for cores, ref in enumerate((low, high)):
        for r in range(count):
            place = aligned(((chip ^ r) % count) * rows, rows)
            lanes = aligned((core ^ cores) * width, width)
            out_ref[place, lanes] = take_chunk(ref, r, 0, rows, width)


def spread_down(where, low, high, hidden, width):
    chips, total, _ = low.shape
    count = chips // 2
    into = pl.BlockSpec((count, total, 128), lambda b, where: (b ^ (where[0] // count), 0, 0))
    return pl.pallas_call(
        spread_down_kernel,
        grid_spec=pltpu.PrefetchScalarGridSpec(
            num_scalar_prefetch=1,
            grid=(2,),
            in_specs=[into] * 2,
            out_specs=pl.BlockSpec((hidden // 2, width), lambda b, where: (b, 0)),
        ),
        out_shape=jax.ShapeDtypeStruct((hidden, width), F32),
        compiler_params=params(),
        cost_estimate=cost(5),
        name="spread_down",
    )(where, low, high)


def spread_token_kernel(where_ref, low, high, *out_refs):
    chip, core = where_ref[0], where_ref[1]
    count = low.shape[0]
    rows = out_refs[0].shape[2] // count
    width = out_refs[0].shape[3]
    for cores, ref in enumerate((low, high)):
        for r in range(count):
            place = aligned(((chip ^ r) % count) * rows, rows)
            for kind, out_ref in enumerate(out_refs):
                at = kind * rows * width // 128
                out_ref[core ^ cores, 0, place, :] = take_chunk(ref, r, at, rows, width)


def spread_token(where, low, high, span, width, kinds):
    chips, total, _ = low.shape
    count = chips // 2
    rows = span // (2 * chips)
    into = pl.BlockSpec((count, total, 128), lambda b, where: (b ^ (where[0] // count), 0, 0))
    out = pl.BlockSpec((2, 1, count * rows, width), lambda b, where: (0, b, 0, 0))
    made = pl.pallas_call(
        spread_token_kernel,
        grid_spec=pltpu.PrefetchScalarGridSpec(
            num_scalar_prefetch=1, grid=(2,), in_specs=[into] * 2, out_specs=[out] * kinds
        ),
        out_shape=[jax.ShapeDtypeStruct((2, 2, count * rows, width), F32)] * kinds,
        compiler_params=params(),
        cost_estimate=cost(5),
        name="spread_token",
    )(where, low, high)
    return [array.reshape(span, width) for array in made]


def picked_head(pos_ref, low, high, head):
    place = pos_ref[head]
    count = low.shape[0]
    return jnp.where(
        place < count, low[place % count].astype(F32), high[place % count].astype(F32)
    )


def head_spread_kernel(pos_ref, low_ref, high_ref, q_ref, k_ref, v_ref):
    span, width = q_ref.shape
    half = span // 2
    for pair in range(width // 128):
        at = pair * 128
        first = picked_head(pos_ref, low_ref, high_ref, 2 * pair)
        second = picked_head(pos_ref, low_ref, high_ref, 2 * pair + 1)
        low, high = pair_up(first, second)
        q_ref[:, at : at + 128] = low[:span]
        k_ref[:, at : at + 128] = high[:span]
        v_ref[:half, at : at + 128] = low[span:]
        v_ref[half:, at : at + 128] = high[span:]


def cross_head_spread_kernel(pos_ref, low_ref, high_ref, k_ref, v_ref):
    for pair in range(k_ref.shape[1] // 128):
        at = pair * 128
        first = picked_head(pos_ref, low_ref, high_ref, 2 * pair)
        second = picked_head(pos_ref, low_ref, high_ref, 2 * pair + 1)
        k_ref[:, at : at + 128], v_ref[:, at : at + 128] = pair_up(first, second)


def per_device(
    inputs,
    encoded,
    cotangent,
    doc_ids,
    buckets,
    gain_self,
    query_self,
    key_self,
    value_self,
    output_self,
    position_bias,
    gain_cross,
    query_cross,
    key_cross,
    value_cross,
    output_cross,
    gain_dense,
    dense_gate,
    dense_up,
    dense_down,
):
    micro_count, _, rows, width = inputs.shape
    part = encoded.shape[2]
    heads = position_bias.shape[1]
    dp, fs = lax.axis_size("dp"), lax.axis_size("fsdp")
    me, shard = lax.axis_index("dp"), lax.axis_index("fsdp")
    core, chips = me % 2, dp // 2
    length = rows * dp
    tokens = micro_count * rows
    copies = dp // heads
    head = me // copies
    span = width // fs
    half = span // 2
    hidden = dense_down.shape[0]
    chip_bits = [1 << place for place in range(1, dp.bit_length() - 1)]
    x_order, z_order = chip_bits, chip_bits[1:] + chip_bits[:1]
    paired = fs == 2
    chunked = paired and half % (16 * chips) == 0 and hidden % (16 * chips) == 0
    chunked = chunked and hidden % 128 == 0

    def chip_of(j, order=x_order):
        last = len(order) - 1
        return sum(((j // bit) % 2) << (last - place) for place, bit in enumerate(order))

    def swap_dp(values, bit):
        return lax.ppermute(values, "dp", [(j, j ^ bit) for j in range(dp)])

    def swap_fs(values):
        return lax.ppermute(values, "fsdp", [(j, 1 - j) for j in range(2)])

    def after(values, *others):
        return lax.optimization_barrier((values, *others))[0]

    def half_rows(values):
        return jnp.stack([lax.dynamic_slice_in_dim(w, core * half, half, axis=0) for w in values])

    def both_halves(sent):
        got = swap_fs(sent)
        return got, swap_dp(got, 1)

    def gather_rows(values):
        return [lax.all_gather(w, "fsdp", axis=0, tiled=True) for w in values]

    def both_tokens(values):
        if paired:
            return jnp.concatenate([values, swap_fs(values)], axis=0)
        return lax.all_gather(values, "fsdp", axis=0, tiled=True)

    def reduce_chips(kept, got, order=x_order):
        total = kept.astype(F32) + got.astype(F32)
        for bit in order[1:]:
            count = total.shape[0] // 2
            sent, total = total[count:].astype(BF16), total[:count]
            total = total + swap_dp(sent, bit).astype(F32)
        return total.astype(BF16)

    def gather_chips(values, order=x_order):
        for bit in reversed(order):
            values = jnp.concatenate([values, swap_dp(values, bit)], axis=0)
        return values, swap_dp(values, 1)

    x, g, e = inputs[:, 0], cotangent[:, 0], encoded[:, 0]

    low, offsets = [x], [0]
    for bit in reversed(chip_bits[1:]):
        low = low + [swap_dp(piece, bit) for piece in low]
        offsets = offsets + [offset | bit for offset in offsets]
    high = [swap_dp(piece, 2) for piece in low]
    near, far = jnp.stack(low), jnp.stack(high)
    offsets = [offset ^ more for more in (0, 2, 1, 3) for offset in offsets]
    source = me ^ jnp.array(offsets, jnp.int32)
    e_all = lax.all_gather(e, "dp", axis=0)

    gains = jnp.stack([gain_self, gain_cross, gain_dense])
    own_head = lambda w: lax.dynamic_slice_in_dim(w, head * 64, 64, axis=1)
    if paired:
        pad = jnp.pad(position_bias.reshape(1, -1), ((0, 0), (0, span - position_bias.size)))
        small = jnp.concatenate([gains, pad], axis=0)
        small_got = swap_fs(small)
        head_pack = jnp.concatenate([own_head(w) for w in (query_self, key_self, value_self)], 1)
        head_got = swap_fs(head_pack)
        first, second = (
            jnp.where(shard == which, mine, got)
            for which, mine, got in ((0, small, small_got), (1, small, small_got))
        )
        gains = jnp.concatenate([first[:3], second[:3]], axis=1)
        bias_all = jnp.concatenate(
            [piece[3, : position_bias.size].reshape(position_bias.shape) for piece in (first, second)]
        )
        head_whole = jnp.where(
            shard == 0,
            jnp.concatenate([head_pack, head_got]),
            jnp.concatenate([head_got, head_pack]),
        )
        other = (1 - shard) * span
        starts = jnp.stack([shard * span, other + core * half, other + (1 - core) * half])
        starts = starts.astype(jnp.int32)
        kv_own = (key_cross, value_cross)
        near_own = (output_self, query_cross, output_cross)
        near_got = swap_fs(half_rows(near_own + kv_own))
        theirs = jnp.stack(
            [
                lax.dynamic_slice(w, (core * half, (1 - shard) * hidden), (half, hidden))
                for w in (dense_gate, dense_up)
            ]
        )
        dense_own = (dense_gate, dense_up)
        which = jnp.stack([shard, core]).astype(jnp.int32)
        dense_starts = jnp.concatenate([starts, which])
    else:
        gains = lax.all_gather(gains, "fsdp", axis=1, tiled=True)
        bias_all = lax.all_gather(position_bias, "fsdp", axis=0, tiled=True)
        kv_own, kv_more = gather_rows((key_cross, value_cross)), ()
        near_own, near_more = gather_rows((output_self, query_cross, output_cross)), ()
        first_own, first_more = gather_rows((query_self, key_self, value_self)), ()
        head_whole = jnp.concatenate([own_head(w) for w in first_own], axis=1)
        dense_own = [
            lax.all_to_all(w, "fsdp", 1, 0, tiled=True) for w in (dense_gate, dense_up)
        ]
        dense_more = ()
        starts = jnp.zeros((1,), jnp.int32)
        dense_starts = jnp.zeros((3,), jnp.int32)
        g_group = both_tokens(g.reshape(tokens, width))
    gains, bias_all = gains.astype(F32), bias_all.astype(F32)
    head_w = jnp.concatenate(
        [head_whole[:, at : at + 64] for at in (0, 0, 64, 64, 128, 128)], axis=1
    )

    marks = jnp.arange(bias_all.shape[0], dtype=jnp.int32)
    edges = jnp.sum((buckets[:, None] < marks[None, :]).astype(jnp.int32), axis=0)
    bias_values = lax.dynamic_slice_in_dim(bias_all, head, 1, axis=1)[:, 0]
    table = bias_table(edges, bias_values, length)
    x_groups = [near, far, swap_dp(near, 1), swap_dp(after(far, table), 1)]
    doc_row = jnp.broadcast_to(doc_ids[:, 0, :, None], (micro_count, dp, rows))
    doc_row = doc_row.reshape(micro_count, length)
    doc_col = doc_row[:, :, None]

    n_all, qkv, mixed = pl.pallas_call(
        functools.partial(self_forward_kernel, len(x_groups)),
        out_shape=[
            jax.ShapeDtypeStruct((dp, micro_count, rows, width), BF16),
            jax.ShapeDtypeStruct((length, 384), BF16),
            jax.ShapeDtypeStruct((length, 128), BF16),
        ],
        in_specs=[smem()] + [vmem()] * (len(x_groups) + 5),
        out_specs=[vmem()] * 3,
        compiler_params=params(),
        cost_estimate=cost(12),
        name="self_forward",
    )(source, *x_groups, gains[0:1], head_w, table, doc_row, doc_col)
    o1_heads = lax.all_to_all(mixed.reshape(dp, rows, 128), "dp", 0, 0, tiled=True)[::copies]

    if paired:
        near_more = kv_more = (near_got, swap_dp(after(near_got, mixed), 1))
        dense_got = swap_fs(after(theirs, near_got, mixed))
    ke, ve = cross_kv(starts, e_all, *kv_own, kv_more)

    row32 = jax.ShapeDtypeStruct((tokens, width), F32)
    row16 = jax.ShapeDtypeStruct((tokens, width), BF16)
    left, x1, q2, x2, n3 = pl.pallas_call(
        functools.partial(mid_forward_kernel, len(near_more)),
        out_shape=[
            jax.ShapeDtypeStruct((3, tokens, width), BF16), row32, row16, row32, row16
        ],
        in_specs=[smem()] + [vmem()] * (8 + len(near_more)),
        out_specs=[vmem()] * 5,
        scratch_shapes=[pltpu.VMEM((tokens, width), BF16)] * 3,
        compiler_params=params(),
        cost_estimate=cost(12),
        name="mid_forward",
    )(starts, o1_heads, x, gains, ke, ve, *near_own, *near_more)

    if paired:
        dense_more = (dense_got, swap_dp(after(dense_got, n3), 1))
        g_rows = g.reshape(tokens, width)
        g_got = swap_fs(after(g_rows, dense_got))
        n_got = swap_fs(n3)
        back, y32, _, dn3, _ = dense_layer(
            dense_starts, n3, g_rows, *dense_own, dense_down, dense_more, tokens
        )
        back_mate = swap_dp(back, 1)
        back_got, _, y16, _, d16 = dense_layer(
            dense_starts,
            after(n_got, dn3),
            g_got,
            *dense_own,
            dense_down,
            dense_more,
            tokens,
        )
        back_got_mate = swap_dp(back_got, 1)
        dn3_more = swap_fs(d16)
    else:
        n_group = both_tokens(n3)
        back, _, y16, _, d16 = dense_layer(
            dense_starts, n_group, g_group, *dense_own, dense_down, dense_more, tokens
        )
        dn3 = jnp.zeros((tokens, width), F32)
        dn3_more = lax.psum_scatter(d16, "fsdp", scatter_dimension=0, tiled=True)
        dense_out = lax.psum_scatter(y16, "fsdp", scatter_dimension=0, tiled=True).astype(F32)
        outputs = (x2 + dense_out).astype(BF16)

    if chunked:
        where = jnp.stack([chip_of(me), core, shard, chip_of(me, z_order)]).astype(jnp.int32)
        own_kept, own_sent, down_kept, down_sent, far_kept, far_sent = chunk_weights(
            dense_weight_kernel,
            where,
            (n3, n_got, g_rows, g_got, back, back_got, back_mate, back_got_mate),
            (
                span // chips * hidden // 128,
                hidden // chips * width // 256,
                span // chips * hidden // 128,
            ),
            chips,
            [
                pltpu.VMEM((max(hidden, half), max(hidden, width // 2)), F32),
                pltpu.VMEM((4 * tokens, width), BF16),
            ],
            7,
            "dense_weight",
        )
        dn3_more = after(dn3_more, own_sent)
        own_got, down_got = swap_dp(own_sent, z_order[0]), swap_dp(down_sent, x_order[0])
        far_got = swap_fs(far_sent)

    right, gx1, do1_heads, dkv, dc_two = pl.pallas_call(
        functools.partial(mid_backward_kernel, len(near_more)),
        out_shape=[
            jax.ShapeDtypeStruct((tokens, 3 * width), BF16),
            row32,
            jax.ShapeDtypeStruct((heads, rows, 128), BF16),
            jax.ShapeDtypeStruct((heads, dp, micro_count, part, 128), BF16),
            jax.ShapeDtypeStruct((2, width), F32),
        ],
        in_specs=[smem()] + [vmem()] * (12 + len(near_more)),
        out_specs=[vmem()] * 5,
        scratch_shapes=[
            pltpu.VMEM((tokens, width), F32),
            pltpu.VMEM((tokens, width), BF16),
            pltpu.VMEM((tokens, width), BF16),
        ],
        compiler_params=params(),
        cost_estimate=cost(16),
        name="mid_backward",
    )(starts, g, dn3, dn3_more, x1, x2, gains, q2, ke, ve, *near_own, *near_more)
    do1 = lax.all_to_all(
        jnp.repeat(do1_heads, copies, axis=0) if copies > 1 else do1_heads, "dp", 0, 0, tiled=True
    ).reshape(length, 128)

    if chunked:
        views = left.reshape(3, tokens, 2, 2 * half)
        own = lax.dynamic_index_in_dim(views, shard, 2, keepdims=False)
        sent = lax.dynamic_index_in_dim(views, 1 - shard, 2, keepdims=False)
        got = swap_fs(after(sent, dn3_more))
        left_views = jnp.concatenate([own, got], axis=1).reshape(3, 2 * tokens, 2, half)

        def left_features(which):
            picked = lax.dynamic_index_in_dim(left_views, which, 2, keepdims=False)
            return picked.transpose(1, 0, 2).reshape(2 * tokens, 3 * half)

        left_mate = swap_dp(left_features(1 - core), 1)
        right_got = swap_fs(right)
        far_kept = swap_fs(after(far_kept, right_got))
        do1 = after(do1, left_mate, own_got, down_got, far_got)

    dqkv, table_grad = pl.pallas_call(
        self_backward_kernel,
        out_shape=[
            jax.ShapeDtypeStruct((length, 384), BF16),
            jax.ShapeDtypeStruct((TILE, length), F32),
        ],
        in_specs=[vmem()] * 5,
        out_specs=[vmem()] * 2,
        scratch_shapes=[pltpu.VMEM((length, 128), F32), pltpu.VMEM((length, 128), F32)],
        compiler_params=params(),
        cost_estimate=cost(10),
        name="self_backward",
    )(qkv, do1, table, doc_row, doc_col)
    if chunked:
        dqkv = after(dqkv, right_got)
    head_grad = pl.pallas_call(
        head_weight_kernel,
        out_shape=jax.ShapeDtypeStruct((fs, span * 3 // 2, 128), BF16),
        in_specs=[vmem()] * 2,
        out_specs=vmem(),
        compiler_params=params(),
        cost_estimate=cost(6),
        name="head_weight",
    )(n_all, dqkv)
    def sum_shards(values):
        if paired:
            kept = lax.dynamic_index_in_dim(values, shard, 0)
            sent = lax.dynamic_index_in_dim(values, 1 - shard, 0)
            return (kept.astype(F32) + swap_fs(sent).astype(F32)).astype(BF16)
        return lax.psum_scatter(values, "fsdp", scatter_dimension=0, tiled=True)

    head_sum = sum_shards(head_grad)
    if chunked:
        token_kept, token_sent = chunk_weights(
            token_weight_kernel,
            where,
            (
                left_features(core),
                left_mate,
                right,
                right_got,
                swap_dp(right, 1),
                swap_dp(right_got, 1),
            ),
            (3 * half // chips * width // 128,),
            chips,
            [pltpu.VMEM((half, width), F32)],
            5,
            "token_weight",
        )
        head_sum = after(head_sum, token_kept)

    relative = me ^ (jnp.arange(heads, dtype=jnp.int32) * copies)
    head_places = (relative % 2) * chips + chip_of(relative)
    grad_query_self, grad_key_self, grad_value_self = pl.pallas_call(
        head_spread_kernel,
        out_shape=[jax.ShapeDtypeStruct((span, width), F32)] * 3,
        in_specs=[smem(), vmem(), vmem()],
        out_specs=[vmem()] * 3,
        compiler_params=params(),
        cost_estimate=cost(6),
        name="head_spread",
    )(head_places, *gather_chips(head_sum))

    if paired:
        first_own = (query_self, key_self, value_self)
        first_more = both_halves(after(half_rows(first_own), head_sum))
        y16 = swap_fs(after(y16, first_more[0]))
        outputs = (x2 + (y32 + y16.astype(F32))).astype(BF16)
    own_d = lax.all_to_all(dqkv.reshape(dp, rows, 384), "dp", 0, 0, tiled=True)[::copies]
    grad_inputs, dc_one = pl.pallas_call(
        functools.partial(input_grad_kernel, len(first_more)),
        out_shape=[row32, jax.ShapeDtypeStruct((1, width), F32)],
        in_specs=[smem()] + [vmem()] * (7 + len(first_more)),
        out_specs=[vmem()] * 2,
        scratch_shapes=[
            pltpu.VMEM((tokens, 3 * width), BF16),
            pltpu.VMEM((tokens, width), F32),
        ],
        compiler_params=params(),
        cost_estimate=cost(7),
        name="input_grad",
    )(starts, own_d, x, gains, gx1, *first_own, *first_more)

    dkv = dkv.reshape(heads * copies, -1, 128)
    dkv = lax.psum_scatter(dkv, "dp", scatter_dimension=0, tiled=True)[0]
    bit = 1
    while bit < copies:
        got = swap_dp(dkv, bit)
        dkv = jnp.where(
            (me // bit) % 2 == 0, jnp.concatenate([dkv, got]), jnp.concatenate([got, dkv])
        )
        bit *= 2
    cross_grad = pl.pallas_call(
        cross_head_weight_kernel,
        out_shape=jax.ShapeDtypeStruct((fs, span, 128), BF16),
        in_specs=[vmem()] * 2,
        out_specs=vmem(),
        compiler_params=params(),
        cost_estimate=cost(3),
        name="cross_head_weight",
    )(e_all, dkv)
    cross_sum = sum_shards(cross_grad)
    grad_key_cross, grad_value_cross = pl.pallas_call(
        cross_head_spread_kernel,
        out_shape=[jax.ShapeDtypeStruct((span, width), F32)] * 2,
        in_specs=[smem(), vmem(), vmem()],
        out_specs=[vmem()] * 2,
        compiler_params=params(),
        cost_estimate=cost(4),
        name="cross_head_spread",
    )(head_places, *gather_chips(cross_sum))
    own_dkv = dkv.reshape(dp, micro_count * part, 128)
    own_dkv = lax.all_to_all(own_dkv, "dp", 0, 0, tiled=True)[::copies]
    grad_encoded = pl.pallas_call(
        functools.partial(encoder_grad_kernel, len(kv_more)),
        out_shape=jax.ShapeDtypeStruct((micro_count * part, width), F32),
        in_specs=[smem()] + [vmem()] * (3 + len(kv_more)),
        out_specs=vmem(),
        scratch_shapes=[pltpu.VMEM((micro_count * part, width), BF16)] * 2,
        compiler_params=params(),
        cost_estimate=cost(4),
        name="encoder_grad",
    )(starts, own_dkv, *kv_own, *kv_more)

    if chunked:
        dense_low, dense_high = gather_chips(reduce_chips(own_kept, own_got, z_order), z_order)
        down_low, down_high = gather_chips(reduce_chips(down_kept, down_got))
        far_low, far_high = gather_chips(reduce_chips(far_kept, swap_dp(far_got, 2)))
        grad_dense_down = spread_down(where, down_low, down_high, hidden, width)
        grad_dense_gate, grad_dense_up = spread_gate(
            where, dense_low, dense_high, far_low, far_high, hidden, span
        )

        token_sum = after(reduce_chips(token_kept, swap_dp(token_sent, 2)), cross_grad)
        token_low, token_high = gather_chips(token_sum)
        grad_output_cross, grad_query_cross, grad_output_self = spread_token(
            where, token_low, token_high, span, width, 3
        )
    else:

        def over_dp(values):
            return lax.psum(values.astype(BF16), "dp").astype(F32)

        def over_all(a, b):
            made = t_dot(a, b).astype(BF16)
            return over_dp(lax.psum_scatter(made, "fsdp", scatter_dimension=0, tiled=True))

        grad_output_cross, grad_query_cross, grad_output_self = (
            over_all(left[kind], right[:, kind * width : (kind + 1) * width]) for kind in range(3)
        )
        grad_dense_gate, grad_dense_up = (
            over_dp(
                lax.all_to_all(
                    t_dot(n_group, back[:, kind * hidden : (kind + 1) * hidden]).astype(BF16),
                    "fsdp",
                    0,
                    1,
                    tiled=True,
                )
            )
            for kind in range(2)
        )
        grad_dense_down = over_dp(t_dot(back[:, 2 * hidden :], g_group))

    if chunked:
        table_grad = after(table_grad, first_more[1])
    table_sums = jnp.sum(bucket_sums(edges, table_grad, bias_all.shape[0]), axis=1)
    column = (jnp.arange(heads) == head) & (me % copies == 0)
    bias_row = jnp.where(column[None, :], table_sums[:, None], 0.0).reshape(1, -1)
    bias_row = jnp.pad(bias_row, ((0, 0), (0, width - bias_row.shape[1])))
    sums = jnp.concatenate([dc_one, dc_two, bias_row], axis=0)
    if paired:
        sums = sums + swap_fs(sums)
        for bit in [1] + chip_bits:
            sums = sums + swap_dp(sums, bit)
    else:
        sums = lax.psum(sums, ("dp", "fsdp"))
    own = lax.dynamic_slice_in_dim(sums[:3], shard * span, span, axis=1)
    grad_bias = sums[3, : bias_all.size].reshape(bias_all.shape)
    grad_bias = lax.dynamic_slice_in_dim(
        grad_bias, shard * position_bias.shape[0], position_bias.shape[0], axis=0
    )
    shape = (micro_count, 1, rows, width)
    return (
        outputs.reshape(shape),
        grad_inputs.reshape(shape),
        grad_encoded.reshape(micro_count, 1, part, width),
        own[0],
        grad_query_self,
        grad_key_self,
        grad_value_self,
        grad_output_self,
        grad_bias,
        own[2],
        grad_query_cross,
        grad_key_cross,
        grad_value_cross,
        grad_output_cross,
        own[1],
        grad_dense_gate,
        grad_dense_up,
        grad_dense_down,
    )


def solution(mesh):
    matrix = P("fsdp", None)
    token = P(None, "fsdp", "dp", None)
    weights = (
        (P("fsdp"),)
        + (matrix,) * 5
        + (P("fsdp"),)
        + (matrix,) * 4
        + (P("fsdp"),)
        + (matrix,) * 3
    )
    return jax.shard_map(
        per_device,
        mesh=mesh,
        in_specs=(token,) * 3 + (P(None, "fsdp", None), P()) + weights,
        out_specs=(token,) * 3 + weights,
        check_vma=False,
    )
```

```python
import functools

import jax
import jax.numpy as jnp
from jax import lax
from jax.experimental import pallas as pl
from jax.experimental.pallas import tpu as pltpu
from jax.sharding import PartitionSpec as P

EPS = 1e-06
NEGATIVE = -1e30
TILE = 256
F32 = jnp.float32
BF16 = jnp.bfloat16
VMEM_LIMIT = 56 * 1024 * 1024


def vmem():
    return pl.BlockSpec(memory_space=pltpu.VMEM)


def smem():
    return pl.BlockSpec(memory_space=pltpu.SMEM)


def params(limit=VMEM_LIMIT):
    return pltpu.CompilerParams(vmem_limit_bytes=limit)


def cost(microseconds):
    return pl.CostEstimate(
        flops=int(microseconds * 1.15e9),
        bytes_accessed=int(microseconds * 3.69e6),
        transcendentals=0,
    )


def aligned(start, size):
    return pl.ds(pl.multiple_of(start, size), size)


def dot(left, right):
    return jnp.dot(left, right, preferred_element_type=F32)


def dot_t(left, right):
    return lax.dot_general(left, right, (((1,), (1,)), ((), ())), preferred_element_type=F32)


def t_dot(left, right):
    return lax.dot_general(left, right, (((0,), (0,)), ((), ())), preferred_element_type=F32)


def norm_rows(values, gain):
    return values * lax.rsqrt(jnp.mean(values * values, axis=-1, keepdims=True) + EPS) * gain


def norm_back(values, gain, grad):
    r = lax.rsqrt(jnp.mean(values * values, axis=-1, keepdims=True) + EPS)
    scaled = grad * gain
    inner = jnp.mean(scaled * values, axis=-1, keepdims=True)
    back = r * scaled - values * (r * r * r * inner)
    return back, jnp.sum(grad * (values * r), axis=0, keepdims=True)


def low_lanes(rows):
    return lax.broadcasted_iota(jnp.int32, (rows, 128), 1) < 64


def pair_up(first, second):
    lane = low_lanes(first.shape[0])
    low = jnp.where(lane, first, pltpu.roll(second, 64, 1))
    high = jnp.where(lane, pltpu.roll(first, 64, 1), second)
    return low, high


def keep_half(values, half):
    lane = low_lanes(values.shape[0])
    return jnp.where(lane if half == 0 else ~lane, values, jnp.zeros_like(values))


def softmax_rows(scores):
    top = jnp.max(scores, axis=-1, keepdims=True)
    raised = jnp.exp(scores - top)
    return raised * (1.0 / jnp.sum(raised, axis=-1, keepdims=True))


def table_kernel(edge_ref, value_ref, out_ref):
    rows, length = out_ref.shape
    bucket_count = value_ref.shape[0]
    for start in range(0, length, TILE):
        place = (rows, TILE)
        apart = (
            lax.broadcasted_iota(jnp.int32, place, 0)
            - lax.broadcasted_iota(jnp.int32, place, 1)
            + (length - rows - start)
        )
        value = jnp.full(place, value_ref[0], F32)
        for bucket in range(1, bucket_count):
            value = jnp.where(apart >= edge_ref[bucket], value_ref[bucket], value)
        out_ref[:, start : start + TILE] = jnp.where(apart >= 0, value, NEGATIVE)


def bias_table(edges, values, length):
    return pl.pallas_call(
        table_kernel,
        out_shape=jax.ShapeDtypeStruct((TILE, length), F32),
        in_specs=[smem(), smem()],
        out_specs=vmem(),
        cost_estimate=cost(4),
        name="bias_table",
    )(edges, values)


def bucket_kernel(edge_ref, grad_ref, out_ref):
    rows, length = grad_ref.shape
    bucket_count = out_ref.shape[0]
    above = [jnp.zeros((8, TILE), F32) for _ in range(bucket_count)]
    for start in range(0, length, TILE):
        for row in range(0, rows, 8):
            place = (8, TILE)
            apart = (
                lax.broadcasted_iota(jnp.int32, place, 0)
                - lax.broadcasted_iota(jnp.int32, place, 1)
                + (length - rows - start + row)
            )
            tile = grad_ref[row : row + 8, start : start + TILE]
            for bucket in range(bucket_count):
                above[bucket] = above[bucket] + jnp.where(apart >= edge_ref[bucket], tile, 0.0)
    for bucket in range(bucket_count):
        rest = above[bucket + 1] if bucket + 1 < bucket_count else 0.0
        part = jnp.sum(above[bucket] - rest, axis=0, keepdims=True)
        out_ref[bucket : bucket + 1, :] = part[:, :128] + part[:, 128:]


def bucket_sums(edges, grad, bucket_count):
    return pl.pallas_call(
        bucket_kernel,
        out_shape=jax.ShapeDtypeStruct((bucket_count, 128), F32),
        in_specs=[smem(), vmem()],
        out_specs=vmem(),
        cost_estimate=cost(7),
        name="bucket_sums",
    )(edges, grad)


def times(x_ref, starts_ref, pieces):
    if len(pieces) == 1:
        return dot(x_ref[...], pieces[0])
    total = None
    for place, piece in enumerate(pieces):
        rows = piece.shape[0]
        part = dot(x_ref[:, aligned(starts_ref[place], rows)], piece)
        total = part if total is None else total + part
    return total


def times_back(out_ref, starts_ref, terms):
    for place in range(len(terms[0][1])):
        total = sum(dot_t(d, pieces[place]) for d, pieces in terms)
        rows = terms[0][1][place].shape[0]
        if len(terms[0][1]) == 1:
            out_ref[...] = total
        else:
            out_ref[:, aligned(starts_ref[place], rows)] = total


def pieces_of(own_ref, more, index):
    return [own_ref[...]] + [ref[index] for ref in more]


def self_scores(q, k, table, doc_col, doc_row):
    scores = dot_t(q, k) + table
    return jnp.where(doc_col == doc_row, scores, NEGATIVE)


def self_forward_kernel(groups, source_ref, *refs):
    x_refs = refs[:groups]
    gain_ref, w_ref, table_ref, doc_row_ref, doc_col_ref, n_ref, qkv_ref, o_ref = refs[groups:]
    count, _, rows, width = x_refs[0].shape
    length = groups * count * rows
    lane = lax.broadcasted_iota(jnp.int32, (rows, 384), 1) % 128 < 64
    together = min(TILE // rows, count)
    for place, x_ref in enumerate(x_refs):
        for first in range(0, count, together):
            parts = []
            for inner in range(first, first + together):
                x = x_ref[inner].astype(F32).reshape(2 * rows, width)
                n = norm_rows(x, gain_ref[...]).astype(BF16)
                n_ref[source_ref[place * count + inner]] = n.reshape(2, rows, width)
                parts.append(n)
            made = dot(jnp.concatenate(parts, axis=0), w_ref[...])
            for inner in range(together):
                at = 2 * rows * inner
                picked = jnp.where(lane, made[at : at + rows], made[at + rows : at + 2 * rows])
                own = source_ref[place * count + first + inner]
                qkv_ref[aligned(own * rows, rows), :] = picked.astype(BF16)
    for block in range(length // TILE):
        start, stop = block * TILE, (block + 1) * TILE
        table = table_ref[:, length - stop :]
        q = qkv_ref[start:stop, 0:128]
        k = qkv_ref[:stop, 128:256]
        v = qkv_ref[:stop, 256:384]
        mixed = []
        for half in range(2):
            scores = self_scores(
                keep_half(q, half),
                k,
                table,
                doc_col_ref[half, start:stop, :],
                doc_row_ref[half : half + 1, :stop],
            )
            mixed.append(dot(softmax_rows(scores).astype(BF16), v))
        o_ref[start:stop, :] = jnp.where(low_lanes(TILE), mixed[0], mixed[1]).astype(BF16)


def self_backward_kernel(
    qkv_ref, do_ref, table_ref, doc_row_ref, doc_col_ref, dqkv_ref, grad_ref, dk_ref, dv_ref
):
    length = qkv_ref.shape[0]
    grad_ref[...] = jnp.zeros_like(grad_ref)
    dk_ref[...] = jnp.zeros_like(dk_ref)
    dv_ref[...] = jnp.zeros_like(dv_ref)
    for block in range(length // TILE):
        start, count = block * TILE, (block + 1) * TILE
        table = table_ref[:, length - count :]
        k = qkv_ref[:count, 128:256]
        v = qkv_ref[:count, 256:384]
        made = []
        for half in range(2):
            q = keep_half(qkv_ref[start:count, 0:128], half)
            do = keep_half(do_ref[start:count, :], half)
            p = softmax_rows(
                self_scores(
                    q,
                    k,
                    table,
                    doc_col_ref[half, start:count, :],
                    doc_row_ref[half : half + 1, :count],
                )
            )
            dp = dot_t(do, v)
            ds = (p * (dp - jnp.sum(p * dp, axis=-1, keepdims=True))).astype(BF16)
            grad_ref[:, length - count :] += ds.astype(F32)
            made.append(dot(ds, k))
            dk_ref[:count, :] += t_dot(ds, q)
            dv_ref[:count, :] += t_dot(p.astype(BF16), do)
        dq = jnp.where(low_lanes(TILE), made[0], made[1])
        dqkv_ref[start:count, 0:128] = dq.astype(BF16)
    dqkv_ref[:, 128:256] = dk_ref[...].astype(BF16)
    dqkv_ref[:, 256:384] = dv_ref[...].astype(BF16)


def head_weight_kernel(n_ref, d_ref, out_ref):
    blocks, _, rows, width = n_ref.shape
    shards = out_ref.shape[0]
    span = width // shards
    lane = lax.broadcasted_iota(jnp.int32, (blocks * rows, 384), 1) % 128 < 64
    d = d_ref[...]
    zero = jnp.zeros_like(d)
    right = [jnp.where(lane, d, zero), jnp.where(lane, zero, d)]
    half = span // 2
    for shard in range(shards):
        total = jnp.zeros((span, 384), F32)
        for micro in range(2):
            left = n_ref[:, micro, :, shard * span : (shard + 1) * span]
            total = total + t_dot(left.reshape(blocks * rows, span), right[micro])
        q, k, v = (
            total[:, at : at + 128] + pltpu.roll(total[:, at : at + 128], 64, 1)
            for at in (0, 128, 256)
        )
        out_ref[shard, :span, :] = jnp.where(low_lanes(span), q, k).astype(BF16)
        out_ref[shard, span:, :] = jnp.where(low_lanes(half), v[:half], v[half:]).astype(BF16)


def cross_kv_kernel(split, starts_ref, e_ref, wk_ref, wv_ref, *refs):
    more, (ke_ref, ve_ref) = refs[:split], refs[split:]
    blocks, _, part, _ = e_ref.shape
    for index, (own_ref, out_ref) in enumerate(((wk_ref, ke_ref), (wv_ref, ve_ref)), 3):
        total = None
        pieces = pieces_of(own_ref, more, index)
        for place, piece in enumerate(pieces):
            rows = piece.shape[0]
            if split:
                left = e_ref[:, 0, :, aligned(starts_ref[place], rows)]
            else:
                left = e_ref[:, 0]
            made = dot(left.reshape(blocks * part, rows), piece)
            total = made if total is None else total + made
        out_ref[0] = total.astype(BF16)


def cross_kv(starts, e_all, wk, wv, more):
    blocks, micro, part, width = e_all.shape
    whole = lambda array: pl.BlockSpec(array.shape, lambda m, s: (0,) * array.ndim)
    out = pl.BlockSpec((1, blocks * part, width), lambda m, s: (m, 0, 0))
    return pl.pallas_call(
        functools.partial(cross_kv_kernel, len(more)),
        grid_spec=pltpu.PrefetchScalarGridSpec(
            num_scalar_prefetch=1,
            grid=(micro,),
            in_specs=[pl.BlockSpec((blocks, 1, part, width), lambda m, s: (0, m, 0, 0))]
            + [whole(array) for array in (wk, wv, *more)],
            out_specs=[out, out],
        ),
        out_shape=[jax.ShapeDtypeStruct((micro, blocks * part, width), BF16)] * 2,
        compiler_params=params(),
        cost_estimate=cost(8),
        name="cross_kv",
    )(starts, e_all, wk, wv, *more)


def mid_forward_kernel(split, starts_ref, o1_ref, x_ref, gain_ref, ke_ref, ve_ref, wo, wq, wc, *refs):
    more = refs[:split]
    left_ref, x1_ref, q2_ref, x2_ref, n3_ref, o1c_ref, n2_ref, o2_ref = refs[split:]
    heads, rows, _ = o1_ref.shape
    width = x_ref.shape[-1]
    for pair in range(heads // 2):
        at = pair * 128
        low, high = pair_up(o1_ref[2 * pair].astype(F32), o1_ref[2 * pair + 1].astype(F32))
        o1c_ref[0:rows, at : at + 128] = low.astype(BF16)
        o1c_ref[rows : 2 * rows, at : at + 128] = high.astype(BF16)
    x = x_ref[...].astype(F32).reshape(2 * rows, width)
    x1 = x + times(o1c_ref, starts_ref, pieces_of(wo, more, 0))
    x1_ref[...] = x1
    n2_ref[...] = norm_rows(x1, gain_ref[1:2]).astype(BF16)
    q2_ref[...] = times(n2_ref, starts_ref, pieces_of(wq, more, 1)).astype(BF16)
    for micro in range(2):
        for pair in range(heads // 2):
            at = pair * 128
            span = slice(micro * rows, (micro + 1) * rows)
            q = q2_ref[span, at : at + 128]
            both = jnp.concatenate([keep_half(q, 0), keep_half(q, 1)], axis=0)
            p = softmax_rows(dot_t(both, ke_ref[micro, :, at : at + 128]))
            o = dot(p.astype(BF16), ve_ref[micro, :, at : at + 128])
            o2_ref[span, at : at + 128] = jnp.where(
                low_lanes(rows), o[:rows], o[rows:]
            ).astype(BF16)
    x2 = x1 + times(o2_ref, starts_ref, pieces_of(wc, more, 2))
    x2_ref[...] = x2
    n3_ref[...] = norm_rows(x2, gain_ref[2:3]).astype(BF16)
    left_ref[0] = o2_ref[...]
    left_ref[1] = n2_ref[...]
    left_ref[2] = o1c_ref[...]


def mid_backward_kernel(
    split, starts_ref, slots_ref, g_ref, dn3_ref, more_ref, x1_ref, x2_ref, gain_ref, q2_ref, ke_ref, ve_ref,
    wo, wq, wc, *refs
):
    more = refs[:split]
    right_ref, gx1_ref, do1_ref, keep_ref, send_ref, dc_ref, back_ref, do2_ref, dq2_ref = refs[split:]
    heads, rows, _ = do1_ref.shape
    blocks, micros, part = keep_ref.shape[1:4]
    even = slots_ref[heads // 2] == 0
    width = x1_ref.shape[-1]
    dn3 = dn3_ref[...] + more_ref[...].astype(F32)
    back, dc = norm_back(x2_ref[...], gain_ref[2:3], dn3)
    dc_ref[0:1, :] = dc
    gx2 = g_ref[...].astype(F32).reshape(2 * rows, width) + back
    gx2b = gx2.astype(BF16)
    right_ref[:, 0:width] = gx2b
    times_back(back_ref, starts_ref, [(gx2b, pieces_of(wc, more, 2))])
    do2_ref[...] = back_ref[...].astype(BF16)
    for micro in range(2):
        for pair in range(heads // 2):
            at = pair * 128
            span = slice(micro * rows, (micro + 1) * rows)
            q = q2_ref[span, at : at + 128]
            do = do2_ref[span, at : at + 128]
            q = jnp.concatenate([keep_half(q, 0), keep_half(q, 1)], axis=0)
            do = jnp.concatenate([keep_half(do, 0), keep_half(do, 1)], axis=0)
            k = ke_ref[micro, :, at : at + 128]
            v = ve_ref[micro, :, at : at + 128]
            p = softmax_rows(dot_t(q, k))
            dp = dot_t(do, v)
            ds = (p * (dp - jnp.sum(p * dp, axis=-1, keepdims=True))).astype(BF16)
            dq = dot(ds, k)
            dq2_ref[span, at : at + 128] = jnp.where(
                low_lanes(rows), dq[:rows], dq[rows:]
            ).astype(BF16)
            low, high = pair_up(t_dot(ds, q), t_dot(p.astype(BF16), do))
            kept, sent = jnp.where(even, low, high), jnp.where(even, high, low)
            slot = slots_ref[pair]
            keep_ref[slot, :, micro] = kept.astype(BF16).reshape(blocks, part, 128)
            send_ref[slot, :, micro] = sent.astype(BF16).reshape(blocks, part, 128)
    right_ref[:, width : 2 * width] = dq2_ref[...]
    times_back(back_ref, starts_ref, [(dq2_ref[...], pieces_of(wq, more, 1))])
    back, dc = norm_back(x1_ref[...], gain_ref[1:2], back_ref[...])
    dc_ref[1:2, :] = dc
    gx1 = gx2 + back
    gx1_ref[...] = gx1
    gx1b = gx1.astype(BF16)
    right_ref[:, 2 * width :] = gx1b
    times_back(back_ref, starts_ref, [(gx1b, pieces_of(wo, more, 0))])
    for pair in range(heads // 2):
        at = pair * 128
        do1 = back_ref[:, at : at + 128].astype(BF16).astype(F32)
        low, high = pair_up(do1[:rows], do1[rows:])
        do1_ref[2 * pair] = low.astype(BF16)
        do1_ref[2 * pair + 1] = high.astype(BF16)


def input_grad_kernel(split, starts_ref, d_ref, x_ref, gain_ref, gx1_ref, wq, wk, wv, *refs):
    more = refs[:split]
    out_ref, dc_ref, all_ref, back_ref = refs[split:]
    heads, rows, _ = d_ref.shape
    width = x_ref.shape[-1]
    for kind in range(3):
        for pair in range(heads // 2):
            lanes = slice(kind * 128, (kind + 1) * 128)
            low, high = pair_up(
                d_ref[2 * pair, :, lanes].astype(F32), d_ref[2 * pair + 1, :, lanes].astype(F32)
            )
            at = kind * width + pair * 128
            all_ref[0:rows, at : at + 128] = low.astype(BF16)
            all_ref[rows : 2 * rows, at : at + 128] = high.astype(BF16)
    terms = [
        (all_ref[:, kind * width : (kind + 1) * width], pieces_of(own, more, kind))
        for kind, own in enumerate((wq, wk, wv))
    ]
    times_back(back_ref, starts_ref, terms)
    x = x_ref[...].astype(F32).reshape(2 * rows, width)
    back, dc = norm_back(x, gain_ref[0:1], back_ref[...])
    dc_ref[...] = dc
    out_ref[...] = gx1_ref[...] + back


def encoder_grad_kernel(split, starts_ref, d_ref, wk, wv, *refs):
    more = refs[:split]
    out_ref, k_ref, v_ref = refs[split:]
    for pair in range(d_ref.shape[0] // 2):
        at = pair * 128
        low, high = pair_up(d_ref[2 * pair].astype(F32), d_ref[2 * pair + 1].astype(F32))
        k_ref[:, at : at + 128] = low.astype(BF16)
        v_ref[:, at : at + 128] = high.astype(BF16)
    terms = [(k_ref[...], pieces_of(wk, more, 3)), (v_ref[...], pieces_of(wv, more, 4))]
    times_back(out_ref, starts_ref, terms)


def cross_head_weight_kernel(e_ref, d_ref, out_ref):
    blocks, micro, part, width = e_ref.shape
    shards, span, _ = out_ref.shape
    for shard in range(shards):
        left = e_ref[:, :, :, shard * span : (shard + 1) * span]
        left = left.reshape(blocks * micro * part, span)
        out_ref[shard] = t_dot(left, d_ref[...]).astype(BF16)


def dense_kernel(split, starts_ref, n_ref, g_ref, wg, wu, wd_ref, *refs):
    more = refs[:split]
    back_ref, y_ref, ylow_ref, d_ref, dlow_ref = refs[split:]
    hidden = wd_ref.shape[0]
    gate, up = pieces_of(wg, more, 0), pieces_of(wu, more, 1)
    a = times(n_ref, starts_ref, gate)
    b = times(n_ref, starts_ref, up)
    scale = 0.7978845608028654
    cubed = 0.044715
    inner = jnp.tanh(scale * (a + cubed * (a * a * a)))
    gelu = 0.5 * a * (1.0 + inner)
    slope = 0.5 * (1.0 + inner) + 0.5 * a * (1.0 - inner * inner) * (
        scale * (1.0 + 3.0 * cubed * (a * a))
    )
    hid = (gelu * b).astype(BF16)
    dh = dot_t(g_ref[...], wd_ref[...])
    da = (dh * b * slope).astype(BF16)
    db = (dh * gelu).astype(BF16)
    times_back(d_ref, starts_ref, [(da, gate), (db, up)])
    dlow_ref[...] = d_ref[...].astype(BF16)
    y = dot(hid, wd_ref[...])
    y_ref[...] = y
    ylow_ref[...] = y.astype(BF16)
    back_ref[:, 0:hidden] = da
    back_ref[:, hidden : 2 * hidden] = db
    back_ref[:, 2 * hidden : 3 * hidden] = hid
    if more:
        shard, other = starts_ref[len(more) + 1], 1 - starts_ref[len(more) + 2]
        put_features(back_ref, 3 * hidden, n_ref, g_ref, shard, other)


def put_features(out_ref, at, n_ref, g_ref, shard, core):
    quarter = n_ref.shape[1] // 4
    for side, place in enumerate((2 * shard + core, 2 * (1 - shard) + core)):
        lanes = slice(at + side * quarter, at + (side + 1) * quarter)
        out_ref[:, lanes] = n_ref[:, aligned(place * quarter, quarter)]
    lanes = slice(at + 2 * quarter, at + 4 * quarter)
    out_ref[:, lanes] = g_ref[:, aligned(core * 2 * quarter, 2 * quarter)]


def dense_layer(starts, n, g, wg, wu, wd, more, step):
    count, width = n.shape
    hidden = wd.shape[0]
    which = starts.shape[0] - 2
    back = 3 * hidden + (width if more else 0)
    row = lambda size: pl.BlockSpec((step, size), lambda i, s: (i, 0))
    whole = lambda array: pl.BlockSpec(array.shape, lambda i, s: (0,) * array.ndim)
    column = pl.BlockSpec((wg.shape[0], hidden), lambda i, s: (0, s[which]))
    made = lambda size, kind: jax.ShapeDtypeStruct((count, size), kind)
    return pl.pallas_call(
        functools.partial(dense_kernel, len(more)),
        grid_spec=pltpu.PrefetchScalarGridSpec(
            num_scalar_prefetch=1,
            grid=(count // step,),
            in_specs=[row(width), row(width), column, column, whole(wd)]
            + [whole(array) for array in more],
            out_specs=[row(back)] + [row(width)] * 4,
        ),
        out_shape=[made(back, BF16)]
        + [made(width, F32), made(width, BF16), made(width, F32), made(width, BF16)],
        compiler_params=params(),
        cost_estimate=cost(13),
        name="dense_layer",
    )(starts, n, g, wg, wu, wd, *more)


def put_chunk(ref, slot, at, value):
    rows, width = value.shape
    for block in range(width // 128):
        ref[slot, at + block * rows : at + (block + 1) * rows, :] = value[
            :, block * 128 : (block + 1) * 128
        ].astype(BF16)


def take_chunk(ref, slot, at, rows, width):
    return jnp.concatenate(
        [
            ref[slot, at + block * rows : at + (block + 1) * rows, :].astype(F32)
            for block in range(width // 128)
        ],
        axis=1,
    )


def put_all(scratch_ref, first, count, chip, chunk_refs, at, width, masks):
    slots = [(ref, slot) for ref in chunk_refs for slot in range(ref.shape[0])]
    rows = count // len(slots)
    for (ref, slot), mask in zip(slots, masks):
        chunk = scratch_ref[aligned(first + (chip ^ mask) * rows, rows), :width]
        put_chunk(ref, slot, at, chunk)


def dense_weight_kernel(
    x_masks, z_masks, where_ref, n0_ref, n1_ref, g0_ref, g1_ref, own0_ref, own1_ref, mate0_ref, mate1_ref, keep_ref,
    send_ref, down_keep_ref, down_send_ref, far_keep_ref, far_send_ref, scratch_ref, left_ref
):
    tokens, width = n0_ref.shape
    hidden = (own0_ref.shape[1] - width) // 3
    quarter = width // 4
    at = keep_ref.shape[1] // 2
    core, shard, chip = where_ref[1], where_ref[2], where_ref[3]
    put_features(left_ref.at[:tokens], 0, n0_ref, g0_ref, shard, core)
    put_features(left_ref.at[tokens : 2 * tokens], 0, n1_ref, g1_ref, shard, core)
    left_ref[2 * tokens : 3 * tokens, :] = mate0_ref[:, 3 * hidden :]
    left_ref[3 * tokens :, :] = mate1_ref[:, 3 * hidden :]

    def whole(kind):
        span = slice(kind * hidden, (kind + 1) * hidden)
        refs = (own0_ref, own1_ref, mate0_ref, mate1_ref)
        return jnp.concatenate([ref[:, span] for ref in refs], axis=0)

    for kind in range(2):
        right = whole(kind)
        for side, (masks, refs) in enumerate(
            ((z_masks, (keep_ref, send_ref)), (x_masks, (far_keep_ref, far_send_ref)))
        ):
            value = t_dot(left_ref[:, side * quarter : (side + 1) * quarter], right)
            scratch_ref[:quarter, :hidden] = value
            put_all(scratch_ref, 0, quarter, chip, refs, kind * at, hidden, masks)
    value = t_dot(whole(2), left_ref[:, 2 * quarter :])
    scratch_ref[:, : 2 * quarter] = value
    refs = (down_keep_ref, down_send_ref)
    put_all(scratch_ref, 0, hidden, chip, refs, 0, 2 * quarter, x_masks)


def token_weight_kernel(
    where_ref, left_ref, left_more_ref, right_ref, right_more_ref, mine_ref, mate_ref, scratch_ref
):
    kinds, _, span = left_more_ref.shape
    width = right_ref.shape[1] // kinds
    chip, core, shard = where_ref[0], where_ref[1], where_ref[2]
    half = span // 2
    masks = range(mine_ref.shape[0])
    at = half // len(masks) * width // 128
    for kind in range(kinds):
        lanes = slice(kind * width, (kind + 1) * width)
        left = [left_ref[kind, :, aligned(shard * span, span)], left_more_ref[kind]]
        right = [right_ref[:, lanes], right_more_ref[:, lanes]]
        scratch_ref[...] = t_dot(jnp.concatenate(left, axis=0), jnp.concatenate(right, axis=0))
        for ref, own in ((mine_ref, core), (mate_ref, 1 - core)):
            put_all(scratch_ref, own * half, half, chip, (ref,), kind * at, width, masks)


def chunk_weights(kernel, where, operands, counts, slots, scratches, length, name):
    shapes = []
    for count in counts:
        shapes += [jax.ShapeDtypeStruct((slots, count, 128), BF16)] * 2
    return pl.pallas_call(
        kernel,
        out_shape=shapes,
        in_specs=[smem()] + [vmem()] * len(operands),
        out_specs=[vmem()] * len(shapes),
        scratch_shapes=scratches,
        compiler_params=params(),
        cost_estimate=cost(length),
        name=name,
    )(where, *operands)


def spread_dense_kernel(where_ref, in_ref, gate_ref, up_ref, down_ref):
    shard = where_ref[2]
    hidden = gate_ref.shape[3] // 2
    rows = gate_ref.shape[2] // 2
    at = rows * hidden // 128
    tall = down_ref.shape[0] // 2
    half = down_ref.shape[1] // 2
    for piece in range(4):
        chip, core = piece // 2, piece % 2
        place = slice(chip * rows, (chip + 1) * rows)
        for side, start in enumerate((0, 4 * at)):
            lanes = aligned((shard ^ side) * hidden, hidden)
            for kind, out_ref in enumerate((gate_ref, up_ref)):
                chunk = take_chunk(in_ref, piece, start + kind * at, rows, hidden)
                out_ref[core, 0, place, lanes] = chunk
        chunk = take_chunk(in_ref, piece, 2 * at, tall, half)
        down_ref[chip * tall : (chip + 1) * tall, core * half : (core + 1) * half] = chunk


def spread_dense(where, pieces, hidden, span, width):
    count, total, _ = pieces.shape
    steps = count // 4
    rows = span // count
    out = pl.BlockSpec((2, 1, 2 * rows, 2 * hidden), lambda q, where: (0, q, 0, 0))
    made = pl.pallas_call(
        spread_dense_kernel,
        grid_spec=pltpu.PrefetchScalarGridSpec(
            num_scalar_prefetch=1,
            grid=(steps,),
            in_specs=[pl.BlockSpec((4, total, 128), lambda q, where: (q, 0, 0))],
            out_specs=[out, out, pl.BlockSpec((hidden // steps, width), lambda q, where: (q, 0))],
        ),
        out_shape=[jax.ShapeDtypeStruct((2, steps, 2 * rows, 2 * hidden), F32)] * 2
        + [jax.ShapeDtypeStruct((hidden, width), F32)],
        compiler_params=params(),
        cost_estimate=cost(10),
        name="spread_dense",
    )(where, pieces)
    return made[0].reshape(span, 2 * hidden), made[1].reshape(span, 2 * hidden), made[2]


def spread_token_kernel(where_ref, low, high, *out_refs):
    chip, core = where_ref[0], where_ref[1]
    count = low.shape[0]
    rows = out_refs[0].shape[2] // count
    width = out_refs[0].shape[3]
    for cores, ref in enumerate((low, high)):
        for r in range(count):
            place = aligned(((chip ^ r) % count) * rows, rows)
            for kind, out_ref in enumerate(out_refs):
                at = kind * rows * width // 128
                out_ref[core ^ cores, 0, place, :] = take_chunk(ref, r, at, rows, width)


def spread_token(where, low, high, span, width, kinds):
    chips, total, _ = low.shape
    count = chips // 2
    rows = span // (2 * chips)
    into = pl.BlockSpec((count, total, 128), lambda b, where: (b ^ (where[0] // count), 0, 0))
    out = pl.BlockSpec((2, 1, count * rows, width), lambda b, where: (0, b, 0, 0))
    made = pl.pallas_call(
        spread_token_kernel,
        grid_spec=pltpu.PrefetchScalarGridSpec(
            num_scalar_prefetch=1, grid=(2,), in_specs=[into] * 2, out_specs=[out] * kinds
        ),
        out_shape=[jax.ShapeDtypeStruct((2, 2, count * rows, width), F32)] * kinds,
        compiler_params=params(),
        cost_estimate=cost(5),
        name="spread_token",
    )(where, low, high)
    return [array.reshape(span, width) for array in made]


def picked_head(pos_ref, low, high, head):
    place = pos_ref[head]
    count = low.shape[0]
    return jnp.where(
        place < count, low[place % count].astype(F32), high[place % count].astype(F32)
    )


def head_spread_kernel(pos_ref, low_ref, high_ref, q_ref, k_ref, v_ref):
    span, width = q_ref.shape
    half = span // 2
    for pair in range(width // 128):
        at = pair * 128
        first = picked_head(pos_ref, low_ref, high_ref, 2 * pair)
        second = picked_head(pos_ref, low_ref, high_ref, 2 * pair + 1)
        low, high = pair_up(first, second)
        q_ref[:, at : at + 128] = low[:span]
        k_ref[:, at : at + 128] = high[:span]
        v_ref[:half, at : at + 128] = low[span:]
        v_ref[half:, at : at + 128] = high[span:]


def cross_head_spread_kernel(pos_ref, low_ref, high_ref, k_ref, v_ref):
    for pair in range(k_ref.shape[1] // 128):
        at = pair * 128
        first = picked_head(pos_ref, low_ref, high_ref, 2 * pair)
        second = picked_head(pos_ref, low_ref, high_ref, 2 * pair + 1)
        k_ref[:, at : at + 128], v_ref[:, at : at + 128] = pair_up(first, second)


def per_device(
    inputs,
    encoded,
    cotangent,
    doc_ids,
    buckets,
    gain_self,
    query_self,
    key_self,
    value_self,
    output_self,
    position_bias,
    gain_cross,
    query_cross,
    key_cross,
    value_cross,
    output_cross,
    gain_dense,
    dense_gate,
    dense_up,
    dense_down,
):
    micro_count, _, rows, width = inputs.shape
    part = encoded.shape[2]
    heads = position_bias.shape[1]
    dp, fs = lax.axis_size("dp"), lax.axis_size("fsdp")
    me, shard = lax.axis_index("dp"), lax.axis_index("fsdp")
    core, chips = me % 2, dp // 2
    length = rows * dp
    tokens = micro_count * rows
    copies = dp // heads
    head = me // copies
    span = width // fs
    half = span // 2
    hidden = dense_down.shape[0]
    chip_bits = [1 << place for place in range(1, dp.bit_length() - 1)]
    x_order, z_order = chip_bits, chip_bits[1:] + chip_bits[:1]
    paired = fs == 2
    chunked = paired and half % (16 * chips) == 0 and hidden % (16 * chips) == 0
    chunked = chunked and hidden % 128 == 0

    def chip_of(j, order=x_order):
        last = len(order) - 1
        return sum(((j // bit) % 2) << (last - place) for place, bit in enumerate(order))

    def swap_dp(values, bit):
        return lax.ppermute(values, "dp", [(j, j ^ bit) for j in range(dp)])

    def swap_fs(values):
        return lax.ppermute(values, "fsdp", [(j, 1 - j) for j in range(2)])

    def after(values, *others):
        return lax.optimization_barrier((values, *others))[0]

    def half_rows(values):
        return jnp.stack([lax.dynamic_slice_in_dim(w, core * half, half, axis=0) for w in values])

    def both_halves(sent):
        got = swap_fs(sent)
        return got, swap_dp(got, 1)

    def gather_rows(values):
        return [lax.all_gather(w, "fsdp", axis=0, tiled=True) for w in values]

    def both_tokens(values):
        if paired:
            return jnp.concatenate([values, swap_fs(values)], axis=0)
        return lax.all_gather(values, "fsdp", axis=0, tiled=True)

    def reduce_chips(kept, got, order=x_order, marks=()):
        total = kept.astype(F32) + got.astype(F32)
        for place, bit in enumerate(order[1:]):
            count = total.shape[0] // 2
            sent, total = total[count:].astype(BF16), total[:count]
            if place < len(marks):
                sent = after(sent, marks[place])
            total = total + swap_dp(sent, bit).astype(F32)
        return total.astype(BF16)

    def gather_chips(values, order=x_order):
        for bit in reversed(order):
            values = jnp.concatenate([values, swap_dp(values, bit)], axis=0)
        return values, swap_dp(values, 1)

    x, g, e = inputs[:, 0], cotangent[:, 0], encoded[:, 0]

    low, offsets = [x], [0]
    for bit in reversed(chip_bits[1:]):
        low = low + [swap_dp(piece, bit) for piece in low]
        offsets = offsets + [offset | bit for offset in offsets]
    high = [swap_dp(piece, 2) for piece in low]
    near, far = jnp.stack(low), jnp.stack(high)
    offsets = [offset ^ more for more in (0, 2, 1, 3) for offset in offsets]
    source = me ^ jnp.array(offsets, jnp.int32)
    e_all = lax.all_gather(e, "dp", axis=0)

    gains = jnp.stack([gain_self, gain_cross, gain_dense])
    own_head = lambda w: lax.dynamic_slice_in_dim(w, head * 64, 64, axis=1)
    if paired:
        pad = jnp.pad(position_bias.reshape(1, -1), ((0, 0), (0, span - position_bias.size)))
        small = jnp.concatenate([gains, pad], axis=0)
        small_got = swap_fs(small)
        head_pack = jnp.concatenate([own_head(w) for w in (query_self, key_self, value_self)], 1)
        head_got = swap_fs(head_pack)
        first, second = (
            jnp.where(shard == which, mine, got)
            for which, mine, got in ((0, small, small_got), (1, small, small_got))
        )
        gains = jnp.concatenate([first[:3], second[:3]], axis=1)
        bias_all = jnp.concatenate(
            [piece[3, : position_bias.size].reshape(position_bias.shape) for piece in (first, second)]
        )
        head_whole = jnp.where(
            shard == 0,
            jnp.concatenate([head_pack, head_got]),
            jnp.concatenate([head_got, head_pack]),
        )
        other = (1 - shard) * span
        starts = jnp.stack([shard * span, other + core * half, other + (1 - core) * half])
        starts = starts.astype(jnp.int32)
        kv_own = (key_cross, value_cross)
        near_own = (output_self, query_cross, output_cross)
        near_got = swap_fs(after(half_rows(near_own + kv_own), small_got, head_got))
        theirs = jnp.stack(
            [
                lax.dynamic_slice(w, (core * half, (1 - shard) * hidden), (half, hidden))
                for w in (dense_gate, dense_up)
            ]
        )
        dense_own = (dense_gate, dense_up)
        which = jnp.stack([shard, core]).astype(jnp.int32)
        dense_starts = jnp.concatenate([starts, which])
    else:
        gains = lax.all_gather(gains, "fsdp", axis=1, tiled=True)
        bias_all = lax.all_gather(position_bias, "fsdp", axis=0, tiled=True)
        kv_own, kv_more = gather_rows((key_cross, value_cross)), ()
        near_own, near_more = gather_rows((output_self, query_cross, output_cross)), ()
        first_own, first_more = gather_rows((query_self, key_self, value_self)), ()
        head_whole = jnp.concatenate([own_head(w) for w in first_own], axis=1)
        dense_own = [
            lax.all_to_all(w, "fsdp", 1, 0, tiled=True) for w in (dense_gate, dense_up)
        ]
        dense_more = ()
        starts = jnp.zeros((1,), jnp.int32)
        dense_starts = jnp.zeros((3,), jnp.int32)
        g_group = both_tokens(g.reshape(tokens, width))
    gains, bias_all = gains.astype(F32), bias_all.astype(F32)
    head_w = jnp.concatenate(
        [head_whole[:, at : at + 64] for at in (0, 0, 64, 64, 128, 128)], axis=1
    )

    marks = jnp.arange(bias_all.shape[0], dtype=jnp.int32)
    edges = jnp.sum((buckets[:, None] < marks[None, :]).astype(jnp.int32), axis=0)
    bias_values = lax.dynamic_slice_in_dim(bias_all, head, 1, axis=1)[:, 0]
    table = bias_table(edges, bias_values, length)
    x_groups = [near, far, swap_dp(near, 1), swap_dp(after(far, table), 1)]
    doc_row = jnp.broadcast_to(doc_ids[:, 0, :, None], (micro_count, dp, rows))
    doc_row = doc_row.reshape(micro_count, length)
    doc_col = doc_row[:, :, None]

    n_all, qkv, mixed = pl.pallas_call(
        functools.partial(self_forward_kernel, len(x_groups)),
        out_shape=[
            jax.ShapeDtypeStruct((dp, micro_count, rows, width), BF16),
            jax.ShapeDtypeStruct((length, 384), BF16),
            jax.ShapeDtypeStruct((length, 128), BF16),
        ],
        in_specs=[smem()] + [vmem()] * (len(x_groups) + 5),
        out_specs=[vmem()] * 3,
        compiler_params=params(),
        cost_estimate=cost(12),
        name="self_forward",
    )(source, *x_groups, gains[0:1], head_w, table, doc_row, doc_col)
    o1_heads = lax.all_to_all(mixed.reshape(dp, rows, 128), "dp", 0, 0, tiled=True)[::copies]

    if paired:
        near_more = kv_more = (near_got, swap_dp(after(near_got, mixed), 1))
        dense_got = swap_fs(after(theirs, near_got, mixed))
    ke, ve = cross_kv(starts, e_all, *kv_own, kv_more)

    row32 = jax.ShapeDtypeStruct((tokens, width), F32)
    row16 = jax.ShapeDtypeStruct((tokens, width), BF16)
    left, x1, q2, x2, n3 = pl.pallas_call(
        functools.partial(mid_forward_kernel, len(near_more)),
        out_shape=[
            jax.ShapeDtypeStruct((3, tokens, width), BF16), row32, row16, row32, row16
        ],
        in_specs=[smem()] + [vmem()] * (8 + len(near_more)),
        out_specs=[vmem()] * 5,
        scratch_shapes=[pltpu.VMEM((tokens, width), BF16)] * 3,
        compiler_params=params(),
        cost_estimate=cost(12),
        name="mid_forward",
    )(starts, o1_heads, x, gains, ke, ve, *near_own, *near_more)

    if paired:
        dense_more = (dense_got, swap_dp(after(dense_got, n3), 1))
        g_rows = g.reshape(tokens, width)
        g_got = swap_fs(after(g_rows, dense_got))
        n_got = swap_fs(n3)
        views = left.reshape(3, tokens, 2, span)
        left_got = swap_fs(lax.dynamic_index_in_dim(views, 1 - shard, 2, keepdims=False))
        back, y32, _, dn3, _ = dense_layer(
            dense_starts, n3, g_rows, *dense_own, dense_down, dense_more, tokens
        )
        back_mate = swap_dp(back, 1)
        back_got, _, y16, _, d16 = dense_layer(
            dense_starts,
            after(n_got, dn3, left_got),
            g_got,
            *dense_own,
            dense_down,
            dense_more,
            tokens,
        )
        back_got_mate = swap_dp(back_got, 1)
        dn3_more = swap_fs(d16)
    else:
        n_group = both_tokens(n3)
        back, _, y16, _, d16 = dense_layer(
            dense_starts, n_group, g_group, *dense_own, dense_down, dense_more, tokens
        )
        dn3 = jnp.zeros((tokens, width), F32)
        dn3_more = lax.psum_scatter(d16, "fsdp", scatter_dimension=0, tiled=True)
        dense_out = lax.psum_scatter(y16, "fsdp", scatter_dimension=0, tiled=True).astype(F32)
        outputs = (x2 + dense_out).astype(BF16)

    if chunked:
        where = jnp.stack([chip_of(me), core, shard, me // 2]).astype(jnp.int32)
        masks = [
            [
                sum(((slot >> (len(order) - 1 - at)) & 1) * (bit // 2) for at, bit in enumerate(order))
                for slot in range(chips)
            ]
            for order in (x_order, z_order)
        ]
        own_kept, own_sent, down_kept, down_sent, far_kept, far_sent = chunk_weights(
            functools.partial(dense_weight_kernel, *masks),
            where,
            (after(n3, dn3_more), n_got, g_rows, g_got, back, back_got, back_mate, back_got_mate),
            (
                span // chips * hidden // 128,
                hidden // chips * width // 256,
                span // chips * hidden // 128,
            ),
            chips // 2,
            [
                pltpu.VMEM((max(hidden, half), max(hidden, width // 2)), F32),
                pltpu.VMEM((4 * tokens, width), BF16),
            ],
            7,
            "dense_weight",
        )
        dn3_more = after(dn3_more, own_sent)
        own_got, down_got = swap_dp(own_sent, z_order[0]), swap_dp(down_sent, x_order[0])
        far_got, far_kept = swap_fs(far_sent), swap_fs(far_kept)

    straight = chunked and copies == 1
    if straight:
        slots = jnp.append(chip_of(me ^ (2 * jnp.arange(heads // 2))), core).astype(jnp.int32)
    else:
        slots = jnp.append(jnp.arange(heads // 2), 0).astype(jnp.int32)
    right, gx1, do1_heads, dkv_kept, dkv_sent, dc_two = pl.pallas_call(
        functools.partial(mid_backward_kernel, len(near_more)),
        out_shape=[
            jax.ShapeDtypeStruct((tokens, 3 * width), BF16),
            row32,
            jax.ShapeDtypeStruct((heads, rows, 128), BF16),
            jax.ShapeDtypeStruct((heads // 2, dp, micro_count, part, 128), BF16),
            jax.ShapeDtypeStruct((heads // 2, dp, micro_count, part, 128), BF16),
            jax.ShapeDtypeStruct((2, width), F32),
        ],
        in_specs=[smem()] * 2 + [vmem()] * (12 + len(near_more)),
        out_specs=[vmem()] * 6,
        scratch_shapes=[
            pltpu.VMEM((tokens, width), F32),
            pltpu.VMEM((tokens, width), BF16),
            pltpu.VMEM((tokens, width), BF16),
        ],
        compiler_params=params(),
        cost_estimate=cost(16),
        name="mid_backward",
    )(starts, slots, g, dn3, dn3_more, x1, x2, gains, q2, ke, ve, *near_own, *near_more)
    do1 = lax.all_to_all(
        jnp.repeat(do1_heads, copies, axis=0) if copies > 1 else do1_heads, "dp", 0, 0, tiled=True
    ).reshape(length, 128)

    if chunked:
        right_got = swap_fs(right)
        if straight:
            dkv_got = swap_dp(dkv_sent, 1)
            do1 = after(do1, dkv_got)
        do1 = after(do1, own_got, down_got, far_got)

    dqkv, table_grad = pl.pallas_call(
        self_backward_kernel,
        out_shape=[
            jax.ShapeDtypeStruct((length, 384), BF16),
            jax.ShapeDtypeStruct((TILE, length), F32),
        ],
        in_specs=[vmem()] * 5,
        out_specs=[vmem()] * 2,
        scratch_shapes=[pltpu.VMEM((length, 128), F32), pltpu.VMEM((length, 128), F32)],
        compiler_params=params(),
        cost_estimate=cost(10),
        name="self_backward",
    )(qkv, do1, table, doc_row, doc_col)
    if chunked:
        dqkv = after(dqkv, right_got, far_kept)
    head_grad = pl.pallas_call(
        head_weight_kernel,
        out_shape=jax.ShapeDtypeStruct((fs, span * 3 // 2, 128), BF16),
        in_specs=[vmem()] * 2,
        out_specs=vmem(),
        compiler_params=params(),
        cost_estimate=cost(6),
        name="head_weight",
    )(n_all, dqkv)
    def sum_shards(values):
        if paired:
            kept = lax.dynamic_index_in_dim(values, shard, 0)
            sent = lax.dynamic_index_in_dim(values, 1 - shard, 0)
            return (kept.astype(F32) + swap_fs(sent).astype(F32)).astype(BF16)
        return lax.psum_scatter(values, "fsdp", scatter_dimension=0, tiled=True)

    head_sum = sum_shards(head_grad)
    if chunked:
        token_kept, token_sent = chunk_weights(
            token_weight_kernel,
            where,
            (after(left, head_grad), left_got, right, right_got),
            (3 * half // chips * width // 128,),
            chips,
            [pltpu.VMEM((span, width), F32)],
            6,
            "token_weight",
        )
        token_got = swap_dp(token_sent, 1)
        head_sum = after(head_sum, token_kept)

    relative = me ^ (jnp.arange(heads, dtype=jnp.int32) * copies)
    head_places = (relative % 2) * chips + chip_of(relative)
    grad_query_self, grad_key_self, grad_value_self = pl.pallas_call(
        head_spread_kernel,
        out_shape=[jax.ShapeDtypeStruct((span, width), F32)] * 3,
        in_specs=[smem(), vmem(), vmem()],
        out_specs=[vmem()] * 3,
        compiler_params=params(),
        cost_estimate=cost(6),
        name="head_spread",
    )(head_places, *gather_chips(head_sum))

    if paired:
        first_own = (query_self, key_self, value_self)
        first_more = both_halves(after(half_rows(first_own), head_sum))
        y16 = swap_fs(after(y16, first_more[0]))
        outputs = (x2 + (y32 + y16.astype(F32))).astype(BF16)
    own_d = lax.all_to_all(dqkv.reshape(dp, rows, 384), "dp", 0, 0, tiled=True)[::copies]
    grad_inputs, dc_one = pl.pallas_call(
        functools.partial(input_grad_kernel, len(first_more)),
        out_shape=[row32, jax.ShapeDtypeStruct((1, width), F32)],
        in_specs=[smem()] + [vmem()] * (7 + len(first_more)),
        out_specs=[vmem()] * 2,
        scratch_shapes=[
            pltpu.VMEM((tokens, 3 * width), BF16),
            pltpu.VMEM((tokens, width), F32),
        ],
        compiler_params=params(),
        cost_estimate=cost(7),
        name="input_grad",
    )(starts, own_d, x, gains, gx1, *first_own, *first_more)

    if straight:
        dkv = reduce_chips(dkv_kept, dkv_got, [1] + x_order).reshape(-1, 128)
    else:
        dkv = jnp.stack([dkv_kept, dkv_sent], axis=1).reshape(heads * copies, -1, 128)
        dkv = lax.psum_scatter(dkv, "dp", scatter_dimension=0, tiled=True)[0]
        bit = 1
        while bit < copies:
            got = swap_dp(dkv, bit)
            dkv = jnp.where(
                (me // bit) % 2 == 0, jnp.concatenate([dkv, got]), jnp.concatenate([got, dkv])
            )
            bit *= 2
    cross_grad = pl.pallas_call(
        cross_head_weight_kernel,
        out_shape=jax.ShapeDtypeStruct((fs, span, 128), BF16),
        in_specs=[vmem()] * 2,
        out_specs=vmem(),
        compiler_params=params(),
        cost_estimate=cost(3),
        name="cross_head_weight",
    )(e_all, dkv)
    cross_sum = sum_shards(cross_grad)
    grad_key_cross, grad_value_cross = pl.pallas_call(
        cross_head_spread_kernel,
        out_shape=[jax.ShapeDtypeStruct((span, width), F32)] * 2,
        in_specs=[smem(), vmem(), vmem()],
        out_specs=[vmem()] * 2,
        compiler_params=params(),
        cost_estimate=cost(4),
        name="cross_head_spread",
    )(head_places, *gather_chips(cross_sum))
    own_dkv = dkv.reshape(dp, micro_count * part, 128)
    own_dkv = lax.all_to_all(own_dkv, "dp", 0, 0, tiled=True)[::copies]
    grad_encoded = pl.pallas_call(
        functools.partial(encoder_grad_kernel, len(kv_more)),
        out_shape=jax.ShapeDtypeStruct((micro_count * part, width), F32),
        in_specs=[smem()] + [vmem()] * (3 + len(kv_more)),
        out_specs=vmem(),
        scratch_shapes=[pltpu.VMEM((micro_count * part, width), BF16)] * 2,
        compiler_params=params(),
        cost_estimate=cost(4),
        name="encoder_grad",
    )(starts, own_dkv, *kv_own, *kv_more)

    if chunked:
        sums = (
            reduce_chips(own_kept, own_got, z_order, (right, token_kept)),
            reduce_chips(down_kept, down_got, x_order, (right, token_kept)),
            reduce_chips(
                far_kept, swap_dp(after(far_got, right), x_order[0]), x_order, (dqkv, token_kept)
            ),
        )
        pieces = lax.all_gather(jnp.concatenate(sums, axis=1), "dp", axis=0, tiled=True)
        grad_dense_gate, grad_dense_up, grad_dense_down = spread_dense(
            where, pieces, hidden, span, width
        )
        token_sum = after(reduce_chips(token_kept, token_got, [1] + x_order), cross_grad)
        token_low, token_high = gather_chips(token_sum)
        grad_output_cross, grad_query_cross, grad_output_self = spread_token(
            where, token_low, token_high, span, width, 3
        )
    else:

        def over_dp(values):
            return lax.psum(values.astype(BF16), "dp").astype(F32)

        def over_all(a, b):
            made = t_dot(a, b).astype(BF16)
            return over_dp(lax.psum_scatter(made, "fsdp", scatter_dimension=0, tiled=True))

        grad_output_cross, grad_query_cross, grad_output_self = (
            over_all(left[kind], right[:, kind * width : (kind + 1) * width]) for kind in range(3)
        )
        grad_dense_gate, grad_dense_up = (
            over_dp(
                lax.all_to_all(
                    t_dot(n_group, back[:, kind * hidden : (kind + 1) * hidden]).astype(BF16),
                    "fsdp",
                    0,
                    1,
                    tiled=True,
                )
            )
            for kind in range(2)
        )
        grad_dense_down = over_dp(t_dot(back[:, 2 * hidden :], g_group))

    if chunked:
        table_grad = after(table_grad, first_more[1])
    table_sums = jnp.sum(bucket_sums(edges, table_grad, bias_all.shape[0]), axis=1)
    column = (jnp.arange(heads) == head) & (me % copies == 0)
    bias_row = jnp.where(column[None, :], table_sums[:, None], 0.0).reshape(1, -1)
    bias_row = jnp.pad(bias_row, ((0, 0), (0, width - bias_row.shape[1])))
    sums = jnp.concatenate([dc_one, dc_two, bias_row], axis=0)
    if paired:
        sums = sums + swap_fs(sums)
        for bit in [1] + chip_bits:
            sums = sums + swap_dp(sums, bit)
    else:
        sums = lax.psum(sums, ("dp", "fsdp"))
    own = lax.dynamic_slice_in_dim(sums[:3], shard * span, span, axis=1)
    grad_bias = sums[3, : bias_all.size].reshape(bias_all.shape)
    grad_bias = lax.dynamic_slice_in_dim(
        grad_bias, shard * position_bias.shape[0], position_bias.shape[0], axis=0
    )
    shape = (micro_count, 1, rows, width)
    return (
        outputs.reshape(shape),
        grad_inputs.reshape(shape),
        grad_encoded.reshape(micro_count, 1, part, width),
        own[0],
        grad_query_self,
        grad_key_self,
        grad_value_self,
        grad_output_self,
        grad_bias,
        own[2],
        grad_query_cross,
        grad_key_cross,
        grad_value_cross,
        grad_output_cross,
        own[1],
        grad_dense_gate,
        grad_dense_up,
        grad_dense_down,
    )


def solution(mesh):
    matrix = P("fsdp", None)
    token = P(None, "fsdp", "dp", None)
    weights = (
        (P("fsdp"),)
        + (matrix,) * 5
        + (P("fsdp"),)
        + (matrix,) * 4
        + (P("fsdp"),)
        + (matrix,) * 3
    )
    return jax.shard_map(
        per_device,
        mesh=mesh,
        in_specs=(token,) * 3 + (P(None, "fsdp", None), P()) + weights,
        out_specs=(token,) * 3 + weights,
        check_vma=False,
    )
```

```python
import functools

import jax
import jax.numpy as jnp
from jax import lax
from jax.experimental import pallas as pl
from jax.experimental.pallas import tpu as pltpu
from jax.sharding import PartitionSpec as P

EPS = 1e-06
NEGATIVE = -1e30
TILE = 256
F32 = jnp.float32
BF16 = jnp.bfloat16
VMEM_LIMIT = 56 * 1024 * 1024


def vmem():
    return pl.BlockSpec(memory_space=pltpu.VMEM)


def smem():
    return pl.BlockSpec(memory_space=pltpu.SMEM)


def params(limit=VMEM_LIMIT):
    return pltpu.CompilerParams(vmem_limit_bytes=limit)


def cost(microseconds):
    return pl.CostEstimate(
        flops=int(microseconds * 1.15e9),
        bytes_accessed=int(microseconds * 3.69e6),
        transcendentals=0,
    )


def aligned(start, size):
    return pl.ds(pl.multiple_of(start, size), size)


def dot(left, right):
    return jnp.dot(left, right, preferred_element_type=F32)


def dot_t(left, right):
    return lax.dot_general(left, right, (((1,), (1,)), ((), ())), preferred_element_type=F32)


def t_dot(left, right):
    return lax.dot_general(left, right, (((0,), (0,)), ((), ())), preferred_element_type=F32)


def norm_rows(values, gain):
    return values * lax.rsqrt(jnp.mean(values * values, axis=-1, keepdims=True) + EPS) * gain


def norm_back(values, gain, grad):
    r = lax.rsqrt(jnp.mean(values * values, axis=-1, keepdims=True) + EPS)
    scaled = grad * gain
    inner = jnp.mean(scaled * values, axis=-1, keepdims=True)
    back = r * scaled - values * (r * r * r * inner)
    return back, jnp.sum(grad * (values * r), axis=0, keepdims=True)


def low_lanes(rows):
    return lax.broadcasted_iota(jnp.int32, (rows, 128), 1) < 64


def pair_up(first, second):
    lane = low_lanes(first.shape[0])
    low = jnp.where(lane, first, pltpu.roll(second, 64, 1))
    high = jnp.where(lane, pltpu.roll(first, 64, 1), second)
    return low, high


def keep_half(values, half):
    lane = low_lanes(values.shape[0])
    return jnp.where(lane if half == 0 else ~lane, values, jnp.zeros_like(values))


def softmax_rows(scores):
    top = jnp.max(scores, axis=-1, keepdims=True)
    raised = jnp.exp(scores - top)
    return raised * (1.0 / jnp.sum(raised, axis=-1, keepdims=True))


def table_kernel(edge_ref, value_ref, out_ref):
    rows, length = out_ref.shape
    bucket_count = value_ref.shape[0]
    for start in range(0, length, TILE):
        place = (rows, TILE)
        apart = (
            lax.broadcasted_iota(jnp.int32, place, 0)
            - lax.broadcasted_iota(jnp.int32, place, 1)
            + (length - rows - start)
        )
        value = jnp.full(place, value_ref[0], F32)
        for bucket in range(1, bucket_count):
            value = jnp.where(apart >= edge_ref[bucket], value_ref[bucket], value)
        out_ref[:, start : start + TILE] = jnp.where(apart >= 0, value, NEGATIVE)


def bias_table(edges, values, length):
    return pl.pallas_call(
        table_kernel,
        out_shape=jax.ShapeDtypeStruct((TILE, length), F32),
        in_specs=[smem(), smem()],
        out_specs=vmem(),
        cost_estimate=cost(4),
        name="bias_table",
    )(edges, values)


def bucket_kernel(edge_ref, grad_ref, out_ref):
    rows, length = grad_ref.shape
    bucket_count = out_ref.shape[0]
    above = [jnp.zeros((8, TILE), F32) for _ in range(bucket_count)]
    for start in range(0, length, TILE):
        for row in range(0, rows, 8):
            place = (8, TILE)
            apart = (
                lax.broadcasted_iota(jnp.int32, place, 0)
                - lax.broadcasted_iota(jnp.int32, place, 1)
                + (length - rows - start + row)
            )
            tile = grad_ref[row : row + 8, start : start + TILE]
            for bucket in range(bucket_count):
                above[bucket] = above[bucket] + jnp.where(apart >= edge_ref[bucket], tile, 0.0)
    for bucket in range(bucket_count):
        rest = above[bucket + 1] if bucket + 1 < bucket_count else 0.0
        part = jnp.sum(above[bucket] - rest, axis=0, keepdims=True)
        out_ref[bucket : bucket + 1, :] = part[:, :128] + part[:, 128:]


def bucket_sums(edges, grad, bucket_count):
    return pl.pallas_call(
        bucket_kernel,
        out_shape=jax.ShapeDtypeStruct((bucket_count, 128), F32),
        in_specs=[smem(), vmem()],
        out_specs=vmem(),
        cost_estimate=cost(7),
        name="bucket_sums",
    )(edges, grad)


def times(x_ref, starts_ref, pieces):
    if len(pieces) == 1:
        return dot(x_ref[...], pieces[0])
    total = None
    for place, piece in enumerate(pieces):
        rows = piece.shape[0]
        part = dot(x_ref[:, aligned(starts_ref[place], rows)], piece)
        total = part if total is None else total + part
    return total


def times_back(out_ref, starts_ref, terms):
    for place in range(len(terms[0][1])):
        total = sum(dot_t(d, pieces[place]) for d, pieces in terms)
        rows = terms[0][1][place].shape[0]
        if len(terms[0][1]) == 1:
            out_ref[...] = total
        else:
            out_ref[:, aligned(starts_ref[place], rows)] = total


def pieces_of(own_ref, more, index):
    return [own_ref[...]] + [ref[index] for ref in more]


def self_scores(q, k, table, doc_col, doc_row):
    scores = dot_t(q, k) + table
    return jnp.where(doc_col == doc_row, scores, NEGATIVE)


def self_forward_kernel(groups, source_ref, *refs):
    x_refs = refs[:groups]
    gain_ref, w_ref, table_ref, doc_row_ref, doc_col_ref, n_ref, qkv_ref, o_ref = refs[groups:]
    count, _, rows, width = x_refs[0].shape
    length = groups * count * rows
    lane = lax.broadcasted_iota(jnp.int32, (rows, 384), 1) % 128 < 64
    together = min(TILE // rows, count)
    for place, x_ref in enumerate(x_refs):
        for first in range(0, count, together):
            parts = []
            for inner in range(first, first + together):
                x = x_ref[inner].astype(F32).reshape(2 * rows, width)
                n = norm_rows(x, gain_ref[...]).astype(BF16)
                n_ref[source_ref[place * count + inner]] = n.reshape(2, rows, width)
                parts.append(n)
            made = dot(jnp.concatenate(parts, axis=0), w_ref[...])
            for inner in range(together):
                at = 2 * rows * inner
                picked = jnp.where(lane, made[at : at + rows], made[at + rows : at + 2 * rows])
                own = source_ref[place * count + first + inner]
                qkv_ref[aligned(own * rows, rows), :] = picked.astype(BF16)
    for block in range(length // TILE):
        start, stop = block * TILE, (block + 1) * TILE
        table = table_ref[:, length - stop :]
        q = qkv_ref[start:stop, 0:128]
        k = qkv_ref[:stop, 128:256]
        v = qkv_ref[:stop, 256:384]
        mixed = []
        for half in range(2):
            scores = self_scores(
                keep_half(q, half),
                k,
                table,
                doc_col_ref[half, start:stop, :],
                doc_row_ref[half : half + 1, :stop],
            )
            mixed.append(dot(softmax_rows(scores).astype(BF16), v))
        o_ref[start:stop, :] = jnp.where(low_lanes(TILE), mixed[0], mixed[1]).astype(BF16)


def self_backward_kernel(
    qkv_ref, do_ref, table_ref, doc_row_ref, doc_col_ref, dqkv_ref, grad_ref, dk_ref, dv_ref
):
    length = qkv_ref.shape[0]
    grad_ref[...] = jnp.zeros_like(grad_ref)
    dk_ref[...] = jnp.zeros_like(dk_ref)
    dv_ref[...] = jnp.zeros_like(dv_ref)
    for block in range(length // TILE):
        start, count = block * TILE, (block + 1) * TILE
        table = table_ref[:, length - count :]
        k = qkv_ref[:count, 128:256]
        v = qkv_ref[:count, 256:384]
        made = []
        for half in range(2):
            q = keep_half(qkv_ref[start:count, 0:128], half)
            do = keep_half(do_ref[start:count, :], half)
            p = softmax_rows(
                self_scores(
                    q,
                    k,
                    table,
                    doc_col_ref[half, start:count, :],
                    doc_row_ref[half : half + 1, :count],
                )
            )
            dp = dot_t(do, v)
            ds = (p * (dp - jnp.sum(p * dp, axis=-1, keepdims=True))).astype(BF16)
            grad_ref[:, length - count :] += ds.astype(F32)
            made.append(dot(ds, k))
            dk_ref[:count, :] += t_dot(ds, q)
            dv_ref[:count, :] += t_dot(p.astype(BF16), do)
        dq = jnp.where(low_lanes(TILE), made[0], made[1])
        dqkv_ref[start:count, 0:128] = dq.astype(BF16)
    dqkv_ref[:, 128:256] = dk_ref[...].astype(BF16)
    dqkv_ref[:, 256:384] = dv_ref[...].astype(BF16)


def head_weight_kernel(n_ref, d_ref, out_ref):
    blocks, _, rows, width = n_ref.shape
    shards = out_ref.shape[0]
    span = width // shards
    lane = lax.broadcasted_iota(jnp.int32, (blocks * rows, 384), 1) % 128 < 64
    d = d_ref[...]
    zero = jnp.zeros_like(d)
    right = [jnp.where(lane, d, zero), jnp.where(lane, zero, d)]
    half = span // 2
    for shard in range(shards):
        total = jnp.zeros((span, 384), F32)
        for micro in range(2):
            left = n_ref[:, micro, :, shard * span : (shard + 1) * span]
            total = total + t_dot(left.reshape(blocks * rows, span), right[micro])
        q, k, v = (
            total[:, at : at + 128] + pltpu.roll(total[:, at : at + 128], 64, 1)
            for at in (0, 128, 256)
        )
        out_ref[shard, :span, :] = jnp.where(low_lanes(span), q, k).astype(BF16)
        out_ref[shard, span:, :] = jnp.where(low_lanes(half), v[:half], v[half:]).astype(BF16)


def cross_kv_kernel(split, starts_ref, e_ref, wk_ref, wv_ref, *refs):
    more, (ke_ref, ve_ref) = refs[:split], refs[split:]
    blocks, _, part, _ = e_ref.shape
    for index, (own_ref, out_ref) in enumerate(((wk_ref, ke_ref), (wv_ref, ve_ref)), 3):
        total = None
        pieces = pieces_of(own_ref, more, index)
        for place, piece in enumerate(pieces):
            rows = piece.shape[0]
            if split:
                left = e_ref[:, 0, :, aligned(starts_ref[place], rows)]
            else:
                left = e_ref[:, 0]
            made = dot(left.reshape(blocks * part, rows), piece)
            total = made if total is None else total + made
        out_ref[0] = total.astype(BF16)


def cross_kv(starts, e_all, wk, wv, more):
    blocks, micro, part, width = e_all.shape
    whole = lambda array: pl.BlockSpec(array.shape, lambda m, s: (0,) * array.ndim)
    out = pl.BlockSpec((1, blocks * part, width), lambda m, s: (m, 0, 0))
    return pl.pallas_call(
        functools.partial(cross_kv_kernel, len(more)),
        grid_spec=pltpu.PrefetchScalarGridSpec(
            num_scalar_prefetch=1,
            grid=(micro,),
            in_specs=[pl.BlockSpec((blocks, 1, part, width), lambda m, s: (0, m, 0, 0))]
            + [whole(array) for array in (wk, wv, *more)],
            out_specs=[out, out],
        ),
        out_shape=[jax.ShapeDtypeStruct((micro, blocks * part, width), BF16)] * 2,
        compiler_params=params(),
        cost_estimate=cost(8),
        name="cross_kv",
    )(starts, e_all, wk, wv, *more)


def mid_forward_kernel(split, starts_ref, o1_ref, x_ref, gain_ref, ke_ref, ve_ref, wo, wq, wc, *refs):
    more = refs[:split]
    left_ref, x1_ref, q2_ref, x2_ref, n3_ref, o1c_ref, n2_ref, o2_ref = refs[split:]
    heads, rows, _ = o1_ref.shape
    width = x_ref.shape[-1]
    for pair in range(heads // 2):
        at = pair * 128
        low, high = pair_up(o1_ref[2 * pair].astype(F32), o1_ref[2 * pair + 1].astype(F32))
        o1c_ref[0:rows, at : at + 128] = low.astype(BF16)
        o1c_ref[rows : 2 * rows, at : at + 128] = high.astype(BF16)
    x = x_ref[...].astype(F32).reshape(2 * rows, width)
    x1 = x + times(o1c_ref, starts_ref, pieces_of(wo, more, 0))
    x1_ref[...] = x1
    n2_ref[...] = norm_rows(x1, gain_ref[1:2]).astype(BF16)
    q2_ref[...] = times(n2_ref, starts_ref, pieces_of(wq, more, 1)).astype(BF16)
    for micro in range(2):
        for pair in range(heads // 2):
            at = pair * 128
            span = slice(micro * rows, (micro + 1) * rows)
            q = q2_ref[span, at : at + 128]
            both = jnp.concatenate([keep_half(q, 0), keep_half(q, 1)], axis=0)
            p = softmax_rows(dot_t(both, ke_ref[micro, :, at : at + 128]))
            o = dot(p.astype(BF16), ve_ref[micro, :, at : at + 128])
            o2_ref[span, at : at + 128] = jnp.where(
                low_lanes(rows), o[:rows], o[rows:]
            ).astype(BF16)
    x2 = x1 + times(o2_ref, starts_ref, pieces_of(wc, more, 2))
    x2_ref[...] = x2
    n3_ref[...] = norm_rows(x2, gain_ref[2:3]).astype(BF16)
    left_ref[0] = o2_ref[...]
    left_ref[1] = n2_ref[...]
    left_ref[2] = o1c_ref[...]


def cross_backward_kernel(
    split, starts_ref, slots_ref, g_ref, dn3_ref, more_ref, x2_ref, gain_ref, q2_ref, ke_ref, ve_ref,
    wc, *refs
):
    more = refs[:split]
    right_ref, gx2_ref, keep_ref, send_ref, dc_ref, back_ref, do2_ref = refs[split:]
    blocks, micros, part = keep_ref.shape[1:4]
    tokens, width = x2_ref.shape
    rows = tokens // micros
    pairs = width // 128
    even = slots_ref[pairs] == 0
    dn3 = dn3_ref[...] + more_ref[...].astype(F32)
    back, dc_ref[...] = norm_back(x2_ref[...], gain_ref[2:3], dn3)
    gx2 = g_ref[...].astype(F32) + back
    gx2_ref[...] = gx2
    gx2b = gx2.astype(BF16)
    right_ref[:, 0:width] = gx2b
    times_back(back_ref, starts_ref, [(gx2b, pieces_of(wc, more, 2))])
    do2_ref[...] = back_ref[...].astype(BF16)
    for micro in range(micros):
        for pair in range(pairs):
            at = pair * 128
            span = slice(micro * rows, (micro + 1) * rows)
            q = q2_ref[span, at : at + 128]
            do = do2_ref[span, at : at + 128]
            q = jnp.concatenate([keep_half(q, 0), keep_half(q, 1)], axis=0)
            do = jnp.concatenate([keep_half(do, 0), keep_half(do, 1)], axis=0)
            k = ke_ref[micro, :, at : at + 128]
            v = ve_ref[micro, :, at : at + 128]
            p = softmax_rows(dot_t(q, k))
            dp = dot_t(do, v)
            ds = (p * (dp - jnp.sum(p * dp, axis=-1, keepdims=True))).astype(BF16)
            dq = dot(ds, k)
            right_ref[span, width + at : width + at + 128] = jnp.where(
                low_lanes(rows), dq[:rows], dq[rows:]
            ).astype(BF16)
            low, high = pair_up(t_dot(ds, q), t_dot(p.astype(BF16), do))
            kept, sent = jnp.where(even, low, high), jnp.where(even, high, low)
            slot = slots_ref[pair]
            keep_ref[slot, :, micro] = kept.astype(BF16).reshape(blocks, part, 128)
            send_ref[slot, :, micro] = sent.astype(BF16).reshape(blocks, part, 128)


def mid_backward_kernel(split, starts_ref, right_ref, gx2_ref, x1_ref, gain_ref, wo, wq, *refs):
    more = refs[:split]
    gx1_ref, low_ref, do1_ref, dc_ref, back_ref = refs[split:]
    heads, rows, _ = do1_ref.shape
    width = x1_ref.shape[-1]
    times_back(back_ref, starts_ref, [(right_ref[:, width:], pieces_of(wq, more, 1))])
    back, dc_ref[...] = norm_back(x1_ref[...], gain_ref[1:2], back_ref[...])
    gx1 = gx2_ref[...] + back
    gx1_ref[...] = gx1
    gx1b = gx1.astype(BF16)
    low_ref[...] = gx1b
    times_back(back_ref, starts_ref, [(gx1b, pieces_of(wo, more, 0))])
    for pair in range(heads // 2):
        at = pair * 128
        do1 = back_ref[:, at : at + 128].astype(BF16).astype(F32)
        low, high = pair_up(do1[:rows], do1[rows:])
        do1_ref[2 * pair] = low.astype(BF16)
        do1_ref[2 * pair + 1] = high.astype(BF16)


def input_grad_kernel(split, starts_ref, d_ref, x_ref, gain_ref, gx1_ref, wq, wk, wv, *refs):
    more = refs[:split]
    out_ref, dc_ref, all_ref, back_ref = refs[split:]
    heads, rows, _ = d_ref.shape
    width = x_ref.shape[-1]
    for kind in range(3):
        for pair in range(heads // 2):
            lanes = slice(kind * 128, (kind + 1) * 128)
            low, high = pair_up(
                d_ref[2 * pair, :, lanes].astype(F32), d_ref[2 * pair + 1, :, lanes].astype(F32)
            )
            at = kind * width + pair * 128
            all_ref[0:rows, at : at + 128] = low.astype(BF16)
            all_ref[rows : 2 * rows, at : at + 128] = high.astype(BF16)
    terms = [
        (all_ref[:, kind * width : (kind + 1) * width], pieces_of(own, more, kind))
        for kind, own in enumerate((wq, wk, wv))
    ]
    times_back(back_ref, starts_ref, terms)
    x = x_ref[...].astype(F32).reshape(2 * rows, width)
    back, dc = norm_back(x, gain_ref[0:1], back_ref[...])
    dc_ref[...] = dc
    out_ref[...] = gx1_ref[...] + back


def encoder_grad_kernel(split, starts_ref, d_ref, wk, wv, *refs):
    more = refs[:split]
    out_ref, k_ref, v_ref = refs[split:]
    for pair in range(d_ref.shape[0] // 2):
        at = pair * 128
        low, high = pair_up(d_ref[2 * pair].astype(F32), d_ref[2 * pair + 1].astype(F32))
        k_ref[:, at : at + 128] = low.astype(BF16)
        v_ref[:, at : at + 128] = high.astype(BF16)
    terms = [(k_ref[...], pieces_of(wk, more, 3)), (v_ref[...], pieces_of(wv, more, 4))]
    times_back(out_ref, starts_ref, terms)


def cross_head_weight_kernel(e_ref, d_ref, out_ref):
    blocks, micro, part, width = e_ref.shape
    shards, span, _ = out_ref.shape
    for shard in range(shards):
        left = e_ref[:, :, :, shard * span : (shard + 1) * span]
        left = left.reshape(blocks * micro * part, span)
        out_ref[shard] = t_dot(left, d_ref[...]).astype(BF16)


def dense_kernel(split, starts_ref, n_ref, g_ref, wg, wu, wd_ref, *refs):
    more = refs[:split]
    back_ref, y_ref, ylow_ref, d_ref, dlow_ref = refs[split:]
    hidden = wd_ref.shape[0]
    gate, up = pieces_of(wg, more, 0), pieces_of(wu, more, 1)
    a = times(n_ref, starts_ref, gate)
    b = times(n_ref, starts_ref, up)
    scale = 0.7978845608028654
    cubed = 0.044715
    inner = jnp.tanh(scale * (a + cubed * (a * a * a)))
    gelu = 0.5 * a * (1.0 + inner)
    slope = 0.5 * (1.0 + inner) + 0.5 * a * (1.0 - inner * inner) * (
        scale * (1.0 + 3.0 * cubed * (a * a))
    )
    hid = (gelu * b).astype(BF16)
    dh = dot_t(g_ref[...], wd_ref[...])
    da = (dh * b * slope).astype(BF16)
    db = (dh * gelu).astype(BF16)
    times_back(d_ref, starts_ref, [(da, gate), (db, up)])
    dlow_ref[...] = d_ref[...].astype(BF16)
    y = dot(hid, wd_ref[...])
    y_ref[...] = y
    ylow_ref[...] = y.astype(BF16)
    back_ref[:, 0:hidden] = da
    back_ref[:, hidden : 2 * hidden] = db
    back_ref[:, 2 * hidden : 3 * hidden] = hid
    if more:
        shard, other = starts_ref[len(more) + 1], 1 - starts_ref[len(more) + 2]
        put_features(back_ref, 3 * hidden, n_ref, g_ref, shard, other)


def put_features(out_ref, at, n_ref, g_ref, shard, core):
    quarter = n_ref.shape[1] // 4
    for side, place in enumerate((2 * shard + core, 2 * (1 - shard) + core)):
        lanes = slice(at + side * quarter, at + (side + 1) * quarter)
        out_ref[:, lanes] = n_ref[:, aligned(place * quarter, quarter)]
    lanes = slice(at + 2 * quarter, at + 4 * quarter)
    out_ref[:, lanes] = g_ref[:, aligned(core * 2 * quarter, 2 * quarter)]


def dense_layer(starts, n, g, wg, wu, wd, more, step):
    count, width = n.shape
    hidden = wd.shape[0]
    which = starts.shape[0] - 2
    back = 3 * hidden + (width if more else 0)
    row = lambda size: pl.BlockSpec((step, size), lambda i, s: (i, 0))
    whole = lambda array: pl.BlockSpec(array.shape, lambda i, s: (0,) * array.ndim)
    column = pl.BlockSpec((wg.shape[0], hidden), lambda i, s: (0, s[which]))
    made = lambda size, kind: jax.ShapeDtypeStruct((count, size), kind)
    return pl.pallas_call(
        functools.partial(dense_kernel, len(more)),
        grid_spec=pltpu.PrefetchScalarGridSpec(
            num_scalar_prefetch=1,
            grid=(count // step,),
            in_specs=[row(width), row(width), column, column, whole(wd)]
            + [whole(array) for array in more],
            out_specs=[row(back)] + [row(width)] * 4,
        ),
        out_shape=[made(back, BF16)]
        + [made(width, F32), made(width, BF16), made(width, F32), made(width, BF16)],
        compiler_params=params(),
        cost_estimate=cost(13),
        name="dense_layer",
    )(starts, n, g, wg, wu, wd, *more)


def put_chunk(ref, slot, at, value):
    rows, width = value.shape
    for block in range(width // 128):
        ref[slot, at + block * rows : at + (block + 1) * rows, :] = value[
            :, block * 128 : (block + 1) * 128
        ].astype(BF16)


def take_chunk(ref, slot, at, rows, width):
    return jnp.concatenate(
        [
            ref[slot, at + block * rows : at + (block + 1) * rows, :].astype(F32)
            for block in range(width // 128)
        ],
        axis=1,
    )


def put_all(scratch_ref, first, count, chip, chunk_refs, at, width, masks):
    slots = [(ref, slot) for ref in chunk_refs for slot in range(ref.shape[0])]
    rows = count // len(slots)
    for (ref, slot), mask in zip(slots, masks):
        chunk = scratch_ref[aligned(first + (chip ^ mask) * rows, rows), :width]
        put_chunk(ref, slot, at, chunk)


def dense_weight_kernel(
    x_masks, z_masks, where_ref, n0_ref, n1_ref, g0_ref, g1_ref, own0_ref, own1_ref, mate0_ref, mate1_ref, keep_ref,
    send_ref, down_keep_ref, down_send_ref, far_keep_ref, far_send_ref, scratch_ref, left_ref
):
    tokens, width = n0_ref.shape
    hidden = (own0_ref.shape[1] - width) // 3
    quarter = width // 4
    at = keep_ref.shape[1] // 2
    core, shard, chip = where_ref[0], where_ref[1], where_ref[2]
    put_features(left_ref.at[:tokens], 0, n0_ref, g0_ref, shard, core)
    put_features(left_ref.at[tokens : 2 * tokens], 0, n1_ref, g1_ref, shard, core)
    left_ref[2 * tokens : 3 * tokens, :] = mate0_ref[:, 3 * hidden :]
    left_ref[3 * tokens :, :] = mate1_ref[:, 3 * hidden :]

    def whole(kind):
        span = slice(kind * hidden, (kind + 1) * hidden)
        refs = (own0_ref, own1_ref, mate0_ref, mate1_ref)
        return jnp.concatenate([ref[:, span] for ref in refs], axis=0)

    for kind in range(2):
        right = whole(kind)
        for side, (masks, refs) in enumerate(
            ((z_masks, (keep_ref, send_ref)), (x_masks, (far_keep_ref, far_send_ref)))
        ):
            value = t_dot(left_ref[:, side * quarter : (side + 1) * quarter], right)
            scratch_ref[:quarter, :hidden] = value
            put_all(scratch_ref, 0, quarter, chip, refs, kind * at, hidden, masks)
    value = t_dot(whole(2), left_ref[:, 2 * quarter :])
    scratch_ref[:, : 2 * quarter] = value
    refs = (down_keep_ref, down_send_ref)
    put_all(scratch_ref, 0, hidden, chip, refs, 0, 2 * quarter, x_masks)


def token_weight_kernel(
    masks, where_ref, left_ref, left_more_ref, right_ref, right_more_ref, last_ref, last_more_ref,
    mine_ref, mate_ref, scratch_ref
):
    kinds, _, span = left_more_ref.shape
    width = last_ref.shape[1]
    core, shard, chip = where_ref[0], where_ref[1], where_ref[2]
    half = span // 2
    at = half // len(masks) * width // 128
    for kind in range(kinds):
        lanes = slice(kind * width, (kind + 1) * width)
        left = [left_ref[kind, :, aligned(shard * span, span)], left_more_ref[kind]]
        if kind < kinds - 1:
            right = [right_ref[:, lanes], right_more_ref[:, lanes]]
        else:
            right = [last_ref[...], last_more_ref[...]]
        scratch_ref[...] = t_dot(jnp.concatenate(left, axis=0), jnp.concatenate(right, axis=0))
        for ref, own in ((mine_ref, core), (mate_ref, 1 - core)):
            put_all(scratch_ref, own * half, half, chip, (ref,), kind * at, width, masks)


def chunk_weights(kernel, where, operands, counts, slots, scratches, length, name):
    shapes = []
    for count in counts:
        shapes += [jax.ShapeDtypeStruct((slots, count, 128), BF16)] * 2
    return pl.pallas_call(
        kernel,
        out_shape=shapes,
        in_specs=[smem()] + [vmem()] * len(operands),
        out_specs=[vmem()] * len(shapes),
        scratch_shapes=scratches,
        compiler_params=params(),
        cost_estimate=cost(length),
        name=name,
    )(where, *operands)


def head_rows(in_ref, at, rows, outs):
    for pair in range(in_ref.shape[0] // 2):
        lanes = slice(pair * 128, (pair + 1) * 128)
        first = in_ref[2 * pair, at : at + rows, :].astype(F32)
        second = in_ref[2 * pair + 1, at : at + rows, :].astype(F32)
        for (out_ref, place), value in zip(outs, pair_up(first, second)):
            out_ref[place, lanes] = value


def head_spread(in_ref, at, q_ref, k_ref, v_ref):
    span = q_ref.shape[0]
    half = span // 2
    head_rows(in_ref, at, span, ((q_ref, slice(None)), (k_ref, slice(None))))
    head_rows(in_ref, at + span, half, ((v_ref, slice(0, half)), (v_ref, slice(half, span))))


def first_spread_kernel(where_ref, in_ref, gate_ref, up_ref, down_ref, q_ref, k_ref, v_ref):
    shard = where_ref[1]
    hidden = gate_ref.shape[3] // 2
    rows = gate_ref.shape[2] // 2
    at = rows * hidden // 128
    tall = down_ref.shape[0] // 2
    half = down_ref.shape[1] // 2
    for piece in range(4):
        chip, core = piece // 2, piece % 2
        place = slice(chip * rows, (chip + 1) * rows)
        for side, start in enumerate((0, 4 * at)):
            lanes = aligned((shard ^ side) * hidden, hidden)
            for kind, out_ref in enumerate((gate_ref, up_ref)):
                chunk = take_chunk(in_ref, piece, start + kind * at, rows, hidden)
                out_ref[core, 0, place, lanes] = chunk
        chunk = take_chunk(in_ref, piece, 2 * at, tall, half)
        down_ref[chip * tall : (chip + 1) * tall, core * half : (core + 1) * half] = chunk
    head_spread(in_ref, 6 * at, q_ref, k_ref, v_ref)


def second_spread_kernel(where_ref, in_ref, *out_refs):
    kinds = len(out_refs) - 2
    k_ref, v_ref = out_refs[kinds:]
    rows, width = out_refs[0].shape[2] // 2, out_refs[0].shape[3]
    at = rows * width // 128
    for piece in range(4):
        chip, core = piece // 2, piece % 2
        for kind in range(kinds):
            chunk = take_chunk(in_ref, piece, kind * at, rows, width)
            out_refs[kind][core, 0, chip * rows : (chip + 1) * rows, :] = chunk
    span = k_ref.shape[0]
    head_rows(in_ref, kinds * at, span, ((k_ref, slice(None)), (v_ref, slice(None))))


def spread(kernel, where, pieces, outs, length, name):
    count, total, _ = pieces.shape
    steps = count // 4
    specs, shapes = [], []
    for (rows, cols), kind in outs:
        if kind == "core":
            shapes.append((2, steps, rows // (2 * steps), cols))
            block = (2, 1, rows // (2 * steps), cols)
            specs.append(pl.BlockSpec(block, lambda q, where: (0, q, 0, 0)))
        elif kind == "chip":
            shapes.append((rows, cols))
            specs.append(pl.BlockSpec((rows // steps, cols), lambda q, where: (q, 0)))
        else:
            shapes.append((rows, cols))
            specs.append(pl.BlockSpec((rows, cols // steps), lambda q, where: (0, q)))
    made = pl.pallas_call(
        kernel,
        grid_spec=pltpu.PrefetchScalarGridSpec(
            num_scalar_prefetch=1,
            grid=(steps,),
            in_specs=[pl.BlockSpec((4, total, 128), lambda q, where: (q, 0, 0))],
            out_specs=specs,
        ),
        out_shape=[jax.ShapeDtypeStruct(shape, F32) for shape in shapes],
        compiler_params=params(),
        cost_estimate=cost(length),
        name=name,
    )(where, pieces)
    return [array.reshape(shape) for array, (shape, _) in zip(made, outs)]


def plain_head_kernel(in_ref, *out_refs):
    span = out_refs[0].shape[0]
    if len(out_refs) == 3:
        head_spread(in_ref, 0, *out_refs)
    else:
        head_rows(in_ref, 0, span, [(out_ref, slice(None)) for out_ref in out_refs])


def plain_head_spread(pieces, span, width, kinds):
    return pl.pallas_call(
        plain_head_kernel,
        out_shape=[jax.ShapeDtypeStruct((span, width), F32)] * kinds,
        in_specs=[vmem()],
        out_specs=[vmem()] * kinds,
        compiler_params=params(),
        name="plain_head_spread",
    )(pieces)


def per_device(
    inputs,
    encoded,
    cotangent,
    doc_ids,
    buckets,
    gain_self,
    query_self,
    key_self,
    value_self,
    output_self,
    position_bias,
    gain_cross,
    query_cross,
    key_cross,
    value_cross,
    output_cross,
    gain_dense,
    dense_gate,
    dense_up,
    dense_down,
):
    micro_count, _, rows, width = inputs.shape
    part = encoded.shape[2]
    heads = position_bias.shape[1]
    dp, fs = lax.axis_size("dp"), lax.axis_size("fsdp")
    me, shard = lax.axis_index("dp"), lax.axis_index("fsdp")
    core, chips = me % 2, dp // 2
    length = rows * dp
    tokens = micro_count * rows
    copies = dp // heads
    head = me // copies
    span = width // fs
    half = span // 2
    hidden = dense_down.shape[0]
    chip_bits = [1 << place for place in range(1, dp.bit_length() - 1)]
    x_order, z_order = chip_bits, chip_bits[1:] + chip_bits[:1]
    paired = fs == 2
    chunked = paired and half % (16 * chips) == 0 and hidden % (16 * chips) == 0
    chunked = chunked and hidden % 128 == 0 and dp == heads and dp % 4 == 0

    def chip_of(j):
        last = len(x_order) - 1
        return sum(((j // bit) % 2) << (last - place) for place, bit in enumerate(x_order))

    def swap_dp(values, bit):
        return lax.ppermute(values, "dp", [(j, j ^ bit) for j in range(dp)])

    def swap_fs(values):
        return lax.ppermute(values, "fsdp", [(j, 1 - j) for j in range(2)])

    def after(values, *others):
        return lax.optimization_barrier((values, *others))[0]

    def half_rows(values):
        return jnp.stack([lax.dynamic_slice_in_dim(w, core * half, half, axis=0) for w in values])

    def both_halves(sent):
        got = swap_fs(sent)
        return got, swap_dp(got, 1)

    def quarter(bit):
        return 2 * ((me // bit) % 2) + core

    def quarter_starts(bit):
        rows = [(1 - shard) * span + (quarter(bit) ^ more) * (half // 2) for more in (0, 2, 1, 3)]
        return jnp.stack([shard * span] + rows).astype(jnp.int32)

    def gather_rows(values):
        return [lax.all_gather(w, "fsdp", axis=0, tiled=True) for w in values]

    def both_tokens(values):
        if paired:
            return jnp.concatenate([values, swap_fs(values)], axis=0)
        return lax.all_gather(values, "fsdp", axis=0, tiled=True)

    def reduce_chips(kept, got, order=x_order, marks=()):
        total = kept.astype(F32) + got.astype(F32)
        for place, bit in enumerate(order[1:]):
            count = total.shape[0] // 2
            sent, total = total[count:].astype(BF16), total[:count]
            if place < len(marks):
                sent = after(sent, marks[place])
            total = total + swap_dp(sent, bit).astype(F32)
        return total.astype(BF16)

    x, g, e = inputs[:, 0], cotangent[:, 0], encoded[:, 0]

    low, offsets = [x], [0]
    for bit in reversed(chip_bits[1:]):
        low = low + [swap_dp(piece, bit) for piece in low]
        offsets = offsets + [offset | bit for offset in offsets]
    high = [swap_dp(piece, 2) for piece in low]
    near, far = jnp.stack(low), jnp.stack(high)
    offsets = [offset ^ more for more in (0, 2, 1, 3) for offset in offsets]
    source = me ^ jnp.array(offsets, jnp.int32)
    e_all = lax.all_gather(e, "dp", axis=0)

    gains = jnp.stack([gain_self, gain_cross, gain_dense])
    own_head = lambda w: lax.dynamic_slice_in_dim(w, head * 64, 64, axis=1)
    if paired:
        pad = jnp.pad(position_bias.reshape(1, -1), ((0, 0), (0, span - position_bias.size)))
        small = jnp.concatenate([gains, pad], axis=0)
        small_got = swap_fs(small)
        head_pack = jnp.concatenate([own_head(w) for w in (query_self, key_self, value_self)], 1)
        head_got = swap_fs(head_pack)
        first, second = (
            jnp.where(shard == which, mine, got)
            for which, mine, got in ((0, small, small_got), (1, small, small_got))
        )
        gains = jnp.concatenate([first[:3], second[:3]], axis=1)
        bias_all = jnp.concatenate(
            [piece[3, : position_bias.size].reshape(position_bias.shape) for piece in (first, second)]
        )
        head_whole = jnp.where(
            shard == 0,
            jnp.concatenate([head_pack, head_got]),
            jnp.concatenate([head_got, head_pack]),
        )
        other = (1 - shard) * span
        half_starts = jnp.stack([shard * span, other + core * half, other + (1 - core) * half])
        half_starts = half_starts.astype(jnp.int32)
        near_bit, dense_bit = chip_bits[0], chip_bits[1]
        starts = quarter_starts(near_bit)
        kv_own = (key_cross, value_cross)
        near_own = (output_self, query_cross, output_cross)
        near_sent = jnp.stack(
            [
                lax.dynamic_slice_in_dim(w, quarter(near_bit) * (half // 2), half // 2, axis=0)
                for w in near_own + kv_own
            ]
        )
        near_got = swap_fs(after(near_sent, small_got, head_got))
        near_far = swap_dp(near_got, near_bit)
        theirs = jnp.stack(
            [
                lax.dynamic_slice(
                    w,
                    (quarter(dense_bit) * (half // 2), (1 - shard) * hidden),
                    (half // 2, hidden),
                )
                for w in (dense_gate, dense_up)
            ]
        )
        dense_got = swap_fs(after(theirs, near_got))
        dense_own = (dense_gate, dense_up)
        which = jnp.stack([shard, core]).astype(jnp.int32)
        dense_starts = jnp.concatenate([quarter_starts(dense_bit), which])
    else:
        gains = lax.all_gather(gains, "fsdp", axis=1, tiled=True)
        bias_all = lax.all_gather(position_bias, "fsdp", axis=0, tiled=True)
        kv_own, kv_more = gather_rows((key_cross, value_cross)), ()
        near_own, near_more = gather_rows((output_self, query_cross, output_cross)), ()
        first_own, first_more = gather_rows((query_self, key_self, value_self)), ()
        half_starts = jnp.zeros((1,), jnp.int32)
        head_whole = jnp.concatenate([own_head(w) for w in first_own], axis=1)
        dense_own = [
            lax.all_to_all(w, "fsdp", 1, 0, tiled=True) for w in (dense_gate, dense_up)
        ]
        dense_more = ()
        starts = jnp.zeros((1,), jnp.int32)
        dense_starts = jnp.zeros((3,), jnp.int32)
        g_group = both_tokens(g.reshape(tokens, width))
    gains, bias_all = gains.astype(F32), bias_all.astype(F32)
    head_w = jnp.concatenate(
        [head_whole[:, at : at + 64] for at in (0, 0, 64, 64, 128, 128)], axis=1
    )

    marks = jnp.arange(bias_all.shape[0], dtype=jnp.int32)
    edges = jnp.sum((buckets[:, None] < marks[None, :]).astype(jnp.int32), axis=0)
    bias_values = lax.dynamic_slice_in_dim(bias_all, head, 1, axis=1)[:, 0]
    table = bias_table(edges, bias_values, length)
    x_groups = [near, far, swap_dp(near, 1), swap_dp(after(far, table), 1)]
    doc_row = jnp.broadcast_to(doc_ids[:, 0, :, None], (micro_count, dp, rows))
    doc_row = doc_row.reshape(micro_count, length)
    doc_col = doc_row[:, :, None]

    n_all, qkv, mixed = pl.pallas_call(
        functools.partial(self_forward_kernel, len(x_groups)),
        out_shape=[
            jax.ShapeDtypeStruct((dp, micro_count, rows, width), BF16),
            jax.ShapeDtypeStruct((length, 384), BF16),
            jax.ShapeDtypeStruct((length, 128), BF16),
        ],
        in_specs=[smem()] + [vmem()] * (len(x_groups) + 5),
        out_specs=[vmem()] * 3,
        compiler_params=params(),
        cost_estimate=cost(12),
        name="self_forward",
    )(source, *x_groups, gains[0:1], head_w, table, doc_row, doc_col)
    o1_heads = lax.all_to_all(mixed.reshape(dp, rows, 128), "dp", 0, 0, tiled=True)[::copies]

    if paired:
        near_more = (near_got, near_far, swap_dp(near_got, 1), swap_dp(after(near_far, mixed), 1))
        kv_more = near_more
        dense_far = swap_dp(after(dense_got, mixed), dense_bit)
    ke, ve = cross_kv(starts, e_all, *kv_own, kv_more)

    row32 = jax.ShapeDtypeStruct((tokens, width), F32)
    row16 = jax.ShapeDtypeStruct((tokens, width), BF16)
    left, x1, q2, x2, n3 = pl.pallas_call(
        functools.partial(mid_forward_kernel, len(near_more)),
        out_shape=[
            jax.ShapeDtypeStruct((3, tokens, width), BF16), row32, row16, row32, row16
        ],
        in_specs=[smem()] + [vmem()] * (8 + len(near_more)),
        out_specs=[vmem()] * 5,
        scratch_shapes=[pltpu.VMEM((tokens, width), BF16)] * 3,
        compiler_params=params(),
        cost_estimate=cost(12),
        name="mid_forward",
    )(starts, o1_heads, x, gains, ke, ve, *near_own, *near_more)

    if paired:
        dense_more = (
            dense_got,
            dense_far,
            swap_dp(after(dense_got, o1_heads), 1),
            swap_dp(after(dense_far, o1_heads), 1),
        )
        g_rows = g.reshape(tokens, width)
        g_got = swap_fs(after(g_rows, dense_got))
        n_got = swap_fs(n3)
        views = left.reshape(3, tokens, 2, span)
        left_got = swap_fs(lax.dynamic_index_in_dim(views, 1 - shard, 2, keepdims=False))
        back, y32, _, dn3, _ = dense_layer(
            dense_starts, n3, g_rows, *dense_own, dense_down, dense_more, tokens
        )
        back_mate = swap_dp(back, 1)
        back_got, _, y16, _, d16 = dense_layer(
            dense_starts,
            after(n_got, dn3, left_got),
            g_got,
            *dense_own,
            dense_down,
            dense_more,
            tokens,
        )
        back_got_mate = swap_dp(back_got, 1)
        dn3_more = swap_fs(d16)
    else:
        n_group = both_tokens(n3)
        back, _, y16, _, d16 = dense_layer(
            dense_starts, n_group, g_group, *dense_own, dense_down, dense_more, tokens
        )
        dn3 = jnp.zeros((tokens, width), F32)
        dn3_more = lax.psum_scatter(d16, "fsdp", scatter_dimension=0, tiled=True)
        dense_out = lax.psum_scatter(y16, "fsdp", scatter_dimension=0, tiled=True).astype(F32)
        outputs = (x2 + dense_out).astype(BF16)

    if chunked:
        where = jnp.stack([core, shard, me // 2]).astype(jnp.int32)
        masks = [
            [
                sum(((slot >> (len(order) - 1 - at)) & 1) * (bit // 2) for at, bit in enumerate(order))
                for slot in range(chips)
            ]
            for order in (x_order, z_order)
        ]
        own_kept, own_sent, down_kept, down_sent, far_kept, far_sent = chunk_weights(
            functools.partial(dense_weight_kernel, *masks),
            where,
            (after(n3, dn3_more), n_got, g_rows, g_got, back, back_got, back_mate, back_got_mate),
            (
                span // chips * hidden // 128,
                hidden // chips * width // 256,
                span // chips * hidden // 128,
            ),
            chips // 2,
            [
                pltpu.VMEM((max(hidden, half), max(hidden, width // 2)), F32),
                pltpu.VMEM((4 * tokens, width), BF16),
            ],
            7,
            "dense_weight",
        )
        dn3_more = after(dn3_more, own_sent)
        own_got, down_got = swap_dp(own_sent, z_order[0]), swap_dp(down_sent, x_order[0])
        far_got, far_kept = swap_fs(far_sent), swap_fs(far_kept)

    straight = chunked
    if straight:
        slots = jnp.append(chip_of(me ^ (2 * jnp.arange(heads // 2))), core).astype(jnp.int32)
    else:
        slots = jnp.append(jnp.arange(heads // 2), 0).astype(jnp.int32)
    g_rows = g.reshape(tokens, width)
    right, gx2, dkv_kept, dkv_sent, dc_dense = pl.pallas_call(
        functools.partial(cross_backward_kernel, len(near_more)),
        out_shape=[
            jax.ShapeDtypeStruct((tokens, 2 * width), BF16),
            row32,
            jax.ShapeDtypeStruct((heads // 2, dp, micro_count, part, 128), BF16),
            jax.ShapeDtypeStruct((heads // 2, dp, micro_count, part, 128), BF16),
            jax.ShapeDtypeStruct((1, width), F32),
        ],
        in_specs=[smem()] * 2 + [vmem()] * (9 + len(near_more)),
        out_specs=[vmem()] * 5,
        scratch_shapes=[pltpu.VMEM((tokens, width), F32), pltpu.VMEM((tokens, width), BF16)],
        compiler_params=params(),
        cost_estimate=cost(15),
        name="cross_backward",
    )(starts, slots, g_rows, dn3, dn3_more, x2, gains, q2, ke, ve, near_own[2], *near_more)
    if chunked:
        gx2 = after(gx2, own_got, down_got, far_got)
    gx1, last, do1_heads, dc_cross = pl.pallas_call(
        functools.partial(mid_backward_kernel, len(near_more)),
        out_shape=[
            row32,
            row16,
            jax.ShapeDtypeStruct((heads, rows, 128), BF16),
            jax.ShapeDtypeStruct((1, width), F32),
        ],
        in_specs=[smem()] + [vmem()] * (6 + len(near_more)),
        out_specs=[vmem()] * 4,
        scratch_shapes=[pltpu.VMEM((tokens, width), F32)],
        compiler_params=params(),
        cost_estimate=cost(6),
        name="mid_backward",
    )(starts, right, gx2, x1, gains, *near_own[:2], *near_more)
    do1 = lax.all_to_all(
        jnp.repeat(do1_heads, copies, axis=0) if copies > 1 else do1_heads, "dp", 0, 0, tiled=True
    ).reshape(length, 128)

    if chunked:
        right_got, last_got = swap_fs(right), swap_fs(last)
        if straight:
            dkv_got = swap_dp(dkv_sent, 1)

    dqkv, table_grad = pl.pallas_call(
        self_backward_kernel,
        out_shape=[
            jax.ShapeDtypeStruct((length, 384), BF16),
            jax.ShapeDtypeStruct((TILE, length), F32),
        ],
        in_specs=[vmem()] * 5,
        out_specs=[vmem()] * 2,
        scratch_shapes=[pltpu.VMEM((length, 128), F32), pltpu.VMEM((length, 128), F32)],
        compiler_params=params(),
        cost_estimate=cost(10),
        name="self_backward",
    )(qkv, do1, table, doc_row, doc_col)
    if chunked:
        dqkv = after(dqkv, right_got, last_got, far_kept, dkv_got)
    head_grad = pl.pallas_call(
        head_weight_kernel,
        out_shape=jax.ShapeDtypeStruct((fs, span * 3 // 2, 128), BF16),
        in_specs=[vmem()] * 2,
        out_specs=vmem(),
        compiler_params=params(),
        cost_estimate=cost(6),
        name="head_weight",
    )(n_all, dqkv)
    def sum_shards(values):
        if paired:
            kept = lax.dynamic_index_in_dim(values, shard, 0)
            sent = lax.dynamic_index_in_dim(values, 1 - shard, 0)
            return (kept.astype(F32) + swap_fs(sent).astype(F32)).astype(BF16)
        return lax.psum_scatter(values, "fsdp", scatter_dimension=0, tiled=True)

    head_sum = sum_shards(head_grad)
    if chunked:
        token_kept, token_sent = chunk_weights(
            functools.partial(token_weight_kernel, masks[0]),
            where,
            (after(left, head_grad), left_got, right, right_got, last, last_got),
            (3 * half // chips * width // 128,),
            chips,
            [pltpu.VMEM((span, width), F32)],
            6,
            "token_weight",
        )
        token_got = swap_dp(token_sent, 1)
    if paired:
        first_own = (query_self, key_self, value_self)
        first_more = both_halves(after(half_rows(first_own), head_sum))
        y16 = swap_fs(after(y16, first_more[0]))
        outputs = (x2 + (y32 + y16.astype(F32))).astype(BF16)
    own_d = lax.all_to_all(dqkv.reshape(dp, rows, 384), "dp", 0, 0, tiled=True)[::copies]
    grad_inputs, dc_one = pl.pallas_call(
        functools.partial(input_grad_kernel, len(first_more)),
        out_shape=[row32, jax.ShapeDtypeStruct((1, width), F32)],
        in_specs=[smem()] + [vmem()] * (7 + len(first_more)),
        out_specs=[vmem()] * 2,
        scratch_shapes=[
            pltpu.VMEM((tokens, 3 * width), BF16),
            pltpu.VMEM((tokens, width), F32),
        ],
        compiler_params=params(),
        cost_estimate=cost(7),
        name="input_grad",
    )(half_starts, own_d, x, gains, gx1, *first_own, *first_more)

    if straight:
        dkv = reduce_chips(dkv_kept, dkv_got, [1] + x_order).reshape(-1, 128)
    else:
        dkv = jnp.stack([dkv_kept, dkv_sent], axis=1).reshape(heads * copies, -1, 128)
        dkv = lax.psum_scatter(dkv, "dp", scatter_dimension=0, tiled=True)[0]
        bit = 1
        while bit < copies:
            got = swap_dp(dkv, bit)
            dkv = jnp.where(
                (me // bit) % 2 == 0, jnp.concatenate([dkv, got]), jnp.concatenate([got, dkv])
            )
            bit *= 2
    cross_grad = pl.pallas_call(
        cross_head_weight_kernel,
        out_shape=jax.ShapeDtypeStruct((fs, span, 128), BF16),
        in_specs=[vmem()] * 2,
        out_specs=vmem(),
        compiler_params=params(),
        cost_estimate=cost(3),
        name="cross_head_weight",
    )(e_all, dkv)
    cross_sum = sum_shards(cross_grad)
    own_dkv = dkv.reshape(dp, micro_count * part, 128)
    own_dkv = lax.all_to_all(own_dkv, "dp", 0, 0, tiled=True)[::copies]
    grad_encoded = pl.pallas_call(
        functools.partial(encoder_grad_kernel, len(kv_more)),
        out_shape=jax.ShapeDtypeStruct((micro_count * part, width), F32),
        in_specs=[smem()] + [vmem()] * (3 + len(kv_more)),
        out_specs=vmem(),
        scratch_shapes=[pltpu.VMEM((micro_count * part, width), BF16)] * 2,
        compiler_params=params(),
        cost_estimate=cost(4),
        name="encoder_grad",
    )(starts, own_dkv, *kv_own, *kv_more)

    if chunked:
        own_sum = reduce_chips(own_kept, own_got, z_order, (do1_heads, dqkv))
        down_sum = reduce_chips(down_kept, down_got, x_order, (do1_heads, dqkv))
        far_got = swap_dp(after(far_got, do1_heads), x_order[0])
        far_sum = reduce_chips(far_kept, far_got, x_order, (dqkv, head_grad))
        token_sum = reduce_chips(token_kept, token_got, [1] + x_order)

        def gather(*values):
            return lax.all_gather(jnp.concatenate(values, axis=1), "dp", axis=0, tiled=True)

        square, wide = (span, width), (span, fs * hidden)
        first_pieces = gather(own_sum, down_sum, far_sum, head_sum)
        (
            grad_dense_gate,
            grad_dense_up,
            grad_dense_down,
            grad_query_self,
            grad_key_self,
            grad_value_self,
        ) = spread(
            first_spread_kernel,
            where,
            first_pieces,
            [(wide, "core"), (wide, "core"), ((hidden, width), "chip")] + [(square, "head")] * 3,
            12,
            "first_spread",
        )
        (
            grad_output_cross,
            grad_query_cross,
            grad_output_self,
            grad_key_cross,
            grad_value_cross,
        ) = spread(
            second_spread_kernel,
            where,
            gather(after(token_sum, first_pieces), cross_sum),
            [(square, "core")] * 3 + [(square, "head")] * 2,
            8,
            "second_spread",
        )
    else:

        def all_heads(values, kinds):
            pieces = lax.all_gather(values, "dp", axis=0, tiled=True)[::copies]
            return plain_head_spread(pieces, span, width, kinds)

        grad_query_self, grad_key_self, grad_value_self = all_heads(head_sum, 3)
        grad_key_cross, grad_value_cross = all_heads(cross_sum, 2)
        right = jnp.concatenate([right, last], axis=1)

        def over_dp(values):
            return lax.psum(values.astype(BF16), "dp").astype(F32)

        def over_all(a, b):
            made = t_dot(a, b).astype(BF16)
            return over_dp(lax.psum_scatter(made, "fsdp", scatter_dimension=0, tiled=True))

        grad_output_cross, grad_query_cross, grad_output_self = (
            over_all(left[kind], right[:, kind * width : (kind + 1) * width]) for kind in range(3)
        )
        grad_dense_gate, grad_dense_up = (
            over_dp(
                lax.all_to_all(
                    t_dot(n_group, back[:, kind * hidden : (kind + 1) * hidden]).astype(BF16),
                    "fsdp",
                    0,
                    1,
                    tiled=True,
                )
            )
            for kind in range(2)
        )
        grad_dense_down = over_dp(t_dot(back[:, 2 * hidden :], g_group))

    if chunked:
        table_grad = after(table_grad, first_more[1])
    table_sums = jnp.sum(bucket_sums(edges, table_grad, bias_all.shape[0]), axis=1)
    column = (jnp.arange(heads) == head) & (me % copies == 0)
    bias_row = jnp.where(column[None, :], table_sums[:, None], 0.0).reshape(1, -1)
    bias_row = jnp.pad(bias_row, ((0, 0), (0, width - bias_row.shape[1])))
    sums = jnp.concatenate([dc_one, dc_dense, dc_cross, bias_row], axis=0)
    if paired:
        sums = sums + swap_fs(sums)
        for bit in [1] + chip_bits:
            sums = sums + swap_dp(sums, bit)
    else:
        sums = lax.psum(sums, ("dp", "fsdp"))
    own = lax.dynamic_slice_in_dim(sums[:3], shard * span, span, axis=1)
    grad_bias = sums[3, : bias_all.size].reshape(bias_all.shape)
    grad_bias = lax.dynamic_slice_in_dim(
        grad_bias, shard * position_bias.shape[0], position_bias.shape[0], axis=0
    )
    shape = (micro_count, 1, rows, width)
    return (
        outputs.reshape(shape),
        grad_inputs.reshape(shape),
        grad_encoded.reshape(micro_count, 1, part, width),
        own[0],
        grad_query_self,
        grad_key_self,
        grad_value_self,
        grad_output_self,
        grad_bias,
        own[2],
        grad_query_cross,
        grad_key_cross,
        grad_value_cross,
        grad_output_cross,
        own[1],
        grad_dense_gate,
        grad_dense_up,
        grad_dense_down,
    )


def solution(mesh):
    matrix = P("fsdp", None)
    token = P(None, "fsdp", "dp", None)
    weights = (
        (P("fsdp"),)
        + (matrix,) * 5
        + (P("fsdp"),)
        + (matrix,) * 4
        + (P("fsdp"),)
        + (matrix,) * 3
    )
    return jax.shard_map(
        per_device,
        mesh=mesh,
        in_specs=(token,) * 3 + (P(None, "fsdp", None), P()) + weights,
        out_specs=(token,) * 3 + weights,
        check_vma=False,
    )
```

```python
import functools

import jax
import jax.numpy as jnp
from jax import lax
from jax.experimental import pallas as pl
from jax.experimental.pallas import tpu as pltpu
from jax.sharding import PartitionSpec as P

EPS = 1e-06
NEGATIVE = -1e30
TILE = 256
F32 = jnp.float32
BF16 = jnp.bfloat16
VMEM_LIMIT = 56 * 1024 * 1024


def vmem():
    return pl.BlockSpec(memory_space=pltpu.VMEM)


def smem():
    return pl.BlockSpec(memory_space=pltpu.SMEM)


def params(limit=VMEM_LIMIT):
    return pltpu.CompilerParams(vmem_limit_bytes=limit)


def cost(microseconds):
    return pl.CostEstimate(
        flops=int(microseconds * 1.15e9),
        bytes_accessed=int(microseconds * 3.69e6),
        transcendentals=0,
    )


def aligned(start, size):
    return pl.ds(pl.multiple_of(start, size), size)


def dot(left, right):
    return jnp.dot(left, right, preferred_element_type=F32)


def dot_t(left, right):
    return lax.dot_general(left, right, (((1,), (1,)), ((), ())), preferred_element_type=F32)


def t_dot(left, right):
    return lax.dot_general(left, right, (((0,), (0,)), ((), ())), preferred_element_type=F32)


def norm_rows(values, gain):
    return values * lax.rsqrt(jnp.mean(values * values, axis=-1, keepdims=True) + EPS) * gain


def norm_back(values, gain, grad):
    r = lax.rsqrt(jnp.mean(values * values, axis=-1, keepdims=True) + EPS)
    scaled = grad * gain
    inner = jnp.mean(scaled * values, axis=-1, keepdims=True)
    back = r * scaled - values * (r * r * r * inner)
    return back, jnp.sum(grad * (values * r), axis=0, keepdims=True)


def low_lanes(rows):
    return lax.broadcasted_iota(jnp.int32, (rows, 128), 1) < 64


def pair_up(first, second):
    lane = low_lanes(first.shape[0])
    low = jnp.where(lane, first, pltpu.roll(second, 64, 1))
    high = jnp.where(lane, pltpu.roll(first, 64, 1), second)
    return low, high


def keep_half(values, half):
    lane = low_lanes(values.shape[0])
    return jnp.where(lane if half == 0 else ~lane, values, jnp.zeros_like(values))


def softmax_rows(scores):
    top = jnp.max(scores, axis=-1, keepdims=True)
    raised = jnp.exp(scores - top)
    return raised * (1.0 / jnp.sum(raised, axis=-1, keepdims=True))


def table_kernel(edge_ref, value_ref, out_ref):
    rows, length = out_ref.shape
    bucket_count = value_ref.shape[0]
    for start in range(0, length, TILE):
        place = (rows, TILE)
        apart = (
            lax.broadcasted_iota(jnp.int32, place, 0)
            - lax.broadcasted_iota(jnp.int32, place, 1)
            + (length - rows - start)
        )
        value = jnp.full(place, value_ref[0], F32)
        for bucket in range(1, bucket_count):
            value = jnp.where(apart >= edge_ref[bucket], value_ref[bucket], value)
        out_ref[:, start : start + TILE] = jnp.where(apart >= 0, value, NEGATIVE)


def bias_table(edges, values, length):
    return pl.pallas_call(
        table_kernel,
        out_shape=jax.ShapeDtypeStruct((TILE, length), F32),
        in_specs=[smem(), smem()],
        out_specs=vmem(),
        cost_estimate=cost(4),
        name="bias_table",
    )(edges, values)


def bucket_kernel(edge_ref, grad_ref, out_ref):
    rows, length = grad_ref.shape
    bucket_count = out_ref.shape[0]
    above = [jnp.zeros((8, TILE), F32) for _ in range(bucket_count)]
    for start in range(0, length, TILE):
        for row in range(0, rows, 8):
            place = (8, TILE)
            apart = (
                lax.broadcasted_iota(jnp.int32, place, 0)
                - lax.broadcasted_iota(jnp.int32, place, 1)
                + (length - rows - start + row)
            )
            tile = grad_ref[row : row + 8, start : start + TILE]
            for bucket in range(bucket_count):
                above[bucket] = above[bucket] + jnp.where(apart >= edge_ref[bucket], tile, 0.0)
    for bucket in range(bucket_count):
        rest = above[bucket + 1] if bucket + 1 < bucket_count else 0.0
        part = jnp.sum(above[bucket] - rest, axis=0, keepdims=True)
        out_ref[bucket : bucket + 1, :] = part[:, :128] + part[:, 128:]


def bucket_sums(edges, grad, bucket_count):
    return pl.pallas_call(
        bucket_kernel,
        out_shape=jax.ShapeDtypeStruct((bucket_count, 128), F32),
        in_specs=[smem(), vmem()],
        out_specs=vmem(),
        cost_estimate=cost(7),
        name="bucket_sums",
    )(edges, grad)


def times(x_ref, starts_ref, pieces):
    if len(pieces) == 1:
        return dot(x_ref[...], pieces[0])
    total = None
    for place, piece in enumerate(pieces):
        rows = piece.shape[0]
        part = dot(x_ref[:, aligned(starts_ref[place], rows)], piece)
        total = part if total is None else total + part
    return total


def times_back(out_ref, starts_ref, terms):
    for place in range(len(terms[0][1])):
        total = sum(dot_t(d, pieces[place]) for d, pieces in terms)
        rows = terms[0][1][place].shape[0]
        if len(terms[0][1]) == 1:
            out_ref[...] = total
        else:
            out_ref[:, aligned(starts_ref[place], rows)] = total


def pack_kernel(counts, where_ref, *refs):
    total = sum(counts)
    weights, outs, sem = refs[:total], refs[total:-1], refs[-1]
    copies = []
    for place, w_ref in enumerate(weights):
        kind = 0 if place < counts[0] else 1
        out_ref = outs[kind].at[place - kind * counts[0]]
        rows, cols = outs[kind].shape[1:]
        source = w_ref.at[aligned(where_ref[kind], rows), :]
        if kind:
            source = w_ref.at[aligned(where_ref[kind], rows), aligned(where_ref[2], cols)]
        copies.append(pltpu.make_async_copy(source, out_ref, sem.at[place]))
    for copy in copies:
        copy.start()
    for copy in copies:
        copy.wait()


def pack(where, first, second, rows, cols):
    anywhere = pl.BlockSpec(memory_space=pl.ANY)
    counts = (len(first), len(second))
    return pl.pallas_call(
        functools.partial(pack_kernel, counts),
        out_shape=[
            jax.ShapeDtypeStruct((counts[0], rows, first[0].shape[1]), BF16),
            jax.ShapeDtypeStruct((counts[1], rows, cols), BF16),
        ],
        in_specs=[smem()] + [anywhere] * sum(counts),
        out_specs=[anywhere] * 2,
        scratch_shapes=[pltpu.SemaphoreType.DMA((sum(counts),))],
        cost_estimate=cost(2),
        name="pack",
    )(where, *first, *second)


def pieces_of(own_ref, more, index):
    return [own_ref[...]] + [ref[index] for ref in more]


def self_scores(q, k, table, doc_col, doc_row):
    scores = dot_t(q, k) + table
    return jnp.where(doc_col == doc_row, scores, NEGATIVE)


def self_forward_kernel(groups, source_ref, *refs):
    x_refs = refs[:groups]
    gain_ref, w_ref, table_ref, doc_row_ref, doc_col_ref, n_ref, qkv_ref, o_ref = refs[groups:]
    count, _, rows, width = x_refs[0].shape
    length = groups * count * rows
    lane = lax.broadcasted_iota(jnp.int32, (rows, 384), 1) % 128 < 64
    together = min(TILE // rows, count)
    for place, x_ref in enumerate(x_refs):
        for first in range(0, count, together):
            parts = []
            for inner in range(first, first + together):
                x = x_ref[inner].astype(F32).reshape(2 * rows, width)
                n = norm_rows(x, gain_ref[...]).astype(BF16)
                n_ref[source_ref[place * count + inner]] = n.reshape(2, rows, width)
                parts.append(n)
            made = dot(jnp.concatenate(parts, axis=0), w_ref[...])
            for inner in range(together):
                at = 2 * rows * inner
                picked = jnp.where(lane, made[at : at + rows], made[at + rows : at + 2 * rows])
                own = source_ref[place * count + first + inner]
                qkv_ref[aligned(own * rows, rows), :] = picked.astype(BF16)
    for block in range(length // TILE):
        start, stop = block * TILE, (block + 1) * TILE
        table = table_ref[:, length - stop :]
        q = qkv_ref[start:stop, 0:128]
        k = qkv_ref[:stop, 128:256]
        v = qkv_ref[:stop, 256:384]
        mixed = []
        for half in range(2):
            scores = self_scores(
                keep_half(q, half),
                k,
                table,
                doc_col_ref[half, start:stop, :],
                doc_row_ref[half : half + 1, :stop],
            )
            mixed.append(dot(softmax_rows(scores).astype(BF16), v))
        o_ref[start:stop, :] = jnp.where(low_lanes(TILE), mixed[0], mixed[1]).astype(BF16)


def self_backward_kernel(
    qkv_ref, do_ref, table_ref, doc_row_ref, doc_col_ref, dqkv_ref, grad_ref, dk_ref, dv_ref
):
    length = qkv_ref.shape[0]
    grad_ref[...] = jnp.zeros_like(grad_ref)
    dk_ref[...] = jnp.zeros_like(dk_ref)
    dv_ref[...] = jnp.zeros_like(dv_ref)
    for block in range(length // TILE):
        start, count = block * TILE, (block + 1) * TILE
        table = table_ref[:, length - count :]
        k = qkv_ref[:count, 128:256]
        v = qkv_ref[:count, 256:384]
        made = []
        for half in range(2):
            q = keep_half(qkv_ref[start:count, 0:128], half)
            do = keep_half(do_ref[start:count, :], half)
            p = softmax_rows(
                self_scores(
                    q,
                    k,
                    table,
                    doc_col_ref[half, start:count, :],
                    doc_row_ref[half : half + 1, :count],
                )
            )
            dp = dot_t(do, v)
            ds = (p * (dp - jnp.sum(p * dp, axis=-1, keepdims=True))).astype(BF16)
            grad_ref[:, length - count :] += ds.astype(F32)
            made.append(dot(ds, k))
            dk_ref[:count, :] += t_dot(ds, q)
            dv_ref[:count, :] += t_dot(p.astype(BF16), do)
        dq = jnp.where(low_lanes(TILE), made[0], made[1])
        dqkv_ref[start:count, 0:128] = dq.astype(BF16)
    dqkv_ref[:, 128:256] = dk_ref[...].astype(BF16)
    dqkv_ref[:, 256:384] = dv_ref[...].astype(BF16)


def head_weight_kernel(n_ref, d_ref, out_ref):
    blocks, _, rows, width = n_ref.shape
    shards = out_ref.shape[0]
    span = width // shards
    lane = lax.broadcasted_iota(jnp.int32, (blocks * rows, 384), 1) % 128 < 64
    d = d_ref[...]
    zero = jnp.zeros_like(d)
    right = [jnp.where(lane, d, zero), jnp.where(lane, zero, d)]
    half = span // 2
    for shard in range(shards):
        total = jnp.zeros((span, 384), F32)
        for micro in range(2):
            left = n_ref[:, micro, :, shard * span : (shard + 1) * span]
            total = total + t_dot(left.reshape(blocks * rows, span), right[micro])
        q, k, v = (
            total[:, at : at + 128] + pltpu.roll(total[:, at : at + 128], 64, 1)
            for at in (0, 128, 256)
        )
        out_ref[shard, :span, :] = jnp.where(low_lanes(span), q, k).astype(BF16)
        out_ref[shard, span:, :] = jnp.where(low_lanes(half), v[:half], v[half:]).astype(BF16)


def cross_kv_kernel(split, starts_ref, e_ref, wk_ref, wv_ref, *refs):
    more, (ke_ref, ve_ref) = refs[:split], refs[split:]
    blocks, _, part, _ = e_ref.shape
    for index, (own_ref, out_ref) in enumerate(((wk_ref, ke_ref), (wv_ref, ve_ref)), 3):
        total = None
        pieces = pieces_of(own_ref, more, index)
        for place, piece in enumerate(pieces):
            rows = piece.shape[0]
            if split:
                left = e_ref[:, 0, :, aligned(starts_ref[place], rows)]
            else:
                left = e_ref[:, 0]
            made = dot(left.reshape(blocks * part, rows), piece)
            total = made if total is None else total + made
        out_ref[0] = total.astype(BF16)


def cross_kv(starts, e_all, wk, wv, more):
    blocks, micro, part, width = e_all.shape
    whole = lambda array: pl.BlockSpec(array.shape, lambda m, s: (0,) * array.ndim)
    out = pl.BlockSpec((1, blocks * part, width), lambda m, s: (m, 0, 0))
    return pl.pallas_call(
        functools.partial(cross_kv_kernel, len(more)),
        grid_spec=pltpu.PrefetchScalarGridSpec(
            num_scalar_prefetch=1,
            grid=(micro,),
            in_specs=[pl.BlockSpec((blocks, 1, part, width), lambda m, s: (0, m, 0, 0))]
            + [whole(array) for array in (wk, wv, *more)],
            out_specs=[out, out],
        ),
        out_shape=[jax.ShapeDtypeStruct((micro, blocks * part, width), BF16)] * 2,
        compiler_params=params(),
        cost_estimate=cost(8),
        name="cross_kv",
    )(starts, e_all, wk, wv, *more)


def mid_forward_kernel(split, starts_ref, o1_ref, x_ref, gain_ref, ke_ref, ve_ref, wo, wq, wc, *refs):
    more = refs[:split]
    left_ref, x1_ref, q2_ref, x2_ref, n3_ref, sent_ref, o1c_ref, n2_ref, o2_ref = refs[split:]
    heads, rows, _ = o1_ref.shape
    width = x_ref.shape[-1]
    for pair in range(heads // 2):
        at = pair * 128
        low, high = pair_up(o1_ref[2 * pair].astype(F32), o1_ref[2 * pair + 1].astype(F32))
        o1c_ref[0:rows, at : at + 128] = low.astype(BF16)
        o1c_ref[rows : 2 * rows, at : at + 128] = high.astype(BF16)
    x = x_ref[...].astype(F32).reshape(2 * rows, width)
    x1 = x + times(o1c_ref, starts_ref, pieces_of(wo, more, 0))
    x1_ref[...] = x1
    n2_ref[...] = norm_rows(x1, gain_ref[1:2]).astype(BF16)
    q2_ref[...] = times(n2_ref, starts_ref, pieces_of(wq, more, 1)).astype(BF16)
    for micro in range(2):
        for pair in range(heads // 2):
            at = pair * 128
            span = slice(micro * rows, (micro + 1) * rows)
            q = q2_ref[span, at : at + 128]
            both = jnp.concatenate([keep_half(q, 0), keep_half(q, 1)], axis=0)
            p = softmax_rows(dot_t(both, ke_ref[micro, :, at : at + 128]))
            o = dot(p.astype(BF16), ve_ref[micro, :, at : at + 128])
            o2_ref[span, at : at + 128] = jnp.where(
                low_lanes(rows), o[:rows], o[rows:]
            ).astype(BF16)
    x2 = x1 + times(o2_ref, starts_ref, pieces_of(wc, more, 2))
    x2_ref[...] = x2
    n3_ref[...] = norm_rows(x2, gain_ref[2:3]).astype(BF16)
    left_ref[0] = o2_ref[...]
    left_ref[1] = n2_ref[...]
    left_ref[2] = o1c_ref[...]
    if split:
        span = sent_ref.shape[2]
        for kind in range(3):
            sent_ref[kind] = left_ref[kind, :, aligned(span - starts_ref[0], span)]


def cross_backward_kernel(
    split, starts_ref, slots_ref, g_ref, dn3_ref, more_ref, x2_ref, gain_ref, q2_ref, ke_ref, ve_ref,
    wc, *refs
):
    more = refs[:split]
    right_ref, gx2_ref, keep_ref, send_ref, dc_ref, back_ref, do2_ref = refs[split:]
    blocks, micros, part = keep_ref.shape[1:4]
    tokens, width = x2_ref.shape
    rows = tokens // micros
    pairs = width // 128
    even = slots_ref[pairs] == 0
    dn3 = dn3_ref[...] + more_ref[...].astype(F32)
    back, dc_ref[...] = norm_back(x2_ref[...], gain_ref[2:3], dn3)
    gx2 = g_ref[...].astype(F32) + back
    gx2_ref[...] = gx2
    gx2b = gx2.astype(BF16)
    right_ref[:, 0:width] = gx2b
    times_back(back_ref, starts_ref, [(gx2b, pieces_of(wc, more, 2))])
    do2_ref[...] = back_ref[...].astype(BF16)
    for micro in range(micros):
        for pair in range(pairs):
            at = pair * 128
            span = slice(micro * rows, (micro + 1) * rows)
            q = q2_ref[span, at : at + 128]
            do = do2_ref[span, at : at + 128]
            q = jnp.concatenate([keep_half(q, 0), keep_half(q, 1)], axis=0)
            do = jnp.concatenate([keep_half(do, 0), keep_half(do, 1)], axis=0)
            k = ke_ref[micro, :, at : at + 128]
            v = ve_ref[micro, :, at : at + 128]
            p = softmax_rows(dot_t(q, k))
            dp = dot_t(do, v)
            ds = (p * (dp - jnp.sum(p * dp, axis=-1, keepdims=True))).astype(BF16)
            dq = dot(ds, k)
            right_ref[span, width + at : width + at + 128] = jnp.where(
                low_lanes(rows), dq[:rows], dq[rows:]
            ).astype(BF16)
            low, high = pair_up(t_dot(ds, q), t_dot(p.astype(BF16), do))
            kept, sent = jnp.where(even, low, high), jnp.where(even, high, low)
            slot = slots_ref[pair]
            keep_ref[slot, :, micro] = kept.astype(BF16).reshape(blocks, part, 128)
            send_ref[slot, :, micro] = sent.astype(BF16).reshape(blocks, part, 128)


def mid_backward_kernel(split, starts_ref, right_ref, gx2_ref, x1_ref, gain_ref, wo, wq, *refs):
    more = refs[:split]
    gx1_ref, low_ref, do1_ref, dc_ref, back_ref = refs[split:]
    heads, rows, _ = do1_ref.shape
    width = x1_ref.shape[-1]
    times_back(back_ref, starts_ref, [(right_ref[:, width:], pieces_of(wq, more, 1))])
    back, dc_ref[...] = norm_back(x1_ref[...], gain_ref[1:2], back_ref[...])
    gx1 = gx2_ref[...] + back
    gx1_ref[...] = gx1
    gx1b = gx1.astype(BF16)
    low_ref[...] = gx1b
    times_back(back_ref, starts_ref, [(gx1b, pieces_of(wo, more, 0))])
    for pair in range(heads // 2):
        at = pair * 128
        do1 = back_ref[:, at : at + 128].astype(BF16).astype(F32)
        low, high = pair_up(do1[:rows], do1[rows:])
        do1_ref[2 * pair] = low.astype(BF16)
        do1_ref[2 * pair + 1] = high.astype(BF16)


def input_grad_kernel(split, starts_ref, d_ref, x_ref, gain_ref, gx1_ref, wq, wk, wv, *refs):
    more = refs[:split]
    out_ref, dc_ref, all_ref, back_ref = refs[split:]
    heads, rows, _ = d_ref.shape
    width = x_ref.shape[-1]
    for kind in range(3):
        for pair in range(heads // 2):
            lanes = slice(kind * 128, (kind + 1) * 128)
            low, high = pair_up(
                d_ref[2 * pair, :, lanes].astype(F32), d_ref[2 * pair + 1, :, lanes].astype(F32)
            )
            at = kind * width + pair * 128
            all_ref[0:rows, at : at + 128] = low.astype(BF16)
            all_ref[rows : 2 * rows, at : at + 128] = high.astype(BF16)
    terms = [
        (all_ref[:, kind * width : (kind + 1) * width], pieces_of(own, more, kind))
        for kind, own in enumerate((wq, wk, wv))
    ]
    times_back(back_ref, starts_ref, terms)
    x = x_ref[...].astype(F32).reshape(2 * rows, width)
    back, dc = norm_back(x, gain_ref[0:1], back_ref[...])
    dc_ref[...] = dc
    out_ref[...] = gx1_ref[...] + back


def encoder_grad_kernel(split, starts_ref, d_ref, wk, wv, *refs):
    more = refs[:split]
    out_ref, k_ref, v_ref = refs[split:]
    for pair in range(d_ref.shape[0] // 2):
        at = pair * 128
        low, high = pair_up(d_ref[2 * pair].astype(F32), d_ref[2 * pair + 1].astype(F32))
        k_ref[:, at : at + 128] = low.astype(BF16)
        v_ref[:, at : at + 128] = high.astype(BF16)
    terms = [(k_ref[...], pieces_of(wk, more, 3)), (v_ref[...], pieces_of(wv, more, 4))]
    times_back(out_ref, starts_ref, terms)


def cross_head_weight_kernel(e_ref, d_ref, out_ref):
    blocks, micro, part, width = e_ref.shape
    shards, span, _ = out_ref.shape
    for shard in range(shards):
        left = e_ref[:, :, :, shard * span : (shard + 1) * span]
        left = left.reshape(blocks * micro * part, span)
        out_ref[shard] = t_dot(left, d_ref[...]).astype(BF16)


def dense_kernel(split, starts_ref, n_ref, g_ref, wg, wu, wd_ref, *refs):
    more = refs[:split]
    back_ref, y_ref, ylow_ref, d_ref, dlow_ref = refs[split:]
    hidden = wd_ref.shape[0]
    gate, up = pieces_of(wg, more, 0), pieces_of(wu, more, 1)
    a = times(n_ref, starts_ref, gate)
    b = times(n_ref, starts_ref, up)
    scale = 0.7978845608028654
    cubed = 0.044715
    inner = jnp.tanh(scale * (a + cubed * (a * a * a)))
    gelu = 0.5 * a * (1.0 + inner)
    slope = 0.5 * (1.0 + inner) + 0.5 * a * (1.0 - inner * inner) * (
        scale * (1.0 + 3.0 * cubed * (a * a))
    )
    hid = (gelu * b).astype(BF16)
    dh = dot_t(g_ref[...], wd_ref[...])
    da = (dh * b * slope).astype(BF16)
    db = (dh * gelu).astype(BF16)
    times_back(d_ref, starts_ref, [(da, gate), (db, up)])
    dlow_ref[...] = d_ref[...].astype(BF16)
    y = dot(hid, wd_ref[...])
    y_ref[...] = y
    ylow_ref[...] = y.astype(BF16)
    back_ref[:, 0:hidden] = da
    back_ref[:, hidden : 2 * hidden] = db
    back_ref[:, 2 * hidden : 3 * hidden] = hid
    if more:
        shard, other = starts_ref[len(more) + 1], 1 - starts_ref[len(more) + 2]
        put_features(back_ref, 3 * hidden, n_ref, g_ref, shard, other)


def put_features(out_ref, at, n_ref, g_ref, shard, core):
    quarter = n_ref.shape[1] // 4
    for side, place in enumerate((2 * shard + core, 2 * (1 - shard) + core)):
        lanes = slice(at + side * quarter, at + (side + 1) * quarter)
        out_ref[:, lanes] = n_ref[:, aligned(place * quarter, quarter)]
    lanes = slice(at + 2 * quarter, at + 4 * quarter)
    out_ref[:, lanes] = g_ref[:, aligned(core * 2 * quarter, 2 * quarter)]


def dense_layer(starts, n, g, wg, wu, wd, more, step):
    count, width = n.shape
    hidden = wd.shape[0]
    which = starts.shape[0] - 2
    back = 3 * hidden + (width if more else 0)
    row = lambda size: pl.BlockSpec((step, size), lambda i, s: (i, 0))
    whole = lambda array: pl.BlockSpec(array.shape, lambda i, s: (0,) * array.ndim)
    column = pl.BlockSpec((wg.shape[0], hidden), lambda i, s: (0, s[which]))
    made = lambda size, kind: jax.ShapeDtypeStruct((count, size), kind)
    return pl.pallas_call(
        functools.partial(dense_kernel, len(more)),
        grid_spec=pltpu.PrefetchScalarGridSpec(
            num_scalar_prefetch=1,
            grid=(count // step,),
            in_specs=[row(width), row(width), column, column, whole(wd)]
            + [whole(array) for array in more],
            out_specs=[row(back)] + [row(width)] * 4,
        ),
        out_shape=[made(back, BF16)]
        + [made(width, F32), made(width, BF16), made(width, F32), made(width, BF16)],
        compiler_params=params(),
        cost_estimate=cost(13),
        name="dense_layer",
    )(starts, n, g, wg, wu, wd, *more)


def put_chunk(ref, slot, at, value):
    rows, width = value.shape
    for block in range(width // 128):
        ref[slot, at + block * rows : at + (block + 1) * rows, :] = value[
            :, block * 128 : (block + 1) * 128
        ].astype(BF16)


def take_chunk(ref, slot, at, rows, width):
    return jnp.concatenate(
        [
            ref[slot, at + block * rows : at + (block + 1) * rows, :].astype(F32)
            for block in range(width // 128)
        ],
        axis=1,
    )


def put_all(scratch_ref, first, count, chip, chunk_refs, at, width, masks):
    slots = [(ref, slot) for ref in chunk_refs for slot in range(ref.shape[0])]
    rows = count // len(slots)
    for (ref, slot), mask in zip(slots, masks):
        chunk = scratch_ref[aligned(first + (chip ^ mask) * rows, rows), :width]
        put_chunk(ref, slot, at, chunk)


def dense_weight_kernel(
    x_masks, z_masks, where_ref, n0_ref, n1_ref, g0_ref, g1_ref, own0_ref, own1_ref, mate0_ref, mate1_ref, keep_ref,
    send_ref, down_keep_ref, down_send_ref, far_keep_ref, far_send_ref, scratch_ref, left_ref
):
    tokens, width = n0_ref.shape
    hidden = (own0_ref.shape[1] - width) // 3
    quarter = width // 4
    at = keep_ref.shape[1] // 2
    core, shard, chip = where_ref[0], where_ref[1], where_ref[2]
    put_features(left_ref.at[:tokens], 0, n0_ref, g0_ref, shard, core)
    put_features(left_ref.at[tokens : 2 * tokens], 0, n1_ref, g1_ref, shard, core)
    left_ref[2 * tokens : 3 * tokens, :] = mate0_ref[:, 3 * hidden :]
    left_ref[3 * tokens :, :] = mate1_ref[:, 3 * hidden :]

    def whole(kind):
        span = slice(kind * hidden, (kind + 1) * hidden)
        refs = (own0_ref, own1_ref, mate0_ref, mate1_ref)
        return jnp.concatenate([ref[:, span] for ref in refs], axis=0)

    for kind in range(2):
        right = whole(kind)
        for side, (masks, refs) in enumerate(
            ((z_masks, (keep_ref, send_ref)), (x_masks, (far_keep_ref, far_send_ref)))
        ):
            value = t_dot(left_ref[:, side * quarter : (side + 1) * quarter], right)
            scratch_ref[:quarter, :hidden] = value
            put_all(scratch_ref, 0, quarter, chip, refs, kind * at, hidden, masks)
    value = t_dot(whole(2), left_ref[:, 2 * quarter :])
    scratch_ref[:, : 2 * quarter] = value
    refs = (down_keep_ref, down_send_ref)
    put_all(scratch_ref, 0, hidden, chip, refs, 0, 2 * quarter, x_masks)


def token_weight_kernel(
    masks, where_ref, left_ref, left_more_ref, right_ref, right_more_ref, last_ref, last_more_ref,
    mine_ref, mate_ref, scratch_ref
):
    kinds, _, span = left_more_ref.shape
    width = last_ref.shape[1]
    core, shard, chip = where_ref[0], where_ref[1], where_ref[2]
    half = span // 2
    at = half // len(masks) * width // 128
    for kind in range(kinds):
        lanes = slice(kind * width, (kind + 1) * width)
        left = [left_ref[kind, :, aligned(shard * span, span)], left_more_ref[kind]]
        if kind < kinds - 1:
            right = [right_ref[:, lanes], right_more_ref[:, lanes]]
        else:
            right = [last_ref[...], last_more_ref[...]]
        scratch_ref[...] = t_dot(jnp.concatenate(left, axis=0), jnp.concatenate(right, axis=0))
        for ref, own in ((mine_ref, core), (mate_ref, 1 - core)):
            put_all(scratch_ref, own * half, half, chip, (ref,), kind * at, width, masks)


def chunk_weights(kernel, where, operands, counts, slots, scratches, length, name):
    shapes = []
    for count in counts:
        shapes += [jax.ShapeDtypeStruct((slots, count, 128), BF16)] * 2
    return pl.pallas_call(
        kernel,
        out_shape=shapes,
        in_specs=[smem()] + [vmem()] * len(operands),
        out_specs=[vmem()] * len(shapes),
        scratch_shapes=scratches,
        compiler_params=params(),
        cost_estimate=cost(length),
        name=name,
    )(where, *operands)


def head_rows(in_ref, at, rows, outs):
    for pair in range(in_ref.shape[0] // 2):
        lanes = slice(pair * 128, (pair + 1) * 128)
        first = in_ref[2 * pair, at : at + rows, :].astype(F32)
        second = in_ref[2 * pair + 1, at : at + rows, :].astype(F32)
        for (out_ref, place), value in zip(outs, pair_up(first, second)):
            out_ref[place, lanes] = value


def head_spread(in_ref, at, q_ref, k_ref, v_ref):
    span = q_ref.shape[0]
    half = span // 2
    head_rows(in_ref, at, span, ((q_ref, slice(None)), (k_ref, slice(None))))
    head_rows(in_ref, at + span, half, ((v_ref, slice(0, half)), (v_ref, slice(half, span))))


def spread_kernel(where_ref, in_ref, gate_ref, up_ref, down_ref, q_ref, k_ref, v_ref, *out_refs):
    shard = where_ref[1]
    hidden = gate_ref.shape[3] // 2
    rows = gate_ref.shape[2] // 2
    at = rows * hidden // 128
    tall = down_ref.shape[0] // 2
    half = down_ref.shape[1] // 2
    span = q_ref.shape[0]
    kinds = len(out_refs) - 2
    width = out_refs[0].shape[3]
    base = 6 * at + 3 * span // 2
    step = rows * width // 128
    for piece in range(4):
        chip, core = piece // 2, piece % 2
        place = slice(chip * rows, (chip + 1) * rows)
        for side, start in enumerate((0, 4 * at)):
            lanes = aligned((shard ^ side) * hidden, hidden)
            for kind, out_ref in enumerate((gate_ref, up_ref)):
                chunk = take_chunk(in_ref, piece, start + kind * at, rows, hidden)
                out_ref[core, 0, place, lanes] = chunk
        chunk = take_chunk(in_ref, piece, 2 * at, tall, half)
        down_ref[chip * tall : (chip + 1) * tall, core * half : (core + 1) * half] = chunk
        for kind in range(kinds):
            chunk = take_chunk(in_ref, piece, base + kind * step, rows, width)
            out_refs[kind][core, 0, place, :] = chunk
    head_spread(in_ref, 6 * at, q_ref, k_ref, v_ref)
    k_ref, v_ref = out_refs[kinds:]
    head_rows(in_ref, base + kinds * step, span, ((k_ref, slice(None)), (v_ref, slice(None))))


def spread(where, pieces, outs):
    count, total, _ = pieces.shape
    steps = count // 4
    specs, shapes = [], []
    for (rows, cols), kind in outs:
        if kind == "core":
            shapes.append((2, steps, rows // (2 * steps), cols))
            block = (2, 1, rows // (2 * steps), cols)
            specs.append(pl.BlockSpec(block, lambda q, where: (0, q, 0, 0)))
        elif kind == "chip":
            shapes.append((rows, cols))
            specs.append(pl.BlockSpec((rows // steps, cols), lambda q, where: (q, 0)))
        else:
            shapes.append((rows, cols))
            specs.append(pl.BlockSpec((rows, cols // steps), lambda q, where: (0, q)))
    made = pl.pallas_call(
        spread_kernel,
        grid_spec=pltpu.PrefetchScalarGridSpec(
            num_scalar_prefetch=1,
            grid=(steps,),
            in_specs=[pl.BlockSpec((4, total, 128), lambda q, where: (q, 0, 0))],
            out_specs=specs,
        ),
        out_shape=[jax.ShapeDtypeStruct(shape, F32) for shape in shapes],
        compiler_params=params(),
        cost_estimate=cost(20),
        name="spread",
    )(where, pieces)
    return [array.reshape(shape) for array, (shape, _) in zip(made, outs)]


def plain_head_kernel(in_ref, *out_refs):
    span = out_refs[0].shape[0]
    if len(out_refs) == 3:
        head_spread(in_ref, 0, *out_refs)
    else:
        head_rows(in_ref, 0, span, [(out_ref, slice(None)) for out_ref in out_refs])


def plain_head_spread(pieces, span, width, kinds):
    return pl.pallas_call(
        plain_head_kernel,
        out_shape=[jax.ShapeDtypeStruct((span, width), F32)] * kinds,
        in_specs=[vmem()],
        out_specs=[vmem()] * kinds,
        compiler_params=params(),
        name="plain_head_spread",
    )(pieces)


def per_device(
    inputs,
    encoded,
    cotangent,
    doc_ids,
    buckets,
    gain_self,
    query_self,
    key_self,
    value_self,
    output_self,
    position_bias,
    gain_cross,
    query_cross,
    key_cross,
    value_cross,
    output_cross,
    gain_dense,
    dense_gate,
    dense_up,
    dense_down,
):
    micro_count, _, rows, width = inputs.shape
    part = encoded.shape[2]
    heads = position_bias.shape[1]
    dp, fs = lax.axis_size("dp"), lax.axis_size("fsdp")
    me, shard = lax.axis_index("dp"), lax.axis_index("fsdp")
    core, chips = me % 2, dp // 2
    length = rows * dp
    tokens = micro_count * rows
    copies = dp // heads
    head = me // copies
    span = width // fs
    half = span // 2
    hidden = dense_down.shape[0]
    chip_bits = [1 << place for place in range(1, dp.bit_length() - 1)]
    x_order, z_order = chip_bits, chip_bits[1:] + chip_bits[:1]
    paired = fs == 2
    chunked = paired and half % (16 * chips) == 0 and hidden % (16 * chips) == 0
    chunked = chunked and hidden % 128 == 0 and dp == heads and dp % 4 == 0

    def chip_of(j):
        last = len(x_order) - 1
        return sum(((j // bit) % 2) << (last - place) for place, bit in enumerate(x_order))

    def swap_dp(values, bit):
        return lax.ppermute(values, "dp", [(j, j ^ bit) for j in range(dp)])

    def swap_fs(values):
        return lax.ppermute(values, "fsdp", [(j, 1 - j) for j in range(2)])

    def after(values, *others):
        return lax.optimization_barrier((values, *others))[0]

    def half_rows(values):
        return jnp.stack([lax.dynamic_slice_in_dim(w, core * half, half, axis=0) for w in values])

    def both_halves(sent):
        got = swap_fs(sent)
        return got, swap_dp(got, 1)

    def quarter(bit):
        return 2 * ((me // bit) % 2) + core

    def quarter_starts(bit):
        rows = [(1 - shard) * span + (quarter(bit) ^ more) * (half // 2) for more in (0, 2, 1, 3)]
        return jnp.stack([shard * span] + rows).astype(jnp.int32)

    def gather_rows(values):
        return [lax.all_gather(w, "fsdp", axis=0, tiled=True) for w in values]

    def both_tokens(values):
        if paired:
            return jnp.concatenate([values, swap_fs(values)], axis=0)
        return lax.all_gather(values, "fsdp", axis=0, tiled=True)

    def reduce_chips(kept, got, order=x_order, marks=()):
        total = kept.astype(F32) + got.astype(F32)
        for place, bit in enumerate(order[1:]):
            count = total.shape[0] // 2
            sent, total = total[count:].astype(BF16), total[:count]
            if place < len(marks):
                sent = after(sent, marks[place])
            total = total + swap_dp(sent, bit).astype(F32)
        return total.astype(BF16)

    x, g, e = inputs[:, 0], cotangent[:, 0], encoded[:, 0]

    low, offsets = [x], [0]
    for bit in reversed(chip_bits[1:]):
        low = low + [swap_dp(piece, bit) for piece in low]
        offsets = offsets + [offset | bit for offset in offsets]
    high = [swap_dp(piece, 2) for piece in low]
    near, far = jnp.stack(low), jnp.stack(high)
    offsets = [offset ^ more for more in (0, 2, 1, 3) for offset in offsets]
    source = me ^ jnp.array(offsets, jnp.int32)
    e_all = lax.all_gather(e, "dp", axis=0)

    gains = jnp.stack([gain_self, gain_cross, gain_dense])
    own_head = lambda w: lax.dynamic_slice_in_dim(w, head * 64, 64, axis=1)
    if paired:
        pad = jnp.pad(position_bias.reshape(1, -1), ((0, 0), (0, span - position_bias.size)))
        small = jnp.concatenate([gains, pad], axis=0)
        small_got = swap_fs(small)
        head_pack = jnp.concatenate([own_head(w) for w in (query_self, key_self, value_self)], 1)
        head_got = swap_fs(head_pack)
        first, second = (
            jnp.where(shard == which, mine, got)
            for which, mine, got in ((0, small, small_got), (1, small, small_got))
        )
        gains = jnp.concatenate([first[:3], second[:3]], axis=1)
        bias_all = jnp.concatenate(
            [piece[3, : position_bias.size].reshape(position_bias.shape) for piece in (first, second)]
        )
        head_whole = jnp.where(
            shard == 0,
            jnp.concatenate([head_pack, head_got]),
            jnp.concatenate([head_got, head_pack]),
        )
        other = (1 - shard) * span
        half_starts = jnp.stack([shard * span, other + core * half, other + (1 - core) * half])
        half_starts = half_starts.astype(jnp.int32)
        near_bit, dense_bit = chip_bits[0], chip_bits[1]
        starts = quarter_starts(near_bit)
        kv_own = (key_cross, value_cross)
        near_own = (output_self, query_cross, output_cross)
        picked = [quarter(near_bit) * (half // 2), quarter(dense_bit) * (half // 2)]
        near_sent, theirs = pack(
            jnp.stack(picked + [(1 - shard) * hidden]).astype(jnp.int32),
            near_own + kv_own,
            (dense_gate, dense_up),
            half // 2,
            hidden,
        )
        near_got = swap_fs(near_sent)
        near_far = swap_dp(near_got, near_bit)
        dense_got = swap_fs(after(theirs, near_got))
        dense_own = (dense_gate, dense_up)
        which = jnp.stack([shard, core]).astype(jnp.int32)
        dense_starts = jnp.concatenate([quarter_starts(dense_bit), which])
    else:
        gains = lax.all_gather(gains, "fsdp", axis=1, tiled=True)
        bias_all = lax.all_gather(position_bias, "fsdp", axis=0, tiled=True)
        kv_own, kv_more = gather_rows((key_cross, value_cross)), ()
        near_own, near_more = gather_rows((output_self, query_cross, output_cross)), ()
        first_own, first_more = gather_rows((query_self, key_self, value_self)), ()
        half_starts = jnp.zeros((1,), jnp.int32)
        head_whole = jnp.concatenate([own_head(w) for w in first_own], axis=1)
        dense_own = [
            lax.all_to_all(w, "fsdp", 1, 0, tiled=True) for w in (dense_gate, dense_up)
        ]
        dense_more = ()
        starts = jnp.zeros((1,), jnp.int32)
        dense_starts = jnp.zeros((3,), jnp.int32)
        g_group = both_tokens(g.reshape(tokens, width))
    gains, bias_all = gains.astype(F32), bias_all.astype(F32)
    head_w = jnp.concatenate(
        [head_whole[:, at : at + 64] for at in (0, 0, 64, 64, 128, 128)], axis=1
    )

    marks = jnp.arange(bias_all.shape[0], dtype=jnp.int32)
    edges = jnp.sum((buckets[:, None] < marks[None, :]).astype(jnp.int32), axis=0)
    bias_values = lax.dynamic_slice_in_dim(bias_all, head, 1, axis=1)[:, 0]
    table = bias_table(edges, bias_values, length)
    x_groups = [near, far, swap_dp(near, 1), swap_dp(after(far, table), 1)]
    doc_row = jnp.broadcast_to(doc_ids[:, 0, :, None], (micro_count, dp, rows))
    doc_row = doc_row.reshape(micro_count, length)
    doc_col = doc_row[:, :, None]

    n_all, qkv, mixed = pl.pallas_call(
        functools.partial(self_forward_kernel, len(x_groups)),
        out_shape=[
            jax.ShapeDtypeStruct((dp, micro_count, rows, width), BF16),
            jax.ShapeDtypeStruct((length, 384), BF16),
            jax.ShapeDtypeStruct((length, 128), BF16),
        ],
        in_specs=[smem()] + [vmem()] * (len(x_groups) + 5),
        out_specs=[vmem()] * 3,
        compiler_params=params(),
        cost_estimate=cost(12),
        name="self_forward",
    )(source, *x_groups, gains[0:1], head_w, table, doc_row, doc_col)
    o1_heads = lax.all_to_all(mixed.reshape(dp, rows, 128), "dp", 0, 0, tiled=True)[::copies]

    if paired:
        near_more = (near_got, near_far, swap_dp(near_got, 1), swap_dp(after(near_far, mixed), 1))
        kv_more = near_more
        dense_far = swap_dp(after(dense_got, mixed), dense_bit)
    ke, ve = cross_kv(starts, e_all, *kv_own, kv_more)

    row32 = jax.ShapeDtypeStruct((tokens, width), F32)
    row16 = jax.ShapeDtypeStruct((tokens, width), BF16)
    left, x1, q2, x2, n3, left_sent = pl.pallas_call(
        functools.partial(mid_forward_kernel, len(near_more)),
        out_shape=[
            jax.ShapeDtypeStruct((3, tokens, width), BF16),
            row32,
            row16,
            row32,
            row16,
            jax.ShapeDtypeStruct((3, tokens, span), BF16),
        ],
        in_specs=[smem()] + [vmem()] * (8 + len(near_more)),
        out_specs=[vmem()] * 6,
        scratch_shapes=[pltpu.VMEM((tokens, width), BF16)] * 3,
        compiler_params=params(),
        cost_estimate=cost(12),
        name="mid_forward",
    )(starts, o1_heads, x, gains, ke, ve, *near_own, *near_more)

    if paired:
        dense_more = (
            dense_got,
            dense_far,
            swap_dp(after(dense_got, o1_heads), 1),
            swap_dp(after(dense_far, o1_heads), 1),
        )
        g_rows = g.reshape(tokens, width)
        g_got = swap_fs(after(g_rows, dense_got))
        n_got = swap_fs(n3)
        left_got = swap_fs(left_sent)
        back, y32, _, dn3, _ = dense_layer(
            dense_starts, n3, g_rows, *dense_own, dense_down, dense_more, tokens
        )
        back_mate = swap_dp(back, 1)
        back_got, _, y16, _, d16 = dense_layer(
            dense_starts,
            after(n_got, dn3, left_got),
            g_got,
            *dense_own,
            dense_down,
            dense_more,
            tokens,
        )
        back_got_mate = swap_dp(back_got, 1)
        dn3_more = swap_fs(d16)
    else:
        n_group = both_tokens(n3)
        back, _, y16, _, d16 = dense_layer(
            dense_starts, n_group, g_group, *dense_own, dense_down, dense_more, tokens
        )
        dn3 = jnp.zeros((tokens, width), F32)
        dn3_more = lax.psum_scatter(d16, "fsdp", scatter_dimension=0, tiled=True)
        dense_out = lax.psum_scatter(y16, "fsdp", scatter_dimension=0, tiled=True).astype(F32)
        outputs = (x2 + dense_out).astype(BF16)

    if chunked:
        where = jnp.stack([core, shard, me // 2]).astype(jnp.int32)
        masks = [
            [
                sum(((slot >> (len(order) - 1 - at)) & 1) * (bit // 2) for at, bit in enumerate(order))
                for slot in range(chips)
            ]
            for order in (x_order, z_order)
        ]
        own_kept, own_sent, down_kept, down_sent, far_kept, far_sent = chunk_weights(
            functools.partial(dense_weight_kernel, *masks),
            where,
            (after(n3, dn3_more), n_got, g_rows, g_got, back, back_got, back_mate, back_got_mate),
            (
                span // chips * hidden // 128,
                hidden // chips * width // 256,
                span // chips * hidden // 128,
            ),
            chips // 2,
            [
                pltpu.VMEM((max(hidden, half), max(hidden, width // 2)), F32),
                pltpu.VMEM((4 * tokens, width), BF16),
            ],
            7,
            "dense_weight",
        )
        dn3_more = after(dn3_more, own_sent)
        own_got, down_got = swap_dp(own_sent, z_order[0]), swap_dp(down_sent, x_order[0])
        far_got = swap_fs(far_sent)

    straight = chunked
    if straight:
        slots = jnp.append(chip_of(me ^ (2 * jnp.arange(heads // 2))), core).astype(jnp.int32)
    else:
        slots = jnp.append(jnp.arange(heads // 2), 0).astype(jnp.int32)
    g_rows = g.reshape(tokens, width)
    right, gx2, dkv_kept, dkv_sent, dc_dense = pl.pallas_call(
        functools.partial(cross_backward_kernel, len(near_more)),
        out_shape=[
            jax.ShapeDtypeStruct((tokens, 2 * width), BF16),
            row32,
            jax.ShapeDtypeStruct((heads // 2, dp, micro_count, part, 128), BF16),
            jax.ShapeDtypeStruct((heads // 2, dp, micro_count, part, 128), BF16),
            jax.ShapeDtypeStruct((1, width), F32),
        ],
        in_specs=[smem()] * 2 + [vmem()] * (9 + len(near_more)),
        out_specs=[vmem()] * 5,
        scratch_shapes=[pltpu.VMEM((tokens, width), F32), pltpu.VMEM((tokens, width), BF16)],
        compiler_params=params(),
        cost_estimate=cost(15),
        name="cross_backward",
    )(starts, slots, g_rows, dn3, dn3_more, x2, gains, q2, ke, ve, near_own[2], *near_more)
    if chunked:
        gx2 = after(gx2, own_got, down_got, far_got)
    gx1, last, do1_heads, dc_cross = pl.pallas_call(
        functools.partial(mid_backward_kernel, len(near_more)),
        out_shape=[
            row32,
            row16,
            jax.ShapeDtypeStruct((heads, rows, 128), BF16),
            jax.ShapeDtypeStruct((1, width), F32),
        ],
        in_specs=[smem()] + [vmem()] * (6 + len(near_more)),
        out_specs=[vmem()] * 4,
        scratch_shapes=[pltpu.VMEM((tokens, width), F32)],
        compiler_params=params(),
        cost_estimate=cost(6),
        name="mid_backward",
    )(starts, right, gx2, x1, gains, *near_own[:2], *near_more)
    do1 = lax.all_to_all(
        jnp.repeat(do1_heads, copies, axis=0) if copies > 1 else do1_heads, "dp", 0, 0, tiled=True
    ).reshape(length, 128)

    if chunked:
        right_got, last_got = swap_fs(after(right, do1_heads)), swap_fs(last)
        far_kept = swap_fs(after(far_kept, right_got, last_got))
        if straight:
            dkv_got = swap_dp(after(dkv_sent, do1_heads), 1)
            dkv_total = dkv_kept.astype(F32) + dkv_got.astype(F32)
            dkv_far = swap_dp(dkv_total[chips // 2 :].astype(BF16), x_order[0])

    dqkv, table_grad = pl.pallas_call(
        self_backward_kernel,
        out_shape=[
            jax.ShapeDtypeStruct((length, 384), BF16),
            jax.ShapeDtypeStruct((TILE, length), F32),
        ],
        in_specs=[vmem()] * 5,
        out_specs=[vmem()] * 2,
        scratch_shapes=[pltpu.VMEM((length, 128), F32), pltpu.VMEM((length, 128), F32)],
        compiler_params=params(),
        cost_estimate=cost(10),
        name="self_backward",
    )(qkv, do1, table, doc_row, doc_col)
    if chunked:
        dqkv = after(dqkv, right_got, last_got, dkv_far)
    head_grad = pl.pallas_call(
        head_weight_kernel,
        out_shape=jax.ShapeDtypeStruct((fs, span * 3 // 2, 128), BF16),
        in_specs=[vmem()] * 2,
        out_specs=vmem(),
        compiler_params=params(),
        cost_estimate=cost(6),
        name="head_weight",
    )(n_all, dqkv)
    def sum_shards(values):
        if paired:
            kept = lax.dynamic_index_in_dim(values, shard, 0)
            sent = lax.dynamic_index_in_dim(values, 1 - shard, 0)
            return (kept.astype(F32) + swap_fs(sent).astype(F32)).astype(BF16)
        return lax.psum_scatter(values, "fsdp", scatter_dimension=0, tiled=True)

    head_sum = sum_shards(head_grad)
    if chunked:
        token_kept, token_sent = chunk_weights(
            functools.partial(token_weight_kernel, masks[0]),
            where,
            (after(left, head_grad), left_got, right, right_got, last, last_got),
            (3 * half // chips * width // 128,),
            chips,
            [pltpu.VMEM((span, width), F32)],
            6,
            "token_weight",
        )
        token_got = swap_dp(token_sent, 1)
    if paired:
        first_own = (query_self, key_self, value_self)
        first_more = both_halves(after(half_rows(first_own), head_sum))
        y16 = swap_fs(after(y16, first_more[0]))
        outputs = (x2 + (y32 + y16.astype(F32))).astype(BF16)
    own_d = lax.all_to_all(dqkv.reshape(dp, rows, 384), "dp", 0, 0, tiled=True)[::copies]
    grad_inputs, dc_one = pl.pallas_call(
        functools.partial(input_grad_kernel, len(first_more)),
        out_shape=[row32, jax.ShapeDtypeStruct((1, width), F32)],
        in_specs=[smem()] + [vmem()] * (7 + len(first_more)),
        out_specs=[vmem()] * 2,
        scratch_shapes=[
            pltpu.VMEM((tokens, 3 * width), BF16),
            pltpu.VMEM((tokens, width), F32),
        ],
        compiler_params=params(),
        cost_estimate=cost(7),
        name="input_grad",
    )(half_starts, own_d, x, gains, gx1, *first_own, *first_more)

    if straight:
        dkv = reduce_chips(dkv_total[: chips // 2], dkv_far).reshape(-1, 128)
    else:
        dkv = jnp.stack([dkv_kept, dkv_sent], axis=1).reshape(heads * copies, -1, 128)
        dkv = lax.psum_scatter(dkv, "dp", scatter_dimension=0, tiled=True)[0]
        bit = 1
        while bit < copies:
            got = swap_dp(dkv, bit)
            dkv = jnp.where(
                (me // bit) % 2 == 0, jnp.concatenate([dkv, got]), jnp.concatenate([got, dkv])
            )
            bit *= 2
    cross_grad = pl.pallas_call(
        cross_head_weight_kernel,
        out_shape=jax.ShapeDtypeStruct((fs, span, 128), BF16),
        in_specs=[vmem()] * 2,
        out_specs=vmem(),
        compiler_params=params(),
        cost_estimate=cost(3),
        name="cross_head_weight",
    )(e_all, dkv)
    cross_sum = sum_shards(cross_grad)
    own_dkv = dkv.reshape(dp, micro_count * part, 128)
    own_dkv = lax.all_to_all(own_dkv, "dp", 0, 0, tiled=True)[::copies]
    grad_encoded = pl.pallas_call(
        functools.partial(encoder_grad_kernel, len(kv_more)),
        out_shape=jax.ShapeDtypeStruct((micro_count * part, width), F32),
        in_specs=[smem()] + [vmem()] * (3 + len(kv_more)),
        out_specs=vmem(),
        scratch_shapes=[pltpu.VMEM((micro_count * part, width), BF16)] * 2,
        compiler_params=params(),
        cost_estimate=cost(4),
        name="encoder_grad",
    )(starts, own_dkv, *kv_own, *kv_more)

    if chunked:
        sums = (
            reduce_chips(own_kept, own_got, z_order, (do1, dqkv)),
            reduce_chips(down_kept, down_got, x_order, (do1, dqkv)),
            reduce_chips(
                far_kept, swap_dp(after(far_got, do1), x_order[0]), x_order, (dqkv, head_grad)
            ),
            head_sum,
            reduce_chips(token_kept, token_got, [1] + x_order),
            cross_sum,
        )
        pieces = lax.all_gather(jnp.concatenate(sums, axis=1), "dp", axis=0, tiled=True)
        square, wide = (span, width), (span, fs * hidden)
        (
            grad_dense_gate,
            grad_dense_up,
            grad_dense_down,
            grad_query_self,
            grad_key_self,
            grad_value_self,
            grad_output_cross,
            grad_query_cross,
            grad_output_self,
            grad_key_cross,
            grad_value_cross,
        ) = spread(
            where,
            pieces,
            [(wide, "core")] * 2
            + [((hidden, width), "chip")]
            + [(square, "head")] * 3
            + [(square, "core")] * 3
            + [(square, "head")] * 2,
        )
    else:

        def all_heads(values, kinds):
            pieces = lax.all_gather(values, "dp", axis=0, tiled=True)[::copies]
            return plain_head_spread(pieces, span, width, kinds)

        grad_query_self, grad_key_self, grad_value_self = all_heads(head_sum, 3)
        grad_key_cross, grad_value_cross = all_heads(cross_sum, 2)
        right = jnp.concatenate([right, last], axis=1)

        def over_dp(values):
            return lax.psum(values.astype(BF16), "dp").astype(F32)

        def over_all(a, b):
            made = t_dot(a, b).astype(BF16)
            return over_dp(lax.psum_scatter(made, "fsdp", scatter_dimension=0, tiled=True))

        grad_output_cross, grad_query_cross, grad_output_self = (
            over_all(left[kind], right[:, kind * width : (kind + 1) * width]) for kind in range(3)
        )
        grad_dense_gate, grad_dense_up = (
            over_dp(
                lax.all_to_all(
                    t_dot(n_group, back[:, kind * hidden : (kind + 1) * hidden]).astype(BF16),
                    "fsdp",
                    0,
                    1,
                    tiled=True,
                )
            )
            for kind in range(2)
        )
        grad_dense_down = over_dp(t_dot(back[:, 2 * hidden :], g_group))

    if chunked:
        table_grad = after(table_grad, first_more[1])
    table_sums = jnp.sum(bucket_sums(edges, table_grad, bias_all.shape[0]), axis=1)
    column = (jnp.arange(heads) == head) & (me % copies == 0)
    bias_row = jnp.where(column[None, :], table_sums[:, None], 0.0).reshape(1, -1)
    bias_row = jnp.pad(bias_row, ((0, 0), (0, width - bias_row.shape[1])))
    sums = jnp.concatenate([dc_one, dc_dense, dc_cross, bias_row], axis=0)
    if paired:
        sums = sums + swap_fs(sums)
        for bit in [1] + chip_bits:
            sums = sums + swap_dp(sums, bit)
    else:
        sums = lax.psum(sums, ("dp", "fsdp"))
    own = lax.dynamic_slice_in_dim(sums[:3], shard * span, span, axis=1)
    grad_bias = sums[3, : bias_all.size].reshape(bias_all.shape)
    grad_bias = lax.dynamic_slice_in_dim(
        grad_bias, shard * position_bias.shape[0], position_bias.shape[0], axis=0
    )
    shape = (micro_count, 1, rows, width)
    return (
        outputs.reshape(shape),
        grad_inputs.reshape(shape),
        grad_encoded.reshape(micro_count, 1, part, width),
        own[0],
        grad_query_self,
        grad_key_self,
        grad_value_self,
        grad_output_self,
        grad_bias,
        own[2],
        grad_query_cross,
        grad_key_cross,
        grad_value_cross,
        grad_output_cross,
        own[1],
        grad_dense_gate,
        grad_dense_up,
        grad_dense_down,
    )


def solution(mesh):
    matrix = P("fsdp", None)
    token = P(None, "fsdp", "dp", None)
    weights = (
        (P("fsdp"),)
        + (matrix,) * 5
        + (P("fsdp"),)
        + (matrix,) * 4
        + (P("fsdp"),)
        + (matrix,) * 3
    )
    return jax.shard_map(
        per_device,
        mesh=mesh,
        in_specs=(token,) * 3 + (P(None, "fsdp", None), P()) + weights,
        out_specs=(token,) * 3 + weights,
        check_vma=False,
    )
```

```python
import functools

import jax
import jax.numpy as jnp
from jax import lax
from jax.experimental import pallas as pl
from jax.experimental.pallas import tpu as pltpu
from jax.sharding import PartitionSpec as P

EPS = 1e-06
NEGATIVE = -1e30
TILE = 256
F32 = jnp.float32
BF16 = jnp.bfloat16
VMEM_LIMIT = 56 * 1024 * 1024


def vmem():
    return pl.BlockSpec(memory_space=pltpu.VMEM)


def smem():
    return pl.BlockSpec(memory_space=pltpu.SMEM)


def params(limit=VMEM_LIMIT):
    return pltpu.CompilerParams(vmem_limit_bytes=limit)


def cost(microseconds):
    return pl.CostEstimate(
        flops=int(microseconds * 1.15e9),
        bytes_accessed=int(microseconds * 3.69e6),
        transcendentals=0,
    )


def aligned(start, size):
    return pl.ds(pl.multiple_of(start, size), size)


def dot(left, right):
    return jnp.dot(left, right, preferred_element_type=F32)


def dot_t(left, right):
    return lax.dot_general(left, right, (((1,), (1,)), ((), ())), preferred_element_type=F32)


def t_dot(left, right):
    return lax.dot_general(left, right, (((0,), (0,)), ((), ())), preferred_element_type=F32)


def norm_rows(values, gain):
    return values * lax.rsqrt(jnp.mean(values * values, axis=-1, keepdims=True) + EPS) * gain


def norm_back(values, gain, grad):
    r = lax.rsqrt(jnp.mean(values * values, axis=-1, keepdims=True) + EPS)
    scaled = grad * gain
    inner = jnp.mean(scaled * values, axis=-1, keepdims=True)
    back = r * scaled - values * (r * r * r * inner)
    return back, jnp.sum(grad * (values * r), axis=0, keepdims=True)


def low_lanes(rows):
    return lax.broadcasted_iota(jnp.int32, (rows, 128), 1) < 64


def pair_up(first, second):
    lane = low_lanes(first.shape[0])
    low = jnp.where(lane, first, pltpu.roll(second, 64, 1))
    high = jnp.where(lane, pltpu.roll(first, 64, 1), second)
    return low, high


def keep_half(values, half):
    lane = low_lanes(values.shape[0])
    return jnp.where(lane if half == 0 else ~lane, values, jnp.zeros_like(values))


def softmax_rows(scores):
    top = jnp.max(scores, axis=-1, keepdims=True)
    raised = jnp.exp(scores - top)
    return raised * (1.0 / jnp.sum(raised, axis=-1, keepdims=True))


def table_kernel(edge_ref, value_ref, out_ref):
    rows, length = out_ref.shape
    bucket_count = value_ref.shape[0]
    for start in range(0, length, TILE):
        place = (rows, TILE)
        apart = (
            lax.broadcasted_iota(jnp.int32, place, 0)
            - lax.broadcasted_iota(jnp.int32, place, 1)
            + (length - rows - start)
        )
        value = jnp.full(place, value_ref[0], F32)
        for bucket in range(1, bucket_count):
            value = jnp.where(apart >= edge_ref[bucket], value_ref[bucket], value)
        out_ref[:, start : start + TILE] = jnp.where(apart >= 0, value, NEGATIVE)


def bias_table(edges, values, length):
    return pl.pallas_call(
        table_kernel,
        out_shape=jax.ShapeDtypeStruct((TILE, length), F32),
        in_specs=[smem(), smem()],
        out_specs=vmem(),
        cost_estimate=cost(4),
        name="bias_table",
    )(edges, values)


def bucket_kernel(edge_ref, grad_ref, out_ref):
    rows, length = grad_ref.shape
    bucket_count = out_ref.shape[0]
    above = [jnp.zeros((8, TILE), F32) for _ in range(bucket_count)]
    for start in range(0, length, TILE):
        for row in range(0, rows, 8):
            place = (8, TILE)
            apart = (
                lax.broadcasted_iota(jnp.int32, place, 0)
                - lax.broadcasted_iota(jnp.int32, place, 1)
                + (length - rows - start + row)
            )
            tile = grad_ref[row : row + 8, start : start + TILE]
            for bucket in range(bucket_count):
                above[bucket] = above[bucket] + jnp.where(apart >= edge_ref[bucket], tile, 0.0)
    for bucket in range(bucket_count):
        rest = above[bucket + 1] if bucket + 1 < bucket_count else 0.0
        part = jnp.sum(above[bucket] - rest, axis=0, keepdims=True)
        out_ref[bucket : bucket + 1, :] = part[:, :128] + part[:, 128:]


def bucket_sums(edges, grad, bucket_count):
    return pl.pallas_call(
        bucket_kernel,
        out_shape=jax.ShapeDtypeStruct((bucket_count, 128), F32),
        in_specs=[smem(), vmem()],
        out_specs=vmem(),
        cost_estimate=cost(7),
        name="bucket_sums",
    )(edges, grad)


def times(x_ref, starts_ref, pieces):
    if len(pieces) == 1:
        return dot(x_ref[...], pieces[0])
    total = None
    for place, piece in enumerate(pieces):
        rows = piece.shape[0]
        part = dot(x_ref[:, aligned(starts_ref[place], rows)], piece)
        total = part if total is None else total + part
    return total


def times_back(out_ref, starts_ref, terms):
    for place in range(len(terms[0][1])):
        total = sum(dot_t(d, pieces[place]) for d, pieces in terms)
        rows = terms[0][1][place].shape[0]
        if len(terms[0][1]) == 1:
            out_ref[...] = total
        else:
            out_ref[:, aligned(starts_ref[place], rows)] = total


def pack_kernel(counts, where_ref, *refs):
    total = sum(counts)
    first_ref, second_ref = refs[total:]
    for place in range(counts[0]):
        first_ref[place] = refs[place][...]
    for place in range(counts[1]):
        second_ref[place] = refs[counts[0] + place][...]


def pack(where, first, second, rows, cols):
    width = first[0].shape[1]
    counts = (len(first), len(second))
    return pl.pallas_call(
        functools.partial(pack_kernel, counts),
        grid_spec=pltpu.PrefetchScalarGridSpec(
            num_scalar_prefetch=1,
            grid=(1,),
            in_specs=[pl.BlockSpec((rows, width), lambda i, where: (where[0], 0))] * counts[0]
            + [pl.BlockSpec((rows, cols), lambda i, where: (where[1], where[2]))] * counts[1],
            out_specs=[
                pl.BlockSpec((counts[0], rows, width), lambda i, where: (0, 0, 0)),
                pl.BlockSpec((counts[1], rows, cols), lambda i, where: (0, 0, 0)),
            ],
        ),
        out_shape=[
            jax.ShapeDtypeStruct((counts[0], rows, width), BF16),
            jax.ShapeDtypeStruct((counts[1], rows, cols), BF16),
        ],
        compiler_params=params(),
        cost_estimate=cost(3),
        name="pack",
    )(where, *first, *second)


def pieces_of(own_ref, more, index):
    return [own_ref[...]] + [ref[index] for ref in more]


def self_scores(q, k, table, doc_col, doc_row):
    scores = dot_t(q, k) + table
    return jnp.where(doc_col == doc_row, scores, NEGATIVE)


def self_forward_kernel(groups, source_ref, *refs):
    x_refs = refs[:groups]
    gain_ref, w_ref, table_ref, doc_row_ref, doc_col_ref, n_ref, qkv_ref, o_ref = refs[groups:]
    count, _, rows, width = x_refs[0].shape
    length = groups * count * rows
    lane = lax.broadcasted_iota(jnp.int32, (rows, 384), 1) % 128 < 64
    together = min(TILE // rows, count)
    for place, x_ref in enumerate(x_refs):
        for first in range(0, count, together):
            parts = []
            for inner in range(first, first + together):
                x = x_ref[inner].astype(F32).reshape(2 * rows, width)
                n = norm_rows(x, gain_ref[...]).astype(BF16)
                n_ref[source_ref[place * count + inner]] = n.reshape(2, rows, width)
                parts.append(n)
            made = dot(jnp.concatenate(parts, axis=0), w_ref[...])
            for inner in range(together):
                at = 2 * rows * inner
                picked = jnp.where(lane, made[at : at + rows], made[at + rows : at + 2 * rows])
                own = source_ref[place * count + first + inner]
                qkv_ref[aligned(own * rows, rows), :] = picked.astype(BF16)
    for block in range(length // TILE):
        start, stop = block * TILE, (block + 1) * TILE
        table = table_ref[:, length - stop :]
        q = qkv_ref[start:stop, 0:128]
        k = qkv_ref[:stop, 128:256]
        v = qkv_ref[:stop, 256:384]
        mixed = []
        for half in range(2):
            scores = self_scores(
                keep_half(q, half),
                k,
                table,
                doc_col_ref[half, start:stop, :],
                doc_row_ref[half : half + 1, :stop],
            )
            mixed.append(dot(softmax_rows(scores).astype(BF16), v))
        o_ref[start:stop, :] = jnp.where(low_lanes(TILE), mixed[0], mixed[1]).astype(BF16)


def self_backward_kernel(
    qkv_ref, do_ref, table_ref, doc_row_ref, doc_col_ref, dqkv_ref, grad_ref, dk_ref, dv_ref
):
    length = qkv_ref.shape[0]
    grad_ref[...] = jnp.zeros_like(grad_ref)
    dk_ref[...] = jnp.zeros_like(dk_ref)
    dv_ref[...] = jnp.zeros_like(dv_ref)
    for block in range(length // TILE):
        start, count = block * TILE, (block + 1) * TILE
        table = table_ref[:, length - count :]
        k = qkv_ref[:count, 128:256]
        v = qkv_ref[:count, 256:384]
        made = []
        for half in range(2):
            q = keep_half(qkv_ref[start:count, 0:128], half)
            do = keep_half(do_ref[start:count, :], half)
            p = softmax_rows(
                self_scores(
                    q,
                    k,
                    table,
                    doc_col_ref[half, start:count, :],
                    doc_row_ref[half : half + 1, :count],
                )
            )
            dp = dot_t(do, v)
            ds = (p * (dp - jnp.sum(p * dp, axis=-1, keepdims=True))).astype(BF16)
            grad_ref[:, length - count :] += ds.astype(F32)
            made.append(dot(ds, k))
            dk_ref[:count, :] += t_dot(ds, q)
            dv_ref[:count, :] += t_dot(p.astype(BF16), do)
        dq = jnp.where(low_lanes(TILE), made[0], made[1])
        dqkv_ref[start:count, 0:128] = dq.astype(BF16)
    dqkv_ref[:, 128:256] = dk_ref[...].astype(BF16)
    dqkv_ref[:, 256:384] = dv_ref[...].astype(BF16)


def head_weight_kernel(n_ref, d_ref, out_ref):
    blocks, _, rows, width = n_ref.shape
    shards = out_ref.shape[0]
    span = width // shards
    lane = lax.broadcasted_iota(jnp.int32, (blocks * rows, 384), 1) % 128 < 64
    d = d_ref[...]
    zero = jnp.zeros_like(d)
    right = [jnp.where(lane, d, zero), jnp.where(lane, zero, d)]
    half = span // 2
    for shard in range(shards):
        total = jnp.zeros((span, 384), F32)
        for micro in range(2):
            left = n_ref[:, micro, :, shard * span : (shard + 1) * span]
            total = total + t_dot(left.reshape(blocks * rows, span), right[micro])
        q, k, v = (
            total[:, at : at + 128] + pltpu.roll(total[:, at : at + 128], 64, 1)
            for at in (0, 128, 256)
        )
        out_ref[shard, :span, :] = jnp.where(low_lanes(span), q, k).astype(BF16)
        out_ref[shard, span:, :] = jnp.where(low_lanes(half), v[:half], v[half:]).astype(BF16)


def cross_kv_kernel(split, starts_ref, e_ref, wk_ref, wv_ref, *refs):
    more, (ke_ref, ve_ref) = refs[:split], refs[split:]
    blocks, _, part, _ = e_ref.shape
    for index, (own_ref, out_ref) in enumerate(((wk_ref, ke_ref), (wv_ref, ve_ref)), 3):
        total = None
        pieces = pieces_of(own_ref, more, index)
        for place, piece in enumerate(pieces):
            rows = piece.shape[0]
            if split:
                left = e_ref[:, 0, :, aligned(starts_ref[place], rows)]
            else:
                left = e_ref[:, 0]
            made = dot(left.reshape(blocks * part, rows), piece)
            total = made if total is None else total + made
        out_ref[0] = total.astype(BF16)


def cross_kv(starts, e_all, wk, wv, more):
    blocks, micro, part, width = e_all.shape
    whole = lambda array: pl.BlockSpec(array.shape, lambda m, s: (0,) * array.ndim)
    out = pl.BlockSpec((1, blocks * part, width), lambda m, s: (m, 0, 0))
    return pl.pallas_call(
        functools.partial(cross_kv_kernel, len(more)),
        grid_spec=pltpu.PrefetchScalarGridSpec(
            num_scalar_prefetch=1,
            grid=(micro,),
            in_specs=[pl.BlockSpec((blocks, 1, part, width), lambda m, s: (0, m, 0, 0))]
            + [whole(array) for array in (wk, wv, *more)],
            out_specs=[out, out],
        ),
        out_shape=[jax.ShapeDtypeStruct((micro, blocks * part, width), BF16)] * 2,
        compiler_params=params(),
        cost_estimate=cost(8),
        name="cross_kv",
    )(starts, e_all, wk, wv, *more)


def mid_forward_kernel(split, starts_ref, o1_ref, x_ref, gain_ref, ke_ref, ve_ref, wo, wq, wc, *refs):
    more = refs[:split]
    left_ref, x1_ref, q2_ref, x2_ref, n3_ref, sent_ref, o1c_ref, n2_ref, o2_ref = refs[split:]
    heads, rows, _ = o1_ref.shape
    width = x_ref.shape[-1]
    for pair in range(heads // 2):
        at = pair * 128
        low, high = pair_up(o1_ref[2 * pair].astype(F32), o1_ref[2 * pair + 1].astype(F32))
        o1c_ref[0:rows, at : at + 128] = low.astype(BF16)
        o1c_ref[rows : 2 * rows, at : at + 128] = high.astype(BF16)
    x = x_ref[...].astype(F32).reshape(2 * rows, width)
    x1 = x + times(o1c_ref, starts_ref, pieces_of(wo, more, 0))
    x1_ref[...] = x1
    n2_ref[...] = norm_rows(x1, gain_ref[1:2]).astype(BF16)
    q2_ref[...] = times(n2_ref, starts_ref, pieces_of(wq, more, 1)).astype(BF16)
    for micro in range(2):
        for pair in range(heads // 2):
            at = pair * 128
            span = slice(micro * rows, (micro + 1) * rows)
            q = q2_ref[span, at : at + 128]
            both = jnp.concatenate([keep_half(q, 0), keep_half(q, 1)], axis=0)
            p = softmax_rows(dot_t(both, ke_ref[micro, :, at : at + 128]))
            o = dot(p.astype(BF16), ve_ref[micro, :, at : at + 128])
            o2_ref[span, at : at + 128] = jnp.where(
                low_lanes(rows), o[:rows], o[rows:]
            ).astype(BF16)
    x2 = x1 + times(o2_ref, starts_ref, pieces_of(wc, more, 2))
    x2_ref[...] = x2
    n3_ref[...] = norm_rows(x2, gain_ref[2:3]).astype(BF16)
    left_ref[0] = o2_ref[...]
    left_ref[1] = n2_ref[...]
    left_ref[2] = o1c_ref[...]
    if split:
        span = sent_ref.shape[2]
        for kind in range(3):
            sent_ref[kind] = left_ref[kind, :, aligned(span - starts_ref[0], span)]


def cross_backward_kernel(
    split, starts_ref, slots_ref, g_ref, dn3_ref, more_ref, x2_ref, gain_ref, q2_ref, ke_ref, ve_ref,
    wc, *refs
):
    more = refs[:split]
    right_ref, gx2_ref, keep_ref, send_ref, dc_ref, back_ref, do2_ref = refs[split:]
    blocks, micros, part = keep_ref.shape[1:4]
    tokens, width = x2_ref.shape
    rows = tokens // micros
    pairs = width // 128
    even = slots_ref[pairs] == 0
    dn3 = dn3_ref[...] + more_ref[...].astype(F32)
    back, dc_ref[...] = norm_back(x2_ref[...], gain_ref[2:3], dn3)
    gx2 = g_ref[...].astype(F32) + back
    gx2_ref[...] = gx2
    gx2b = gx2.astype(BF16)
    right_ref[:, 0:width] = gx2b
    times_back(back_ref, starts_ref, [(gx2b, pieces_of(wc, more, 2))])
    do2_ref[...] = back_ref[...].astype(BF16)
    for micro in range(micros):
        for pair in range(pairs):
            at = pair * 128
            span = slice(micro * rows, (micro + 1) * rows)
            q = q2_ref[span, at : at + 128]
            do = do2_ref[span, at : at + 128]
            q = jnp.concatenate([keep_half(q, 0), keep_half(q, 1)], axis=0)
            do = jnp.concatenate([keep_half(do, 0), keep_half(do, 1)], axis=0)
            k = ke_ref[micro, :, at : at + 128]
            v = ve_ref[micro, :, at : at + 128]
            p = softmax_rows(dot_t(q, k))
            dp = dot_t(do, v)
            ds = (p * (dp - jnp.sum(p * dp, axis=-1, keepdims=True))).astype(BF16)
            dq = dot(ds, k)
            right_ref[span, width + at : width + at + 128] = jnp.where(
                low_lanes(rows), dq[:rows], dq[rows:]
            ).astype(BF16)
            low, high = pair_up(t_dot(ds, q), t_dot(p.astype(BF16), do))
            kept, sent = jnp.where(even, low, high), jnp.where(even, high, low)
            slot = slots_ref[pair]
            keep_ref[slot, :, micro] = kept.astype(BF16).reshape(blocks, part, 128)
            send_ref[slot, :, micro] = sent.astype(BF16).reshape(blocks, part, 128)


def mid_backward_kernel(split, starts_ref, right_ref, gx2_ref, x1_ref, gain_ref, wo, wq, *refs):
    more = refs[:split]
    gx1_ref, low_ref, do1_ref, dc_ref, back_ref = refs[split:]
    heads, rows, _ = do1_ref.shape
    width = x1_ref.shape[-1]
    times_back(back_ref, starts_ref, [(right_ref[:, width:], pieces_of(wq, more, 1))])
    back, dc_ref[...] = norm_back(x1_ref[...], gain_ref[1:2], back_ref[...])
    gx1 = gx2_ref[...] + back
    gx1_ref[...] = gx1
    gx1b = gx1.astype(BF16)
    low_ref[...] = gx1b
    times_back(back_ref, starts_ref, [(gx1b, pieces_of(wo, more, 0))])
    for pair in range(heads // 2):
        at = pair * 128
        do1 = back_ref[:, at : at + 128].astype(BF16).astype(F32)
        low, high = pair_up(do1[:rows], do1[rows:])
        do1_ref[2 * pair] = low.astype(BF16)
        do1_ref[2 * pair + 1] = high.astype(BF16)


def input_grad_kernel(split, starts_ref, d_ref, x_ref, gain_ref, gx1_ref, wq, wk, wv, *refs):
    more = refs[:split]
    out_ref, dc_ref, all_ref, back_ref = refs[split:]
    heads, rows, _ = d_ref.shape
    width = x_ref.shape[-1]
    for kind in range(3):
        for pair in range(heads // 2):
            lanes = slice(kind * 128, (kind + 1) * 128)
            low, high = pair_up(
                d_ref[2 * pair, :, lanes].astype(F32), d_ref[2 * pair + 1, :, lanes].astype(F32)
            )
            at = kind * width + pair * 128
            all_ref[0:rows, at : at + 128] = low.astype(BF16)
            all_ref[rows : 2 * rows, at : at + 128] = high.astype(BF16)
    terms = [
        (all_ref[:, kind * width : (kind + 1) * width], pieces_of(own, more, kind))
        for kind, own in enumerate((wq, wk, wv))
    ]
    times_back(back_ref, starts_ref, terms)
    x = x_ref[...].astype(F32).reshape(2 * rows, width)
    back, dc = norm_back(x, gain_ref[0:1], back_ref[...])
    dc_ref[...] = dc
    out_ref[...] = gx1_ref[...] + back


def encoder_grad_kernel(split, starts_ref, d_ref, wk, wv, *refs):
    more = refs[:split]
    out_ref, k_ref, v_ref = refs[split:]
    for pair in range(d_ref.shape[0] // 2):
        at = pair * 128
        low, high = pair_up(d_ref[2 * pair].astype(F32), d_ref[2 * pair + 1].astype(F32))
        k_ref[:, at : at + 128] = low.astype(BF16)
        v_ref[:, at : at + 128] = high.astype(BF16)
    terms = [(k_ref[...], pieces_of(wk, more, 3)), (v_ref[...], pieces_of(wv, more, 4))]
    times_back(out_ref, starts_ref, terms)


def cross_head_weight_kernel(e_ref, d_ref, out_ref):
    blocks, micro, part, width = e_ref.shape
    shards, span, _ = out_ref.shape
    for shard in range(shards):
        left = e_ref[:, :, :, shard * span : (shard + 1) * span]
        left = left.reshape(blocks * micro * part, span)
        out_ref[shard] = t_dot(left, d_ref[...]).astype(BF16)


def dense_kernel(split, starts_ref, n_ref, g_ref, wg, wu, wd_ref, *refs):
    more = refs[:split]
    back_ref, y_ref, ylow_ref, d_ref, dlow_ref = refs[split:]
    hidden = wd_ref.shape[0]
    gate, up = pieces_of(wg, more, 0), pieces_of(wu, more, 1)
    a = times(n_ref, starts_ref, gate)
    b = times(n_ref, starts_ref, up)
    scale = 0.7978845608028654
    cubed = 0.044715
    inner = jnp.tanh(scale * (a + cubed * (a * a * a)))
    gelu = 0.5 * a * (1.0 + inner)
    slope = 0.5 * (1.0 + inner) + 0.5 * a * (1.0 - inner * inner) * (
        scale * (1.0 + 3.0 * cubed * (a * a))
    )
    hid = (gelu * b).astype(BF16)
    dh = dot_t(g_ref[...], wd_ref[...])
    da = (dh * b * slope).astype(BF16)
    db = (dh * gelu).astype(BF16)
    times_back(d_ref, starts_ref, [(da, gate), (db, up)])
    dlow_ref[...] = d_ref[...].astype(BF16)
    y = dot(hid, wd_ref[...])
    y_ref[...] = y
    ylow_ref[...] = y.astype(BF16)
    back_ref[:, 0:hidden] = da
    back_ref[:, hidden : 2 * hidden] = db
    back_ref[:, 2 * hidden : 3 * hidden] = hid
    if more:
        shard, other = starts_ref[len(more) + 1], 1 - starts_ref[len(more) + 2]
        put_features(back_ref, 3 * hidden, n_ref, g_ref, shard, other)


def put_features(out_ref, at, n_ref, g_ref, shard, core):
    quarter = n_ref.shape[1] // 4
    for side, place in enumerate((2 * shard + core, 2 * (1 - shard) + core)):
        lanes = slice(at + side * quarter, at + (side + 1) * quarter)
        out_ref[:, lanes] = n_ref[:, aligned(place * quarter, quarter)]
    lanes = slice(at + 2 * quarter, at + 4 * quarter)
    out_ref[:, lanes] = g_ref[:, aligned(core * 2 * quarter, 2 * quarter)]


def dense_layer(starts, n, g, wg, wu, wd, more, step):
    count, width = n.shape
    hidden = wd.shape[0]
    which = starts.shape[0] - 2
    back = 3 * hidden + (width if more else 0)
    row = lambda size: pl.BlockSpec((step, size), lambda i, s: (i, 0))
    whole = lambda array: pl.BlockSpec(array.shape, lambda i, s: (0,) * array.ndim)
    column = pl.BlockSpec((wg.shape[0], hidden), lambda i, s: (0, s[which]))
    made = lambda size, kind: jax.ShapeDtypeStruct((count, size), kind)
    return pl.pallas_call(
        functools.partial(dense_kernel, len(more)),
        grid_spec=pltpu.PrefetchScalarGridSpec(
            num_scalar_prefetch=1,
            grid=(count // step,),
            in_specs=[row(width), row(width), column, column, whole(wd)]
            + [whole(array) for array in more],
            out_specs=[row(back)] + [row(width)] * 4,
        ),
        out_shape=[made(back, BF16)]
        + [made(width, F32), made(width, BF16), made(width, F32), made(width, BF16)],
        compiler_params=params(),
        cost_estimate=cost(13),
        name="dense_layer",
    )(starts, n, g, wg, wu, wd, *more)


def put_chunk(ref, slot, at, value):
    rows, width = value.shape
    for block in range(width // 128):
        ref[slot, at + block * rows : at + (block + 1) * rows, :] = value[
            :, block * 128 : (block + 1) * 128
        ].astype(BF16)


def take_chunk(ref, slot, at, rows, width):
    return jnp.concatenate(
        [
            ref[slot, at + block * rows : at + (block + 1) * rows, :].astype(F32)
            for block in range(width // 128)
        ],
        axis=1,
    )


def put_all(scratch_ref, first, count, chip, chunk_refs, at, width, masks):
    slots = [(ref, slot) for ref in chunk_refs for slot in range(ref.shape[0])]
    rows = count // len(slots)
    for (ref, slot), mask in zip(slots, masks):
        chunk = scratch_ref[aligned(first + (chip ^ mask) * rows, rows), :width]
        put_chunk(ref, slot, at, chunk)


def dense_weight_kernel(
    x_masks, z_masks, where_ref, n0_ref, n1_ref, g0_ref, g1_ref, own0_ref, own1_ref, mate0_ref, mate1_ref, keep_ref,
    send_ref, down_keep_ref, down_send_ref, far_keep_ref, far_send_ref, scratch_ref, left_ref
):
    tokens, width = n0_ref.shape
    hidden = (own0_ref.shape[1] - width) // 3
    quarter = width // 4
    at = keep_ref.shape[1] // 2
    core, shard, chip = where_ref[0], where_ref[1], where_ref[2]
    put_features(left_ref.at[:tokens], 0, n0_ref, g0_ref, shard, core)
    put_features(left_ref.at[tokens : 2 * tokens], 0, n1_ref, g1_ref, shard, core)
    left_ref[2 * tokens : 3 * tokens, :] = mate0_ref[:, 3 * hidden :]
    left_ref[3 * tokens :, :] = mate1_ref[:, 3 * hidden :]

    def whole(kind):
        span = slice(kind * hidden, (kind + 1) * hidden)
        refs = (own0_ref, own1_ref, mate0_ref, mate1_ref)
        return jnp.concatenate([ref[:, span] for ref in refs], axis=0)

    for kind in range(2):
        right = whole(kind)
        for side, (masks, refs) in enumerate(
            ((z_masks, (keep_ref, send_ref)), (x_masks, (far_keep_ref, far_send_ref)))
        ):
            value = t_dot(left_ref[:, side * quarter : (side + 1) * quarter], right)
            scratch_ref[:quarter, :hidden] = value
            put_all(scratch_ref, 0, quarter, chip, refs, kind * at, hidden, masks)
    value = t_dot(whole(2), left_ref[:, 2 * quarter :])
    scratch_ref[:, : 2 * quarter] = value
    refs = (down_keep_ref, down_send_ref)
    put_all(scratch_ref, 0, hidden, chip, refs, 0, 2 * quarter, x_masks)


def token_weight_kernel(
    masks, where_ref, left_ref, left_more_ref, right_ref, right_more_ref, last_ref, last_more_ref,
    mine_ref, mate_ref, scratch_ref
):
    kinds, _, span = left_more_ref.shape
    width = last_ref.shape[1]
    core, shard, chip = where_ref[0], where_ref[1], where_ref[2]
    half = span // 2
    at = half // len(masks) * width // 128
    for kind in range(kinds):
        lanes = slice(kind * width, (kind + 1) * width)
        left = [left_ref[kind, :, aligned(shard * span, span)], left_more_ref[kind]]
        if kind < kinds - 1:
            right = [right_ref[:, lanes], right_more_ref[:, lanes]]
        else:
            right = [last_ref[...], last_more_ref[...]]
        scratch_ref[...] = t_dot(jnp.concatenate(left, axis=0), jnp.concatenate(right, axis=0))
        for ref, own in ((mine_ref, core), (mate_ref, 1 - core)):
            put_all(scratch_ref, own * half, half, chip, (ref,), kind * at, width, masks)


def chunk_weights(kernel, where, operands, counts, slots, scratches, length, name):
    shapes = []
    for count in counts:
        shapes += [jax.ShapeDtypeStruct((slots, count, 128), BF16)] * 2
    return pl.pallas_call(
        kernel,
        out_shape=shapes,
        in_specs=[smem()] + [vmem()] * len(operands),
        out_specs=[vmem()] * len(shapes),
        scratch_shapes=scratches,
        compiler_params=params(),
        cost_estimate=cost(length),
        name=name,
    )(where, *operands)


def head_rows(in_ref, at, rows, outs):
    for pair in range(in_ref.shape[0] // 2):
        lanes = slice(pair * 128, (pair + 1) * 128)
        first = in_ref[2 * pair, at : at + rows, :].astype(F32)
        second = in_ref[2 * pair + 1, at : at + rows, :].astype(F32)
        for (out_ref, place), value in zip(outs, pair_up(first, second)):
            out_ref[place, lanes] = value


def head_spread(in_ref, at, q_ref, k_ref, v_ref):
    span = q_ref.shape[0]
    half = span // 2
    head_rows(in_ref, at, span, ((q_ref, slice(None)), (k_ref, slice(None))))
    head_rows(in_ref, at + span, half, ((v_ref, slice(0, half)), (v_ref, slice(half, span))))


def spread_kernel(where_ref, in_ref, gate_ref, up_ref, down_ref, q_ref, k_ref, v_ref, *out_refs):
    shard = where_ref[1]
    hidden = gate_ref.shape[3] // 2
    rows = gate_ref.shape[2] // 2
    at = rows * hidden // 128
    tall = down_ref.shape[0] // 2
    half = down_ref.shape[1] // 2
    span = q_ref.shape[0]
    kinds = len(out_refs) - 2
    width = out_refs[0].shape[3]
    base = 6 * at + 3 * span // 2
    step = rows * width // 128
    for piece in range(4):
        chip, core = piece // 2, piece % 2
        place = slice(chip * rows, (chip + 1) * rows)
        for side, start in enumerate((0, 4 * at)):
            lanes = aligned((shard ^ side) * hidden, hidden)
            for kind, out_ref in enumerate((gate_ref, up_ref)):
                chunk = take_chunk(in_ref, piece, start + kind * at, rows, hidden)
                out_ref[core, 0, place, lanes] = chunk
        chunk = take_chunk(in_ref, piece, 2 * at, tall, half)
        down_ref[chip * tall : (chip + 1) * tall, core * half : (core + 1) * half] = chunk
        for kind in range(kinds):
            chunk = take_chunk(in_ref, piece, base + kind * step, rows, width)
            out_refs[kind][core, 0, place, :] = chunk
    head_spread(in_ref, 6 * at, q_ref, k_ref, v_ref)
    k_ref, v_ref = out_refs[kinds:]
    head_rows(in_ref, base + kinds * step, span, ((k_ref, slice(None)), (v_ref, slice(None))))


def spread(where, pieces, outs):
    count, total, _ = pieces.shape
    steps = count // 4
    specs, shapes = [], []
    for (rows, cols), kind in outs:
        if kind == "core":
            shapes.append((2, steps, rows // (2 * steps), cols))
            block = (2, 1, rows // (2 * steps), cols)
            specs.append(pl.BlockSpec(block, lambda q, where: (0, q, 0, 0)))
        elif kind == "chip":
            shapes.append((rows, cols))
            specs.append(pl.BlockSpec((rows // steps, cols), lambda q, where: (q, 0)))
        else:
            shapes.append((rows, cols))
            specs.append(pl.BlockSpec((rows, cols // steps), lambda q, where: (0, q)))
    made = pl.pallas_call(
        spread_kernel,
        grid_spec=pltpu.PrefetchScalarGridSpec(
            num_scalar_prefetch=1,
            grid=(steps,),
            in_specs=[pl.BlockSpec((4, total, 128), lambda q, where: (q, 0, 0))],
            out_specs=specs,
        ),
        out_shape=[jax.ShapeDtypeStruct(shape, F32) for shape in shapes],
        compiler_params=params(),
        cost_estimate=cost(20),
        name="spread",
    )(where, pieces)
    return [array.reshape(shape) for array, (shape, _) in zip(made, outs)]


def plain_head_kernel(in_ref, *out_refs):
    span = out_refs[0].shape[0]
    if len(out_refs) == 3:
        head_spread(in_ref, 0, *out_refs)
    else:
        head_rows(in_ref, 0, span, [(out_ref, slice(None)) for out_ref in out_refs])


def plain_head_spread(pieces, span, width, kinds):
    return pl.pallas_call(
        plain_head_kernel,
        out_shape=[jax.ShapeDtypeStruct((span, width), F32)] * kinds,
        in_specs=[vmem()],
        out_specs=[vmem()] * kinds,
        compiler_params=params(),
        name="plain_head_spread",
    )(pieces)


def per_device(
    inputs,
    encoded,
    cotangent,
    doc_ids,
    buckets,
    gain_self,
    query_self,
    key_self,
    value_self,
    output_self,
    position_bias,
    gain_cross,
    query_cross,
    key_cross,
    value_cross,
    output_cross,
    gain_dense,
    dense_gate,
    dense_up,
    dense_down,
):
    micro_count, _, rows, width = inputs.shape
    part = encoded.shape[2]
    heads = position_bias.shape[1]
    dp, fs = lax.axis_size("dp"), lax.axis_size("fsdp")
    me, shard = lax.axis_index("dp"), lax.axis_index("fsdp")
    core, chips = me % 2, dp // 2
    length = rows * dp
    tokens = micro_count * rows
    copies = dp // heads
    head = me // copies
    span = width // fs
    half = span // 2
    hidden = dense_down.shape[0]
    chip_bits = [1 << place for place in range(1, dp.bit_length() - 1)]
    x_order, z_order = chip_bits, chip_bits[1:] + chip_bits[:1]
    paired = fs == 2
    chunked = paired and half % (16 * chips) == 0 and hidden % (16 * chips) == 0
    chunked = chunked and hidden % 128 == 0 and dp == heads and dp % 4 == 0

    def chip_of(j):
        last = len(x_order) - 1
        return sum(((j // bit) % 2) << (last - place) for place, bit in enumerate(x_order))

    def swap_dp(values, bit):
        return lax.ppermute(values, "dp", [(j, j ^ bit) for j in range(dp)])

    def swap_fs(values):
        return lax.ppermute(values, "fsdp", [(j, 1 - j) for j in range(2)])

    def after(values, *others):
        return lax.optimization_barrier((values, *others))[0]

    def half_rows(values):
        return jnp.stack([lax.dynamic_slice_in_dim(w, core * half, half, axis=0) for w in values])

    def both_halves(sent):
        got = swap_fs(sent)
        return got, swap_dp(got, 1)

    def quarter(bit):
        return 2 * ((me // bit) % 2) + core

    def quarter_starts(bit):
        rows = [(1 - shard) * span + (quarter(bit) ^ more) * (half // 2) for more in (0, 2, 1, 3)]
        return jnp.stack([shard * span] + rows).astype(jnp.int32)

    def gather_rows(values):
        return [lax.all_gather(w, "fsdp", axis=0, tiled=True) for w in values]

    def both_tokens(values):
        if paired:
            return jnp.concatenate([values, swap_fs(values)], axis=0)
        return lax.all_gather(values, "fsdp", axis=0, tiled=True)

    def reduce_chips(kept, got, order=x_order, marks=()):
        total = kept.astype(F32) + got.astype(F32)
        for place, bit in enumerate(order[1:]):
            count = total.shape[0] // 2
            sent, total = total[count:].astype(BF16), total[:count]
            if place < len(marks):
                sent = after(sent, marks[place])
            total = total + swap_dp(sent, bit).astype(F32)
        return total.astype(BF16)

    x, g, e = inputs[:, 0], cotangent[:, 0], encoded[:, 0]

    low, offsets = [x], [0]
    for bit in reversed(chip_bits[1:]):
        low = low + [swap_dp(piece, bit) for piece in low]
        offsets = offsets + [offset | bit for offset in offsets]
    high = [swap_dp(piece, 2) for piece in low]
    near, far = jnp.stack(low), jnp.stack(high)
    offsets = [offset ^ more for more in (0, 2, 1, 3) for offset in offsets]
    source = me ^ jnp.array(offsets, jnp.int32)
    e_all = lax.all_gather(e, "dp", axis=0)

    gains = jnp.stack([gain_self, gain_cross, gain_dense])
    own_head = lambda w: lax.dynamic_slice_in_dim(w, head * 64, 64, axis=1)
    if paired:
        pad = jnp.pad(position_bias.reshape(1, -1), ((0, 0), (0, span - position_bias.size)))
        small = jnp.concatenate([gains, pad], axis=0)
        small_got = swap_fs(small)
        head_pack = jnp.concatenate([own_head(w) for w in (query_self, key_self, value_self)], 1)
        head_got = swap_fs(head_pack)
        first, second = (
            jnp.where(shard == which, mine, got)
            for which, mine, got in ((0, small, small_got), (1, small, small_got))
        )
        gains = jnp.concatenate([first[:3], second[:3]], axis=1)
        bias_all = jnp.concatenate(
            [piece[3, : position_bias.size].reshape(position_bias.shape) for piece in (first, second)]
        )
        head_whole = jnp.where(
            shard == 0,
            jnp.concatenate([head_pack, head_got]),
            jnp.concatenate([head_got, head_pack]),
        )
        other = (1 - shard) * span
        half_starts = jnp.stack([shard * span, other + core * half, other + (1 - core) * half])
        half_starts = half_starts.astype(jnp.int32)
        near_bit, dense_bit = chip_bits[0], chip_bits[1]
        starts = quarter_starts(near_bit)
        kv_own = (key_cross, value_cross)
        near_own = (output_self, query_cross, output_cross)
        near_sent, theirs = pack(
            jnp.stack([quarter(near_bit), quarter(dense_bit), 1 - shard]).astype(jnp.int32),
            near_own + kv_own,
            (dense_gate, dense_up),
            half // 2,
            hidden,
        )
        near_got = swap_fs(near_sent)
        near_far = swap_dp(near_got, near_bit)
        dense_got = swap_fs(after(theirs, near_got))
        dense_own = (dense_gate, dense_up)
        which = jnp.stack([shard, core]).astype(jnp.int32)
        dense_starts = jnp.concatenate([quarter_starts(dense_bit), which])
    else:
        gains = lax.all_gather(gains, "fsdp", axis=1, tiled=True)
        bias_all = lax.all_gather(position_bias, "fsdp", axis=0, tiled=True)
        kv_own, kv_more = gather_rows((key_cross, value_cross)), ()
        near_own, near_more = gather_rows((output_self, query_cross, output_cross)), ()
        first_own, first_more = gather_rows((query_self, key_self, value_self)), ()
        half_starts = jnp.zeros((1,), jnp.int32)
        head_whole = jnp.concatenate([own_head(w) for w in first_own], axis=1)
        dense_own = [
            lax.all_to_all(w, "fsdp", 1, 0, tiled=True) for w in (dense_gate, dense_up)
        ]
        dense_more = ()
        starts = jnp.zeros((1,), jnp.int32)
        dense_starts = jnp.zeros((3,), jnp.int32)
        g_group = both_tokens(g.reshape(tokens, width))
    gains, bias_all = gains.astype(F32), bias_all.astype(F32)
    head_w = jnp.concatenate(
        [head_whole[:, at : at + 64] for at in (0, 0, 64, 64, 128, 128)], axis=1
    )

    marks = jnp.arange(bias_all.shape[0], dtype=jnp.int32)
    edges = jnp.sum((buckets[:, None] < marks[None, :]).astype(jnp.int32), axis=0)
    bias_values = lax.dynamic_slice_in_dim(bias_all, head, 1, axis=1)[:, 0]
    table = bias_table(edges, bias_values, length)
    x_groups = [near, far, swap_dp(near, 1), swap_dp(after(far, table), 1)]
    doc_row = jnp.broadcast_to(doc_ids[:, 0, :, None], (micro_count, dp, rows))
    doc_row = doc_row.reshape(micro_count, length)
    doc_col = doc_row[:, :, None]

    n_all, qkv, mixed = pl.pallas_call(
        functools.partial(self_forward_kernel, len(x_groups)),
        out_shape=[
            jax.ShapeDtypeStruct((dp, micro_count, rows, width), BF16),
            jax.ShapeDtypeStruct((length, 384), BF16),
            jax.ShapeDtypeStruct((length, 128), BF16),
        ],
        in_specs=[smem()] + [vmem()] * (len(x_groups) + 5),
        out_specs=[vmem()] * 3,
        compiler_params=params(),
        cost_estimate=cost(12),
        name="self_forward",
    )(source, *x_groups, gains[0:1], head_w, table, doc_row, doc_col)
    if paired:
        mixed = after(mixed, dense_got)
    o1_heads = lax.all_to_all(mixed.reshape(dp, rows, 128), "dp", 0, 0, tiled=True)[::copies]

    if paired:
        near_more = (near_got, near_far, swap_dp(near_got, 1), swap_dp(after(near_far, mixed), 1))
        kv_more = near_more
        dense_far = swap_dp(after(dense_got, mixed), dense_bit)
    ke, ve = cross_kv(starts, e_all, *kv_own, kv_more)

    row32 = jax.ShapeDtypeStruct((tokens, width), F32)
    row16 = jax.ShapeDtypeStruct((tokens, width), BF16)
    left, x1, q2, x2, n3, left_sent = pl.pallas_call(
        functools.partial(mid_forward_kernel, len(near_more)),
        out_shape=[
            jax.ShapeDtypeStruct((3, tokens, width), BF16),
            row32,
            row16,
            row32,
            row16,
            jax.ShapeDtypeStruct((3, tokens, span), BF16),
        ],
        in_specs=[smem()] + [vmem()] * (8 + len(near_more)),
        out_specs=[vmem()] * 6,
        scratch_shapes=[pltpu.VMEM((tokens, width), BF16)] * 3,
        compiler_params=params(),
        cost_estimate=cost(12),
        name="mid_forward",
    )(starts, o1_heads, x, gains, ke, ve, *near_own, *near_more)

    if paired:
        dense_more = (
            dense_got,
            dense_far,
            swap_dp(after(dense_got, ke), 1),
            swap_dp(after(dense_far, ke), 1),
        )
        g_rows = g.reshape(tokens, width)
        g_got = swap_fs(after(g_rows, dense_got))
        n_got = swap_fs(n3)
        left_got = swap_fs(left_sent)
        back, y32, _, dn3, _ = dense_layer(
            dense_starts, n3, g_rows, *dense_own, dense_down, dense_more, tokens
        )
        back_mate = swap_dp(back, 1)
        back_got, _, y16, _, d16 = dense_layer(
            dense_starts,
            after(n_got, dn3, left_got),
            g_got,
            *dense_own,
            dense_down,
            dense_more,
            tokens,
        )
        back_got_mate = swap_dp(back_got, 1)
        dn3_more = swap_fs(after(d16, back_mate))
    else:
        n_group = both_tokens(n3)
        back, _, y16, _, d16 = dense_layer(
            dense_starts, n_group, g_group, *dense_own, dense_down, dense_more, tokens
        )
        dn3 = jnp.zeros((tokens, width), F32)
        dn3_more = lax.psum_scatter(d16, "fsdp", scatter_dimension=0, tiled=True)
        dense_out = lax.psum_scatter(y16, "fsdp", scatter_dimension=0, tiled=True).astype(F32)
        outputs = (x2 + dense_out).astype(BF16)

    if chunked:
        where = jnp.stack([core, shard, me // 2]).astype(jnp.int32)
        masks = [
            [
                sum(((slot >> (len(order) - 1 - at)) & 1) * (bit // 2) for at, bit in enumerate(order))
                for slot in range(chips)
            ]
            for order in (x_order, z_order)
        ]
        own_kept, own_sent, down_kept, down_sent, far_kept, far_sent = chunk_weights(
            functools.partial(dense_weight_kernel, *masks),
            where,
            (after(n3, dn3_more), n_got, g_rows, g_got, back, back_got, back_mate, back_got_mate),
            (
                span // chips * hidden // 128,
                hidden // chips * width // 256,
                span // chips * hidden // 128,
            ),
            chips // 2,
            [
                pltpu.VMEM((max(hidden, half), max(hidden, width // 2)), F32),
                pltpu.VMEM((4 * tokens, width), BF16),
            ],
            7,
            "dense_weight",
        )
        dn3_more = after(dn3_more, own_sent)
        own_got, down_got = swap_dp(own_sent, z_order[0]), swap_dp(down_sent, x_order[0])
        far_got = swap_fs(far_sent)

    straight = chunked
    if straight:
        slots = jnp.append(chip_of(me ^ (2 * jnp.arange(heads // 2))), core).astype(jnp.int32)
    else:
        slots = jnp.append(jnp.arange(heads // 2), 0).astype(jnp.int32)
    g_rows = g.reshape(tokens, width)
    right, gx2, dkv_kept, dkv_sent, dc_dense = pl.pallas_call(
        functools.partial(cross_backward_kernel, len(near_more)),
        out_shape=[
            jax.ShapeDtypeStruct((tokens, 2 * width), BF16),
            row32,
            jax.ShapeDtypeStruct((heads // 2, dp, micro_count, part, 128), BF16),
            jax.ShapeDtypeStruct((heads // 2, dp, micro_count, part, 128), BF16),
            jax.ShapeDtypeStruct((1, width), F32),
        ],
        in_specs=[smem()] * 2 + [vmem()] * (9 + len(near_more)),
        out_specs=[vmem()] * 5,
        scratch_shapes=[pltpu.VMEM((tokens, width), F32), pltpu.VMEM((tokens, width), BF16)],
        compiler_params=params(),
        cost_estimate=cost(15),
        name="cross_backward",
    )(starts, slots, g_rows, dn3, dn3_more, x2, gains, q2, ke, ve, near_own[2], *near_more)
    if chunked:
        gx2 = after(gx2, own_got, down_got, far_got)
    gx1, last, do1_heads, dc_cross = pl.pallas_call(
        functools.partial(mid_backward_kernel, len(near_more)),
        out_shape=[
            row32,
            row16,
            jax.ShapeDtypeStruct((heads, rows, 128), BF16),
            jax.ShapeDtypeStruct((1, width), F32),
        ],
        in_specs=[smem()] + [vmem()] * (6 + len(near_more)),
        out_specs=[vmem()] * 4,
        scratch_shapes=[pltpu.VMEM((tokens, width), F32)],
        compiler_params=params(),
        cost_estimate=cost(6),
        name="mid_backward",
    )(starts, right, gx2, x1, gains, *near_own[:2], *near_more)
    do1 = lax.all_to_all(
        jnp.repeat(do1_heads, copies, axis=0) if copies > 1 else do1_heads, "dp", 0, 0, tiled=True
    ).reshape(length, 128)

    if chunked:
        right_got, last_got = swap_fs(after(right, do1_heads)), swap_fs(last)
        far_kept = swap_fs(after(far_kept, right_got, last_got))
        if straight:
            dkv_got = swap_dp(after(dkv_sent, do1_heads), 1)
            dkv_total = dkv_kept.astype(F32) + dkv_got.astype(F32)
            dkv_far = swap_dp(dkv_total[chips // 2 :].astype(BF16), x_order[0])
        far_x = swap_dp(far_got, x_order[0])
        do1 = after(do1, far_x, dkv_got)

    dqkv, table_grad = pl.pallas_call(
        self_backward_kernel,
        out_shape=[
            jax.ShapeDtypeStruct((length, 384), BF16),
            jax.ShapeDtypeStruct((TILE, length), F32),
        ],
        in_specs=[vmem()] * 5,
        out_specs=[vmem()] * 2,
        scratch_shapes=[pltpu.VMEM((length, 128), F32), pltpu.VMEM((length, 128), F32)],
        compiler_params=params(),
        cost_estimate=cost(10),
        name="self_backward",
    )(qkv, do1, table, doc_row, doc_col)
    if chunked:
        dqkv = after(dqkv, right_got, last_got, dkv_far)
    if chunked:
        token_kept, token_sent = chunk_weights(
            functools.partial(token_weight_kernel, masks[1]),
            where,
            (left, left_got, right, right_got, last, last_got),
            (3 * half // chips * width // 128,),
            chips,
            [pltpu.VMEM((span, width), F32)],
            6,
            "token_weight",
        )
        token_got = swap_dp(token_sent, 1)
        dqkv = after(dqkv, token_kept)
    head_grad = pl.pallas_call(
        head_weight_kernel,
        out_shape=jax.ShapeDtypeStruct((fs, span * 3 // 2, 128), BF16),
        in_specs=[vmem()] * 2,
        out_specs=vmem(),
        compiler_params=params(),
        cost_estimate=cost(6),
        name="head_weight",
    )(n_all, dqkv)
    def sum_shards(values):
        if paired:
            kept = lax.dynamic_index_in_dim(values, shard, 0)
            sent = lax.dynamic_index_in_dim(values, 1 - shard, 0)
            return (kept.astype(F32) + swap_fs(sent).astype(F32)).astype(BF16)
        return lax.psum_scatter(values, "fsdp", scatter_dimension=0, tiled=True)

    head_sum = sum_shards(head_grad)

    if paired:
        first_own = (query_self, key_self, value_self)
        first_more = both_halves(after(half_rows(first_own), head_sum))
        y16 = swap_fs(after(y16, first_more[0]))
        outputs = (x2 + (y32 + y16.astype(F32))).astype(BF16)
    own_d = lax.all_to_all(dqkv.reshape(dp, rows, 384), "dp", 0, 0, tiled=True)[::copies]
    grad_inputs, dc_one = pl.pallas_call(
        functools.partial(input_grad_kernel, len(first_more)),
        out_shape=[row32, jax.ShapeDtypeStruct((1, width), F32)],
        in_specs=[smem()] + [vmem()] * (7 + len(first_more)),
        out_specs=[vmem()] * 2,
        scratch_shapes=[
            pltpu.VMEM((tokens, 3 * width), BF16),
            pltpu.VMEM((tokens, width), F32),
        ],
        compiler_params=params(),
        cost_estimate=cost(7),
        name="input_grad",
    )(half_starts, own_d, x, gains, gx1, *first_own, *first_more)

    if straight:
        dkv = reduce_chips(dkv_total[: chips // 2], dkv_far).reshape(-1, 128)
    else:
        dkv = jnp.stack([dkv_kept, dkv_sent], axis=1).reshape(heads * copies, -1, 128)
        dkv = lax.psum_scatter(dkv, "dp", scatter_dimension=0, tiled=True)[0]
        bit = 1
        while bit < copies:
            got = swap_dp(dkv, bit)
            dkv = jnp.where(
                (me // bit) % 2 == 0, jnp.concatenate([dkv, got]), jnp.concatenate([got, dkv])
            )
            bit *= 2
    cross_grad = pl.pallas_call(
        cross_head_weight_kernel,
        out_shape=jax.ShapeDtypeStruct((fs, span, 128), BF16),
        in_specs=[vmem()] * 2,
        out_specs=vmem(),
        compiler_params=params(),
        cost_estimate=cost(3),
        name="cross_head_weight",
    )(e_all, dkv)
    cross_sum = sum_shards(cross_grad)
    own_dkv = dkv.reshape(dp, micro_count * part, 128)
    own_dkv = lax.all_to_all(own_dkv, "dp", 0, 0, tiled=True)[::copies]
    grad_encoded = pl.pallas_call(
        functools.partial(encoder_grad_kernel, len(kv_more)),
        out_shape=jax.ShapeDtypeStruct((micro_count * part, width), F32),
        in_specs=[smem()] + [vmem()] * (3 + len(kv_more)),
        out_specs=vmem(),
        scratch_shapes=[pltpu.VMEM((micro_count * part, width), BF16)] * 2,
        compiler_params=params(),
        cost_estimate=cost(4),
        name="encoder_grad",
    )(starts, own_dkv, *kv_own, *kv_more)

    if chunked:
        sums = (
            reduce_chips(own_kept, own_got, z_order, (do1, dqkv)),
            reduce_chips(down_kept, down_got, x_order, (do1, dqkv)),
            reduce_chips(far_kept, far_x, x_order, (dqkv, head_grad)),
            head_sum,
            reduce_chips(token_kept, token_got, [1] + z_order),
            cross_sum,
        )
        pieces = lax.all_gather(jnp.concatenate(sums, axis=1), "dp", axis=0, tiled=True)
        square, wide = (span, width), (span, fs * hidden)
        (
            grad_dense_gate,
            grad_dense_up,
            grad_dense_down,
            grad_query_self,
            grad_key_self,
            grad_value_self,
            grad_output_cross,
            grad_query_cross,
            grad_output_self,
            grad_key_cross,
            grad_value_cross,
        ) = spread(
            where,
            pieces,
            [(wide, "core")] * 2
            + [((hidden, width), "chip")]
            + [(square, "head")] * 3
            + [(square, "core")] * 3
            + [(square, "head")] * 2,
        )
    else:

        def all_heads(values, kinds):
            pieces = lax.all_gather(values, "dp", axis=0, tiled=True)[::copies]
            return plain_head_spread(pieces, span, width, kinds)

        grad_query_self, grad_key_self, grad_value_self = all_heads(head_sum, 3)
        grad_key_cross, grad_value_cross = all_heads(cross_sum, 2)
        right = jnp.concatenate([right, last], axis=1)

        def over_dp(values):
            return lax.psum(values.astype(BF16), "dp").astype(F32)

        def over_all(a, b):
            made = t_dot(a, b).astype(BF16)
            return over_dp(lax.psum_scatter(made, "fsdp", scatter_dimension=0, tiled=True))

        grad_output_cross, grad_query_cross, grad_output_self = (
            over_all(left[kind], right[:, kind * width : (kind + 1) * width]) for kind in range(3)
        )
        grad_dense_gate, grad_dense_up = (
            over_dp(
                lax.all_to_all(
                    t_dot(n_group, back[:, kind * hidden : (kind + 1) * hidden]).astype(BF16),
                    "fsdp",
                    0,
                    1,
                    tiled=True,
                )
            )
            for kind in range(2)
        )
        grad_dense_down = over_dp(t_dot(back[:, 2 * hidden :], g_group))

    if chunked:
        table_grad = after(table_grad, first_more[1])
    table_sums = jnp.sum(bucket_sums(edges, table_grad, bias_all.shape[0]), axis=1)
    column = (jnp.arange(heads) == head) & (me % copies == 0)
    bias_row = jnp.where(column[None, :], table_sums[:, None], 0.0).reshape(1, -1)
    bias_row = jnp.pad(bias_row, ((0, 0), (0, width - bias_row.shape[1])))
    sums = jnp.concatenate([dc_one, dc_dense, dc_cross, bias_row], axis=0)
    if paired:
        sums = sums + swap_fs(sums)
        for bit in [1] + chip_bits:
            sums = sums + swap_dp(sums, bit)
    else:
        sums = lax.psum(sums, ("dp", "fsdp"))
    own = lax.dynamic_slice_in_dim(sums[:3], shard * span, span, axis=1)
    grad_bias = sums[3, : bias_all.size].reshape(bias_all.shape)
    grad_bias = lax.dynamic_slice_in_dim(
        grad_bias, shard * position_bias.shape[0], position_bias.shape[0], axis=0
    )
    shape = (micro_count, 1, rows, width)
    return (
        outputs.reshape(shape),
        grad_inputs.reshape(shape),
        grad_encoded.reshape(micro_count, 1, part, width),
        own[0],
        grad_query_self,
        grad_key_self,
        grad_value_self,
        grad_output_self,
        grad_bias,
        own[2],
        grad_query_cross,
        grad_key_cross,
        grad_value_cross,
        grad_output_cross,
        own[1],
        grad_dense_gate,
        grad_dense_up,
        grad_dense_down,
    )


def solution(mesh):
    matrix = P("fsdp", None)
    token = P(None, "fsdp", "dp", None)
    weights = (
        (P("fsdp"),)
        + (matrix,) * 5
        + (P("fsdp"),)
        + (matrix,) * 4
        + (P("fsdp"),)
        + (matrix,) * 3
    )
    return jax.shard_map(
        per_device,
        mesh=mesh,
        in_specs=(token,) * 3 + (P(None, "fsdp", None), P()) + weights,
        out_specs=(token,) * 3 + weights,
        check_vma=False,
    )
```

```python
import functools

import jax
import jax.numpy as jnp
from jax import lax
from jax.experimental import pallas as pl
from jax.experimental.pallas import tpu as pltpu
from jax.sharding import PartitionSpec as P

EPS = 1e-06
NEGATIVE = -1e30
TILE = 256
F32 = jnp.float32
BF16 = jnp.bfloat16
VMEM_LIMIT = 26 * 1024 * 1024
VMEM_MOST = 56 * 1024 * 1024


def vmem():
    return pl.BlockSpec(memory_space=pltpu.VMEM)


def smem():
    return pl.BlockSpec(memory_space=pltpu.SMEM)


def params(limit=VMEM_LIMIT):
    return pltpu.CompilerParams(vmem_limit_bytes=limit)


def cost(microseconds):
    return pl.CostEstimate(
        flops=int(microseconds * 1.15e9),
        bytes_accessed=int(microseconds * 3.69e6),
        transcendentals=0,
    )


def aligned(start, size):
    return pl.ds(pl.multiple_of(start, size), size)


def dot(left, right):
    return jnp.dot(left, right, preferred_element_type=F32)


def dot_t(left, right):
    return lax.dot_general(left, right, (((1,), (1,)), ((), ())), preferred_element_type=F32)


def t_dot(left, right):
    return lax.dot_general(left, right, (((0,), (0,)), ((), ())), preferred_element_type=F32)


def norm_rows(values, gain):
    return values * lax.rsqrt(jnp.mean(values * values, axis=-1, keepdims=True) + EPS) * gain


def norm_back(values, gain, grad):
    r = lax.rsqrt(jnp.mean(values * values, axis=-1, keepdims=True) + EPS)
    scaled = grad * gain
    inner = jnp.mean(scaled * values, axis=-1, keepdims=True)
    back = r * scaled - values * (r * r * r * inner)
    return back, jnp.sum(grad * (values * r), axis=0, keepdims=True)


def low_lanes(rows):
    return lax.broadcasted_iota(jnp.int32, (rows, 128), 1) < 64


def pair_up(first, second):
    lane = low_lanes(first.shape[0])
    low = jnp.where(lane, first, pltpu.roll(second, 64, 1))
    high = jnp.where(lane, pltpu.roll(first, 64, 1), second)
    return low, high


def keep_half(values, half):
    lane = low_lanes(values.shape[0])
    return jnp.where(lane if half == 0 else ~lane, values, jnp.zeros_like(values))


def softmax_rows(scores):
    top = jnp.max(scores, axis=-1, keepdims=True)
    raised = jnp.exp(scores - top)
    return raised * (1.0 / jnp.sum(raised, axis=-1, keepdims=True))


def table_kernel(edge_ref, value_ref, out_ref):
    rows, length = out_ref.shape
    bucket_count = value_ref.shape[0]
    for start in range(0, length, TILE):
        place = (rows, TILE)
        apart = (
            lax.broadcasted_iota(jnp.int32, place, 0)
            - lax.broadcasted_iota(jnp.int32, place, 1)
            + (length - rows - start)
        )
        value = jnp.full(place, value_ref[0], F32)
        for bucket in range(1, bucket_count):
            value = jnp.where(apart >= edge_ref[bucket], value_ref[bucket], value)
        out_ref[:, start : start + TILE] = jnp.where(apart >= 0, value, NEGATIVE)


def bias_table(edges, values, length):
    return pl.pallas_call(
        table_kernel,
        out_shape=jax.ShapeDtypeStruct((TILE, length), F32),
        in_specs=[smem(), smem()],
        out_specs=vmem(),
        cost_estimate=cost(4),
        name="bias_table",
    )(edges, values)


def bucket_kernel(edge_ref, grad_ref, out_ref):
    rows, length = grad_ref.shape
    bucket_count = out_ref.shape[0]
    above = [jnp.zeros((8, TILE), F32) for _ in range(bucket_count)]
    for start in range(0, length, TILE):
        for row in range(0, rows, 8):
            place = (8, TILE)
            apart = (
                lax.broadcasted_iota(jnp.int32, place, 0)
                - lax.broadcasted_iota(jnp.int32, place, 1)
                + (length - rows - start + row)
            )
            tile = grad_ref[row : row + 8, start : start + TILE]
            for bucket in range(bucket_count):
                above[bucket] = above[bucket] + jnp.where(apart >= edge_ref[bucket], tile, 0.0)
    for bucket in range(bucket_count):
        rest = above[bucket + 1] if bucket + 1 < bucket_count else 0.0
        part = jnp.sum(above[bucket] - rest, axis=0, keepdims=True)
        out_ref[bucket : bucket + 1, :] = part[:, :128] + part[:, 128:]


def bucket_sums(edges, grad, bucket_count):
    return pl.pallas_call(
        bucket_kernel,
        out_shape=jax.ShapeDtypeStruct((bucket_count, 128), F32),
        in_specs=[smem(), vmem()],
        out_specs=vmem(),
        cost_estimate=cost(7),
        name="bucket_sums",
    )(edges, grad)


def times(x_ref, starts_ref, pieces):
    if len(pieces) == 1:
        return dot(x_ref[...], pieces[0])
    total = None
    for place, piece in enumerate(pieces):
        rows = piece.shape[0]
        part = dot(x_ref[:, aligned(starts_ref[place], rows)], piece)
        total = part if total is None else total + part
    return total


def times_back(out_ref, starts_ref, terms):
    for place in range(len(terms[0][1])):
        total = sum(dot_t(d, pieces[place]) for d, pieces in terms)
        rows = terms[0][1][place].shape[0]
        if len(terms[0][1]) == 1:
            out_ref[...] = total
        else:
            out_ref[:, aligned(starts_ref[place], rows)] = total


def pack_kernel(counts, where_ref, *refs):
    total = sum(counts)
    first_ref, second_ref = refs[total:]
    for place in range(counts[0]):
        first_ref[place] = refs[place][...]
    for place in range(counts[1]):
        second_ref[place] = refs[counts[0] + place][...]


def pack(where, first, second, rows, cols):
    width = first[0].shape[1]
    counts = (len(first), len(second))
    return pl.pallas_call(
        functools.partial(pack_kernel, counts),
        grid_spec=pltpu.PrefetchScalarGridSpec(
            num_scalar_prefetch=1,
            grid=(1,),
            in_specs=[pl.BlockSpec((rows, width), lambda i, where: (where[0], 0))] * counts[0]
            + [pl.BlockSpec((rows, cols), lambda i, where: (where[1], where[2]))] * counts[1],
            out_specs=[
                pl.BlockSpec((counts[0], rows, width), lambda i, where: (0, 0, 0)),
                pl.BlockSpec((counts[1], rows, cols), lambda i, where: (0, 0, 0)),
            ],
        ),
        out_shape=[
            jax.ShapeDtypeStruct((counts[0], rows, width), BF16),
            jax.ShapeDtypeStruct((counts[1], rows, cols), BF16),
        ],
        compiler_params=params(VMEM_MOST),
        cost_estimate=cost(3),
        name="pack",
    )(where, *first, *second)


def part_specs(arrays, count, index):
    return [
        pl.BlockSpec((count,) + array.shape[1:], lambda *_: (index, 0, 0)) for array in arrays
    ]


def pieces_of(own_ref, more, index):
    return [own_ref[...]] + [ref[index] for ref in more]


def self_scores(q, k, table, doc_col, doc_row):
    scores = dot_t(q, k) + table
    return jnp.where(doc_col == doc_row, scores, NEGATIVE)


def self_forward_kernel(groups, source_ref, *refs):
    x_refs = refs[:groups]
    gain_ref, w_ref, table_ref, doc_row_ref, doc_col_ref, n_ref, qkv_ref, o_ref = refs[groups:]
    count, _, rows, width = x_refs[0].shape
    length = groups * count * rows
    lane = lax.broadcasted_iota(jnp.int32, (rows, 384), 1) % 128 < 64
    together = min(TILE // rows, count)
    for place, x_ref in enumerate(x_refs):
        for first in range(0, count, together):
            parts = []
            for inner in range(first, first + together):
                x = x_ref[inner].astype(F32).reshape(2 * rows, width)
                n = norm_rows(x, gain_ref[...]).astype(BF16)
                n_ref[source_ref[place * count + inner]] = n.reshape(2, rows, width)
                parts.append(n)
            made = dot(jnp.concatenate(parts, axis=0), w_ref[...])
            for inner in range(together):
                at = 2 * rows * inner
                picked = jnp.where(lane, made[at : at + rows], made[at + rows : at + 2 * rows])
                own = source_ref[place * count + first + inner]
                qkv_ref[aligned(own * rows, rows), :] = picked.astype(BF16)
    for block in range(length // TILE):
        start, stop = block * TILE, (block + 1) * TILE
        table = table_ref[:, length - stop :]
        q = qkv_ref[start:stop, 0:128]
        k = qkv_ref[:stop, 128:256]
        v = qkv_ref[:stop, 256:384]
        mixed = []
        for half in range(2):
            scores = self_scores(
                keep_half(q, half),
                k,
                table,
                doc_col_ref[half, start:stop, :],
                doc_row_ref[half : half + 1, :stop],
            )
            mixed.append(dot(softmax_rows(scores).astype(BF16), v))
        o_ref[start:stop, :] = jnp.where(low_lanes(TILE), mixed[0], mixed[1]).astype(BF16)


def self_backward_kernel(
    qkv_ref, do_ref, table_ref, doc_row_ref, doc_col_ref, dqkv_ref, grad_ref, dk_ref, dv_ref
):
    length = qkv_ref.shape[0]
    grad_ref[...] = jnp.zeros_like(grad_ref)
    dk_ref[...] = jnp.zeros_like(dk_ref)
    dv_ref[...] = jnp.zeros_like(dv_ref)
    for block in range(length // TILE):
        start, count = block * TILE, (block + 1) * TILE
        table = table_ref[:, length - count :]
        k = qkv_ref[:count, 128:256]
        v = qkv_ref[:count, 256:384]
        made = []
        for half in range(2):
            q = keep_half(qkv_ref[start:count, 0:128], half)
            do = keep_half(do_ref[start:count, :], half)
            p = softmax_rows(
                self_scores(
                    q,
                    k,
                    table,
                    doc_col_ref[half, start:count, :],
                    doc_row_ref[half : half + 1, :count],
                )
            )
            dp = dot_t(do, v)
            ds = (p * (dp - jnp.sum(p * dp, axis=-1, keepdims=True))).astype(BF16)
            grad_ref[:, length - count :] += ds.astype(F32)
            made.append(dot(ds, k))
            dk_ref[:count, :] += t_dot(ds, q)
            dv_ref[:count, :] += t_dot(p.astype(BF16), do)
        dq = jnp.where(low_lanes(TILE), made[0], made[1])
        dqkv_ref[start:count, 0:128] = dq.astype(BF16)
    dqkv_ref[:, 128:256] = dk_ref[...].astype(BF16)
    dqkv_ref[:, 256:384] = dv_ref[...].astype(BF16)


def head_weight_kernel(n_ref, d_ref, out_ref):
    blocks, _, rows, width = n_ref.shape
    shards = out_ref.shape[0]
    span = width // shards
    lane = lax.broadcasted_iota(jnp.int32, (blocks * rows, 384), 1) % 128 < 64
    d = d_ref[...]
    zero = jnp.zeros_like(d)
    right = [jnp.where(lane, d, zero), jnp.where(lane, zero, d)]
    half = span // 2
    for shard in range(shards):
        total = jnp.zeros((span, 384), F32)
        for micro in range(2):
            left = n_ref[:, micro, :, shard * span : (shard + 1) * span]
            total = total + t_dot(left.reshape(blocks * rows, span), right[micro])
        q, k, v = (
            total[:, at : at + 128] + pltpu.roll(total[:, at : at + 128], 64, 1)
            for at in (0, 128, 256)
        )
        out_ref[shard, :span, :] = jnp.where(low_lanes(span), q, k).astype(BF16)
        out_ref[shard, span:, :] = jnp.where(low_lanes(half), v[:half], v[half:]).astype(BF16)


def cross_kv_kernel(split, starts_ref, e_ref, wk_ref, wv_ref, *refs):
    more, (ke_ref, ve_ref) = refs[:split], refs[split:]
    blocks, _, part, _ = e_ref.shape
    for index, (own_ref, out_ref) in enumerate(((wk_ref, ke_ref), (wv_ref, ve_ref))):
        total = None
        pieces = pieces_of(own_ref, more, index)
        for place, piece in enumerate(pieces):
            rows = piece.shape[0]
            if split:
                left = e_ref[:, 0, :, aligned(starts_ref[place], rows)]
            else:
                left = e_ref[:, 0]
            made = dot(left.reshape(blocks * part, rows), piece)
            total = made if total is None else total + made
        out_ref[0] = total.astype(BF16)


def cross_kv(starts, e_all, wk, wv, more):
    blocks, micro, part, width = e_all.shape
    whole = lambda array: pl.BlockSpec(array.shape, lambda m, s: (0,) * array.ndim)
    out = pl.BlockSpec((1, blocks * part, width), lambda m, s: (m, 0, 0))
    return pl.pallas_call(
        functools.partial(cross_kv_kernel, len(more)),
        grid_spec=pltpu.PrefetchScalarGridSpec(
            num_scalar_prefetch=1,
            grid=(micro,),
            in_specs=[pl.BlockSpec((blocks, 1, part, width), lambda m, s: (0, m, 0, 0))]
            + [whole(wk), whole(wv)]
            + [pl.BlockSpec((2,) + array.shape[1:], lambda m, s: (0, 0, 0)) for array in more],
            out_specs=[out, out],
        ),
        out_shape=[jax.ShapeDtypeStruct((micro, blocks * part, width), BF16)] * 2,
        compiler_params=params(),
        cost_estimate=cost(8),
        name="cross_kv",
    )(starts, e_all, wk, wv, *more)


def mid_forward_kernel(split, starts_ref, o1_ref, x_ref, gain_ref, ke_ref, ve_ref, wo, wq, wc, *refs):
    more, last = refs[:split], refs[split : 2 * split]
    left_ref, x1_ref, q2_ref, x2_ref, n3_ref, sent_ref, o1c_ref, n2_ref, o2_ref = refs[2 * split :]
    heads, rows, _ = o1_ref.shape
    width = x_ref.shape[-1]
    for pair in range(heads // 2):
        at = pair * 128
        low, high = pair_up(o1_ref[2 * pair].astype(F32), o1_ref[2 * pair + 1].astype(F32))
        o1c_ref[0:rows, at : at + 128] = low.astype(BF16)
        o1c_ref[rows : 2 * rows, at : at + 128] = high.astype(BF16)
    x = x_ref[...].astype(F32).reshape(2 * rows, width)
    x1 = x + times(o1c_ref, starts_ref, pieces_of(wo, more, 0))
    x1_ref[...] = x1
    n2_ref[...] = norm_rows(x1, gain_ref[1:2]).astype(BF16)
    q2_ref[...] = times(n2_ref, starts_ref, pieces_of(wq, more, 1)).astype(BF16)
    for micro in range(2):
        for pair in range(heads // 2):
            at = pair * 128
            span = slice(micro * rows, (micro + 1) * rows)
            q = q2_ref[span, at : at + 128]
            both = jnp.concatenate([keep_half(q, 0), keep_half(q, 1)], axis=0)
            p = softmax_rows(dot_t(both, ke_ref[micro, :, at : at + 128]))
            o = dot(p.astype(BF16), ve_ref[micro, :, at : at + 128])
            o2_ref[span, at : at + 128] = jnp.where(
                low_lanes(rows), o[:rows], o[rows:]
            ).astype(BF16)
    x2 = x1 + times(o2_ref, starts_ref, pieces_of(wc, last, 0))
    x2_ref[...] = x2
    n3_ref[...] = norm_rows(x2, gain_ref[2:3]).astype(BF16)
    left_ref[0] = o2_ref[...]
    left_ref[1] = n2_ref[...]
    left_ref[2] = o1c_ref[...]
    if split:
        span = sent_ref.shape[2]
        for kind in range(3):
            sent_ref[kind] = left_ref[kind, :, aligned(span - starts_ref[0], span)]


def cross_backward_kernel(
    split, starts_ref, slots_ref, g_ref, dn3_ref, more_ref, x2_ref, gain_ref, q2_ref, ke_ref, ve_ref,
    wc, *refs
):
    more = refs[:split]
    right_ref, gx2_ref, keep_ref, send_ref, dc_ref, back_ref, do2_ref = refs[split:]
    blocks, micros, part = keep_ref.shape[1:4]
    tokens, width = x2_ref.shape
    rows = tokens // micros
    pairs = width // 128
    even = slots_ref[pairs] == 0
    dn3 = dn3_ref[...] + more_ref[...].astype(F32)
    back, dc_ref[...] = norm_back(x2_ref[...], gain_ref[2:3], dn3)
    gx2 = g_ref[...].astype(F32) + back
    gx2_ref[...] = gx2
    gx2b = gx2.astype(BF16)
    right_ref[:, 0:width] = gx2b
    times_back(back_ref, starts_ref, [(gx2b, pieces_of(wc, more, 0))])
    do2_ref[...] = back_ref[...].astype(BF16)
    for micro in range(micros):
        for pair in range(pairs):
            at = pair * 128
            span = slice(micro * rows, (micro + 1) * rows)
            q = q2_ref[span, at : at + 128]
            do = do2_ref[span, at : at + 128]
            q = jnp.concatenate([keep_half(q, 0), keep_half(q, 1)], axis=0)
            do = jnp.concatenate([keep_half(do, 0), keep_half(do, 1)], axis=0)
            k = ke_ref[micro, :, at : at + 128]
            v = ve_ref[micro, :, at : at + 128]
            p = softmax_rows(dot_t(q, k))
            dp = dot_t(do, v)
            ds = (p * (dp - jnp.sum(p * dp, axis=-1, keepdims=True))).astype(BF16)
            dq = dot(ds, k)
            right_ref[span, width + at : width + at + 128] = jnp.where(
                low_lanes(rows), dq[:rows], dq[rows:]
            ).astype(BF16)
            low, high = pair_up(t_dot(ds, q), t_dot(p.astype(BF16), do))
            kept, sent = jnp.where(even, low, high), jnp.where(even, high, low)
            slot = slots_ref[pair]
            keep_ref[slot, :, micro] = kept.astype(BF16).reshape(blocks, part, 128)
            send_ref[slot, :, micro] = sent.astype(BF16).reshape(blocks, part, 128)


def mid_backward_kernel(split, starts_ref, right_ref, gx2_ref, x1_ref, gain_ref, wo, wq, *refs):
    more = refs[:split]
    gx1_ref, low_ref, do1_ref, dc_ref, back_ref = refs[split:]
    heads, rows, _ = do1_ref.shape
    width = x1_ref.shape[-1]
    times_back(back_ref, starts_ref, [(right_ref[:, width:], pieces_of(wq, more, 1))])
    back, dc_ref[...] = norm_back(x1_ref[...], gain_ref[1:2], back_ref[...])
    gx1 = gx2_ref[...] + back
    gx1_ref[...] = gx1
    gx1b = gx1.astype(BF16)
    low_ref[...] = gx1b
    times_back(back_ref, starts_ref, [(gx1b, pieces_of(wo, more, 0))])
    for pair in range(heads // 2):
        at = pair * 128
        do1 = back_ref[:, at : at + 128].astype(BF16).astype(F32)
        low, high = pair_up(do1[:rows], do1[rows:])
        do1_ref[2 * pair] = low.astype(BF16)
        do1_ref[2 * pair + 1] = high.astype(BF16)


def input_grad_kernel(split, starts_ref, d_ref, x_ref, gain_ref, gx1_ref, wq, wk, wv, *refs):
    more = refs[:split]
    out_ref, dc_ref, all_ref, back_ref = refs[split:]
    heads, rows, _ = d_ref.shape
    width = x_ref.shape[-1]
    for kind in range(3):
        for pair in range(heads // 2):
            lanes = slice(kind * 128, (kind + 1) * 128)
            low, high = pair_up(
                d_ref[2 * pair, :, lanes].astype(F32), d_ref[2 * pair + 1, :, lanes].astype(F32)
            )
            at = kind * width + pair * 128
            all_ref[0:rows, at : at + 128] = low.astype(BF16)
            all_ref[rows : 2 * rows, at : at + 128] = high.astype(BF16)
    terms = [
        (all_ref[:, kind * width : (kind + 1) * width], pieces_of(own, more, kind))
        for kind, own in enumerate((wq, wk, wv))
    ]
    times_back(back_ref, starts_ref, terms)
    x = x_ref[...].astype(F32).reshape(2 * rows, width)
    back, dc = norm_back(x, gain_ref[0:1], back_ref[...])
    dc_ref[...] = dc
    out_ref[...] = gx1_ref[...] + back


def encoder_grad_kernel(split, starts_ref, d_ref, wk, wv, *refs):
    more = refs[:split]
    out_ref, k_ref, v_ref = refs[split:]
    for pair in range(d_ref.shape[0] // 2):
        at = pair * 128
        low, high = pair_up(d_ref[2 * pair].astype(F32), d_ref[2 * pair + 1].astype(F32))
        k_ref[:, at : at + 128] = low.astype(BF16)
        v_ref[:, at : at + 128] = high.astype(BF16)
    terms = [(k_ref[...], pieces_of(wk, more, 0)), (v_ref[...], pieces_of(wv, more, 1))]
    times_back(out_ref, starts_ref, terms)


def cross_head_weight_kernel(e_ref, d_ref, out_ref):
    blocks, micro, part, width = e_ref.shape
    shards, span, _ = out_ref.shape
    for shard in range(shards):
        left = e_ref[:, :, :, shard * span : (shard + 1) * span]
        left = left.reshape(blocks * micro * part, span)
        out_ref[shard] = t_dot(left, d_ref[...]).astype(BF16)


def dense_kernel(split, starts_ref, n_ref, g_ref, wg, wu, wd_ref, *refs):
    more = refs[:split]
    back_ref, y_ref, ylow_ref, d_ref, dlow_ref = refs[split:]
    hidden = wd_ref.shape[0]
    gate, up = pieces_of(wg, more, 0), pieces_of(wu, more, 1)
    a = times(n_ref, starts_ref, gate)
    b = times(n_ref, starts_ref, up)
    scale = 0.7978845608028654
    cubed = 0.044715
    inner = jnp.tanh(scale * (a + cubed * (a * a * a)))
    gelu = 0.5 * a * (1.0 + inner)
    slope = 0.5 * (1.0 + inner) + 0.5 * a * (1.0 - inner * inner) * (
        scale * (1.0 + 3.0 * cubed * (a * a))
    )
    hid = (gelu * b).astype(BF16)
    dh = dot_t(g_ref[...], wd_ref[...])
    da = (dh * b * slope).astype(BF16)
    db = (dh * gelu).astype(BF16)
    times_back(d_ref, starts_ref, [(da, gate), (db, up)])
    dlow_ref[...] = d_ref[...].astype(BF16)
    y = dot(hid, wd_ref[...])
    y_ref[...] = y
    ylow_ref[...] = y.astype(BF16)
    back_ref[:, 0:hidden] = da
    back_ref[:, hidden : 2 * hidden] = db
    back_ref[:, 2 * hidden : 3 * hidden] = hid
    if more:
        shard, other = starts_ref[len(more) + 1], 1 - starts_ref[len(more) + 2]
        put_features(back_ref, 3 * hidden, n_ref, g_ref, shard, other)


def put_features(out_ref, at, n_ref, g_ref, shard, core):
    quarter = n_ref.shape[1] // 4
    for side, place in enumerate((2 * shard + core, 2 * (1 - shard) + core)):
        lanes = slice(at + side * quarter, at + (side + 1) * quarter)
        out_ref[:, lanes] = n_ref[:, aligned(place * quarter, quarter)]
    lanes = slice(at + 2 * quarter, at + 4 * quarter)
    out_ref[:, lanes] = g_ref[:, aligned(core * 2 * quarter, 2 * quarter)]


def dense_layer(starts, n, g, wg, wu, wd, more, step):
    count, width = n.shape
    hidden = wd.shape[0]
    which = starts.shape[0] - 2
    back = 3 * hidden + (width if more else 0)
    row = lambda size: pl.BlockSpec((step, size), lambda i, s: (i, 0))
    whole = lambda array: pl.BlockSpec(array.shape, lambda i, s: (0,) * array.ndim)
    column = pl.BlockSpec((wg.shape[0], hidden), lambda i, s: (0, s[which]))
    made = lambda size, kind: jax.ShapeDtypeStruct((count, size), kind)
    return pl.pallas_call(
        functools.partial(dense_kernel, len(more)),
        grid_spec=pltpu.PrefetchScalarGridSpec(
            num_scalar_prefetch=1,
            grid=(count // step,),
            in_specs=[row(width), row(width), column, column, whole(wd)]
            + [whole(array) for array in more],
            out_specs=[row(back)] + [row(width)] * 4,
        ),
        out_shape=[made(back, BF16)]
        + [made(width, F32), made(width, BF16), made(width, F32), made(width, BF16)],
        compiler_params=params(),
        cost_estimate=cost(13),
        name="dense_layer",
    )(starts, n, g, wg, wu, wd, *more)


def put_chunk(ref, slot, at, value):
    rows, width = value.shape
    for block in range(width // 128):
        ref[slot, at + block * rows : at + (block + 1) * rows, :] = value[
            :, block * 128 : (block + 1) * 128
        ].astype(BF16)


def take_chunk(ref, slot, at, rows, width):
    return jnp.concatenate(
        [
            ref[slot, at + block * rows : at + (block + 1) * rows, :].astype(F32)
            for block in range(width // 128)
        ],
        axis=1,
    )


def put_all(scratch_ref, first, count, chip, chunk_refs, at, width, masks):
    slots = [(ref, slot) for ref in chunk_refs for slot in range(ref.shape[0])]
    rows = count // len(slots)
    for (ref, slot), mask in zip(slots, masks):
        chunk = scratch_ref[aligned(first + (chip ^ mask) * rows, rows), :width]
        put_chunk(ref, slot, at, chunk)


def dense_weight_kernel(
    x_masks, z_masks, where_ref, n0_ref, n1_ref, g0_ref, g1_ref, own0_ref, own1_ref, mate0_ref, mate1_ref, keep_ref,
    send_ref, down_keep_ref, down_send_ref, far_keep_ref, far_send_ref, scratch_ref, left_ref
):
    tokens, width = n0_ref.shape
    hidden = (own0_ref.shape[1] - width) // 3
    quarter = width // 4
    at = keep_ref.shape[1] // 2
    core, shard, chip = where_ref[0], where_ref[1], where_ref[2]
    put_features(left_ref.at[:tokens], 0, n0_ref, g0_ref, shard, core)
    put_features(left_ref.at[tokens : 2 * tokens], 0, n1_ref, g1_ref, shard, core)
    left_ref[2 * tokens : 3 * tokens, :] = mate0_ref[:, 3 * hidden :]
    left_ref[3 * tokens :, :] = mate1_ref[:, 3 * hidden :]

    def whole(kind):
        span = slice(kind * hidden, (kind + 1) * hidden)
        refs = (own0_ref, own1_ref, mate0_ref, mate1_ref)
        return jnp.concatenate([ref[:, span] for ref in refs], axis=0)

    for kind in range(2):
        right = whole(kind)
        for side, (masks, refs) in enumerate(
            ((z_masks, (keep_ref, send_ref)), (x_masks, (far_keep_ref, far_send_ref)))
        ):
            value = t_dot(left_ref[:, side * quarter : (side + 1) * quarter], right)
            scratch_ref[:quarter, :hidden] = value
            put_all(scratch_ref, 0, quarter, chip, refs, kind * at, hidden, masks)
    value = t_dot(whole(2), left_ref[:, 2 * quarter :])
    scratch_ref[:, : 2 * quarter] = value
    refs = (down_keep_ref, down_send_ref)
    put_all(scratch_ref, 0, hidden, chip, refs, 0, 2 * quarter, x_masks)


def token_weight_kernel(
    masks, where_ref, left_ref, left_more_ref, right_ref, right_more_ref, last_ref, last_more_ref,
    mine_ref, mate_ref, scratch_ref
):
    kinds, _, span = left_more_ref.shape
    width = last_ref.shape[1]
    core, shard, chip = where_ref[0], where_ref[1], where_ref[2]
    half = span // 2
    at = half // len(masks) * width // 128
    for kind in range(kinds):
        lanes = slice(kind * width, (kind + 1) * width)
        left = [left_ref[kind, :, aligned(shard * span, span)], left_more_ref[kind]]
        if kind < kinds - 1:
            right = [right_ref[:, lanes], right_more_ref[:, lanes]]
        else:
            right = [last_ref[...], last_more_ref[...]]
        scratch_ref[...] = t_dot(jnp.concatenate(left, axis=0), jnp.concatenate(right, axis=0))
        for ref, own in ((mine_ref, core), (mate_ref, 1 - core)):
            put_all(scratch_ref, own * half, half, chip, (ref,), kind * at, width, masks)


def chunk_weights(kernel, where, operands, counts, slots, scratches, length, name):
    shapes = []
    for count in counts:
        shapes += [jax.ShapeDtypeStruct((slots, count, 128), BF16)] * 2
    return pl.pallas_call(
        kernel,
        out_shape=shapes,
        in_specs=[smem()] + [vmem()] * len(operands),
        out_specs=[vmem()] * len(shapes),
        scratch_shapes=scratches,
        compiler_params=params(),
        cost_estimate=cost(length),
        name=name,
    )(where, *operands)


def head_rows(in_ref, at, rows, outs):
    for pair in range(in_ref.shape[0] // 2):
        lanes = slice(pair * 128, (pair + 1) * 128)
        first = in_ref[2 * pair, at : at + rows, :].astype(F32)
        second = in_ref[2 * pair + 1, at : at + rows, :].astype(F32)
        for (out_ref, place), value in zip(outs, pair_up(first, second)):
            out_ref[place, lanes] = value


def head_spread(in_ref, at, q_ref, k_ref, v_ref):
    span = q_ref.shape[0]
    half = span // 2
    head_rows(in_ref, at, span, ((q_ref, slice(None)), (k_ref, slice(None))))
    head_rows(in_ref, at + span, half, ((v_ref, slice(0, half)), (v_ref, slice(half, span))))


def spread_kernel(where_ref, in_ref, gate_ref, up_ref, down_ref, q_ref, k_ref, v_ref, *out_refs):
    shard = where_ref[1]
    hidden = gate_ref.shape[3] // 2
    rows = gate_ref.shape[2] // 2
    at = rows * hidden // 128
    tall = down_ref.shape[0] // 2
    half = down_ref.shape[1] // 2
    span = q_ref.shape[0]
    kinds = len(out_refs) - 2
    width = out_refs[0].shape[3]
    base = 6 * at + 3 * span // 2
    step = rows * width // 128
    for piece in range(4):
        chip, core = piece // 2, piece % 2
        place = slice(chip * rows, (chip + 1) * rows)
        for side, start in enumerate((0, 4 * at)):
            lanes = aligned((shard ^ side) * hidden, hidden)
            for kind, out_ref in enumerate((gate_ref, up_ref)):
                chunk = take_chunk(in_ref, piece, start + kind * at, rows, hidden)
                out_ref[core, 0, place, lanes] = chunk
        chunk = take_chunk(in_ref, piece, 2 * at, tall, half)
        down_ref[chip * tall : (chip + 1) * tall, core * half : (core + 1) * half] = chunk
        for kind in range(kinds):
            chunk = take_chunk(in_ref, piece, base + kind * step, rows, width)
            out_refs[kind][core, 0, place, :] = chunk
    head_spread(in_ref, 6 * at, q_ref, k_ref, v_ref)
    k_ref, v_ref = out_refs[kinds:]
    head_rows(in_ref, base + kinds * step, span, ((k_ref, slice(None)), (v_ref, slice(None))))


def spread(where, pieces, outs):
    count, total, _ = pieces.shape
    steps = count // 4
    specs, shapes = [], []
    for (rows, cols), kind in outs:
        if kind == "core":
            shapes.append((2, steps, rows // (2 * steps), cols))
            block = (2, 1, rows // (2 * steps), cols)
            specs.append(pl.BlockSpec(block, lambda q, where: (0, q, 0, 0)))
        elif kind == "chip":
            shapes.append((rows, cols))
            specs.append(pl.BlockSpec((rows // steps, cols), lambda q, where: (q, 0)))
        else:
            shapes.append((rows, cols))
            specs.append(pl.BlockSpec((rows, cols // steps), lambda q, where: (0, q)))
    made = pl.pallas_call(
        spread_kernel,
        grid_spec=pltpu.PrefetchScalarGridSpec(
            num_scalar_prefetch=1,
            grid=(steps,),
            in_specs=[pl.BlockSpec((4, total, 128), lambda q, where: (q, 0, 0))],
            out_specs=specs,
        ),
        out_shape=[jax.ShapeDtypeStruct(shape, F32) for shape in shapes],
        compiler_params=params(),
        cost_estimate=cost(20),
        name="spread",
    )(where, pieces)
    return [array.reshape(shape) for array, (shape, _) in zip(made, outs)]


def plain_head_kernel(in_ref, *out_refs):
    span = out_refs[0].shape[0]
    if len(out_refs) == 3:
        head_spread(in_ref, 0, *out_refs)
    else:
        head_rows(in_ref, 0, span, [(out_ref, slice(None)) for out_ref in out_refs])


def plain_head_spread(pieces, span, width, kinds):
    return pl.pallas_call(
        plain_head_kernel,
        out_shape=[jax.ShapeDtypeStruct((span, width), F32)] * kinds,
        in_specs=[vmem()],
        out_specs=[vmem()] * kinds,
        compiler_params=params(),
        name="plain_head_spread",
    )(pieces)


def per_device(
    inputs,
    encoded,
    cotangent,
    doc_ids,
    buckets,
    gain_self,
    query_self,
    key_self,
    value_self,
    output_self,
    position_bias,
    gain_cross,
    query_cross,
    key_cross,
    value_cross,
    output_cross,
    gain_dense,
    dense_gate,
    dense_up,
    dense_down,
):
    micro_count, _, rows, width = inputs.shape
    part = encoded.shape[2]
    heads = position_bias.shape[1]
    dp, fs = lax.axis_size("dp"), lax.axis_size("fsdp")
    me, shard = lax.axis_index("dp"), lax.axis_index("fsdp")
    core, chips = me % 2, dp // 2
    length = rows * dp
    tokens = micro_count * rows
    copies = dp // heads
    head = me // copies
    span = width // fs
    half = span // 2
    hidden = dense_down.shape[0]
    chip_bits = [1 << place for place in range(1, dp.bit_length() - 1)]
    x_order, z_order = chip_bits, chip_bits[1:] + chip_bits[:1]
    paired = fs == 2
    chunked = paired and half % (16 * chips) == 0 and hidden % (16 * chips) == 0
    chunked = chunked and hidden % 128 == 0 and dp == heads and dp % 4 == 0

    def chip_of(j):
        last = len(x_order) - 1
        return sum(((j // bit) % 2) << (last - place) for place, bit in enumerate(x_order))

    def swap_dp(values, bit):
        return lax.ppermute(values, "dp", [(j, j ^ bit) for j in range(dp)])

    def swap_fs(values):
        return lax.ppermute(values, "fsdp", [(j, 1 - j) for j in range(2)])

    def after(values, *others):
        return lax.optimization_barrier((values, *others))[0]

    def half_rows(values):
        return jnp.stack([lax.dynamic_slice_in_dim(w, core * half, half, axis=0) for w in values])

    def both_halves(sent):
        got = swap_fs(sent)
        return got, swap_dp(got, 1)

    def quarter(bit):
        return 2 * ((me // bit) % 2) + core

    def quarter_starts(bit):
        rows = [(1 - shard) * span + (quarter(bit) ^ more) * (half // 2) for more in (0, 2, 1, 3)]
        return jnp.stack([shard * span] + rows).astype(jnp.int32)

    def gather_rows(values):
        return [lax.all_gather(w, "fsdp", axis=0, tiled=True) for w in values]

    def both_tokens(values):
        if paired:
            return jnp.concatenate([values, swap_fs(values)], axis=0)
        return lax.all_gather(values, "fsdp", axis=0, tiled=True)

    def reduce_chips(kept, got, order=x_order, marks=()):
        total = kept.astype(F32) + got.astype(F32)
        for place, bit in enumerate(order[1:]):
            count = total.shape[0] // 2
            sent, total = total[count:].astype(BF16), total[:count]
            if place < len(marks):
                sent = after(sent, marks[place])
            total = total + swap_dp(sent, bit).astype(F32)
        return total.astype(BF16)

    x, g, e = inputs[:, 0], cotangent[:, 0], encoded[:, 0]

    low, offsets = [x], [0]
    for bit in reversed(chip_bits[1:]):
        low = low + [swap_dp(piece, bit) for piece in low]
        offsets = offsets + [offset | bit for offset in offsets]
    high = [swap_dp(piece, 2) for piece in low]
    near, far = jnp.stack(low), jnp.stack(high)
    offsets = [offset ^ more for more in (0, 2, 1, 3) for offset in offsets]
    source = me ^ jnp.array(offsets, jnp.int32)
    e_all = lax.all_gather(e, "dp", axis=0)

    gains = jnp.stack([gain_self, gain_cross, gain_dense])
    own_head = lambda w: lax.dynamic_slice_in_dim(w, head * 64, 64, axis=1)
    if paired:
        pad = jnp.pad(position_bias.reshape(1, -1), ((0, 0), (0, span - position_bias.size)))
        small = jnp.concatenate([gains, pad], axis=0)
        small_got = swap_fs(small)
        head_pack = jnp.concatenate([own_head(w) for w in (query_self, key_self, value_self)], 1)
        head_got = swap_fs(head_pack)
        first, second = (
            jnp.where(shard == which, mine, got)
            for which, mine, got in ((0, small, small_got), (1, small, small_got))
        )
        gains = jnp.concatenate([first[:3], second[:3]], axis=1)
        bias_all = jnp.concatenate(
            [piece[3, : position_bias.size].reshape(position_bias.shape) for piece in (first, second)]
        )
        other = (1 - shard) * span
        half_starts = jnp.stack([shard * span, other + core * half, other + (1 - core) * half])
        half_starts = half_starts.astype(jnp.int32)
        near_bit, dense_bit = chip_bits[0], chip_bits[1]
        starts = quarter_starts(near_bit)
        kv_own = (key_cross, value_cross)
        near_own = (output_self, query_cross, output_cross)
        near_sent, theirs = pack(
            jnp.stack([quarter(near_bit), quarter(dense_bit), 1 - shard]).astype(jnp.int32),
            kv_own + near_own,
            (dense_gate, dense_up),
            half // 2,
            hidden,
        )
        near_got = swap_fs(near_sent)
        near_far = swap_dp(near_got, near_bit)
        dense_got = swap_fs(after(theirs, near_got))
        dense_own = (dense_gate, dense_up)
        which = jnp.stack([shard, core]).astype(jnp.int32)
        dense_starts = jnp.concatenate([quarter_starts(dense_bit), which])
    else:
        gains = lax.all_gather(gains, "fsdp", axis=1, tiled=True)
        bias_all = lax.all_gather(position_bias, "fsdp", axis=0, tiled=True)
        kv_own, kv_more = gather_rows((key_cross, value_cross)), ()
        near_own, near_more = gather_rows((output_self, query_cross, output_cross)), ()
        first_own, first_more = gather_rows((query_self, key_self, value_self)), ()
        half_starts = jnp.zeros((1,), jnp.int32)
        head_whole = jnp.concatenate([own_head(w) for w in first_own], axis=1)
        dense_own = [
            lax.all_to_all(w, "fsdp", 1, 0, tiled=True) for w in (dense_gate, dense_up)
        ]
        dense_more = ()
        starts = jnp.zeros((1,), jnp.int32)
        dense_starts = jnp.zeros((3,), jnp.int32)
        g_group = both_tokens(g.reshape(tokens, width))
    gains, bias_all = gains.astype(F32), bias_all.astype(F32)
    marks = jnp.arange(bias_all.shape[0], dtype=jnp.int32)
    edges = jnp.sum((buckets[:, None] < marks[None, :]).astype(jnp.int32), axis=0)
    bias_values = lax.dynamic_slice_in_dim(bias_all, head, 1, axis=1)[:, 0]
    table = bias_table(edges, bias_values, length)
    x_groups = [near, far, swap_dp(near, 1), swap_dp(after(far, table), 1)]
    doc_row = jnp.broadcast_to(doc_ids[:, 0, :, None], (micro_count, dp, rows))
    doc_row = doc_row.reshape(micro_count, length)
    doc_col = doc_row[:, :, None]

    if paired:
        head_got = after(head_got, *x_groups[2:])
        head_whole = jnp.where(
            shard == 0,
            jnp.concatenate([head_pack, head_got]),
            jnp.concatenate([head_got, head_pack]),
        )
    head_w = jnp.concatenate(
        [head_whole[:, at : at + 64] for at in (0, 0, 64, 64, 128, 128)], axis=1
    )

    n_all, qkv, mixed = pl.pallas_call(
        functools.partial(self_forward_kernel, len(x_groups)),
        out_shape=[
            jax.ShapeDtypeStruct((dp, micro_count, rows, width), BF16),
            jax.ShapeDtypeStruct((length, 384), BF16),
            jax.ShapeDtypeStruct((length, 128), BF16),
        ],
        in_specs=[smem()] + [vmem()] * (len(x_groups) + 5),
        out_specs=[vmem()] * 3,
        compiler_params=params(),
        cost_estimate=cost(12),
        name="self_forward",
    )(source, *x_groups, gains[0:1], head_w, table, doc_row, doc_col)
    if paired:
        mixed = after(mixed, dense_got)
    o1_heads = lax.all_to_all(mixed.reshape(dp, rows, 128), "dp", 0, 0, tiled=True)[::copies]

    if paired:
        near_more = (near_got, near_far, swap_dp(near_got, 1), swap_dp(after(near_far, mixed), 1))
        kv_more = near_more
        dense_far = swap_dp(after(dense_got, mixed), dense_bit)
    ke, ve = cross_kv(starts, e_all, *kv_own, kv_more)

    row32 = jax.ShapeDtypeStruct((tokens, width), F32)
    row16 = jax.ShapeDtypeStruct((tokens, width), BF16)
    left, x1, q2, x2, n3, left_sent = pl.pallas_call(
        functools.partial(mid_forward_kernel, len(near_more)),
        grid=(1,),
        out_shape=[
            jax.ShapeDtypeStruct((3, tokens, width), BF16),
            row32,
            row16,
            row32,
            row16,
            jax.ShapeDtypeStruct((3, tokens, span), BF16),
        ],
        in_specs=[smem()] + [vmem()] * 8 + part_specs(near_more, 2, 1) + part_specs(near_more, 1, 4),
        out_specs=[vmem()] * 6,
        scratch_shapes=[pltpu.VMEM((tokens, width), BF16)] * 3,
        compiler_params=params(),
        cost_estimate=cost(12),
        name="mid_forward",
    )(starts, o1_heads, x, gains, ke, ve, *near_own, *near_more, *near_more)

    if paired:
        dense_more = (
            dense_got,
            dense_far,
            swap_dp(after(dense_got, ke), 1),
            swap_dp(after(dense_far, ke), 1),
        )
        g_rows = g.reshape(tokens, width)
        g_got = swap_fs(after(g_rows, dense_got))
        n_got = swap_fs(n3)
        left_got = swap_fs(left_sent)
        back, y32, _, dn3, _ = dense_layer(
            dense_starts, n3, g_rows, *dense_own, dense_down, dense_more, tokens
        )
        back_mate = swap_dp(back, 1)
        back_got, _, y16, _, d16 = dense_layer(
            dense_starts,
            after(n_got, dn3, left_got),
            g_got,
            *dense_own,
            dense_down,
            dense_more,
            tokens,
        )
        back_got_mate = swap_dp(back_got, 1)
        dn3_more = swap_fs(after(d16, back_mate))
    else:
        n_group = both_tokens(n3)
        back, _, y16, _, d16 = dense_layer(
            dense_starts, n_group, g_group, *dense_own, dense_down, dense_more, tokens
        )
        dn3 = jnp.zeros((tokens, width), F32)
        dn3_more = lax.psum_scatter(d16, "fsdp", scatter_dimension=0, tiled=True)
        dense_out = lax.psum_scatter(y16, "fsdp", scatter_dimension=0, tiled=True).astype(F32)
        outputs = (x2 + dense_out).astype(BF16)

    if chunked:
        where = jnp.stack([core, shard, me // 2]).astype(jnp.int32)
        masks = [
            [
                sum(((slot >> (len(order) - 1 - at)) & 1) * (bit // 2) for at, bit in enumerate(order))
                for slot in range(chips)
            ]
            for order in (x_order, z_order)
        ]
        own_kept, own_sent, down_kept, down_sent, far_kept, far_sent = chunk_weights(
            functools.partial(dense_weight_kernel, *masks),
            where,
            (after(n3, dn3_more), n_got, g_rows, g_got, back, back_got, back_mate, back_got_mate),
            (
                span // chips * hidden // 128,
                hidden // chips * width // 256,
                span // chips * hidden // 128,
            ),
            chips // 2,
            [
                pltpu.VMEM((max(hidden, half), max(hidden, width // 2)), F32),
                pltpu.VMEM((4 * tokens, width), BF16),
            ],
            7,
            "dense_weight",
        )
        dn3_more = after(dn3_more, own_sent)
        own_got, down_got = swap_dp(own_sent, z_order[0]), swap_dp(down_sent, x_order[0])
        far_got = swap_fs(far_sent)

    straight = chunked
    if straight:
        slots = jnp.append(chip_of(me ^ (2 * jnp.arange(heads // 2))), core).astype(jnp.int32)
    else:
        slots = jnp.append(jnp.arange(heads // 2), 0).astype(jnp.int32)
    g_rows = g.reshape(tokens, width)
    right, gx2, dkv_kept, dkv_sent, dc_dense = pl.pallas_call(
        functools.partial(cross_backward_kernel, len(near_more)),
        grid=(1,),
        out_shape=[
            jax.ShapeDtypeStruct((tokens, 2 * width), BF16),
            row32,
            jax.ShapeDtypeStruct((heads // 2, dp, micro_count, part, 128), BF16),
            jax.ShapeDtypeStruct((heads // 2, dp, micro_count, part, 128), BF16),
            jax.ShapeDtypeStruct((1, width), F32),
        ],
        in_specs=[smem()] * 2 + [vmem()] * 9 + part_specs(near_more, 1, 4),
        out_specs=[vmem()] * 5,
        scratch_shapes=[pltpu.VMEM((tokens, width), F32), pltpu.VMEM((tokens, width), BF16)],
        compiler_params=params(),
        cost_estimate=cost(15),
        name="cross_backward",
    )(starts, slots, g_rows, dn3, dn3_more, x2, gains, q2, ke, ve, near_own[2], *near_more)
    if chunked:
        gx2 = after(gx2, own_got, down_got, far_got)
    gx1, last, do1_heads, dc_cross = pl.pallas_call(
        functools.partial(mid_backward_kernel, len(near_more)),
        grid=(1,),
        out_shape=[
            row32,
            row16,
            jax.ShapeDtypeStruct((heads, rows, 128), BF16),
            jax.ShapeDtypeStruct((1, width), F32),
        ],
        in_specs=[smem()] + [vmem()] * 6 + part_specs(near_more, 2, 1),
        out_specs=[vmem()] * 4,
        scratch_shapes=[pltpu.VMEM((tokens, width), F32)],
        compiler_params=params(),
        cost_estimate=cost(6),
        name="mid_backward",
    )(starts, right, gx2, x1, gains, *near_own[:2], *near_more)
    do1 = lax.all_to_all(
        jnp.repeat(do1_heads, copies, axis=0) if copies > 1 else do1_heads, "dp", 0, 0, tiled=True
    ).reshape(length, 128)

    if chunked:
        right_got, last_got = swap_fs(after(right, do1_heads)), swap_fs(last)
        if straight:
            dkv_got = swap_dp(after(dkv_sent, do1_heads), 1)
            dkv_total = dkv_kept.astype(F32) + dkv_got.astype(F32)
            dkv_far = swap_dp(dkv_total[chips // 2 :].astype(BF16), x_order[0])
        token_left = after(left, do1)
        do1 = after(do1, dkv_got)

    dqkv, table_grad = pl.pallas_call(
        self_backward_kernel,
        out_shape=[
            jax.ShapeDtypeStruct((length, 384), BF16),
            jax.ShapeDtypeStruct((TILE, length), F32),
        ],
        in_specs=[vmem()] * 5,
        out_specs=[vmem()] * 2,
        scratch_shapes=[pltpu.VMEM((length, 128), F32), pltpu.VMEM((length, 128), F32)],
        compiler_params=params(),
        cost_estimate=cost(10),
        name="self_backward",
    )(qkv, do1, table, doc_row, doc_col)
    if chunked:
        dqkv = after(dqkv, right_got, last_got)
        far_x = swap_dp(after(far_got, table_grad, dkv_far), x_order[0])
        far_kept = swap_fs(after(far_kept, table_grad))
    if chunked:
        token_kept, token_sent = chunk_weights(
            functools.partial(token_weight_kernel, masks[1]),
            where,
            (token_left, left_got, right, right_got, last, last_got),
            (3 * half // chips * width // 128,),
            chips,
            [pltpu.VMEM((span, width), F32)],
            6,
            "token_weight",
        )
        token_got = swap_dp(token_sent, 1)
        dqkv = after(dqkv, token_kept)
    head_grad = pl.pallas_call(
        head_weight_kernel,
        out_shape=jax.ShapeDtypeStruct((fs, span * 3 // 2, 128), BF16),
        in_specs=[vmem()] * 2,
        out_specs=vmem(),
        compiler_params=params(),
        cost_estimate=cost(6),
        name="head_weight",
    )(n_all, dqkv)
    def sum_shards(values):
        if paired:
            kept = lax.dynamic_index_in_dim(values, shard, 0)
            sent = lax.dynamic_index_in_dim(values, 1 - shard, 0)
            return (kept.astype(F32) + swap_fs(sent).astype(F32)).astype(BF16)
        return lax.psum_scatter(values, "fsdp", scatter_dimension=0, tiled=True)

    head_sum = sum_shards(head_grad)

    if paired:
        first_own = (query_self, key_self, value_self)
        first_more = both_halves(after(half_rows(first_own), head_sum))
        y16 = swap_fs(after(y16, first_more[0]))
        outputs = (x2 + (y32 + y16.astype(F32))).astype(BF16)
    own_d = lax.all_to_all(dqkv.reshape(dp, rows, 384), "dp", 0, 0, tiled=True)[::copies]
    grad_inputs, dc_one = pl.pallas_call(
        functools.partial(input_grad_kernel, len(first_more)),
        out_shape=[row32, jax.ShapeDtypeStruct((1, width), F32)],
        in_specs=[smem()] + [vmem()] * (7 + len(first_more)),
        out_specs=[vmem()] * 2,
        scratch_shapes=[
            pltpu.VMEM((tokens, 3 * width), BF16),
            pltpu.VMEM((tokens, width), F32),
        ],
        compiler_params=params(),
        cost_estimate=cost(7),
        name="input_grad",
    )(half_starts, own_d, x, gains, gx1, *first_own, *first_more)

    if straight:
        dkv = reduce_chips(dkv_total[: chips // 2], dkv_far).reshape(-1, 128)
    else:
        dkv = jnp.stack([dkv_kept, dkv_sent], axis=1).reshape(heads * copies, -1, 128)
        dkv = lax.psum_scatter(dkv, "dp", scatter_dimension=0, tiled=True)[0]
        bit = 1
        while bit < copies:
            got = swap_dp(dkv, bit)
            dkv = jnp.where(
                (me // bit) % 2 == 0, jnp.concatenate([dkv, got]), jnp.concatenate([got, dkv])
            )
            bit *= 2
    cross_grad = pl.pallas_call(
        cross_head_weight_kernel,
        out_shape=jax.ShapeDtypeStruct((fs, span, 128), BF16),
        in_specs=[vmem()] * 2,
        out_specs=vmem(),
        compiler_params=params(),
        cost_estimate=cost(3),
        name="cross_head_weight",
    )(e_all, dkv)
    cross_sum = sum_shards(cross_grad)
    own_dkv = dkv.reshape(dp, micro_count * part, 128)
    own_dkv = lax.all_to_all(own_dkv, "dp", 0, 0, tiled=True)[::copies]
    grad_encoded = pl.pallas_call(
        functools.partial(encoder_grad_kernel, len(kv_more)),
        grid=(1,),
        out_shape=jax.ShapeDtypeStruct((micro_count * part, width), F32),
        in_specs=[smem()] + [vmem()] * 3 + part_specs(kv_more, 2, 0),
        out_specs=vmem(),
        scratch_shapes=[pltpu.VMEM((micro_count * part, width), BF16)] * 2,
        compiler_params=params(),
        cost_estimate=cost(4),
        name="encoder_grad",
    )(starts, own_dkv, *kv_own, *kv_more)

    if chunked:
        sums = (
            reduce_chips(own_kept, own_got, z_order, (do1, dqkv)),
            reduce_chips(down_kept, down_got, x_order, (do1, dqkv)),
            reduce_chips(far_kept, far_x, x_order, (dqkv, head_grad)),
            head_sum,
            reduce_chips(token_kept, token_got, [1] + z_order, (token_kept, dkv_far)),
            cross_sum,
        )
        pieces = lax.all_gather(jnp.concatenate(sums, axis=1), "dp", axis=0, tiled=True)
        square, wide = (span, width), (span, fs * hidden)
        (
            grad_dense_gate,
            grad_dense_up,
            grad_dense_down,
            grad_query_self,
            grad_key_self,
            grad_value_self,
            grad_output_cross,
            grad_query_cross,
            grad_output_self,
            grad_key_cross,
            grad_value_cross,
        ) = spread(
            where,
            pieces,
            [(wide, "core")] * 2
            + [((hidden, width), "chip")]
            + [(square, "head")] * 3
            + [(square, "core")] * 3
            + [(square, "head")] * 2,
        )
    else:

        def all_heads(values, kinds):
            pieces = lax.all_gather(values, "dp", axis=0, tiled=True)[::copies]
            return plain_head_spread(pieces, span, width, kinds)

        grad_query_self, grad_key_self, grad_value_self = all_heads(head_sum, 3)
        grad_key_cross, grad_value_cross = all_heads(cross_sum, 2)
        right = jnp.concatenate([right, last], axis=1)

        def over_dp(values):
            return lax.psum(values.astype(BF16), "dp").astype(F32)

        def over_all(a, b):
            made = t_dot(a, b).astype(BF16)
            return over_dp(lax.psum_scatter(made, "fsdp", scatter_dimension=0, tiled=True))

        grad_output_cross, grad_query_cross, grad_output_self = (
            over_all(left[kind], right[:, kind * width : (kind + 1) * width]) for kind in range(3)
        )
        grad_dense_gate, grad_dense_up = (
            over_dp(
                lax.all_to_all(
                    t_dot(n_group, back[:, kind * hidden : (kind + 1) * hidden]).astype(BF16),
                    "fsdp",
                    0,
                    1,
                    tiled=True,
                )
            )
            for kind in range(2)
        )
        grad_dense_down = over_dp(t_dot(back[:, 2 * hidden :], g_group))

    if chunked:
        table_grad = after(table_grad, first_more[1])
    table_sums = jnp.sum(bucket_sums(edges, table_grad, bias_all.shape[0]), axis=1)
    column = (jnp.arange(heads) == head) & (me % copies == 0)
    bias_row = jnp.where(column[None, :], table_sums[:, None], 0.0).reshape(1, -1)
    bias_row = jnp.pad(bias_row, ((0, 0), (0, width - bias_row.shape[1])))
    sums = jnp.concatenate([dc_one, dc_dense, dc_cross, bias_row], axis=0)
    if paired:
        sums = sums + swap_fs(sums)
        for bit in [1] + chip_bits:
            sums = sums + swap_dp(sums, bit)
    else:
        sums = lax.psum(sums, ("dp", "fsdp"))
    own = lax.dynamic_slice_in_dim(sums[:3], shard * span, span, axis=1)
    grad_bias = sums[3, : bias_all.size].reshape(bias_all.shape)
    grad_bias = lax.dynamic_slice_in_dim(
        grad_bias, shard * position_bias.shape[0], position_bias.shape[0], axis=0
    )
    shape = (micro_count, 1, rows, width)
    return (
        outputs.reshape(shape),
        grad_inputs.reshape(shape),
        grad_encoded.reshape(micro_count, 1, part, width),
        own[0],
        grad_query_self,
        grad_key_self,
        grad_value_self,
        grad_output_self,
        grad_bias,
        own[2],
        grad_query_cross,
        grad_key_cross,
        grad_value_cross,
        grad_output_cross,
        own[1],
        grad_dense_gate,
        grad_dense_up,
        grad_dense_down,
    )


def solution(mesh):
    matrix = P("fsdp", None)
    token = P(None, "fsdp", "dp", None)
    weights = (
        (P("fsdp"),)
        + (matrix,) * 5
        + (P("fsdp"),)
        + (matrix,) * 4
        + (P("fsdp"),)
        + (matrix,) * 3
    )
    return jax.shard_map(
        per_device,
        mesh=mesh,
        in_specs=(token,) * 3 + (P(None, "fsdp", None), P()) + weights,
        out_specs=(token,) * 3 + weights,
        check_vma=False,
    )
```

```python
import functools

import jax
import jax.numpy as jnp
from jax import lax
from jax.experimental import pallas as pl
from jax.experimental.pallas import tpu as pltpu
from jax.sharding import PartitionSpec as P

EPS = 1e-06
NEGATIVE = -1e30
TILE = 256
F32 = jnp.float32
BF16 = jnp.bfloat16
VMEM_LIMIT = 26 * 1024 * 1024
VMEM_MOST = 56 * 1024 * 1024


def vmem():
    return pl.BlockSpec(memory_space=pltpu.VMEM)


def smem():
    return pl.BlockSpec(memory_space=pltpu.SMEM)


def params(limit=VMEM_LIMIT):
    return pltpu.CompilerParams(vmem_limit_bytes=limit)


def cost(microseconds):
    return pl.CostEstimate(
        flops=int(microseconds * 1.15e9),
        bytes_accessed=int(microseconds * 3.69e6),
        transcendentals=0,
    )


def aligned(start, size):
    return pl.ds(pl.multiple_of(start, size), size)


def dot(left, right):
    return jnp.dot(left, right, preferred_element_type=F32)


def dot_t(left, right):
    return lax.dot_general(left, right, (((1,), (1,)), ((), ())), preferred_element_type=F32)


def t_dot(left, right):
    return lax.dot_general(left, right, (((0,), (0,)), ((), ())), preferred_element_type=F32)


def norm_rows(values, gain):
    return values * lax.rsqrt(jnp.mean(values * values, axis=-1, keepdims=True) + EPS) * gain


def norm_back(values, gain, grad):
    r = lax.rsqrt(jnp.mean(values * values, axis=-1, keepdims=True) + EPS)
    scaled = grad * gain
    inner = jnp.mean(scaled * values, axis=-1, keepdims=True)
    back = r * scaled - values * (r * r * r * inner)
    return back, jnp.sum(grad * (values * r), axis=0, keepdims=True)


def low_lanes(rows):
    return lax.broadcasted_iota(jnp.int32, (rows, 128), 1) < 64


def pair_up(first, second):
    lane = low_lanes(first.shape[0])
    low = jnp.where(lane, first, pltpu.roll(second, 64, 1))
    high = jnp.where(lane, pltpu.roll(first, 64, 1), second)
    return low, high


def keep_half(values, half):
    lane = low_lanes(values.shape[0])
    return jnp.where(lane if half == 0 else ~lane, values, jnp.zeros_like(values))


def softmax_rows(scores):
    top = jnp.max(scores, axis=-1, keepdims=True)
    raised = jnp.exp(scores - top)
    return raised * (1.0 / jnp.sum(raised, axis=-1, keepdims=True))


def table_kernel(edge_ref, value_ref, out_ref):
    rows, length = out_ref.shape
    bucket_count = value_ref.shape[0]
    for start in range(0, length, TILE):
        place = (rows, TILE)
        apart = (
            lax.broadcasted_iota(jnp.int32, place, 0)
            - lax.broadcasted_iota(jnp.int32, place, 1)
            + (length - rows - start)
        )
        value = jnp.full(place, value_ref[0], F32)
        for bucket in range(1, bucket_count):
            value = jnp.where(apart >= edge_ref[bucket], value_ref[bucket], value)
        out_ref[:, start : start + TILE] = jnp.where(apart >= 0, value, NEGATIVE)


def bias_table(edges, values, length):
    return pl.pallas_call(
        table_kernel,
        out_shape=jax.ShapeDtypeStruct((TILE, length), F32),
        in_specs=[smem(), smem()],
        out_specs=vmem(),
        cost_estimate=cost(4),
        name="bias_table",
    )(edges, values)


def bucket_kernel(edge_ref, grad_ref, out_ref):
    rows, length = grad_ref.shape
    bucket_count = out_ref.shape[0]
    above = [jnp.zeros((8, TILE), F32) for _ in range(bucket_count)]
    for start in range(0, length, TILE):
        for row in range(0, rows, 8):
            place = (8, TILE)
            apart = (
                lax.broadcasted_iota(jnp.int32, place, 0)
                - lax.broadcasted_iota(jnp.int32, place, 1)
                + (length - rows - start + row)
            )
            tile = grad_ref[row : row + 8, start : start + TILE]
            for bucket in range(bucket_count):
                above[bucket] = above[bucket] + jnp.where(apart >= edge_ref[bucket], tile, 0.0)
    for bucket in range(bucket_count):
        rest = above[bucket + 1] if bucket + 1 < bucket_count else 0.0
        part = jnp.sum(above[bucket] - rest, axis=0, keepdims=True)
        out_ref[bucket : bucket + 1, :] = part[:, :128] + part[:, 128:]


def bucket_sums(edges, grad, bucket_count):
    return pl.pallas_call(
        bucket_kernel,
        out_shape=jax.ShapeDtypeStruct((bucket_count, 128), F32),
        in_specs=[smem(), vmem()],
        out_specs=vmem(),
        cost_estimate=cost(7),
        name="bucket_sums",
    )(edges, grad)


def times(x_ref, starts_ref, pieces):
    if len(pieces) == 1:
        return dot(x_ref[...], pieces[0])
    total = None
    for place, piece in enumerate(pieces):
        rows = piece.shape[0]
        part = dot(x_ref[:, aligned(starts_ref[place], rows)], piece)
        total = part if total is None else total + part
    return total


def times_back(out_ref, starts_ref, terms):
    for place in range(len(terms[0][1])):
        total = sum(dot_t(d, pieces[place]) for d, pieces in terms)
        rows = terms[0][1][place].shape[0]
        if len(terms[0][1]) == 1:
            out_ref[...] = total
        else:
            out_ref[:, aligned(starts_ref[place], rows)] = total


def pack_kernel(counts, where_ref, *refs):
    total = sum(counts)
    first_ref, second_ref = refs[total:]
    for place in range(counts[0]):
        first_ref[place] = refs[place][...]
    for place in range(counts[1]):
        second_ref[place] = refs[counts[0] + place][...]


def pack(where, first, second, rows, cols):
    width = first[0].shape[1]
    counts = (len(first), len(second))
    return pl.pallas_call(
        functools.partial(pack_kernel, counts),
        grid_spec=pltpu.PrefetchScalarGridSpec(
            num_scalar_prefetch=1,
            grid=(1,),
            in_specs=[pl.BlockSpec((rows, width), lambda i, where: (where[0], 0))] * counts[0]
            + [pl.BlockSpec((rows, cols), lambda i, where: (where[1], where[2]))] * counts[1],
            out_specs=[
                pl.BlockSpec((counts[0], rows, width), lambda i, where: (0, 0, 0)),
                pl.BlockSpec((counts[1], rows, cols), lambda i, where: (0, 0, 0)),
            ],
        ),
        out_shape=[
            jax.ShapeDtypeStruct((counts[0], rows, width), BF16),
            jax.ShapeDtypeStruct((counts[1], rows, cols), BF16),
        ],
        compiler_params=params(VMEM_MOST),
        cost_estimate=cost(3),
        name="pack",
    )(where, *first, *second)


def part_specs(arrays, count, index):
    return [
        pl.BlockSpec((count,) + array.shape[1:], lambda *_: (index, 0, 0)) for array in arrays
    ]


def pieces_of(own_ref, more, index):
    return [own_ref[...]] + [ref[index] for ref in more]


def self_scores(q, k, table, doc_col, doc_row):
    scores = dot_t(q, k) + table
    return jnp.where(doc_col == doc_row, scores, NEGATIVE)


def self_forward_kernel(groups, source_ref, *refs):
    x_refs = refs[:groups]
    gain_ref, w_ref, table_ref, doc_row_ref, doc_col_ref, n_ref, qkv_ref, o_ref = refs[groups:]
    count, _, rows, width = x_refs[0].shape
    length = groups * count * rows
    lane = lax.broadcasted_iota(jnp.int32, (rows, 384), 1) % 128 < 64
    together = min(TILE // rows, count)
    for place, x_ref in enumerate(x_refs):
        for first in range(0, count, together):
            parts = []
            for inner in range(first, first + together):
                x = x_ref[inner].astype(F32).reshape(2 * rows, width)
                n = norm_rows(x, gain_ref[...]).astype(BF16)
                n_ref[source_ref[place * count + inner]] = n.reshape(2, rows, width)
                parts.append(n)
            made = dot(jnp.concatenate(parts, axis=0), w_ref[...])
            for inner in range(together):
                at = 2 * rows * inner
                picked = jnp.where(lane, made[at : at + rows], made[at + rows : at + 2 * rows])
                own = source_ref[place * count + first + inner]
                qkv_ref[aligned(own * rows, rows), :] = picked.astype(BF16)
    for block in range(length // TILE):
        start, stop = block * TILE, (block + 1) * TILE
        table = table_ref[:, length - stop :]
        q = qkv_ref[start:stop, 0:128]
        k = qkv_ref[:stop, 128:256]
        v = qkv_ref[:stop, 256:384]
        mixed = []
        for half in range(2):
            scores = self_scores(
                keep_half(q, half),
                k,
                table,
                doc_col_ref[half, start:stop, :],
                doc_row_ref[half : half + 1, :stop],
            )
            mixed.append(dot(softmax_rows(scores).astype(BF16), v))
        o_ref[start:stop, :] = jnp.where(low_lanes(TILE), mixed[0], mixed[1]).astype(BF16)


def self_backward_kernel(
    qkv_ref, do_ref, table_ref, doc_row_ref, doc_col_ref, dqkv_ref, grad_ref, dk_ref, dv_ref
):
    length = qkv_ref.shape[0]
    grad_ref[...] = jnp.zeros_like(grad_ref)
    dk_ref[...] = jnp.zeros_like(dk_ref)
    dv_ref[...] = jnp.zeros_like(dv_ref)
    for block in range(length // TILE):
        start, count = block * TILE, (block + 1) * TILE
        table = table_ref[:, length - count :]
        k = qkv_ref[:count, 128:256]
        v = qkv_ref[:count, 256:384]
        made = []
        for half in range(2):
            q = keep_half(qkv_ref[start:count, 0:128], half)
            do = keep_half(do_ref[start:count, :], half)
            p = softmax_rows(
                self_scores(
                    q,
                    k,
                    table,
                    doc_col_ref[half, start:count, :],
                    doc_row_ref[half : half + 1, :count],
                )
            )
            dp = dot_t(do, v)
            ds = (p * (dp - jnp.sum(p * dp, axis=-1, keepdims=True))).astype(BF16)
            grad_ref[:, length - count :] += ds.astype(F32)
            made.append(dot(ds, k))
            dk_ref[:count, :] += t_dot(ds, q)
            dv_ref[:count, :] += t_dot(p.astype(BF16), do)
        dq = jnp.where(low_lanes(TILE), made[0], made[1])
        dqkv_ref[start:count, 0:128] = dq.astype(BF16)
    dqkv_ref[:, 128:256] = dk_ref[...].astype(BF16)
    dqkv_ref[:, 256:384] = dv_ref[...].astype(BF16)


def head_weight_kernel(n_ref, d_ref, out_ref):
    blocks, _, rows, width = n_ref.shape
    shards = out_ref.shape[0]
    span = width // shards
    lane = lax.broadcasted_iota(jnp.int32, (blocks * rows, 384), 1) % 128 < 64
    d = d_ref[...]
    zero = jnp.zeros_like(d)
    right = [jnp.where(lane, d, zero), jnp.where(lane, zero, d)]
    half = span // 2
    for shard in range(shards):
        total = jnp.zeros((span, 384), F32)
        for micro in range(2):
            left = n_ref[:, micro, :, shard * span : (shard + 1) * span]
            total = total + t_dot(left.reshape(blocks * rows, span), right[micro])
        q, k, v = (
            total[:, at : at + 128] + pltpu.roll(total[:, at : at + 128], 64, 1)
            for at in (0, 128, 256)
        )
        out_ref[shard, :span, :] = jnp.where(low_lanes(span), q, k).astype(BF16)
        out_ref[shard, span:, :] = jnp.where(low_lanes(half), v[:half], v[half:]).astype(BF16)


def cross_kv_kernel(split, starts_ref, e_ref, wk_ref, wv_ref, *refs):
    more, (ke_ref, ve_ref) = refs[:split], refs[split:]
    blocks, _, part, _ = e_ref.shape
    for index, (own_ref, out_ref) in enumerate(((wk_ref, ke_ref), (wv_ref, ve_ref))):
        total = None
        pieces = pieces_of(own_ref, more, index)
        for place, piece in enumerate(pieces):
            rows = piece.shape[0]
            if split:
                left = e_ref[:, 0, :, aligned(starts_ref[place], rows)]
            else:
                left = e_ref[:, 0]
            made = dot(left.reshape(blocks * part, rows), piece)
            total = made if total is None else total + made
        out_ref[0] = total.astype(BF16)


def cross_kv(starts, e_all, wk, wv, more):
    blocks, micro, part, width = e_all.shape
    whole = lambda array: pl.BlockSpec(array.shape, lambda m, s: (0,) * array.ndim)
    out = pl.BlockSpec((1, blocks * part, width), lambda m, s: (m, 0, 0))
    return pl.pallas_call(
        functools.partial(cross_kv_kernel, len(more)),
        grid_spec=pltpu.PrefetchScalarGridSpec(
            num_scalar_prefetch=1,
            grid=(micro,),
            in_specs=[pl.BlockSpec((blocks, 1, part, width), lambda m, s: (0, m, 0, 0))]
            + [whole(wk), whole(wv)]
            + [pl.BlockSpec((2,) + array.shape[1:], lambda m, s: (0, 0, 0)) for array in more],
            out_specs=[out, out],
        ),
        out_shape=[jax.ShapeDtypeStruct((micro, blocks * part, width), BF16)] * 2,
        compiler_params=params(),
        cost_estimate=cost(8),
        name="cross_kv",
    )(starts, e_all, wk, wv, *more)


def mid_forward_kernel(split, starts_ref, o1_ref, x_ref, gain_ref, ke_ref, ve_ref, wo, wq, wc, *refs):
    more, last = refs[:split], refs[split : 2 * split]
    left_ref, x1_ref, q2_ref, x2_ref, n3_ref, sent_ref, o1c_ref, n2_ref, o2_ref = refs[2 * split :]
    heads, rows, _ = o1_ref.shape
    width = x_ref.shape[-1]
    for pair in range(heads // 2):
        at = pair * 128
        low, high = pair_up(o1_ref[2 * pair].astype(F32), o1_ref[2 * pair + 1].astype(F32))
        o1c_ref[0:rows, at : at + 128] = low.astype(BF16)
        o1c_ref[rows : 2 * rows, at : at + 128] = high.astype(BF16)
    x = x_ref[...].astype(F32).reshape(2 * rows, width)
    x1 = x + times(o1c_ref, starts_ref, pieces_of(wo, more, 0))
    x1_ref[...] = x1
    n2_ref[...] = norm_rows(x1, gain_ref[1:2]).astype(BF16)
    q2_ref[...] = times(n2_ref, starts_ref, pieces_of(wq, more, 1)).astype(BF16)
    for micro in range(2):
        for pair in range(heads // 2):
            at = pair * 128
            span = slice(micro * rows, (micro + 1) * rows)
            q = q2_ref[span, at : at + 128]
            both = jnp.concatenate([keep_half(q, 0), keep_half(q, 1)], axis=0)
            p = softmax_rows(dot_t(both, ke_ref[micro, :, at : at + 128]))
            o = dot(p.astype(BF16), ve_ref[micro, :, at : at + 128])
            o2_ref[span, at : at + 128] = jnp.where(
                low_lanes(rows), o[:rows], o[rows:]
            ).astype(BF16)
    x2 = x1 + times(o2_ref, starts_ref, pieces_of(wc, last, 0))
    x2_ref[...] = x2
    n3_ref[...] = norm_rows(x2, gain_ref[2:3]).astype(BF16)
    left_ref[0] = o2_ref[...]
    left_ref[1] = n2_ref[...]
    left_ref[2] = o1c_ref[...]
    if split:
        span = sent_ref.shape[2]
        for kind in range(3):
            sent_ref[kind] = left_ref[kind, :, aligned(span - starts_ref[0], span)]


def cross_backward_kernel(
    split, starts_ref, slots_ref, g_ref, dn3_ref, more_ref, x2_ref, gain_ref, q2_ref, ke_ref, ve_ref,
    wc, *refs
):
    more = refs[:split]
    right_ref, gx2_ref, keep_ref, send_ref, dc_ref, back_ref, do2_ref = refs[split:]
    blocks, micros, part = keep_ref.shape[1:4]
    tokens, width = x2_ref.shape
    rows = tokens // micros
    pairs = width // 128
    even = slots_ref[pairs] == 0
    dn3 = dn3_ref[...] + more_ref[...].astype(F32)
    back, dc_ref[...] = norm_back(x2_ref[...], gain_ref[2:3], dn3)
    gx2 = g_ref[...].astype(F32) + back
    gx2_ref[...] = gx2
    gx2b = gx2.astype(BF16)
    right_ref[:, 0:width] = gx2b
    times_back(back_ref, starts_ref, [(gx2b, pieces_of(wc, more, 0))])
    do2_ref[...] = back_ref[...].astype(BF16)
    for micro in range(micros):
        for pair in range(pairs):
            at = pair * 128
            span = slice(micro * rows, (micro + 1) * rows)
            q = q2_ref[span, at : at + 128]
            do = do2_ref[span, at : at + 128]
            q = jnp.concatenate([keep_half(q, 0), keep_half(q, 1)], axis=0)
            do = jnp.concatenate([keep_half(do, 0), keep_half(do, 1)], axis=0)
            k = ke_ref[micro, :, at : at + 128]
            v = ve_ref[micro, :, at : at + 128]
            p = softmax_rows(dot_t(q, k))
            dp = dot_t(do, v)
            ds = (p * (dp - jnp.sum(p * dp, axis=-1, keepdims=True))).astype(BF16)
            dq = dot(ds, k)
            right_ref[span, width + at : width + at + 128] = jnp.where(
                low_lanes(rows), dq[:rows], dq[rows:]
            ).astype(BF16)
            low, high = pair_up(t_dot(ds, q), t_dot(p.astype(BF16), do))
            kept, sent = jnp.where(even, low, high), jnp.where(even, high, low)
            slot = slots_ref[pair]
            keep_ref[slot, :, micro] = kept.astype(BF16).reshape(blocks, part, 128)
            send_ref[slot, :, micro] = sent.astype(BF16).reshape(blocks, part, 128)


def mid_backward_kernel(split, starts_ref, right_ref, gx2_ref, x1_ref, gain_ref, wo, wq, *refs):
    more = refs[:split]
    gx1_ref, low_ref, do1_ref, dc_ref, back_ref = refs[split:]
    heads, rows, _ = do1_ref.shape
    width = x1_ref.shape[-1]
    times_back(back_ref, starts_ref, [(right_ref[:, width:], pieces_of(wq, more, 1))])
    back, dc_ref[...] = norm_back(x1_ref[...], gain_ref[1:2], back_ref[...])
    gx1 = gx2_ref[...] + back
    gx1_ref[...] = gx1
    gx1b = gx1.astype(BF16)
    low_ref[...] = gx1b
    times_back(back_ref, starts_ref, [(gx1b, pieces_of(wo, more, 0))])
    for pair in range(heads // 2):
        at = pair * 128
        do1 = back_ref[:, at : at + 128].astype(BF16).astype(F32)
        low, high = pair_up(do1[:rows], do1[rows:])
        do1_ref[2 * pair] = low.astype(BF16)
        do1_ref[2 * pair + 1] = high.astype(BF16)


def input_grad_kernel(split, starts_ref, d_ref, x_ref, gain_ref, gx1_ref, wq, wk, wv, *refs):
    more = refs[:split]
    out_ref, dc_ref, all_ref, back_ref = refs[split:]
    heads, rows, _ = d_ref.shape
    width = x_ref.shape[-1]
    for kind in range(3):
        for pair in range(heads // 2):
            lanes = slice(kind * 128, (kind + 1) * 128)
            low, high = pair_up(
                d_ref[2 * pair, :, lanes].astype(F32), d_ref[2 * pair + 1, :, lanes].astype(F32)
            )
            at = kind * width + pair * 128
            all_ref[0:rows, at : at + 128] = low.astype(BF16)
            all_ref[rows : 2 * rows, at : at + 128] = high.astype(BF16)
    terms = [
        (all_ref[:, kind * width : (kind + 1) * width], pieces_of(own, more, kind))
        for kind, own in enumerate((wq, wk, wv))
    ]
    times_back(back_ref, starts_ref, terms)
    x = x_ref[...].astype(F32).reshape(2 * rows, width)
    back, dc = norm_back(x, gain_ref[0:1], back_ref[...])
    dc_ref[...] = dc
    out_ref[...] = gx1_ref[...] + back


def encoder_grad_kernel(split, starts_ref, d_ref, wk, wv, *refs):
    more = refs[:split]
    out_ref, k_ref, v_ref = refs[split:]
    for pair in range(d_ref.shape[0] // 2):
        at = pair * 128
        low, high = pair_up(d_ref[2 * pair].astype(F32), d_ref[2 * pair + 1].astype(F32))
        k_ref[:, at : at + 128] = low.astype(BF16)
        v_ref[:, at : at + 128] = high.astype(BF16)
    terms = [(k_ref[...], pieces_of(wk, more, 0)), (v_ref[...], pieces_of(wv, more, 1))]
    times_back(out_ref, starts_ref, terms)


def cross_head_weight_kernel(e_ref, d_ref, out_ref):
    blocks, micro, part, width = e_ref.shape
    shards, span, _ = out_ref.shape
    for shard in range(shards):
        left = e_ref[:, :, :, shard * span : (shard + 1) * span]
        left = left.reshape(blocks * micro * part, span)
        out_ref[shard] = t_dot(left, d_ref[...]).astype(BF16)


def dense_kernel(split, starts_ref, n_ref, g_ref, wg, wu, wd_ref, *refs):
    more = refs[:split]
    back_ref, y_ref, ylow_ref, d_ref, dlow_ref = refs[split:]
    hidden = wd_ref.shape[0]
    gate, up = pieces_of(wg, more, 0), pieces_of(wu, more, 1)
    a = times(n_ref, starts_ref, gate)
    b = times(n_ref, starts_ref, up)
    scale = 0.7978845608028654
    cubed = 0.044715
    inner = jnp.tanh(scale * (a + cubed * (a * a * a)))
    gelu = 0.5 * a * (1.0 + inner)
    slope = 0.5 * (1.0 + inner) + 0.5 * a * (1.0 - inner * inner) * (
        scale * (1.0 + 3.0 * cubed * (a * a))
    )
    hid = (gelu * b).astype(BF16)
    dh = dot_t(g_ref[...], wd_ref[...])
    da = (dh * b * slope).astype(BF16)
    db = (dh * gelu).astype(BF16)
    times_back(d_ref, starts_ref, [(da, gate), (db, up)])
    dlow_ref[...] = d_ref[...].astype(BF16)
    y = dot(hid, wd_ref[...])
    y_ref[...] = y
    ylow_ref[...] = y.astype(BF16)
    back_ref[:, 0:hidden] = da
    back_ref[:, hidden : 2 * hidden] = db
    back_ref[:, 2 * hidden : 3 * hidden] = hid
    if more:
        shard, other = starts_ref[len(more) + 1], 1 - starts_ref[len(more) + 2]
        put_features(back_ref, 3 * hidden, n_ref, g_ref, shard, other)


def put_features(out_ref, at, n_ref, g_ref, shard, core):
    quarter = n_ref.shape[1] // 4
    for side, place in enumerate((2 * shard + core, 2 * (1 - shard) + core)):
        lanes = slice(at + side * quarter, at + (side + 1) * quarter)
        out_ref[:, lanes] = n_ref[:, aligned(place * quarter, quarter)]
    lanes = slice(at + 2 * quarter, at + 4 * quarter)
    out_ref[:, lanes] = g_ref[:, aligned(core * 2 * quarter, 2 * quarter)]


def dense_layer(starts, n, g, wg, wu, wd, more, step):
    count, width = n.shape
    hidden = wd.shape[0]
    which = starts.shape[0] - 2
    back = 3 * hidden + (width if more else 0)
    row = lambda size: pl.BlockSpec((step, size), lambda i, s: (i, 0))
    whole = lambda array: pl.BlockSpec(array.shape, lambda i, s: (0,) * array.ndim)
    column = pl.BlockSpec((wg.shape[0], hidden), lambda i, s: (0, s[which]))
    made = lambda size, kind: jax.ShapeDtypeStruct((count, size), kind)
    return pl.pallas_call(
        functools.partial(dense_kernel, len(more)),
        grid_spec=pltpu.PrefetchScalarGridSpec(
            num_scalar_prefetch=1,
            grid=(count // step,),
            in_specs=[row(width), row(width), column, column, whole(wd)]
            + [whole(array) for array in more],
            out_specs=[row(back)] + [row(width)] * 4,
        ),
        out_shape=[made(back, BF16)]
        + [made(width, F32), made(width, BF16), made(width, F32), made(width, BF16)],
        compiler_params=params(),
        cost_estimate=cost(13),
        name="dense_layer",
    )(starts, n, g, wg, wu, wd, *more)


def put_chunk(ref, slot, at, value):
    rows, width = value.shape
    for block in range(width // 128):
        ref[slot, at + block * rows : at + (block + 1) * rows, :] = value[
            :, block * 128 : (block + 1) * 128
        ].astype(BF16)


def take_chunk(ref, slot, at, rows, width):
    return jnp.concatenate(
        [
            ref[slot, at + block * rows : at + (block + 1) * rows, :].astype(F32)
            for block in range(width // 128)
        ],
        axis=1,
    )


def put_all(scratch_ref, first, count, chip, chunk_refs, at, width, masks):
    slots = [(ref, slot) for ref in chunk_refs for slot in range(ref.shape[0])]
    rows = count // len(slots)
    for (ref, slot), mask in zip(slots, masks):
        chunk = scratch_ref[aligned(first + (chip ^ mask) * rows, rows), :width]
        put_chunk(ref, slot, at, chunk)


def dense_weight_kernel(
    x_masks, z_masks, where_ref, n0_ref, n1_ref, g0_ref, g1_ref, own0_ref, own1_ref, mate0_ref, mate1_ref, keep_ref,
    send_ref, down_keep_ref, down_send_ref, far_keep_ref, far_send_ref, scratch_ref, left_ref
):
    tokens, width = n0_ref.shape
    hidden = (own0_ref.shape[1] - width) // 3
    quarter = width // 4
    at = keep_ref.shape[1] // 2
    core, shard, chip = where_ref[0], where_ref[1], where_ref[2]
    put_features(left_ref.at[:tokens], 0, n0_ref, g0_ref, shard, core)
    put_features(left_ref.at[tokens : 2 * tokens], 0, n1_ref, g1_ref, shard, core)
    left_ref[2 * tokens : 3 * tokens, :] = mate0_ref[:, 3 * hidden :]
    left_ref[3 * tokens :, :] = mate1_ref[:, 3 * hidden :]

    def whole(kind):
        span = slice(kind * hidden, (kind + 1) * hidden)
        refs = (own0_ref, own1_ref, mate0_ref, mate1_ref)
        return jnp.concatenate([ref[:, span] for ref in refs], axis=0)

    for kind in range(2):
        right = whole(kind)
        for side, (masks, refs) in enumerate(
            ((z_masks, (keep_ref, send_ref)), (x_masks, (far_keep_ref, far_send_ref)))
        ):
            value = t_dot(left_ref[:, side * quarter : (side + 1) * quarter], right)
            scratch_ref[:quarter, :hidden] = value
            put_all(scratch_ref, 0, quarter, chip, refs, kind * at, hidden, masks)
    value = t_dot(whole(2), left_ref[:, 2 * quarter :])
    scratch_ref[:, : 2 * quarter] = value
    refs = (down_keep_ref, down_send_ref)
    put_all(scratch_ref, 0, hidden, chip, refs, 0, 2 * quarter, x_masks)


def token_weight_kernel(
    masks, where_ref, left_ref, left_more_ref, right_ref, right_more_ref, last_ref, last_more_ref,
    mine_ref, mate_ref, scratch_ref
):
    kinds, _, span = left_more_ref.shape
    width = last_ref.shape[1]
    core, shard, chip = where_ref[0], where_ref[1], where_ref[2]
    half = span // 2
    at = half // len(masks) * width // 128
    for kind in range(kinds):
        lanes = slice(kind * width, (kind + 1) * width)
        left = [left_ref[kind, :, aligned(shard * span, span)], left_more_ref[kind]]
        if kind < kinds - 1:
            right = [right_ref[:, lanes], right_more_ref[:, lanes]]
        else:
            right = [last_ref[...], last_more_ref[...]]
        scratch_ref[...] = t_dot(jnp.concatenate(left, axis=0), jnp.concatenate(right, axis=0))
        for ref, own in ((mine_ref, core), (mate_ref, 1 - core)):
            put_all(scratch_ref, own * half, half, chip, (ref,), kind * at, width, masks)


def chunk_weights(kernel, where, operands, counts, slots, scratches, length, name):
    shapes = []
    for count in counts:
        shapes += [jax.ShapeDtypeStruct((slots, count, 128), BF16)] * 2
    return pl.pallas_call(
        kernel,
        out_shape=shapes,
        in_specs=[smem()] + [vmem()] * len(operands),
        out_specs=[vmem()] * len(shapes),
        scratch_shapes=scratches,
        compiler_params=params(),
        cost_estimate=cost(length),
        name=name,
    )(where, *operands)


def head_rows(in_ref, at, rows, outs):
    for pair in range(in_ref.shape[0] // 2):
        lanes = slice(pair * 128, (pair + 1) * 128)
        first = in_ref[2 * pair, at : at + rows, :].astype(F32)
        second = in_ref[2 * pair + 1, at : at + rows, :].astype(F32)
        for (out_ref, place), value in zip(outs, pair_up(first, second)):
            out_ref[place, lanes] = value


def head_spread(in_ref, at, q_ref, k_ref, v_ref):
    span = q_ref.shape[0]
    half = span // 2
    head_rows(in_ref, at, span, ((q_ref, slice(None)), (k_ref, slice(None))))
    head_rows(in_ref, at + span, half, ((v_ref, slice(0, half)), (v_ref, slice(half, span))))


def spread_kernel(where_ref, in_ref, gate_ref, up_ref, down_ref, q_ref, k_ref, v_ref, *out_refs):
    shard = where_ref[1]
    hidden = gate_ref.shape[3] // 2
    rows = gate_ref.shape[2] // 2
    at = rows * hidden // 128
    tall = down_ref.shape[0] // 2
    half = down_ref.shape[1] // 2
    span = q_ref.shape[0]
    kinds = len(out_refs) - 2
    width = out_refs[0].shape[3]
    base = 6 * at + 3 * span // 2
    step = rows * width // 128
    for piece in range(4):
        chip, core = piece // 2, piece % 2
        place = slice(chip * rows, (chip + 1) * rows)
        for side, start in enumerate((0, 4 * at)):
            lanes = aligned((shard ^ side) * hidden, hidden)
            for kind, out_ref in enumerate((gate_ref, up_ref)):
                chunk = take_chunk(in_ref, piece, start + kind * at, rows, hidden)
                out_ref[core, 0, place, lanes] = chunk
        chunk = take_chunk(in_ref, piece, 2 * at, tall, half)
        down_ref[chip * tall : (chip + 1) * tall, core * half : (core + 1) * half] = chunk
        for kind in range(kinds):
            chunk = take_chunk(in_ref, piece, base + kind * step, rows, width)
            out_refs[kind][core, 0, place, :] = chunk
    head_spread(in_ref, 6 * at, q_ref, k_ref, v_ref)
    k_ref, v_ref = out_refs[kinds:]
    head_rows(in_ref, base + kinds * step, span, ((k_ref, slice(None)), (v_ref, slice(None))))


def spread(where, pieces, outs):
    count, total, _ = pieces.shape
    steps = count // 4
    specs, shapes = [], []
    for (rows, cols), kind in outs:
        if kind == "core":
            shapes.append((2, steps, rows // (2 * steps), cols))
            block = (2, 1, rows // (2 * steps), cols)
            specs.append(pl.BlockSpec(block, lambda q, where: (0, q, 0, 0)))
        elif kind == "chip":
            shapes.append((rows, cols))
            specs.append(pl.BlockSpec((rows // steps, cols), lambda q, where: (q, 0)))
        else:
            shapes.append((rows, cols))
            specs.append(pl.BlockSpec((rows, cols // steps), lambda q, where: (0, q)))
    made = pl.pallas_call(
        spread_kernel,
        grid_spec=pltpu.PrefetchScalarGridSpec(
            num_scalar_prefetch=1,
            grid=(steps,),
            in_specs=[pl.BlockSpec((4, total, 128), lambda q, where: (q, 0, 0))],
            out_specs=specs,
        ),
        out_shape=[jax.ShapeDtypeStruct(shape, F32) for shape in shapes],
        compiler_params=params(),
        cost_estimate=cost(20),
        name="spread",
    )(where, pieces)
    return [array.reshape(shape) for array, (shape, _) in zip(made, outs)]


def plain_head_kernel(in_ref, *out_refs):
    span = out_refs[0].shape[0]
    if len(out_refs) == 3:
        head_spread(in_ref, 0, *out_refs)
    else:
        head_rows(in_ref, 0, span, [(out_ref, slice(None)) for out_ref in out_refs])


def plain_head_spread(pieces, span, width, kinds):
    return pl.pallas_call(
        plain_head_kernel,
        out_shape=[jax.ShapeDtypeStruct((span, width), F32)] * kinds,
        in_specs=[vmem()],
        out_specs=[vmem()] * kinds,
        compiler_params=params(),
        name="plain_head_spread",
    )(pieces)


def per_device(
    inputs,
    encoded,
    cotangent,
    doc_ids,
    buckets,
    gain_self,
    query_self,
    key_self,
    value_self,
    output_self,
    position_bias,
    gain_cross,
    query_cross,
    key_cross,
    value_cross,
    output_cross,
    gain_dense,
    dense_gate,
    dense_up,
    dense_down,
):
    micro_count, _, rows, width = inputs.shape
    part = encoded.shape[2]
    heads = position_bias.shape[1]
    dp, fs = lax.axis_size("dp"), lax.axis_size("fsdp")
    me, shard = lax.axis_index("dp"), lax.axis_index("fsdp")
    core, chips = me % 2, dp // 2
    length = rows * dp
    tokens = micro_count * rows
    copies = dp // heads
    head = me // copies
    span = width // fs
    half = span // 2
    hidden = dense_down.shape[0]
    chip_bits = [1 << place for place in range(1, dp.bit_length() - 1)]
    x_order, z_order = chip_bits, chip_bits[1:] + chip_bits[:1]
    paired = fs == 2
    chunked = paired and half % (16 * chips) == 0 and hidden % (16 * chips) == 0
    chunked = chunked and hidden % 128 == 0 and dp == heads and dp % 4 == 0

    def chip_of(j):
        last = len(x_order) - 1
        return sum(((j // bit) % 2) << (last - place) for place, bit in enumerate(x_order))

    def swap_dp(values, bit):
        return lax.ppermute(values, "dp", [(j, j ^ bit) for j in range(dp)])

    def swap_fs(values):
        return lax.ppermute(values, "fsdp", [(j, 1 - j) for j in range(2)])

    def after(values, *others):
        return lax.optimization_barrier((values, *others))[0]

    def half_rows(values):
        return jnp.stack([lax.dynamic_slice_in_dim(w, core * half, half, axis=0) for w in values])

    def both_halves(sent):
        got = swap_fs(sent)
        return got, swap_dp(got, 1)

    def quarter(bit):
        return 2 * ((me // bit) % 2) + core

    def quarter_starts(bit):
        rows = [(1 - shard) * span + (quarter(bit) ^ more) * (half // 2) for more in (0, 2, 1, 3)]
        return jnp.stack([shard * span] + rows).astype(jnp.int32)

    def gather_rows(values):
        return [lax.all_gather(w, "fsdp", axis=0, tiled=True) for w in values]

    def both_tokens(values):
        if paired:
            return jnp.concatenate([values, swap_fs(values)], axis=0)
        return lax.all_gather(values, "fsdp", axis=0, tiled=True)

    def reduce_chips(kept, got, order=x_order, marks=()):
        total = kept.astype(F32) + got.astype(F32)
        for place, bit in enumerate(order[1:]):
            count = total.shape[0] // 2
            sent, total = total[count:].astype(BF16), total[:count]
            if place < len(marks):
                sent = after(sent, marks[place])
            total = total + swap_dp(sent, bit).astype(F32)
        return total.astype(BF16)

    x, g, e = inputs[:, 0], cotangent[:, 0], encoded[:, 0]

    low, offsets = [x], [0]
    for bit in reversed(chip_bits[1:]):
        low = low + [swap_dp(piece, bit) for piece in low]
        offsets = offsets + [offset | bit for offset in offsets]
    high = [swap_dp(piece, 2) for piece in low]
    near, far = jnp.stack(low), jnp.stack(high)
    offsets = [offset ^ more for more in (0, 2, 1, 3) for offset in offsets]
    source = me ^ jnp.array(offsets, jnp.int32)
    e_all = lax.all_gather(e, "dp", axis=0)

    gains = jnp.stack([gain_self, gain_cross, gain_dense])
    own_head = lambda w: lax.dynamic_slice_in_dim(w, head * 64, 64, axis=1)
    if paired:
        pad = jnp.pad(position_bias.reshape(1, -1), ((0, 0), (0, span - position_bias.size)))
        small = jnp.concatenate([gains, pad], axis=0)
        small_got = swap_fs(small)
        head_pack = jnp.concatenate([own_head(w) for w in (query_self, key_self, value_self)], 1)
        head_got = swap_fs(head_pack)
        first, second = (
            jnp.where(shard == which, mine, got)
            for which, mine, got in ((0, small, small_got), (1, small, small_got))
        )
        gains = jnp.concatenate([first[:3], second[:3]], axis=1)
        bias_all = jnp.concatenate(
            [piece[3, : position_bias.size].reshape(position_bias.shape) for piece in (first, second)]
        )
        other = (1 - shard) * span
        half_starts = jnp.stack([shard * span, other + core * half, other + (1 - core) * half])
        half_starts = half_starts.astype(jnp.int32)
        near_bit, dense_bit = chip_bits[0], chip_bits[1]
        starts = quarter_starts(near_bit)
        kv_own = (key_cross, value_cross)
        near_own = (output_self, query_cross, output_cross)
        near_sent, theirs = pack(
            jnp.stack([quarter(near_bit), quarter(dense_bit), 1 - shard]).astype(jnp.int32),
            kv_own + near_own,
            (dense_gate, dense_up),
            half // 2,
            hidden,
        )
        near_got = swap_fs(near_sent)
        near_far = swap_dp(near_got, near_bit)
        dense_got = swap_fs(after(theirs, near_got))
        dense_own = (dense_gate, dense_up)
        which = jnp.stack([shard, core]).astype(jnp.int32)
        dense_starts = jnp.concatenate([quarter_starts(dense_bit), which])
    else:
        gains = lax.all_gather(gains, "fsdp", axis=1, tiled=True)
        bias_all = lax.all_gather(position_bias, "fsdp", axis=0, tiled=True)
        kv_own, kv_more = gather_rows((key_cross, value_cross)), ()
        near_own, near_more = gather_rows((output_self, query_cross, output_cross)), ()
        first_own, first_more = gather_rows((query_self, key_self, value_self)), ()
        half_starts = jnp.zeros((1,), jnp.int32)
        head_whole = jnp.concatenate([own_head(w) for w in first_own], axis=1)
        dense_own = [
            lax.all_to_all(w, "fsdp", 1, 0, tiled=True) for w in (dense_gate, dense_up)
        ]
        dense_more = ()
        starts = jnp.zeros((1,), jnp.int32)
        dense_starts = jnp.zeros((3,), jnp.int32)
        g_group = both_tokens(g.reshape(tokens, width))
    gains, bias_all = gains.astype(F32), bias_all.astype(F32)
    marks = jnp.arange(bias_all.shape[0], dtype=jnp.int32)
    edges = jnp.sum((buckets[:, None] < marks[None, :]).astype(jnp.int32), axis=0)
    bias_values = lax.dynamic_slice_in_dim(bias_all, head, 1, axis=1)[:, 0]
    table = bias_table(edges, bias_values, length)
    x_groups = [near, far, swap_dp(near, 1), swap_dp(after(far, table), 1)]
    doc_row = jnp.broadcast_to(doc_ids[:, 0, :, None], (micro_count, dp, rows))
    doc_row = doc_row.reshape(micro_count, length)
    doc_col = doc_row[:, :, None]

    if paired:
        head_got = after(head_got, *x_groups[2:])
        head_whole = jnp.where(
            shard == 0,
            jnp.concatenate([head_pack, head_got]),
            jnp.concatenate([head_got, head_pack]),
        )
    head_w = jnp.concatenate(
        [head_whole[:, at : at + 64] for at in (0, 0, 64, 64, 128, 128)], axis=1
    )

    n_all, qkv, mixed = pl.pallas_call(
        functools.partial(self_forward_kernel, len(x_groups)),
        out_shape=[
            jax.ShapeDtypeStruct((dp, micro_count, rows, width), BF16),
            jax.ShapeDtypeStruct((length, 384), BF16),
            jax.ShapeDtypeStruct((length, 128), BF16),
        ],
        in_specs=[smem()] + [vmem()] * (len(x_groups) + 5),
        out_specs=[vmem()] * 3,
        compiler_params=params(),
        cost_estimate=cost(12),
        name="self_forward",
    )(source, *x_groups, gains[0:1], head_w, table, doc_row, doc_col)
    if paired:
        mixed = after(mixed, dense_got)
    o1_heads = lax.all_to_all(mixed.reshape(dp, rows, 128), "dp", 0, 0, tiled=True)[::copies]

    if paired:
        near_more = (near_got, near_far, swap_dp(near_got, 1), swap_dp(after(near_far, mixed), 1))
        kv_more = near_more
        dense_far = swap_dp(after(dense_got, mixed), dense_bit)
    ke, ve = cross_kv(starts, e_all, *kv_own, kv_more)

    row32 = jax.ShapeDtypeStruct((tokens, width), F32)
    row16 = jax.ShapeDtypeStruct((tokens, width), BF16)
    left, x1, q2, x2, n3, left_sent = pl.pallas_call(
        functools.partial(mid_forward_kernel, len(near_more)),
        grid=(1,),
        out_shape=[
            jax.ShapeDtypeStruct((3, tokens, width), BF16),
            row32,
            row16,
            row32,
            row16,
            jax.ShapeDtypeStruct((3, tokens, span), BF16),
        ],
        in_specs=[smem()] + [vmem()] * 8 + part_specs(near_more, 2, 1) + part_specs(near_more, 1, 4),
        out_specs=[vmem()] * 6,
        scratch_shapes=[pltpu.VMEM((tokens, width), BF16)] * 3,
        compiler_params=params(),
        cost_estimate=cost(12),
        name="mid_forward",
    )(starts, o1_heads, x, gains, ke, ve, *near_own, *near_more, *near_more)

    if paired:
        dense_more = (
            dense_got,
            dense_far,
            swap_dp(after(dense_got, ke), 1),
            swap_dp(after(dense_far, ke), 1),
        )
        g_rows = g.reshape(tokens, width)
        g_got = swap_fs(after(g_rows, dense_got))
        n_got = swap_fs(n3)
        back, y32, _, dn3, _ = dense_layer(
            dense_starts, n3, g_rows, *dense_own, dense_down, dense_more, tokens
        )
        back_mate = swap_dp(back, 1)
        back_got, _, y16, _, d16 = dense_layer(
            dense_starts,
            after(n_got, dn3),
            g_got,
            *dense_own,
            dense_down,
            dense_more,
            tokens,
        )
        back_got_mate = swap_dp(back_got, 1)
        dn3_more = swap_fs(after(d16, back_mate))
        left_got = swap_fs(after(left_sent, dn3_more))
    else:
        n_group = both_tokens(n3)
        back, _, y16, _, d16 = dense_layer(
            dense_starts, n_group, g_group, *dense_own, dense_down, dense_more, tokens
        )
        dn3 = jnp.zeros((tokens, width), F32)
        dn3_more = lax.psum_scatter(d16, "fsdp", scatter_dimension=0, tiled=True)
        dense_out = lax.psum_scatter(y16, "fsdp", scatter_dimension=0, tiled=True).astype(F32)
        outputs = (x2 + dense_out).astype(BF16)

    if chunked:
        where = jnp.stack([core, shard, me // 2]).astype(jnp.int32)
        masks = [
            [
                sum(((slot >> (len(order) - 1 - at)) & 1) * (bit // 2) for at, bit in enumerate(order))
                for slot in range(chips)
            ]
            for order in (x_order, z_order)
        ]
        own_kept, own_sent, down_kept, down_sent, far_kept, far_sent = chunk_weights(
            functools.partial(dense_weight_kernel, *masks),
            where,
            (after(n3, dn3_more), n_got, g_rows, g_got, back, back_got, back_mate, back_got_mate),
            (
                span // chips * hidden // 128,
                hidden // chips * width // 256,
                span // chips * hidden // 128,
            ),
            chips // 2,
            [
                pltpu.VMEM((max(hidden, half), max(hidden, width // 2)), F32),
                pltpu.VMEM((4 * tokens, width), BF16),
            ],
            7,
            "dense_weight",
        )
        dn3_more = after(dn3_more, own_sent)
        own_got, down_got = swap_dp(own_sent, z_order[0]), swap_dp(down_sent, x_order[0])

    straight = chunked
    if straight:
        slots = jnp.append(chip_of(me ^ (2 * jnp.arange(heads // 2))), core).astype(jnp.int32)
    else:
        slots = jnp.append(jnp.arange(heads // 2), 0).astype(jnp.int32)
    g_rows = g.reshape(tokens, width)
    right, gx2, dkv_kept, dkv_sent, dc_dense = pl.pallas_call(
        functools.partial(cross_backward_kernel, len(near_more)),
        grid=(1,),
        out_shape=[
            jax.ShapeDtypeStruct((tokens, 2 * width), BF16),
            row32,
            jax.ShapeDtypeStruct((heads // 2, dp, micro_count, part, 128), BF16),
            jax.ShapeDtypeStruct((heads // 2, dp, micro_count, part, 128), BF16),
            jax.ShapeDtypeStruct((1, width), F32),
        ],
        in_specs=[smem()] * 2 + [vmem()] * 9 + part_specs(near_more, 1, 4),
        out_specs=[vmem()] * 5,
        scratch_shapes=[pltpu.VMEM((tokens, width), F32), pltpu.VMEM((tokens, width), BF16)],
        compiler_params=params(),
        cost_estimate=cost(15),
        name="cross_backward",
    )(starts, slots, g_rows, dn3, dn3_more, x2, gains, q2, ke, ve, near_own[2], *near_more)
    if chunked:
        gx2 = after(gx2, own_got, down_got, left_got)
    gx1, last, do1_heads, dc_cross = pl.pallas_call(
        functools.partial(mid_backward_kernel, len(near_more)),
        grid=(1,),
        out_shape=[
            row32,
            row16,
            jax.ShapeDtypeStruct((heads, rows, 128), BF16),
            jax.ShapeDtypeStruct((1, width), F32),
        ],
        in_specs=[smem()] + [vmem()] * 6 + part_specs(near_more, 2, 1),
        out_specs=[vmem()] * 4,
        scratch_shapes=[pltpu.VMEM((tokens, width), F32)],
        compiler_params=params(),
        cost_estimate=cost(6),
        name="mid_backward",
    )(starts, right, gx2, x1, gains, *near_own[:2], *near_more)
    do1 = lax.all_to_all(
        jnp.repeat(do1_heads, copies, axis=0) if copies > 1 else do1_heads, "dp", 0, 0, tiled=True
    ).reshape(length, 128)

    if chunked:
        right_got, last_got = swap_fs(after(right, do1_heads)), swap_fs(last)
        far_got = swap_fs(after(far_sent, right_got, last_got))
        if straight:
            dkv_got = swap_dp(after(dkv_sent, do1_heads), 1)
            dkv_total = dkv_kept.astype(F32) + dkv_got.astype(F32)
            dkv_far = swap_dp(dkv_total[chips // 2 :].astype(BF16), x_order[0])
        token_left = after(left, do1, dkv_got)
        token_kept, token_sent = chunk_weights(
            functools.partial(token_weight_kernel, masks[1]),
            where,
            (token_left, left_got, right, right_got, last, last_got),
            (3 * half // chips * width // 128,),
            chips,
            [pltpu.VMEM((span, width), F32)],
            6,
            "token_weight",
        )
        token_total = token_kept.astype(F32) + swap_dp(token_sent, 1).astype(F32)
        token_far = swap_dp(token_total[chips // 2 :].astype(BF16), z_order[0])
        do1 = after(do1, dkv_got, token_kept)

    dqkv, table_grad = pl.pallas_call(
        self_backward_kernel,
        out_shape=[
            jax.ShapeDtypeStruct((length, 384), BF16),
            jax.ShapeDtypeStruct((TILE, length), F32),
        ],
        in_specs=[vmem()] * 5,
        out_specs=[vmem()] * 2,
        scratch_shapes=[pltpu.VMEM((length, 128), F32), pltpu.VMEM((length, 128), F32)],
        compiler_params=params(),
        cost_estimate=cost(10),
        name="self_backward",
    )(qkv, do1, table, doc_row, doc_col)
    if chunked:
        dqkv = after(dqkv, right_got, last_got, dkv_far, token_far)
        far_x = swap_dp(after(far_got, table_grad, dkv_far), x_order[0])
        far_kept = swap_fs(after(far_kept, table_grad))
    head_grad = pl.pallas_call(
        head_weight_kernel,
        out_shape=jax.ShapeDtypeStruct((fs, span * 3 // 2, 128), BF16),
        in_specs=[vmem()] * 2,
        out_specs=vmem(),
        compiler_params=params(),
        cost_estimate=cost(6),
        name="head_weight",
    )(n_all, dqkv)
    def sum_shards(values):
        if paired:
            kept = lax.dynamic_index_in_dim(values, shard, 0)
            sent = lax.dynamic_index_in_dim(values, 1 - shard, 0)
            return (kept.astype(F32) + swap_fs(sent).astype(F32)).astype(BF16)
        return lax.psum_scatter(values, "fsdp", scatter_dimension=0, tiled=True)

    head_sum = sum_shards(head_grad)

    if paired:
        first_own = (query_self, key_self, value_self)
        first_more = both_halves(after(half_rows(first_own), head_sum))
        y16 = swap_fs(after(y16, first_more[0]))
        outputs = (x2 + (y32 + y16.astype(F32))).astype(BF16)
    own_d = lax.all_to_all(dqkv.reshape(dp, rows, 384), "dp", 0, 0, tiled=True)[::copies]
    grad_inputs, dc_one = pl.pallas_call(
        functools.partial(input_grad_kernel, len(first_more)),
        out_shape=[row32, jax.ShapeDtypeStruct((1, width), F32)],
        in_specs=[smem()] + [vmem()] * (7 + len(first_more)),
        out_specs=[vmem()] * 2,
        scratch_shapes=[
            pltpu.VMEM((tokens, 3 * width), BF16),
            pltpu.VMEM((tokens, width), F32),
        ],
        compiler_params=params(),
        cost_estimate=cost(7),
        name="input_grad",
    )(half_starts, own_d, x, gains, gx1, *first_own, *first_more)

    if straight:
        dkv = reduce_chips(dkv_total[: chips // 2], dkv_far).reshape(-1, 128)
    else:
        dkv = jnp.stack([dkv_kept, dkv_sent], axis=1).reshape(heads * copies, -1, 128)
        dkv = lax.psum_scatter(dkv, "dp", scatter_dimension=0, tiled=True)[0]
        bit = 1
        while bit < copies:
            got = swap_dp(dkv, bit)
            dkv = jnp.where(
                (me // bit) % 2 == 0, jnp.concatenate([dkv, got]), jnp.concatenate([got, dkv])
            )
            bit *= 2
    cross_grad = pl.pallas_call(
        cross_head_weight_kernel,
        out_shape=jax.ShapeDtypeStruct((fs, span, 128), BF16),
        in_specs=[vmem()] * 2,
        out_specs=vmem(),
        compiler_params=params(),
        cost_estimate=cost(3),
        name="cross_head_weight",
    )(e_all, dkv)
    cross_sum = sum_shards(cross_grad)
    own_dkv = dkv.reshape(dp, micro_count * part, 128)
    own_dkv = lax.all_to_all(own_dkv, "dp", 0, 0, tiled=True)[::copies]
    grad_encoded = pl.pallas_call(
        functools.partial(encoder_grad_kernel, len(kv_more)),
        grid=(1,),
        out_shape=jax.ShapeDtypeStruct((micro_count * part, width), F32),
        in_specs=[smem()] + [vmem()] * 3 + part_specs(kv_more, 2, 0),
        out_specs=vmem(),
        scratch_shapes=[pltpu.VMEM((micro_count * part, width), BF16)] * 2,
        compiler_params=params(),
        cost_estimate=cost(4),
        name="encoder_grad",
    )(starts, own_dkv, *kv_own, *kv_more)

    if chunked:
        sums = (
            reduce_chips(own_kept, own_got, z_order, (do1, head_grad)),
            reduce_chips(down_kept, down_got, x_order, (do1, head_grad)),
            reduce_chips(far_kept, far_x, x_order),
            head_sum,
            reduce_chips(token_total[: chips // 2], token_far, z_order),
            cross_sum,
        )
        pieces = lax.all_gather(jnp.concatenate(sums, axis=1), "dp", axis=0, tiled=True)
        square, wide = (span, width), (span, fs * hidden)
        (
            grad_dense_gate,
            grad_dense_up,
            grad_dense_down,
            grad_query_self,
            grad_key_self,
            grad_value_self,
            grad_output_cross,
            grad_query_cross,
            grad_output_self,
            grad_key_cross,
            grad_value_cross,
        ) = spread(
            where,
            pieces,
            [(wide, "core")] * 2
            + [((hidden, width), "chip")]
            + [(square, "head")] * 3
            + [(square, "core")] * 3
            + [(square, "head")] * 2,
        )
    else:

        def all_heads(values, kinds):
            pieces = lax.all_gather(values, "dp", axis=0, tiled=True)[::copies]
            return plain_head_spread(pieces, span, width, kinds)

        grad_query_self, grad_key_self, grad_value_self = all_heads(head_sum, 3)
        grad_key_cross, grad_value_cross = all_heads(cross_sum, 2)
        right = jnp.concatenate([right, last], axis=1)

        def over_dp(values):
            return lax.psum(values.astype(BF16), "dp").astype(F32)

        def over_all(a, b):
            made = t_dot(a, b).astype(BF16)
            return over_dp(lax.psum_scatter(made, "fsdp", scatter_dimension=0, tiled=True))

        grad_output_cross, grad_query_cross, grad_output_self = (
            over_all(left[kind], right[:, kind * width : (kind + 1) * width]) for kind in range(3)
        )
        grad_dense_gate, grad_dense_up = (
            over_dp(
                lax.all_to_all(
                    t_dot(n_group, back[:, kind * hidden : (kind + 1) * hidden]).astype(BF16),
                    "fsdp",
                    0,
                    1,
                    tiled=True,
                )
            )
            for kind in range(2)
        )
        grad_dense_down = over_dp(t_dot(back[:, 2 * hidden :], g_group))

    if chunked:
        table_grad = after(table_grad, first_more[1])
    table_sums = jnp.sum(bucket_sums(edges, table_grad, bias_all.shape[0]), axis=1)
    column = (jnp.arange(heads) == head) & (me % copies == 0)
    bias_row = jnp.where(column[None, :], table_sums[:, None], 0.0).reshape(1, -1)
    bias_row = jnp.pad(bias_row, ((0, 0), (0, width - bias_row.shape[1])))
    sums = jnp.concatenate([dc_one, dc_dense, dc_cross, bias_row], axis=0)
    if paired:
        sums = sums + swap_fs(sums)
        for bit in [1] + chip_bits:
            sums = sums + swap_dp(sums, bit)
    else:
        sums = lax.psum(sums, ("dp", "fsdp"))
    own = lax.dynamic_slice_in_dim(sums[:3], shard * span, span, axis=1)
    grad_bias = sums[3, : bias_all.size].reshape(bias_all.shape)
    grad_bias = lax.dynamic_slice_in_dim(
        grad_bias, shard * position_bias.shape[0], position_bias.shape[0], axis=0
    )
    shape = (micro_count, 1, rows, width)
    return (
        outputs.reshape(shape),
        grad_inputs.reshape(shape),
        grad_encoded.reshape(micro_count, 1, part, width),
        own[0],
        grad_query_self,
        grad_key_self,
        grad_value_self,
        grad_output_self,
        grad_bias,
        own[2],
        grad_query_cross,
        grad_key_cross,
        grad_value_cross,
        grad_output_cross,
        own[1],
        grad_dense_gate,
        grad_dense_up,
        grad_dense_down,
    )


def solution(mesh):
    matrix = P("fsdp", None)
    token = P(None, "fsdp", "dp", None)
    weights = (
        (P("fsdp"),)
        + (matrix,) * 5
        + (P("fsdp"),)
        + (matrix,) * 4
        + (P("fsdp"),)
        + (matrix,) * 3
    )
    return jax.shard_map(
        per_device,
        mesh=mesh,
        in_specs=(token,) * 3 + (P(None, "fsdp", None), P()) + weights,
        out_specs=(token,) * 3 + weights,
        check_vma=False,
    )
```

```python
import functools

import jax
import jax.numpy as jnp
from jax import lax
from jax.experimental import pallas as pl
from jax.experimental.pallas import tpu as pltpu
from jax.sharding import PartitionSpec as P

EPS = 1e-06
NEGATIVE = -1e30
TILE = 256
F32 = jnp.float32
BF16 = jnp.bfloat16
VMEM_LIMIT = 26 * 1024 * 1024
VMEM_MOST = 56 * 1024 * 1024


def vmem():
    return pl.BlockSpec(memory_space=pltpu.VMEM)


def smem():
    return pl.BlockSpec(memory_space=pltpu.SMEM)


def params(limit=VMEM_LIMIT):
    return pltpu.CompilerParams(vmem_limit_bytes=limit)


def cost(microseconds):
    return pl.CostEstimate(
        flops=int(microseconds * 1.15e9),
        bytes_accessed=int(microseconds * 3.69e6),
        transcendentals=0,
    )


def aligned(start, size):
    return pl.ds(pl.multiple_of(start, size), size)


def dot(left, right):
    return jnp.dot(left, right, preferred_element_type=F32)


def dot_t(left, right):
    return lax.dot_general(left, right, (((1,), (1,)), ((), ())), preferred_element_type=F32)


def t_dot(left, right):
    return lax.dot_general(left, right, (((0,), (0,)), ((), ())), preferred_element_type=F32)


def norm_rows(values, gain):
    return values * lax.rsqrt(jnp.mean(values * values, axis=-1, keepdims=True) + EPS) * gain


def norm_back(values, gain, grad):
    r = lax.rsqrt(jnp.mean(values * values, axis=-1, keepdims=True) + EPS)
    scaled = grad * gain
    inner = jnp.mean(scaled * values, axis=-1, keepdims=True)
    back = r * scaled - values * (r * r * r * inner)
    return back, jnp.sum(grad * (values * r), axis=0, keepdims=True)


def low_lanes(rows):
    return lax.broadcasted_iota(jnp.int32, (rows, 128), 1) < 64


def pair_up(first, second):
    lane = low_lanes(first.shape[0])
    low = jnp.where(lane, first, pltpu.roll(second, 64, 1))
    high = jnp.where(lane, pltpu.roll(first, 64, 1), second)
    return low, high


def keep_half(values, half):
    lane = low_lanes(values.shape[0])
    return jnp.where(lane if half == 0 else ~lane, values, jnp.zeros_like(values))


def softmax_rows(scores):
    top = jnp.max(scores, axis=-1, keepdims=True)
    raised = jnp.exp(scores - top)
    return raised * (1.0 / jnp.sum(raised, axis=-1, keepdims=True))


def table_kernel(edge_ref, value_ref, out_ref):
    rows, length = out_ref.shape
    bucket_count = value_ref.shape[0]
    for start in range(0, length, TILE):
        place = (rows, TILE)
        apart = (
            lax.broadcasted_iota(jnp.int32, place, 0)
            - lax.broadcasted_iota(jnp.int32, place, 1)
            + (length - rows - start)
        )
        value = jnp.full(place, value_ref[0], F32)
        for bucket in range(1, bucket_count):
            value = jnp.where(apart >= edge_ref[bucket], value_ref[bucket], value)
        out_ref[:, start : start + TILE] = jnp.where(apart >= 0, value, NEGATIVE)


def bias_table(edges, values, length):
    return pl.pallas_call(
        table_kernel,
        out_shape=jax.ShapeDtypeStruct((TILE, length), F32),
        in_specs=[smem(), smem()],
        out_specs=vmem(),
        cost_estimate=cost(4),
        name="bias_table",
    )(edges, values)


def bucket_kernel(edge_ref, grad_ref, out_ref):
    rows, length = grad_ref.shape
    bucket_count = out_ref.shape[0]
    above = [jnp.zeros((8, TILE), F32) for _ in range(bucket_count)]
    for start in range(0, length, TILE):
        for row in range(0, rows, 8):
            place = (8, TILE)
            apart = (
                lax.broadcasted_iota(jnp.int32, place, 0)
                - lax.broadcasted_iota(jnp.int32, place, 1)
                + (length - rows - start + row)
            )
            tile = grad_ref[row : row + 8, start : start + TILE]
            for bucket in range(bucket_count):
                above[bucket] = above[bucket] + jnp.where(apart >= edge_ref[bucket], tile, 0.0)
    for bucket in range(bucket_count):
        rest = above[bucket + 1] if bucket + 1 < bucket_count else 0.0
        part = jnp.sum(above[bucket] - rest, axis=0, keepdims=True)
        out_ref[bucket : bucket + 1, :] = part[:, :128] + part[:, 128:]


def bucket_sums(edges, grad, bucket_count):
    return pl.pallas_call(
        bucket_kernel,
        out_shape=jax.ShapeDtypeStruct((bucket_count, 128), F32),
        in_specs=[smem(), vmem()],
        out_specs=vmem(),
        cost_estimate=cost(7),
        name="bucket_sums",
    )(edges, grad)


def times(x_ref, starts_ref, pieces):
    if len(pieces) == 1:
        return dot(x_ref[...], pieces[0])
    total = None
    for place, piece in enumerate(pieces):
        rows = piece.shape[0]
        part = dot(x_ref[:, aligned(starts_ref[place], rows)], piece)
        total = part if total is None else total + part
    return total


def times_back(out_ref, starts_ref, terms):
    for place in range(len(terms[0][1])):
        total = sum(dot_t(d, pieces[place]) for d, pieces in terms)
        rows = terms[0][1][place].shape[0]
        if len(terms[0][1]) == 1:
            out_ref[...] = total
        else:
            out_ref[:, aligned(starts_ref[place], rows)] = total


def pack_kernel(counts, where_ref, *refs):
    total = sum(counts)
    first_ref, second_ref = refs[total:]
    for place in range(counts[0]):
        first_ref[place] = refs[place][...]
    for place in range(counts[1]):
        second_ref[place] = refs[counts[0] + place][...]


def pack(where, first, second, rows, cols):
    width = first[0].shape[1]
    counts = (len(first), len(second))
    return pl.pallas_call(
        functools.partial(pack_kernel, counts),
        grid_spec=pltpu.PrefetchScalarGridSpec(
            num_scalar_prefetch=1,
            grid=(1,),
            in_specs=[pl.BlockSpec((rows, width), lambda i, where: (where[0], 0))] * counts[0]
            + [pl.BlockSpec((rows, cols), lambda i, where: (where[1], where[2]))] * counts[1],
            out_specs=[
                pl.BlockSpec((counts[0], rows, width), lambda i, where: (0, 0, 0)),
                pl.BlockSpec((counts[1], rows, cols), lambda i, where: (0, 0, 0)),
            ],
        ),
        out_shape=[
            jax.ShapeDtypeStruct((counts[0], rows, width), BF16),
            jax.ShapeDtypeStruct((counts[1], rows, cols), BF16),
        ],
        compiler_params=params(VMEM_MOST),
        cost_estimate=cost(3),
        name="pack",
    )(where, *first, *second)


def part_specs(arrays, count, index):
    return [
        pl.BlockSpec((count,) + array.shape[1:], lambda *_: (index, 0, 0)) for array in arrays
    ]


def pieces_of(own_ref, more, index):
    return [own_ref[...]] + [ref[index] for ref in more]


def self_scores(q, k, table, doc_col, doc_row):
    scores = dot_t(q, k) + table
    return jnp.where(doc_col == doc_row, scores, NEGATIVE)


def self_forward_kernel(groups, source_ref, *refs):
    x_refs = refs[:groups]
    gain_ref, w_ref, table_ref, doc_row_ref, doc_col_ref, n_ref, qkv_ref, o_ref = refs[groups:]
    count, _, rows, width = x_refs[0].shape
    length = groups * count * rows
    lane = lax.broadcasted_iota(jnp.int32, (rows, 384), 1) % 128 < 64
    together = min(TILE // rows, count)
    for place, x_ref in enumerate(x_refs):
        for first in range(0, count, together):
            parts = []
            for inner in range(first, first + together):
                x = x_ref[inner].astype(F32).reshape(2 * rows, width)
                n = norm_rows(x, gain_ref[...]).astype(BF16)
                n_ref[source_ref[place * count + inner]] = n.reshape(2, rows, width)
                parts.append(n)
            made = dot(jnp.concatenate(parts, axis=0), w_ref[...])
            for inner in range(together):
                at = 2 * rows * inner
                picked = jnp.where(lane, made[at : at + rows], made[at + rows : at + 2 * rows])
                own = source_ref[place * count + first + inner]
                qkv_ref[aligned(own * rows, rows), :] = picked.astype(BF16)
    for block in range(length // TILE):
        start, stop = block * TILE, (block + 1) * TILE
        table = table_ref[:, length - stop :]
        q = qkv_ref[start:stop, 0:128]
        k = qkv_ref[:stop, 128:256]
        v = qkv_ref[:stop, 256:384]
        mixed = []
        for half in range(2):
            scores = self_scores(
                keep_half(q, half),
                k,
                table,
                doc_col_ref[half, start:stop, :],
                doc_row_ref[half : half + 1, :stop],
            )
            mixed.append(dot(softmax_rows(scores).astype(BF16), v))
        o_ref[start:stop, :] = jnp.where(low_lanes(TILE), mixed[0], mixed[1]).astype(BF16)


def self_backward_kernel(
    qkv_ref, do_ref, table_ref, doc_row_ref, doc_col_ref, dqkv_ref, grad_ref, dk_ref, dv_ref
):
    length = qkv_ref.shape[0]
    grad_ref[...] = jnp.zeros_like(grad_ref)
    dk_ref[...] = jnp.zeros_like(dk_ref)
    dv_ref[...] = jnp.zeros_like(dv_ref)
    for block in range(length // TILE):
        start, count = block * TILE, (block + 1) * TILE
        table = table_ref[:, length - count :]
        k = qkv_ref[:count, 128:256]
        v = qkv_ref[:count, 256:384]
        made = []
        for half in range(2):
            q = keep_half(qkv_ref[start:count, 0:128], half)
            do = keep_half(do_ref[start:count, :], half)
            p = softmax_rows(
                self_scores(
                    q,
                    k,
                    table,
                    doc_col_ref[half, start:count, :],
                    doc_row_ref[half : half + 1, :count],
                )
            )
            dp = dot_t(do, v)
            ds = (p * (dp - jnp.sum(p * dp, axis=-1, keepdims=True))).astype(BF16)
            grad_ref[:, length - count :] += ds.astype(F32)
            made.append(dot(ds, k))
            dk_ref[:count, :] += t_dot(ds, q)
            dv_ref[:count, :] += t_dot(p.astype(BF16), do)
        dq = jnp.where(low_lanes(TILE), made[0], made[1])
        dqkv_ref[start:count, 0:128] = dq.astype(BF16)
    dqkv_ref[:, 128:256] = dk_ref[...].astype(BF16)
    dqkv_ref[:, 256:384] = dv_ref[...].astype(BF16)


def head_weight_kernel(n_ref, d_ref, out_ref):
    blocks, _, rows, width = n_ref.shape
    shards = out_ref.shape[0]
    span = width // shards
    lane = lax.broadcasted_iota(jnp.int32, (blocks * rows, 384), 1) % 128 < 64
    d = d_ref[...]
    zero = jnp.zeros_like(d)
    right = [jnp.where(lane, d, zero), jnp.where(lane, zero, d)]
    half = span // 2
    for shard in range(shards):
        total = jnp.zeros((span, 384), F32)
        for micro in range(2):
            left = n_ref[:, micro, :, shard * span : (shard + 1) * span]
            total = total + t_dot(left.reshape(blocks * rows, span), right[micro])
        q, k, v = (
            total[:, at : at + 128] + pltpu.roll(total[:, at : at + 128], 64, 1)
            for at in (0, 128, 256)
        )
        out_ref[shard, :span, :] = jnp.where(low_lanes(span), q, k).astype(BF16)
        out_ref[shard, span:, :] = jnp.where(low_lanes(half), v[:half], v[half:]).astype(BF16)


def cross_kv_kernel(split, starts_ref, e_ref, wk_ref, wv_ref, *refs):
    more, (ke_ref, ve_ref) = refs[:split], refs[split:]
    blocks, _, part, _ = e_ref.shape
    for index, (own_ref, out_ref) in enumerate(((wk_ref, ke_ref), (wv_ref, ve_ref))):
        total = None
        pieces = pieces_of(own_ref, more, index)
        for place, piece in enumerate(pieces):
            rows = piece.shape[0]
            if split:
                left = e_ref[:, 0, :, aligned(starts_ref[place], rows)]
            else:
                left = e_ref[:, 0]
            made = dot(left.reshape(blocks * part, rows), piece)
            total = made if total is None else total + made
        out_ref[0] = total.astype(BF16)


def cross_kv(starts, e_all, wk, wv, more):
    blocks, micro, part, width = e_all.shape
    whole = lambda array: pl.BlockSpec(array.shape, lambda m, s: (0,) * array.ndim)
    out = pl.BlockSpec((1, blocks * part, width), lambda m, s: (m, 0, 0))
    return pl.pallas_call(
        functools.partial(cross_kv_kernel, len(more)),
        grid_spec=pltpu.PrefetchScalarGridSpec(
            num_scalar_prefetch=1,
            grid=(micro,),
            in_specs=[pl.BlockSpec((blocks, 1, part, width), lambda m, s: (0, m, 0, 0))]
            + [whole(wk), whole(wv)]
            + [pl.BlockSpec((2,) + array.shape[1:], lambda m, s: (0, 0, 0)) for array in more],
            out_specs=[out, out],
        ),
        out_shape=[jax.ShapeDtypeStruct((micro, blocks * part, width), BF16)] * 2,
        compiler_params=params(VMEM_MOST),
        cost_estimate=cost(8),
        name="cross_kv",
    )(starts, e_all, wk, wv, *more)


def mid_forward_kernel(split, starts_ref, o1_ref, x_ref, gain_ref, ke_ref, ve_ref, wo, wq, wc, *refs):
    more, last = refs[:split], refs[split : 2 * split]
    left_ref, x1_ref, q2_ref, x2_ref, n3_ref, sent_ref, o1c_ref, n2_ref, o2_ref = refs[2 * split :]
    heads, rows, _ = o1_ref.shape
    width = x_ref.shape[-1]
    for pair in range(heads // 2):
        at = pair * 128
        low, high = pair_up(o1_ref[2 * pair].astype(F32), o1_ref[2 * pair + 1].astype(F32))
        o1c_ref[0:rows, at : at + 128] = low.astype(BF16)
        o1c_ref[rows : 2 * rows, at : at + 128] = high.astype(BF16)
    x = x_ref[...].astype(F32).reshape(2 * rows, width)
    x1 = x + times(o1c_ref, starts_ref, pieces_of(wo, more, 0))
    x1_ref[...] = x1
    n2_ref[...] = norm_rows(x1, gain_ref[1:2]).astype(BF16)
    q2_ref[...] = times(n2_ref, starts_ref, pieces_of(wq, more, 1)).astype(BF16)
    for micro in range(2):
        for pair in range(heads // 2):
            at = pair * 128
            span = slice(micro * rows, (micro + 1) * rows)
            q = q2_ref[span, at : at + 128]
            both = jnp.concatenate([keep_half(q, 0), keep_half(q, 1)], axis=0)
            p = softmax_rows(dot_t(both, ke_ref[micro, :, at : at + 128]))
            o = dot(p.astype(BF16), ve_ref[micro, :, at : at + 128])
            o2_ref[span, at : at + 128] = jnp.where(
                low_lanes(rows), o[:rows], o[rows:]
            ).astype(BF16)
    x2 = x1 + times(o2_ref, starts_ref, pieces_of(wc, last, 0))
    x2_ref[...] = x2
    n3_ref[...] = norm_rows(x2, gain_ref[2:3]).astype(BF16)
    left_ref[0] = o2_ref[...]
    left_ref[1] = n2_ref[...]
    left_ref[2] = o1c_ref[...]
    if split:
        span = sent_ref.shape[2]
        for kind in range(3):
            sent_ref[kind] = left_ref[kind, :, aligned(span - starts_ref[0], span)]


def cross_backward_kernel(
    split, starts_ref, slots_ref, g_ref, dn3_ref, more_ref, x2_ref, gain_ref, q2_ref, ke_ref, ve_ref,
    wc, *refs
):
    more = refs[:split]
    right_ref, gx2_ref, keep_ref, send_ref, dc_ref, back_ref, do2_ref = refs[split:]
    blocks, micros, part = keep_ref.shape[1:4]
    tokens, width = x2_ref.shape
    rows = tokens // micros
    pairs = width // 128
    even = slots_ref[pairs] == 0
    dn3 = dn3_ref[...] + more_ref[...].astype(F32)
    back, dc_ref[...] = norm_back(x2_ref[...], gain_ref[2:3], dn3)
    gx2 = g_ref[...].astype(F32) + back
    gx2_ref[...] = gx2
    gx2b = gx2.astype(BF16)
    right_ref[:, 0:width] = gx2b
    times_back(back_ref, starts_ref, [(gx2b, pieces_of(wc, more, 0))])
    do2_ref[...] = back_ref[...].astype(BF16)
    for micro in range(micros):
        for pair in range(pairs):
            at = pair * 128
            span = slice(micro * rows, (micro + 1) * rows)
            q = q2_ref[span, at : at + 128]
            do = do2_ref[span, at : at + 128]
            q = jnp.concatenate([keep_half(q, 0), keep_half(q, 1)], axis=0)
            do = jnp.concatenate([keep_half(do, 0), keep_half(do, 1)], axis=0)
            k = ke_ref[micro, :, at : at + 128]
            v = ve_ref[micro, :, at : at + 128]
            p = softmax_rows(dot_t(q, k))
            dp = dot_t(do, v)
            ds = (p * (dp - jnp.sum(p * dp, axis=-1, keepdims=True))).astype(BF16)
            dq = dot(ds, k)
            right_ref[span, width + at : width + at + 128] = jnp.where(
                low_lanes(rows), dq[:rows], dq[rows:]
            ).astype(BF16)
            low, high = pair_up(t_dot(ds, q), t_dot(p.astype(BF16), do))
            kept, sent = jnp.where(even, low, high), jnp.where(even, high, low)
            slot = slots_ref[pair]
            keep_ref[slot, :, micro] = kept.astype(BF16).reshape(blocks, part, 128)
            send_ref[slot, :, micro] = sent.astype(BF16).reshape(blocks, part, 128)


def mid_backward_kernel(split, starts_ref, right_ref, gx2_ref, x1_ref, gain_ref, wo, wq, *refs):
    more = refs[:split]
    gx1_ref, low_ref, do1_ref, dc_ref, back_ref = refs[split:]
    heads, rows, _ = do1_ref.shape
    width = x1_ref.shape[-1]
    times_back(back_ref, starts_ref, [(right_ref[:, width:], pieces_of(wq, more, 1))])
    back, dc_ref[...] = norm_back(x1_ref[...], gain_ref[1:2], back_ref[...])
    gx1 = gx2_ref[...] + back
    gx1_ref[...] = gx1
    gx1b = gx1.astype(BF16)
    low_ref[...] = gx1b
    times_back(back_ref, starts_ref, [(gx1b, pieces_of(wo, more, 0))])
    for pair in range(heads // 2):
        at = pair * 128
        do1 = back_ref[:, at : at + 128].astype(BF16).astype(F32)
        low, high = pair_up(do1[:rows], do1[rows:])
        do1_ref[2 * pair] = low.astype(BF16)
        do1_ref[2 * pair + 1] = high.astype(BF16)


def input_grad_kernel(split, starts_ref, d_ref, x_ref, gain_ref, gx1_ref, wq, wk, wv, *refs):
    more = refs[:split]
    out_ref, dc_ref, all_ref, back_ref = refs[split:]
    heads, rows, _ = d_ref.shape
    width = x_ref.shape[-1]
    for kind in range(3):
        for pair in range(heads // 2):
            lanes = slice(kind * 128, (kind + 1) * 128)
            low, high = pair_up(
                d_ref[2 * pair, :, lanes].astype(F32), d_ref[2 * pair + 1, :, lanes].astype(F32)
            )
            at = kind * width + pair * 128
            all_ref[0:rows, at : at + 128] = low.astype(BF16)
            all_ref[rows : 2 * rows, at : at + 128] = high.astype(BF16)
    terms = [
        (all_ref[:, kind * width : (kind + 1) * width], pieces_of(own, more, kind))
        for kind, own in enumerate((wq, wk, wv))
    ]
    times_back(back_ref, starts_ref, terms)
    x = x_ref[...].astype(F32).reshape(2 * rows, width)
    back, dc = norm_back(x, gain_ref[0:1], back_ref[...])
    dc_ref[...] = dc
    out_ref[...] = gx1_ref[...] + back


def encoder_grad_kernel(split, starts_ref, d_ref, wk, wv, *refs):
    more = refs[:split]
    out_ref, k_ref, v_ref = refs[split:]
    for pair in range(d_ref.shape[0] // 2):
        at = pair * 128
        low, high = pair_up(d_ref[2 * pair].astype(F32), d_ref[2 * pair + 1].astype(F32))
        k_ref[:, at : at + 128] = low.astype(BF16)
        v_ref[:, at : at + 128] = high.astype(BF16)
    terms = [(k_ref[...], pieces_of(wk, more, 0)), (v_ref[...], pieces_of(wv, more, 1))]
    times_back(out_ref, starts_ref, terms)


def cross_head_weight_kernel(e_ref, d_ref, out_ref):
    blocks, micro, part, width = e_ref.shape
    shards, span, _ = out_ref.shape
    for shard in range(shards):
        left = e_ref[:, :, :, shard * span : (shard + 1) * span]
        left = left.reshape(blocks * micro * part, span)
        out_ref[shard] = t_dot(left, d_ref[...]).astype(BF16)


def dense_kernel(split, starts_ref, n_ref, g_ref, wg, wu, wd_ref, *refs):
    more = refs[:split]
    back_ref, y_ref, ylow_ref, d_ref, dlow_ref = refs[split:]
    hidden = wd_ref.shape[0]
    gate, up = pieces_of(wg, more, 0), pieces_of(wu, more, 1)
    a = times(n_ref, starts_ref, gate)
    b = times(n_ref, starts_ref, up)
    scale = 0.7978845608028654
    cubed = 0.044715
    inner = jnp.tanh(scale * (a + cubed * (a * a * a)))
    gelu = 0.5 * a * (1.0 + inner)
    slope = 0.5 * (1.0 + inner) + 0.5 * a * (1.0 - inner * inner) * (
        scale * (1.0 + 3.0 * cubed * (a * a))
    )
    hid = (gelu * b).astype(BF16)
    dh = dot_t(g_ref[...], wd_ref[...])
    da = (dh * b * slope).astype(BF16)
    db = (dh * gelu).astype(BF16)
    times_back(d_ref, starts_ref, [(da, gate), (db, up)])
    dlow_ref[...] = d_ref[...].astype(BF16)
    y = dot(hid, wd_ref[...])
    y_ref[...] = y
    ylow_ref[...] = y.astype(BF16)
    back_ref[:, 0:hidden] = da
    back_ref[:, hidden : 2 * hidden] = db
    back_ref[:, 2 * hidden : 3 * hidden] = hid
    if more:
        shard, other = starts_ref[len(more) + 1], 1 - starts_ref[len(more) + 2]
        put_features(back_ref, 3 * hidden, n_ref, g_ref, shard, other)


def put_features(out_ref, at, n_ref, g_ref, shard, core):
    quarter = n_ref.shape[1] // 4
    for side, place in enumerate((2 * shard + core, 2 * (1 - shard) + core)):
        lanes = slice(at + side * quarter, at + (side + 1) * quarter)
        out_ref[:, lanes] = n_ref[:, aligned(place * quarter, quarter)]
    lanes = slice(at + 2 * quarter, at + 4 * quarter)
    out_ref[:, lanes] = g_ref[:, aligned(core * 2 * quarter, 2 * quarter)]


def dense_layer(starts, n, g, wg, wu, wd, more, step):
    count, width = n.shape
    hidden = wd.shape[0]
    which = starts.shape[0] - 2
    back = 3 * hidden + (width if more else 0)
    row = lambda size: pl.BlockSpec((step, size), lambda i, s: (i, 0))
    whole = lambda array: pl.BlockSpec(array.shape, lambda i, s: (0,) * array.ndim)
    column = pl.BlockSpec((wg.shape[0], hidden), lambda i, s: (0, s[which]))
    made = lambda size, kind: jax.ShapeDtypeStruct((count, size), kind)
    return pl.pallas_call(
        functools.partial(dense_kernel, len(more)),
        grid_spec=pltpu.PrefetchScalarGridSpec(
            num_scalar_prefetch=1,
            grid=(count // step,),
            in_specs=[row(width), row(width), column, column, whole(wd)]
            + [whole(array) for array in more],
            out_specs=[row(back)] + [row(width)] * 4,
        ),
        out_shape=[made(back, BF16)]
        + [made(width, F32), made(width, BF16), made(width, F32), made(width, BF16)],
        compiler_params=params(),
        cost_estimate=cost(13),
        name="dense_layer",
    )(starts, n, g, wg, wu, wd, *more)


def put_chunk(ref, slot, at, value):
    rows, width = value.shape
    for block in range(width // 128):
        ref[slot, at + block * rows : at + (block + 1) * rows, :] = value[
            :, block * 128 : (block + 1) * 128
        ].astype(BF16)


def take_chunk(ref, slot, at, rows, width):
    return jnp.concatenate(
        [
            ref[slot, at + block * rows : at + (block + 1) * rows, :].astype(F32)
            for block in range(width // 128)
        ],
        axis=1,
    )


def put_all(scratch_ref, first, count, chip, chunk_refs, at, width, masks):
    slots = [(ref, slot) for ref in chunk_refs for slot in range(ref.shape[0])]
    rows = count // len(slots)
    for (ref, slot), mask in zip(slots, masks):
        chunk = scratch_ref[aligned(first + (chip ^ mask) * rows, rows), :width]
        put_chunk(ref, slot, at, chunk)


def dense_weight_kernel(
    x_masks, z_masks, where_ref, n0_ref, n1_ref, g0_ref, g1_ref, own0_ref, own1_ref, mate0_ref, mate1_ref, keep_ref,
    send_ref, down_keep_ref, down_send_ref, far_keep_ref, far_send_ref, scratch_ref, left_ref
):
    tokens, width = n0_ref.shape
    hidden = (own0_ref.shape[1] - width) // 3
    quarter = width // 4
    at = keep_ref.shape[1] // 2
    core, shard, chip = where_ref[0], where_ref[1], where_ref[2]
    put_features(left_ref.at[:tokens], 0, n0_ref, g0_ref, shard, core)
    put_features(left_ref.at[tokens : 2 * tokens], 0, n1_ref, g1_ref, shard, core)
    left_ref[2 * tokens : 3 * tokens, :] = mate0_ref[:, 3 * hidden :]
    left_ref[3 * tokens :, :] = mate1_ref[:, 3 * hidden :]

    def whole(kind):
        span = slice(kind * hidden, (kind + 1) * hidden)
        refs = (own0_ref, own1_ref, mate0_ref, mate1_ref)
        return jnp.concatenate([ref[:, span] for ref in refs], axis=0)

    for kind in range(2):
        right = whole(kind)
        for side, (masks, refs) in enumerate(
            ((z_masks, (keep_ref, send_ref)), (x_masks, (far_keep_ref, far_send_ref)))
        ):
            value = t_dot(left_ref[:, side * quarter : (side + 1) * quarter], right)
            scratch_ref[:quarter, :hidden] = value
            put_all(scratch_ref, 0, quarter, chip, refs, kind * at, hidden, masks)
    value = t_dot(whole(2), left_ref[:, 2 * quarter :])
    scratch_ref[:, : 2 * quarter] = value
    refs = (down_keep_ref, down_send_ref)
    put_all(scratch_ref, 0, hidden, chip, refs, 0, 2 * quarter, x_masks)


def token_weight_kernel(
    masks, where_ref, left_ref, left_more_ref, right_ref, right_more_ref, last_ref, last_more_ref,
    mine_ref, mate_ref, scratch_ref
):
    kinds, _, span = left_more_ref.shape
    width = last_ref.shape[1]
    core, shard, chip = where_ref[0], where_ref[1], where_ref[2]
    half = span // 2
    at = half // len(masks) * width // 128
    for kind in range(kinds):
        lanes = slice(kind * width, (kind + 1) * width)
        left = [left_ref[kind, :, aligned(shard * span, span)], left_more_ref[kind]]
        if kind < kinds - 1:
            right = [right_ref[:, lanes], right_more_ref[:, lanes]]
        else:
            right = [last_ref[...], last_more_ref[...]]
        scratch_ref[...] = t_dot(jnp.concatenate(left, axis=0), jnp.concatenate(right, axis=0))
        for ref, own in ((mine_ref, core), (mate_ref, 1 - core)):
            put_all(scratch_ref, own * half, half, chip, (ref,), kind * at, width, masks)


def chunk_weights(kernel, where, operands, counts, slots, scratches, length, name):
    shapes = []
    for count in counts:
        shapes += [jax.ShapeDtypeStruct((slots, count, 128), BF16)] * 2
    return pl.pallas_call(
        kernel,
        out_shape=shapes,
        in_specs=[smem()] + [vmem()] * len(operands),
        out_specs=[vmem()] * len(shapes),
        scratch_shapes=scratches,
        compiler_params=params(),
        cost_estimate=cost(length),
        name=name,
    )(where, *operands)


def head_rows(in_ref, at, rows, outs):
    for pair in range(in_ref.shape[0] // 2):
        lanes = slice(pair * 128, (pair + 1) * 128)
        first = in_ref[2 * pair, at : at + rows, :].astype(F32)
        second = in_ref[2 * pair + 1, at : at + rows, :].astype(F32)
        for (out_ref, place), value in zip(outs, pair_up(first, second)):
            out_ref[place, lanes] = value


def head_spread(in_ref, at, q_ref, k_ref, v_ref):
    span = q_ref.shape[0]
    half = span // 2
    head_rows(in_ref, at, span, ((q_ref, slice(None)), (k_ref, slice(None))))
    head_rows(in_ref, at + span, half, ((v_ref, slice(0, half)), (v_ref, slice(half, span))))


def spread_kernel(where_ref, in_ref, gate_ref, up_ref, down_ref, q_ref, k_ref, v_ref, *out_refs):
    shard = where_ref[1]
    hidden = gate_ref.shape[3] // 2
    rows = gate_ref.shape[2] // 2
    at = rows * hidden // 128
    tall = down_ref.shape[0] // 2
    half = down_ref.shape[1] // 2
    span = q_ref.shape[0]
    kinds = len(out_refs) - 2
    width = out_refs[0].shape[3]
    base = 6 * at + 3 * span // 2
    step = rows * width // 128
    for piece in range(4):
        chip, core = piece // 2, piece % 2
        place = slice(chip * rows, (chip + 1) * rows)
        for side, start in enumerate((0, 4 * at)):
            lanes = aligned((shard ^ side) * hidden, hidden)
            for kind, out_ref in enumerate((gate_ref, up_ref)):
                chunk = take_chunk(in_ref, piece, start + kind * at, rows, hidden)
                out_ref[core, 0, place, lanes] = chunk
        chunk = take_chunk(in_ref, piece, 2 * at, tall, half)
        down_ref[chip * tall : (chip + 1) * tall, core * half : (core + 1) * half] = chunk
        for kind in range(kinds):
            chunk = take_chunk(in_ref, piece, base + kind * step, rows, width)
            out_refs[kind][core, 0, place, :] = chunk
    head_spread(in_ref, 6 * at, q_ref, k_ref, v_ref)
    k_ref, v_ref = out_refs[kinds:]
    head_rows(in_ref, base + kinds * step, span, ((k_ref, slice(None)), (v_ref, slice(None))))


def spread(where, pieces, outs):
    count, total, _ = pieces.shape
    steps = count // 4
    specs, shapes = [], []
    for (rows, cols), kind in outs:
        if kind == "core":
            shapes.append((2, steps, rows // (2 * steps), cols))
            block = (2, 1, rows // (2 * steps), cols)
            specs.append(pl.BlockSpec(block, lambda q, where: (0, q, 0, 0)))
        elif kind == "chip":
            shapes.append((rows, cols))
            specs.append(pl.BlockSpec((rows // steps, cols), lambda q, where: (q, 0)))
        else:
            shapes.append((rows, cols))
            specs.append(pl.BlockSpec((rows, cols // steps), lambda q, where: (0, q)))
    made = pl.pallas_call(
        spread_kernel,
        grid_spec=pltpu.PrefetchScalarGridSpec(
            num_scalar_prefetch=1,
            grid=(steps,),
            in_specs=[pl.BlockSpec((4, total, 128), lambda q, where: (q, 0, 0))],
            out_specs=specs,
        ),
        out_shape=[jax.ShapeDtypeStruct(shape, F32) for shape in shapes],
        compiler_params=params(VMEM_MOST),
        cost_estimate=cost(20),
        name="spread",
    )(where, pieces)
    return [array.reshape(shape) for array, (shape, _) in zip(made, outs)]


def plain_head_kernel(in_ref, *out_refs):
    span = out_refs[0].shape[0]
    if len(out_refs) == 3:
        head_spread(in_ref, 0, *out_refs)
    else:
        head_rows(in_ref, 0, span, [(out_ref, slice(None)) for out_ref in out_refs])


def plain_head_spread(pieces, span, width, kinds):
    return pl.pallas_call(
        plain_head_kernel,
        out_shape=[jax.ShapeDtypeStruct((span, width), F32)] * kinds,
        in_specs=[vmem()],
        out_specs=[vmem()] * kinds,
        compiler_params=params(),
        name="plain_head_spread",
    )(pieces)


def per_device(
    inputs,
    encoded,
    cotangent,
    doc_ids,
    buckets,
    gain_self,
    query_self,
    key_self,
    value_self,
    output_self,
    position_bias,
    gain_cross,
    query_cross,
    key_cross,
    value_cross,
    output_cross,
    gain_dense,
    dense_gate,
    dense_up,
    dense_down,
):
    micro_count, _, rows, width = inputs.shape
    part = encoded.shape[2]
    heads = position_bias.shape[1]
    dp, fs = lax.axis_size("dp"), lax.axis_size("fsdp")
    me, shard = lax.axis_index("dp"), lax.axis_index("fsdp")
    core, chips = me % 2, dp // 2
    length = rows * dp
    tokens = micro_count * rows
    copies = dp // heads
    head = me // copies
    span = width // fs
    half = span // 2
    hidden = dense_down.shape[0]
    chip_bits = [1 << place for place in range(1, dp.bit_length() - 1)]
    x_order, z_order = chip_bits, chip_bits[1:] + chip_bits[:1]
    paired = fs == 2
    chunked = paired and half % (16 * chips) == 0 and hidden % (16 * chips) == 0
    chunked = chunked and hidden % 128 == 0 and dp == heads and dp % 4 == 0

    def chip_of(j):
        last = len(x_order) - 1
        return sum(((j // bit) % 2) << (last - place) for place, bit in enumerate(x_order))

    def swap_dp(values, bit):
        return lax.ppermute(values, "dp", [(j, j ^ bit) for j in range(dp)])

    def swap_fs(values):
        return lax.ppermute(values, "fsdp", [(j, 1 - j) for j in range(2)])

    def after(values, *others):
        return lax.optimization_barrier((values, *others))[0]

    def half_rows(values):
        return jnp.stack([lax.dynamic_slice_in_dim(w, core * half, half, axis=0) for w in values])

    def both_halves(sent):
        got = swap_fs(sent)
        return got, swap_dp(got, 1)

    def quarter(bit):
        return 2 * ((me // bit) % 2) + core

    def quarter_starts(bit):
        rows = [(1 - shard) * span + (quarter(bit) ^ more) * (half // 2) for more in (0, 2, 1, 3)]
        return jnp.stack([shard * span] + rows).astype(jnp.int32)

    def gather_rows(values):
        return [lax.all_gather(w, "fsdp", axis=0, tiled=True) for w in values]

    def both_tokens(values):
        if paired:
            return jnp.concatenate([values, swap_fs(values)], axis=0)
        return lax.all_gather(values, "fsdp", axis=0, tiled=True)

    def reduce_chips(kept, got, order=x_order, marks=()):
        total = kept.astype(F32) + got.astype(F32)
        for place, bit in enumerate(order[1:]):
            count = total.shape[0] // 2
            sent, total = total[count:].astype(BF16), total[:count]
            if place < len(marks):
                sent = after(sent, marks[place])
            total = total + swap_dp(sent, bit).astype(F32)
        return total.astype(BF16)

    x, g, e = inputs[:, 0], cotangent[:, 0], encoded[:, 0]

    low, offsets = [x], [0]
    for bit in reversed(chip_bits[1:]):
        low = low + [swap_dp(piece, bit) for piece in low]
        offsets = offsets + [offset | bit for offset in offsets]
    high = [swap_dp(piece, 2) for piece in low]
    near, far = jnp.stack(low), jnp.stack(high)
    offsets = [offset ^ more for more in (0, 2, 1, 3) for offset in offsets]
    source = me ^ jnp.array(offsets, jnp.int32)
    e_all = lax.all_gather(e, "dp", axis=0)

    gains = jnp.stack([gain_self, gain_cross, gain_dense])
    own_head = lambda w: lax.dynamic_slice_in_dim(w, head * 64, 64, axis=1)
    if paired:
        pad = jnp.pad(position_bias.reshape(1, -1), ((0, 0), (0, span - position_bias.size)))
        small = jnp.concatenate([gains, pad], axis=0)
        small_got = swap_fs(small)
        head_pack = jnp.concatenate([own_head(w) for w in (query_self, key_self, value_self)], 1)
        head_got = swap_fs(head_pack)
        first, second = (
            jnp.where(shard == which, mine, got)
            for which, mine, got in ((0, small, small_got), (1, small, small_got))
        )
        gains = jnp.concatenate([first[:3], second[:3]], axis=1)
        bias_all = jnp.concatenate(
            [piece[3, : position_bias.size].reshape(position_bias.shape) for piece in (first, second)]
        )
        other = (1 - shard) * span
        half_starts = jnp.stack([shard * span, other + core * half, other + (1 - core) * half])
        half_starts = half_starts.astype(jnp.int32)
        near_bit, dense_bit = chip_bits[0], chip_bits[1]
        starts = quarter_starts(near_bit)
        kv_own = (key_cross, value_cross)
        near_own = (output_self, query_cross, output_cross)
        near_sent, theirs = pack(
            jnp.stack([quarter(near_bit), quarter(dense_bit), 1 - shard]).astype(jnp.int32),
            kv_own + near_own,
            (dense_gate, dense_up),
            half // 2,
            hidden,
        )
        near_got = swap_fs(near_sent)
        near_far = swap_dp(near_got, near_bit)
        dense_got = swap_fs(after(theirs, near_got))
        dense_own = (dense_gate, dense_up)
        which = jnp.stack([shard, core]).astype(jnp.int32)
        dense_starts = jnp.concatenate([quarter_starts(dense_bit), which])
    else:
        gains = lax.all_gather(gains, "fsdp", axis=1, tiled=True)
        bias_all = lax.all_gather(position_bias, "fsdp", axis=0, tiled=True)
        kv_own, kv_more = gather_rows((key_cross, value_cross)), ()
        near_own, near_more = gather_rows((output_self, query_cross, output_cross)), ()
        first_own, first_more = gather_rows((query_self, key_self, value_self)), ()
        half_starts = jnp.zeros((1,), jnp.int32)
        head_whole = jnp.concatenate([own_head(w) for w in first_own], axis=1)
        dense_own = [
            lax.all_to_all(w, "fsdp", 1, 0, tiled=True) for w in (dense_gate, dense_up)
        ]
        dense_more = ()
        starts = jnp.zeros((1,), jnp.int32)
        dense_starts = jnp.zeros((3,), jnp.int32)
        g_group = both_tokens(g.reshape(tokens, width))
    gains, bias_all = gains.astype(F32), bias_all.astype(F32)
    marks = jnp.arange(bias_all.shape[0], dtype=jnp.int32)
    edges = jnp.sum((buckets[:, None] < marks[None, :]).astype(jnp.int32), axis=0)
    bias_values = lax.dynamic_slice_in_dim(bias_all, head, 1, axis=1)[:, 0]
    table = bias_table(edges, bias_values, length)
    x_groups = [near, far, swap_dp(near, 1), swap_dp(after(far, table), 1)]
    doc_row = jnp.broadcast_to(doc_ids[:, 0, :, None], (micro_count, dp, rows))
    doc_row = doc_row.reshape(micro_count, length)
    doc_col = doc_row[:, :, None]

    if paired:
        head_got = after(head_got, *x_groups[2:])
        head_whole = jnp.where(
            shard == 0,
            jnp.concatenate([head_pack, head_got]),
            jnp.concatenate([head_got, head_pack]),
        )
    head_w = jnp.concatenate(
        [head_whole[:, at : at + 64] for at in (0, 0, 64, 64, 128, 128)], axis=1
    )

    n_all, qkv, mixed = pl.pallas_call(
        functools.partial(self_forward_kernel, len(x_groups)),
        out_shape=[
            jax.ShapeDtypeStruct((dp, micro_count, rows, width), BF16),
            jax.ShapeDtypeStruct((length, 384), BF16),
            jax.ShapeDtypeStruct((length, 128), BF16),
        ],
        in_specs=[smem()] + [vmem()] * (len(x_groups) + 5),
        out_specs=[vmem()] * 3,
        compiler_params=params(),
        cost_estimate=cost(12),
        name="self_forward",
    )(source, *x_groups, gains[0:1], head_w, table, doc_row, doc_col)
    if paired:
        mixed = after(mixed, dense_got)
    o1_heads = lax.all_to_all(mixed.reshape(dp, rows, 128), "dp", 0, 0, tiled=True)[::copies]

    if paired:
        near_more = (near_got, near_far, swap_dp(near_got, 1), swap_dp(after(near_far, mixed), 1))
        kv_more = near_more
        dense_far = swap_dp(after(dense_got, mixed), dense_bit)
    ke, ve = cross_kv(starts, e_all, *kv_own, kv_more)

    row32 = jax.ShapeDtypeStruct((tokens, width), F32)
    row16 = jax.ShapeDtypeStruct((tokens, width), BF16)
    left, x1, q2, x2, n3, left_sent = pl.pallas_call(
        functools.partial(mid_forward_kernel, len(near_more)),
        grid=(1,),
        out_shape=[
            jax.ShapeDtypeStruct((3, tokens, width), BF16),
            row32,
            row16,
            row32,
            row16,
            jax.ShapeDtypeStruct((3, tokens, span), BF16),
        ],
        in_specs=[smem()] + [vmem()] * 8 + part_specs(near_more, 2, 1) + part_specs(near_more, 1, 4),
        out_specs=[vmem()] * 6,
        scratch_shapes=[pltpu.VMEM((tokens, width), BF16)] * 3,
        compiler_params=params(VMEM_MOST),
        cost_estimate=cost(12),
        name="mid_forward",
    )(starts, o1_heads, x, gains, ke, ve, *near_own, *near_more, *near_more)

    if paired:
        dense_more = (
            dense_got,
            dense_far,
            swap_dp(after(dense_got, ke), 1),
            swap_dp(after(dense_far, ke), 1),
        )
        g_rows = g.reshape(tokens, width)
        g_got = swap_fs(after(g_rows, dense_got))
        n_got = swap_fs(n3)
        back, y32, _, dn3, _ = dense_layer(
            dense_starts, n3, g_rows, *dense_own, dense_down, dense_more, tokens
        )
        back_mate = swap_dp(back, 1)
        back_got, _, y16, _, d16 = dense_layer(
            dense_starts,
            after(n_got, dn3),
            g_got,
            *dense_own,
            dense_down,
            dense_more,
            tokens,
        )
        back_got_mate = swap_dp(back_got, 1)
        dn3_more = swap_fs(after(d16, back_mate))
        left_got = swap_fs(after(left_sent, dn3_more))
    else:
        n_group = both_tokens(n3)
        back, _, y16, _, d16 = dense_layer(
            dense_starts, n_group, g_group, *dense_own, dense_down, dense_more, tokens
        )
        dn3 = jnp.zeros((tokens, width), F32)
        dn3_more = lax.psum_scatter(d16, "fsdp", scatter_dimension=0, tiled=True)
        dense_out = lax.psum_scatter(y16, "fsdp", scatter_dimension=0, tiled=True).astype(F32)
        outputs = (x2 + dense_out).astype(BF16)

    if chunked:
        where = jnp.stack([core, shard, me // 2]).astype(jnp.int32)
        masks = [
            [
                sum(((slot >> (len(order) - 1 - at)) & 1) * (bit // 2) for at, bit in enumerate(order))
                for slot in range(chips)
            ]
            for order in (x_order, z_order)
        ]
        own_kept, own_sent, down_kept, down_sent, far_kept, far_sent = chunk_weights(
            functools.partial(dense_weight_kernel, *masks),
            where,
            (after(n3, dn3_more), n_got, g_rows, g_got, back, back_got, back_mate, back_got_mate),
            (
                span // chips * hidden // 128,
                hidden // chips * width // 256,
                span // chips * hidden // 128,
            ),
            chips // 2,
            [
                pltpu.VMEM((max(hidden, half), max(hidden, width // 2)), F32),
                pltpu.VMEM((4 * tokens, width), BF16),
            ],
            7,
            "dense_weight",
        )
        dn3_more = after(dn3_more, own_sent)
        own_got, down_got = swap_dp(own_sent, z_order[0]), swap_dp(down_sent, x_order[0])

    straight = chunked
    if straight:
        slots = jnp.append(chip_of(me ^ (2 * jnp.arange(heads // 2))), core).astype(jnp.int32)
    else:
        slots = jnp.append(jnp.arange(heads // 2), 0).astype(jnp.int32)
    g_rows = g.reshape(tokens, width)
    right, gx2, dkv_kept, dkv_sent, dc_dense = pl.pallas_call(
        functools.partial(cross_backward_kernel, len(near_more)),
        grid=(1,),
        out_shape=[
            jax.ShapeDtypeStruct((tokens, 2 * width), BF16),
            row32,
            jax.ShapeDtypeStruct((heads // 2, dp, micro_count, part, 128), BF16),
            jax.ShapeDtypeStruct((heads // 2, dp, micro_count, part, 128), BF16),
            jax.ShapeDtypeStruct((1, width), F32),
        ],
        in_specs=[smem()] * 2 + [vmem()] * 9 + part_specs(near_more, 1, 4),
        out_specs=[vmem()] * 5,
        scratch_shapes=[pltpu.VMEM((tokens, width), F32), pltpu.VMEM((tokens, width), BF16)],
        compiler_params=params(),
        cost_estimate=cost(15),
        name="cross_backward",
    )(starts, slots, g_rows, dn3, dn3_more, x2, gains, q2, ke, ve, near_own[2], *near_more)
    if chunked:
        gx2 = after(gx2, own_got, down_got, left_got)
    gx1, last, do1_heads, dc_cross = pl.pallas_call(
        functools.partial(mid_backward_kernel, len(near_more)),
        grid=(1,),
        out_shape=[
            row32,
            row16,
            jax.ShapeDtypeStruct((heads, rows, 128), BF16),
            jax.ShapeDtypeStruct((1, width), F32),
        ],
        in_specs=[smem()] + [vmem()] * 6 + part_specs(near_more, 2, 1),
        out_specs=[vmem()] * 4,
        scratch_shapes=[pltpu.VMEM((tokens, width), F32)],
        compiler_params=params(),
        cost_estimate=cost(6),
        name="mid_backward",
    )(starts, right, gx2, x1, gains, *near_own[:2], *near_more)
    do1 = lax.all_to_all(
        jnp.repeat(do1_heads, copies, axis=0) if copies > 1 else do1_heads, "dp", 0, 0, tiled=True
    ).reshape(length, 128)

    if chunked:
        right_got, last_got = swap_fs(after(right, do1_heads)), swap_fs(last)
        far_got = swap_fs(after(far_sent, right_got, last_got))
        if straight:
            dkv_got = swap_dp(after(dkv_sent, do1_heads), 1)
            dkv_total = dkv_kept.astype(F32) + dkv_got.astype(F32)
            dkv_far = swap_dp(dkv_total[chips // 2 :].astype(BF16), x_order[0])
        token_left = after(left, do1)
        do1 = after(do1, dkv_got)

    dqkv, table_grad = pl.pallas_call(
        self_backward_kernel,
        out_shape=[
            jax.ShapeDtypeStruct((length, 384), BF16),
            jax.ShapeDtypeStruct((TILE, length), F32),
        ],
        in_specs=[vmem()] * 5,
        out_specs=[vmem()] * 2,
        scratch_shapes=[pltpu.VMEM((length, 128), F32), pltpu.VMEM((length, 128), F32)],
        compiler_params=params(),
        cost_estimate=cost(10),
        name="self_backward",
    )(qkv, do1, table, doc_row, doc_col)
    if chunked:
        dqkv = after(dqkv, right_got, last_got)
        far_x = swap_dp(after(far_got, table_grad, dkv_far), x_order[0])
        far_kept = swap_fs(after(far_kept, table_grad))
    if chunked:
        token_kept, token_sent = chunk_weights(
            functools.partial(token_weight_kernel, masks[1]),
            where,
            (token_left, left_got, right, right_got, last, last_got),
            (3 * half // chips * width // 128,),
            chips,
            [pltpu.VMEM((span, width), F32)],
            6,
            "token_weight",
        )
        token_got = swap_dp(token_sent, 1)
        dqkv = after(dqkv, token_kept)
    head_grad = pl.pallas_call(
        head_weight_kernel,
        out_shape=jax.ShapeDtypeStruct((fs, span * 3 // 2, 128), BF16),
        in_specs=[vmem()] * 2,
        out_specs=vmem(),
        compiler_params=params(),
        cost_estimate=cost(6),
        name="head_weight",
    )(n_all, dqkv)
    def sum_shards(values):
        if paired:
            kept = lax.dynamic_index_in_dim(values, shard, 0)
            sent = lax.dynamic_index_in_dim(values, 1 - shard, 0)
            return (kept.astype(F32) + swap_fs(sent).astype(F32)).astype(BF16)
        return lax.psum_scatter(values, "fsdp", scatter_dimension=0, tiled=True)

    head_sum = sum_shards(head_grad)

    if paired:
        first_own = (query_self, key_self, value_self)
        first_more = both_halves(after(half_rows(first_own), head_sum))
        y16 = swap_fs(after(y16, first_more[0]))
        outputs = (x2 + (y32 + y16.astype(F32))).astype(BF16)
    own_d = lax.all_to_all(dqkv.reshape(dp, rows, 384), "dp", 0, 0, tiled=True)[::copies]
    grad_inputs, dc_one = pl.pallas_call(
        functools.partial(input_grad_kernel, len(first_more)),
        out_shape=[row32, jax.ShapeDtypeStruct((1, width), F32)],
        in_specs=[smem()] + [vmem()] * (7 + len(first_more)),
        out_specs=[vmem()] * 2,
        scratch_shapes=[
            pltpu.VMEM((tokens, 3 * width), BF16),
            pltpu.VMEM((tokens, width), F32),
        ],
        compiler_params=params(),
        cost_estimate=cost(7),
        name="input_grad",
    )(half_starts, own_d, x, gains, gx1, *first_own, *first_more)

    if straight:
        dkv = reduce_chips(dkv_total[: chips // 2], dkv_far).reshape(-1, 128)
    else:
        dkv = jnp.stack([dkv_kept, dkv_sent], axis=1).reshape(heads * copies, -1, 128)
        dkv = lax.psum_scatter(dkv, "dp", scatter_dimension=0, tiled=True)[0]
        bit = 1
        while bit < copies:
            got = swap_dp(dkv, bit)
            dkv = jnp.where(
                (me // bit) % 2 == 0, jnp.concatenate([dkv, got]), jnp.concatenate([got, dkv])
            )
            bit *= 2
    cross_grad = pl.pallas_call(
        cross_head_weight_kernel,
        out_shape=jax.ShapeDtypeStruct((fs, span, 128), BF16),
        in_specs=[vmem()] * 2,
        out_specs=vmem(),
        compiler_params=params(),
        cost_estimate=cost(3),
        name="cross_head_weight",
    )(e_all, dkv)
    cross_sum = sum_shards(cross_grad)
    own_dkv = dkv.reshape(dp, micro_count * part, 128)
    own_dkv = lax.all_to_all(own_dkv, "dp", 0, 0, tiled=True)[::copies]
    grad_encoded = pl.pallas_call(
        functools.partial(encoder_grad_kernel, len(kv_more)),
        grid=(1,),
        out_shape=jax.ShapeDtypeStruct((micro_count * part, width), F32),
        in_specs=[smem()] + [vmem()] * 3 + part_specs(kv_more, 2, 0),
        out_specs=vmem(),
        scratch_shapes=[pltpu.VMEM((micro_count * part, width), BF16)] * 2,
        compiler_params=params(),
        cost_estimate=cost(4),
        name="encoder_grad",
    )(starts, own_dkv, *kv_own, *kv_more)

    if chunked:
        sums = (
            reduce_chips(own_kept, own_got, z_order, (do1, dkv_far)),
            reduce_chips(down_kept, down_got, x_order, (do1, dkv_far)),
            reduce_chips(far_kept, far_x, x_order, (dqkv, head_grad)),
            head_sum,
            reduce_chips(token_kept, token_got, [1] + z_order, (token_kept, dkv_far)),
            cross_sum,
        )
        pieces = lax.all_gather(jnp.concatenate(sums, axis=1), "dp", axis=0, tiled=True)
        square, wide = (span, width), (span, fs * hidden)
        (
            grad_dense_gate,
            grad_dense_up,
            grad_dense_down,
            grad_query_self,
            grad_key_self,
            grad_value_self,
            grad_output_cross,
            grad_query_cross,
            grad_output_self,
            grad_key_cross,
            grad_value_cross,
        ) = spread(
            where,
            pieces,
            [(wide, "core")] * 2
            + [((hidden, width), "chip")]
            + [(square, "head")] * 3
            + [(square, "core")] * 3
            + [(square, "head")] * 2,
        )
    else:

        def all_heads(values, kinds):
            pieces = lax.all_gather(values, "dp", axis=0, tiled=True)[::copies]
            return plain_head_spread(pieces, span, width, kinds)

        grad_query_self, grad_key_self, grad_value_self = all_heads(head_sum, 3)
        grad_key_cross, grad_value_cross = all_heads(cross_sum, 2)
        right = jnp.concatenate([right, last], axis=1)

        def over_dp(values):
            return lax.psum(values.astype(BF16), "dp").astype(F32)

        def over_all(a, b):
            made = t_dot(a, b).astype(BF16)
            return over_dp(lax.psum_scatter(made, "fsdp", scatter_dimension=0, tiled=True))

        grad_output_cross, grad_query_cross, grad_output_self = (
            over_all(left[kind], right[:, kind * width : (kind + 1) * width]) for kind in range(3)
        )
        grad_dense_gate, grad_dense_up = (
            over_dp(
                lax.all_to_all(
                    t_dot(n_group, back[:, kind * hidden : (kind + 1) * hidden]).astype(BF16),
                    "fsdp",
                    0,
                    1,
                    tiled=True,
                )
            )
            for kind in range(2)
        )
        grad_dense_down = over_dp(t_dot(back[:, 2 * hidden :], g_group))

    if chunked:
        table_grad = after(table_grad, first_more[1])
    table_sums = jnp.sum(bucket_sums(edges, table_grad, bias_all.shape[0]), axis=1)
    column = (jnp.arange(heads) == head) & (me % copies == 0)
    bias_row = jnp.where(column[None, :], table_sums[:, None], 0.0).reshape(1, -1)
    bias_row = jnp.pad(bias_row, ((0, 0), (0, width - bias_row.shape[1])))
    sums = jnp.concatenate([dc_one, dc_dense, dc_cross, bias_row], axis=0)
    if paired:
        sums = sums + swap_fs(sums)
        for bit in [1] + chip_bits:
            sums = sums + swap_dp(sums, bit)
    else:
        sums = lax.psum(sums, ("dp", "fsdp"))
    own = lax.dynamic_slice_in_dim(sums[:3], shard * span, span, axis=1)
    grad_bias = sums[3, : bias_all.size].reshape(bias_all.shape)
    grad_bias = lax.dynamic_slice_in_dim(
        grad_bias, shard * position_bias.shape[0], position_bias.shape[0], axis=0
    )
    shape = (micro_count, 1, rows, width)
    return (
        outputs.reshape(shape),
        grad_inputs.reshape(shape),
        grad_encoded.reshape(micro_count, 1, part, width),
        own[0],
        grad_query_self,
        grad_key_self,
        grad_value_self,
        grad_output_self,
        grad_bias,
        own[2],
        grad_query_cross,
        grad_key_cross,
        grad_value_cross,
        grad_output_cross,
        own[1],
        grad_dense_gate,
        grad_dense_up,
        grad_dense_down,
    )


def solution(mesh):
    matrix = P("fsdp", None)
    token = P(None, "fsdp", "dp", None)
    weights = (
        (P("fsdp"),)
        + (matrix,) * 5
        + (P("fsdp"),)
        + (matrix,) * 4
        + (P("fsdp"),)
        + (matrix,) * 3
    )
    return jax.shard_map(
        per_device,
        mesh=mesh,
        in_specs=(token,) * 3 + (P(None, "fsdp", None), P()) + weights,
        out_specs=(token,) * 3 + weights,
        check_vma=False,
    )
```

```python
import functools

import jax
import jax.numpy as jnp
from jax import lax
from jax.experimental import pallas as pl
from jax.experimental.pallas import tpu as pltpu
from jax.sharding import PartitionSpec as P

EPS = 1e-06
NEGATIVE = -1e30
TILE = 256
F32 = jnp.float32
BF16 = jnp.bfloat16
VMEM_LIMIT = 26 * 1024 * 1024
VMEM_MOST = 56 * 1024 * 1024


def vmem():
    return pl.BlockSpec(memory_space=pltpu.VMEM)


def smem():
    return pl.BlockSpec(memory_space=pltpu.SMEM)


def params(limit=VMEM_LIMIT):
    return pltpu.CompilerParams(vmem_limit_bytes=limit)


def cost(microseconds):
    return pl.CostEstimate(
        flops=int(microseconds * 1.15e9),
        bytes_accessed=int(microseconds * 3.69e6),
        transcendentals=0,
    )


def aligned(start, size):
    return pl.ds(pl.multiple_of(start, size), size)


def dot(left, right):
    return jnp.dot(left, right, preferred_element_type=F32)


def dot_t(left, right):
    return lax.dot_general(left, right, (((1,), (1,)), ((), ())), preferred_element_type=F32)


def t_dot(left, right):
    return lax.dot_general(left, right, (((0,), (0,)), ((), ())), preferred_element_type=F32)


def norm_rows(values, gain):
    return values * lax.rsqrt(jnp.mean(values * values, axis=-1, keepdims=True) + EPS) * gain


def norm_back(values, gain, grad):
    r = lax.rsqrt(jnp.mean(values * values, axis=-1, keepdims=True) + EPS)
    scaled = grad * gain
    inner = jnp.mean(scaled * values, axis=-1, keepdims=True)
    back = r * scaled - values * (r * r * r * inner)
    return back, jnp.sum(grad * (values * r), axis=0, keepdims=True)


def low_lanes(rows):
    return lax.broadcasted_iota(jnp.int32, (rows, 128), 1) < 64


def pair_up(first, second):
    lane = low_lanes(first.shape[0])
    low = jnp.where(lane, first, pltpu.roll(second, 64, 1))
    high = jnp.where(lane, pltpu.roll(first, 64, 1), second)
    return low, high


def keep_half(values, half):
    lane = low_lanes(values.shape[0])
    return jnp.where(lane if half == 0 else ~lane, values, jnp.zeros_like(values))


def softmax_rows(scores):
    top = jnp.max(scores, axis=-1, keepdims=True)
    raised = jnp.exp(scores - top)
    return raised * (1.0 / jnp.sum(raised, axis=-1, keepdims=True))


def table_kernel(edge_ref, value_ref, out_ref):
    rows, length = out_ref.shape
    bucket_count = value_ref.shape[0]
    for start in range(0, length, TILE):
        place = (rows, TILE)
        apart = (
            lax.broadcasted_iota(jnp.int32, place, 0)
            - lax.broadcasted_iota(jnp.int32, place, 1)
            + (length - rows - start)
        )
        value = jnp.full(place, value_ref[0], F32)
        for bucket in range(1, bucket_count):
            value = jnp.where(apart >= edge_ref[bucket], value_ref[bucket], value)
        out_ref[:, start : start + TILE] = jnp.where(apart >= 0, value, NEGATIVE)


def bias_table(edges, values, length):
    return pl.pallas_call(
        table_kernel,
        out_shape=jax.ShapeDtypeStruct((TILE, length), F32),
        in_specs=[smem(), smem()],
        out_specs=vmem(),
        cost_estimate=cost(4),
        name="bias_table",
    )(edges, values)


def bucket_kernel(edge_ref, grad_ref, out_ref):
    rows, length = grad_ref.shape
    bucket_count = out_ref.shape[0]
    above = [jnp.zeros((8, TILE), F32) for _ in range(bucket_count)]
    for start in range(0, length, TILE):
        for row in range(0, rows, 8):
            place = (8, TILE)
            apart = (
                lax.broadcasted_iota(jnp.int32, place, 0)
                - lax.broadcasted_iota(jnp.int32, place, 1)
                + (length - rows - start + row)
            )
            tile = grad_ref[row : row + 8, start : start + TILE]
            for bucket in range(bucket_count):
                above[bucket] = above[bucket] + jnp.where(apart >= edge_ref[bucket], tile, 0.0)
    for bucket in range(bucket_count):
        rest = above[bucket + 1] if bucket + 1 < bucket_count else 0.0
        part = jnp.sum(above[bucket] - rest, axis=0, keepdims=True)
        out_ref[bucket : bucket + 1, :] = part[:, :128] + part[:, 128:]


def bucket_sums(edges, grad, bucket_count):
    return pl.pallas_call(
        bucket_kernel,
        out_shape=jax.ShapeDtypeStruct((bucket_count, 128), F32),
        in_specs=[smem(), vmem()],
        out_specs=vmem(),
        cost_estimate=cost(7),
        name="bucket_sums",
    )(edges, grad)


def times(x_ref, starts_ref, pieces):
    if len(pieces) == 1:
        return dot(x_ref[...], pieces[0])
    total = None
    for place, piece in enumerate(pieces):
        rows = piece.shape[0]
        part = dot(x_ref[:, aligned(starts_ref[place], rows)], piece)
        total = part if total is None else total + part
    return total


def times_back(out_ref, starts_ref, terms):
    for place in range(len(terms[0][1])):
        total = sum(dot_t(d, pieces[place]) for d, pieces in terms)
        rows = terms[0][1][place].shape[0]
        if len(terms[0][1]) == 1:
            out_ref[...] = total
        else:
            out_ref[:, aligned(starts_ref[place], rows)] = total


def pack_kernel(counts, where_ref, *refs):
    total = sum(counts)
    first_ref, second_ref = refs[total:]
    for place in range(counts[0]):
        first_ref[place] = refs[place][...]
    for place in range(counts[1]):
        second_ref[place] = refs[counts[0] + place][...]


def pack(where, first, second, rows, cols):
    width = first[0].shape[1]
    counts = (len(first), len(second))
    return pl.pallas_call(
        functools.partial(pack_kernel, counts),
        grid_spec=pltpu.PrefetchScalarGridSpec(
            num_scalar_prefetch=1,
            grid=(1,),
            in_specs=[pl.BlockSpec((rows, width), lambda i, where: (where[0], 0))] * counts[0]
            + [pl.BlockSpec((rows, cols), lambda i, where: (where[1], where[2]))] * counts[1],
            out_specs=[
                pl.BlockSpec((counts[0], rows, width), lambda i, where: (0, 0, 0)),
                pl.BlockSpec((counts[1], rows, cols), lambda i, where: (0, 0, 0)),
            ],
        ),
        out_shape=[
            jax.ShapeDtypeStruct((counts[0], rows, width), BF16),
            jax.ShapeDtypeStruct((counts[1], rows, cols), BF16),
        ],
        compiler_params=params(VMEM_MOST),
        cost_estimate=cost(3),
        name="pack",
    )(where, *first, *second)


def part_specs(arrays, count, index):
    return [
        pl.BlockSpec((count,) + array.shape[1:], lambda *_: (index, 0, 0)) for array in arrays
    ]


def pieces_of(own_ref, more, index):
    return [own_ref[...]] + [ref[index] for ref in more]


def self_scores(q, k, table, doc_col, doc_row):
    scores = dot_t(q, k) + table
    return jnp.where(doc_col == doc_row, scores, NEGATIVE)


def self_forward_kernel(groups, source_ref, *refs):
    x_refs = refs[:groups]
    gain_ref, w_ref, table_ref, doc_row_ref, doc_col_ref, n_ref, qkv_ref, o_ref = refs[groups:]
    count, _, rows, width = x_refs[0].shape
    length = groups * count * rows
    lane = lax.broadcasted_iota(jnp.int32, (rows, 384), 1) % 128 < 64
    together = min(TILE // rows, count)
    for place, x_ref in enumerate(x_refs):
        for first in range(0, count, together):
            parts = []
            for inner in range(first, first + together):
                x = x_ref[inner].astype(F32).reshape(2 * rows, width)
                n = norm_rows(x, gain_ref[...]).astype(BF16)
                n_ref[source_ref[place * count + inner]] = n.reshape(2, rows, width)
                parts.append(n)
            made = dot(jnp.concatenate(parts, axis=0), w_ref[...])
            for inner in range(together):
                at = 2 * rows * inner
                picked = jnp.where(lane, made[at : at + rows], made[at + rows : at + 2 * rows])
                own = source_ref[place * count + first + inner]
                qkv_ref[aligned(own * rows, rows), :] = picked.astype(BF16)
    for block in range(length // TILE):
        start, stop = block * TILE, (block + 1) * TILE
        table = table_ref[:, length - stop :]
        q = qkv_ref[start:stop, 0:128]
        k = qkv_ref[:stop, 128:256]
        v = qkv_ref[:stop, 256:384]
        mixed = []
        for half in range(2):
            scores = self_scores(
                keep_half(q, half),
                k,
                table,
                doc_col_ref[half, start:stop, :],
                doc_row_ref[half : half + 1, :stop],
            )
            mixed.append(dot(softmax_rows(scores).astype(BF16), v))
        o_ref[start:stop, :] = jnp.where(low_lanes(TILE), mixed[0], mixed[1]).astype(BF16)


def self_backward_kernel(
    qkv_ref, do_ref, table_ref, doc_row_ref, doc_col_ref, dqkv_ref, grad_ref, dk_ref, dv_ref
):
    length = qkv_ref.shape[0]
    grad_ref[...] = jnp.zeros_like(grad_ref)
    dk_ref[...] = jnp.zeros_like(dk_ref)
    dv_ref[...] = jnp.zeros_like(dv_ref)
    for block in range(length // TILE):
        start, count = block * TILE, (block + 1) * TILE
        table = table_ref[:, length - count :]
        k = qkv_ref[:count, 128:256]
        v = qkv_ref[:count, 256:384]
        made = []
        for half in range(2):
            q = keep_half(qkv_ref[start:count, 0:128], half)
            do = keep_half(do_ref[start:count, :], half)
            p = softmax_rows(
                self_scores(
                    q,
                    k,
                    table,
                    doc_col_ref[half, start:count, :],
                    doc_row_ref[half : half + 1, :count],
                )
            )
            dp = dot_t(do, v)
            ds = (p * (dp - jnp.sum(p * dp, axis=-1, keepdims=True))).astype(BF16)
            grad_ref[:, length - count :] += ds.astype(F32)
            made.append(dot(ds, k))
            dk_ref[:count, :] += t_dot(ds, q)
            dv_ref[:count, :] += t_dot(p.astype(BF16), do)
        dq = jnp.where(low_lanes(TILE), made[0], made[1])
        dqkv_ref[start:count, 0:128] = dq.astype(BF16)
    dqkv_ref[:, 128:256] = dk_ref[...].astype(BF16)
    dqkv_ref[:, 256:384] = dv_ref[...].astype(BF16)


def head_weight_kernel(n_ref, d_ref, out_ref):
    blocks, _, rows, width = n_ref.shape
    shards = out_ref.shape[0]
    span = width // shards
    lane = lax.broadcasted_iota(jnp.int32, (blocks * rows, 384), 1) % 128 < 64
    d = d_ref[...]
    zero = jnp.zeros_like(d)
    right = [jnp.where(lane, d, zero), jnp.where(lane, zero, d)]
    half = span // 2
    for shard in range(shards):
        total = jnp.zeros((span, 384), F32)
        for micro in range(2):
            left = n_ref[:, micro, :, shard * span : (shard + 1) * span]
            total = total + t_dot(left.reshape(blocks * rows, span), right[micro])
        q, k, v = (
            total[:, at : at + 128] + pltpu.roll(total[:, at : at + 128], 64, 1)
            for at in (0, 128, 256)
        )
        out_ref[shard, :span, :] = jnp.where(low_lanes(span), q, k).astype(BF16)
        out_ref[shard, span:, :] = jnp.where(low_lanes(half), v[:half], v[half:]).astype(BF16)


def cross_kv_kernel(split, starts_ref, e_ref, wk_ref, wv_ref, *refs):
    more, (ke_ref, ve_ref) = refs[:split], refs[split:]
    blocks, _, part, _ = e_ref.shape
    for index, (own_ref, out_ref) in enumerate(((wk_ref, ke_ref), (wv_ref, ve_ref))):
        total = None
        pieces = pieces_of(own_ref, more, index)
        for place, piece in enumerate(pieces):
            rows = piece.shape[0]
            if split:
                left = e_ref[:, 0, :, aligned(starts_ref[place], rows)]
            else:
                left = e_ref[:, 0]
            made = dot(left.reshape(blocks * part, rows), piece)
            total = made if total is None else total + made
        out_ref[0] = total.astype(BF16)


def cross_kv(starts, e_all, wk, wv, more):
    blocks, micro, part, width = e_all.shape
    whole = lambda array: pl.BlockSpec(array.shape, lambda m, s: (0,) * array.ndim)
    out = pl.BlockSpec((1, blocks * part, width), lambda m, s: (m, 0, 0))
    return pl.pallas_call(
        functools.partial(cross_kv_kernel, len(more)),
        grid_spec=pltpu.PrefetchScalarGridSpec(
            num_scalar_prefetch=1,
            grid=(micro,),
            in_specs=[pl.BlockSpec((blocks, 1, part, width), lambda m, s: (0, m, 0, 0))]
            + [whole(wk), whole(wv)]
            + [pl.BlockSpec((2,) + array.shape[1:], lambda m, s: (0, 0, 0)) for array in more],
            out_specs=[out, out],
        ),
        out_shape=[jax.ShapeDtypeStruct((micro, blocks * part, width), BF16)] * 2,
        compiler_params=params(VMEM_MOST),
        cost_estimate=cost(8),
        name="cross_kv",
    )(starts, e_all, wk, wv, *more)


def mid_forward_kernel(split, starts_ref, o1_ref, x_ref, gain_ref, ke_ref, ve_ref, wo, wq, wc, *refs):
    more, last = refs[:split], refs[split : 2 * split]
    left_ref, x1_ref, q2_ref, x2_ref, n3_ref, sent_ref, o1c_ref, n2_ref, o2_ref = refs[2 * split :]
    heads, rows, _ = o1_ref.shape
    width = x_ref.shape[-1]
    for pair in range(heads // 2):
        at = pair * 128
        low, high = pair_up(o1_ref[2 * pair].astype(F32), o1_ref[2 * pair + 1].astype(F32))
        o1c_ref[0:rows, at : at + 128] = low.astype(BF16)
        o1c_ref[rows : 2 * rows, at : at + 128] = high.astype(BF16)
    x = x_ref[...].astype(F32).reshape(2 * rows, width)
    x1 = x + times(o1c_ref, starts_ref, pieces_of(wo, more, 0))
    x1_ref[...] = x1
    n2_ref[...] = norm_rows(x1, gain_ref[1:2]).astype(BF16)
    q2_ref[...] = times(n2_ref, starts_ref, pieces_of(wq, more, 1)).astype(BF16)
    for micro in range(2):
        for pair in range(heads // 2):
            at = pair * 128
            span = slice(micro * rows, (micro + 1) * rows)
            q = q2_ref[span, at : at + 128]
            both = jnp.concatenate([keep_half(q, 0), keep_half(q, 1)], axis=0)
            p = softmax_rows(dot_t(both, ke_ref[micro, :, at : at + 128]))
            o = dot(p.astype(BF16), ve_ref[micro, :, at : at + 128])
            o2_ref[span, at : at + 128] = jnp.where(
                low_lanes(rows), o[:rows], o[rows:]
            ).astype(BF16)
    x2 = x1 + times(o2_ref, starts_ref, pieces_of(wc, last, 0))
    x2_ref[...] = x2
    n3_ref[...] = norm_rows(x2, gain_ref[2:3]).astype(BF16)
    left_ref[0] = o2_ref[...]
    left_ref[1] = n2_ref[...]
    left_ref[2] = o1c_ref[...]
    if split:
        span = sent_ref.shape[2]
        for kind in range(3):
            sent_ref[kind] = left_ref[kind, :, aligned(span - starts_ref[0], span)]


def cross_backward_kernel(
    split, starts_ref, slots_ref, g_ref, dn3_ref, more_ref, x2_ref, gain_ref, q2_ref, ke_ref, ve_ref,
    wc, *refs
):
    more = refs[:split]
    right_ref, gx2_ref, keep_ref, send_ref, dc_ref, back_ref, do2_ref = refs[split:]
    blocks, micros, part = keep_ref.shape[1:4]
    tokens, width = x2_ref.shape
    rows = tokens // micros
    pairs = width // 128
    even = slots_ref[pairs] == 0
    dn3 = dn3_ref[...] + more_ref[...].astype(F32)
    back, dc_ref[...] = norm_back(x2_ref[...], gain_ref[2:3], dn3)
    gx2 = g_ref[...].astype(F32) + back
    gx2_ref[...] = gx2
    gx2b = gx2.astype(BF16)
    right_ref[:, 0:width] = gx2b
    times_back(back_ref, starts_ref, [(gx2b, pieces_of(wc, more, 0))])
    do2_ref[...] = back_ref[...].astype(BF16)
    for micro in range(micros):
        for pair in range(pairs):
            at = pair * 128
            span = slice(micro * rows, (micro + 1) * rows)
            q = q2_ref[span, at : at + 128]
            do = do2_ref[span, at : at + 128]
            q = jnp.concatenate([keep_half(q, 0), keep_half(q, 1)], axis=0)
            do = jnp.concatenate([keep_half(do, 0), keep_half(do, 1)], axis=0)
            k = ke_ref[micro, :, at : at + 128]
            v = ve_ref[micro, :, at : at + 128]
            p = softmax_rows(dot_t(q, k))
            dp = dot_t(do, v)
            ds = (p * (dp - jnp.sum(p * dp, axis=-1, keepdims=True))).astype(BF16)
            dq = dot(ds, k)
            right_ref[span, width + at : width + at + 128] = jnp.where(
                low_lanes(rows), dq[:rows], dq[rows:]
            ).astype(BF16)
            low, high = pair_up(t_dot(ds, q), t_dot(p.astype(BF16), do))
            kept, sent = jnp.where(even, low, high), jnp.where(even, high, low)
            slot = slots_ref[pair]
            keep_ref[slot, :, micro] = kept.astype(BF16).reshape(blocks, part, 128)
            send_ref[slot, :, micro] = sent.astype(BF16).reshape(blocks, part, 128)


def mid_backward_kernel(split, starts_ref, right_ref, gx2_ref, x1_ref, gain_ref, wo, wq, *refs):
    more = refs[:split]
    gx1_ref, low_ref, do1_ref, dc_ref, back_ref = refs[split:]
    heads, rows, _ = do1_ref.shape
    width = x1_ref.shape[-1]
    times_back(back_ref, starts_ref, [(right_ref[:, width:], pieces_of(wq, more, 1))])
    back, dc_ref[...] = norm_back(x1_ref[...], gain_ref[1:2], back_ref[...])
    gx1 = gx2_ref[...] + back
    gx1_ref[...] = gx1
    gx1b = gx1.astype(BF16)
    low_ref[...] = gx1b
    times_back(back_ref, starts_ref, [(gx1b, pieces_of(wo, more, 0))])
    for pair in range(heads // 2):
        at = pair * 128
        do1 = back_ref[:, at : at + 128].astype(BF16).astype(F32)
        low, high = pair_up(do1[:rows], do1[rows:])
        do1_ref[2 * pair] = low.astype(BF16)
        do1_ref[2 * pair + 1] = high.astype(BF16)


def input_grad_kernel(split, starts_ref, d_ref, x_ref, gain_ref, gx1_ref, wq, wk, wv, *refs):
    more = refs[:split]
    out_ref, dc_ref, all_ref, back_ref = refs[split:]
    heads, rows, _ = d_ref.shape
    width = x_ref.shape[-1]
    for kind in range(3):
        for pair in range(heads // 2):
            lanes = slice(kind * 128, (kind + 1) * 128)
            low, high = pair_up(
                d_ref[2 * pair, :, lanes].astype(F32), d_ref[2 * pair + 1, :, lanes].astype(F32)
            )
            at = kind * width + pair * 128
            all_ref[0:rows, at : at + 128] = low.astype(BF16)
            all_ref[rows : 2 * rows, at : at + 128] = high.astype(BF16)
    terms = [
        (all_ref[:, kind * width : (kind + 1) * width], pieces_of(own, more, kind))
        for kind, own in enumerate((wq, wk, wv))
    ]
    times_back(back_ref, starts_ref, terms)
    x = x_ref[...].astype(F32).reshape(2 * rows, width)
    back, dc = norm_back(x, gain_ref[0:1], back_ref[...])
    dc_ref[...] = dc
    out_ref[...] = gx1_ref[...] + back


def encoder_grad_kernel(split, starts_ref, d_ref, wk, wv, *refs):
    more = refs[:split]
    out_ref, k_ref, v_ref = refs[split:]
    for pair in range(d_ref.shape[0] // 2):
        at = pair * 128
        low, high = pair_up(d_ref[2 * pair].astype(F32), d_ref[2 * pair + 1].astype(F32))
        k_ref[:, at : at + 128] = low.astype(BF16)
        v_ref[:, at : at + 128] = high.astype(BF16)
    terms = [(k_ref[...], pieces_of(wk, more, 0)), (v_ref[...], pieces_of(wv, more, 1))]
    times_back(out_ref, starts_ref, terms)


def cross_head_weight_kernel(e_ref, d_ref, out_ref):
    blocks, micro, part, width = e_ref.shape
    shards, span, _ = out_ref.shape
    for shard in range(shards):
        left = e_ref[:, :, :, shard * span : (shard + 1) * span]
        left = left.reshape(blocks * micro * part, span)
        out_ref[shard] = t_dot(left, d_ref[...]).astype(BF16)


def dense_kernel(split, starts_ref, n_ref, g_ref, wg, wu, wd_ref, *refs):
    more = refs[:split]
    back_ref, y_ref, ylow_ref, d_ref, dlow_ref = refs[split:]
    hidden = wd_ref.shape[0]
    gate, up = pieces_of(wg, more, 0), pieces_of(wu, more, 1)
    a = times(n_ref, starts_ref, gate)
    b = times(n_ref, starts_ref, up)
    scale = 0.7978845608028654
    cubed = 0.044715
    inner = jnp.tanh(scale * (a + cubed * (a * a * a)))
    gelu = 0.5 * a * (1.0 + inner)
    slope = 0.5 * (1.0 + inner) + 0.5 * a * (1.0 - inner * inner) * (
        scale * (1.0 + 3.0 * cubed * (a * a))
    )
    hid = (gelu * b).astype(BF16)
    dh = dot_t(g_ref[...], wd_ref[...])
    da = (dh * b * slope).astype(BF16)
    db = (dh * gelu).astype(BF16)
    times_back(d_ref, starts_ref, [(da, gate), (db, up)])
    dlow_ref[...] = d_ref[...].astype(BF16)
    y = dot(hid, wd_ref[...])
    y_ref[...] = y
    ylow_ref[...] = y.astype(BF16)
    back_ref[:, 0:hidden] = da
    back_ref[:, hidden : 2 * hidden] = db
    back_ref[:, 2 * hidden : 3 * hidden] = hid
    if more:
        shard, other = starts_ref[len(more) + 1], 1 - starts_ref[len(more) + 2]
        put_features(back_ref, 3 * hidden, n_ref, g_ref, shard, other)


def put_features(out_ref, at, n_ref, g_ref, shard, core):
    quarter = n_ref.shape[1] // 4
    for side, place in enumerate((2 * shard + core, 2 * (1 - shard) + core)):
        lanes = slice(at + side * quarter, at + (side + 1) * quarter)
        out_ref[:, lanes] = n_ref[:, aligned(place * quarter, quarter)]
    lanes = slice(at + 2 * quarter, at + 4 * quarter)
    out_ref[:, lanes] = g_ref[:, aligned(core * 2 * quarter, 2 * quarter)]


def dense_layer(starts, n, g, wg, wu, wd, more, step):
    count, width = n.shape
    hidden = wd.shape[0]
    which = starts.shape[0] - 2
    back = 3 * hidden + (width if more else 0)
    row = lambda size: pl.BlockSpec((step, size), lambda i, s: (i, 0))
    whole = lambda array: pl.BlockSpec(array.shape, lambda i, s: (0,) * array.ndim)
    column = pl.BlockSpec((wg.shape[0], hidden), lambda i, s: (0, s[which]))
    made = lambda size, kind: jax.ShapeDtypeStruct((count, size), kind)
    return pl.pallas_call(
        functools.partial(dense_kernel, len(more)),
        grid_spec=pltpu.PrefetchScalarGridSpec(
            num_scalar_prefetch=1,
            grid=(count // step,),
            in_specs=[row(width), row(width), column, column, whole(wd)]
            + [whole(array) for array in more],
            out_specs=[row(back)] + [row(width)] * 4,
        ),
        out_shape=[made(back, BF16)]
        + [made(width, F32), made(width, BF16), made(width, F32), made(width, BF16)],
        compiler_params=params(),
        cost_estimate=cost(13),
        name="dense_layer",
    )(starts, n, g, wg, wu, wd, *more)


def put_chunk(ref, slot, at, value):
    rows, width = value.shape
    for block in range(width // 128):
        ref[slot, at + block * rows : at + (block + 1) * rows, :] = value[
            :, block * 128 : (block + 1) * 128
        ].astype(BF16)


def take_chunk(ref, slot, at, rows, width):
    return jnp.concatenate(
        [
            ref[slot, at + block * rows : at + (block + 1) * rows, :].astype(F32)
            for block in range(width // 128)
        ],
        axis=1,
    )


def put_all(scratch_ref, first, count, chip, chunk_refs, at, width, masks):
    slots = [(ref, slot) for ref in chunk_refs for slot in range(ref.shape[0])]
    rows = count // len(slots)
    for (ref, slot), mask in zip(slots, masks):
        chunk = scratch_ref[aligned(first + (chip ^ mask) * rows, rows), :width]
        put_chunk(ref, slot, at, chunk)


def dense_weight_kernel(
    x_masks, z_masks, where_ref, n0_ref, n1_ref, g0_ref, g1_ref, own0_ref, own1_ref, mate0_ref, mate1_ref, keep_ref,
    send_ref, down_keep_ref, down_send_ref, far_keep_ref, far_send_ref, scratch_ref, left_ref
):
    tokens, width = n0_ref.shape
    hidden = (own0_ref.shape[1] - width) // 3
    quarter = width // 4
    at = keep_ref.shape[1] // 2
    core, shard, chip = where_ref[0], where_ref[1], where_ref[2]
    put_features(left_ref.at[:tokens], 0, n0_ref, g0_ref, shard, core)
    put_features(left_ref.at[tokens : 2 * tokens], 0, n1_ref, g1_ref, shard, core)
    left_ref[2 * tokens : 3 * tokens, :] = mate0_ref[:, 3 * hidden :]
    left_ref[3 * tokens :, :] = mate1_ref[:, 3 * hidden :]

    def whole(kind):
        span = slice(kind * hidden, (kind + 1) * hidden)
        refs = (own0_ref, own1_ref, mate0_ref, mate1_ref)
        return jnp.concatenate([ref[:, span] for ref in refs], axis=0)

    for kind in range(2):
        right = whole(kind)
        for side, (masks, refs) in enumerate(
            ((z_masks, (keep_ref, send_ref)), (x_masks, (far_keep_ref, far_send_ref)))
        ):
            value = t_dot(left_ref[:, side * quarter : (side + 1) * quarter], right)
            scratch_ref[:quarter, :hidden] = value
            put_all(scratch_ref, 0, quarter, chip, refs, kind * at, hidden, masks)
    value = t_dot(whole(2), left_ref[:, 2 * quarter :])
    scratch_ref[:, : 2 * quarter] = value
    refs = (down_keep_ref, down_send_ref)
    put_all(scratch_ref, 0, hidden, chip, refs, 0, 2 * quarter, x_masks)


def token_weight_kernel(
    masks, where_ref, left_ref, left_more_ref, right_ref, right_more_ref, last_ref, last_more_ref,
    mine_ref, mate_ref, scratch_ref
):
    kinds, _, span = left_more_ref.shape
    width = last_ref.shape[1]
    core, shard, chip = where_ref[0], where_ref[1], where_ref[2]
    half = span // 2
    at = half // len(masks) * width // 128
    for kind in range(kinds):
        lanes = slice(kind * width, (kind + 1) * width)
        left = [left_ref[kind, :, aligned(shard * span, span)], left_more_ref[kind]]
        if kind < kinds - 1:
            right = [right_ref[:, lanes], right_more_ref[:, lanes]]
        else:
            right = [last_ref[...], last_more_ref[...]]
        scratch_ref[...] = t_dot(jnp.concatenate(left, axis=0), jnp.concatenate(right, axis=0))
        for ref, own in ((mine_ref, core), (mate_ref, 1 - core)):
            put_all(scratch_ref, own * half, half, chip, (ref,), kind * at, width, masks)


def chunk_weights(kernel, where, operands, counts, slots, scratches, length, name):
    shapes = []
    for count in counts:
        shapes += [jax.ShapeDtypeStruct((slots, count, 128), BF16)] * 2
    return pl.pallas_call(
        kernel,
        out_shape=shapes,
        in_specs=[smem()] + [vmem()] * len(operands),
        out_specs=[vmem()] * len(shapes),
        scratch_shapes=scratches,
        compiler_params=params(),
        cost_estimate=cost(length),
        name=name,
    )(where, *operands)


def head_rows(in_ref, at, rows, outs):
    for pair in range(in_ref.shape[0] // 2):
        lanes = slice(pair * 128, (pair + 1) * 128)
        first = in_ref[2 * pair, at : at + rows, :].astype(F32)
        second = in_ref[2 * pair + 1, at : at + rows, :].astype(F32)
        for (out_ref, place), value in zip(outs, pair_up(first, second)):
            out_ref[place, lanes] = value


def head_spread(in_ref, at, q_ref, k_ref, v_ref):
    span = q_ref.shape[0]
    half = span // 2
    head_rows(in_ref, at, span, ((q_ref, slice(None)), (k_ref, slice(None))))
    head_rows(in_ref, at + span, half, ((v_ref, slice(0, half)), (v_ref, slice(half, span))))


def spread_kernel(where_ref, in_ref, gate_ref, up_ref, down_ref, q_ref, k_ref, v_ref, *out_refs):
    shard = where_ref[1]
    hidden = gate_ref.shape[3] // 2
    rows = gate_ref.shape[2] // 2
    at = rows * hidden // 128
    tall = down_ref.shape[0] // 2
    half = down_ref.shape[1] // 2
    span = q_ref.shape[0]
    kinds = len(out_refs) - 2
    width = out_refs[0].shape[3]
    base = 6 * at + 3 * span // 2
    step = rows * width // 128
    for piece in range(4):
        chip, core = piece // 2, piece % 2
        place = slice(chip * rows, (chip + 1) * rows)
        for side, start in enumerate((0, 4 * at)):
            lanes = aligned((shard ^ side) * hidden, hidden)
            for kind, out_ref in enumerate((gate_ref, up_ref)):
                chunk = take_chunk(in_ref, piece, start + kind * at, rows, hidden)
                out_ref[core, 0, place, lanes] = chunk
        chunk = take_chunk(in_ref, piece, 2 * at, tall, half)
        down_ref[chip * tall : (chip + 1) * tall, core * half : (core + 1) * half] = chunk
        for kind in range(kinds):
            chunk = take_chunk(in_ref, piece, base + kind * step, rows, width)
            out_refs[kind][core, 0, place, :] = chunk
    head_spread(in_ref, 6 * at, q_ref, k_ref, v_ref)
    k_ref, v_ref = out_refs[kinds:]
    head_rows(in_ref, base + kinds * step, span, ((k_ref, slice(None)), (v_ref, slice(None))))


def spread(where, pieces, outs):
    count, total, _ = pieces.shape
    steps = count // 4
    specs, shapes = [], []
    for (rows, cols), kind in outs:
        if kind == "core":
            shapes.append((2, steps, rows // (2 * steps), cols))
            block = (2, 1, rows // (2 * steps), cols)
            specs.append(pl.BlockSpec(block, lambda q, where: (0, q, 0, 0)))
        elif kind == "chip":
            shapes.append((rows, cols))
            specs.append(pl.BlockSpec((rows // steps, cols), lambda q, where: (q, 0)))
        else:
            shapes.append((rows, cols))
            specs.append(pl.BlockSpec((rows, cols // steps), lambda q, where: (0, q)))
    made = pl.pallas_call(
        spread_kernel,
        grid_spec=pltpu.PrefetchScalarGridSpec(
            num_scalar_prefetch=1,
            grid=(steps,),
            in_specs=[pl.BlockSpec((4, total, 128), lambda q, where: (q, 0, 0))],
            out_specs=specs,
        ),
        out_shape=[jax.ShapeDtypeStruct(shape, F32) for shape in shapes],
        compiler_params=params(VMEM_MOST),
        cost_estimate=cost(20),
        name="spread",
    )(where, pieces)
    return [array.reshape(shape) for array, (shape, _) in zip(made, outs)]


def plain_head_kernel(in_ref, *out_refs):
    span = out_refs[0].shape[0]
    if len(out_refs) == 3:
        head_spread(in_ref, 0, *out_refs)
    else:
        head_rows(in_ref, 0, span, [(out_ref, slice(None)) for out_ref in out_refs])


def plain_head_spread(pieces, span, width, kinds):
    return pl.pallas_call(
        plain_head_kernel,
        out_shape=[jax.ShapeDtypeStruct((span, width), F32)] * kinds,
        in_specs=[vmem()],
        out_specs=[vmem()] * kinds,
        compiler_params=params(),
        name="plain_head_spread",
    )(pieces)


def per_device(
    inputs,
    encoded,
    cotangent,
    doc_ids,
    buckets,
    gain_self,
    query_self,
    key_self,
    value_self,
    output_self,
    position_bias,
    gain_cross,
    query_cross,
    key_cross,
    value_cross,
    output_cross,
    gain_dense,
    dense_gate,
    dense_up,
    dense_down,
):
    micro_count, _, rows, width = inputs.shape
    part = encoded.shape[2]
    heads = position_bias.shape[1]
    dp, fs = lax.axis_size("dp"), lax.axis_size("fsdp")
    me, shard = lax.axis_index("dp"), lax.axis_index("fsdp")
    core, chips = me % 2, dp // 2
    length = rows * dp
    tokens = micro_count * rows
    copies = dp // heads
    head = me // copies
    span = width // fs
    half = span // 2
    hidden = dense_down.shape[0]
    chip_bits = [1 << place for place in range(1, dp.bit_length() - 1)]
    x_order, z_order = chip_bits, chip_bits[1:] + chip_bits[:1]
    paired = fs == 2
    chunked = paired and half % (16 * chips) == 0 and hidden % (16 * chips) == 0
    chunked = chunked and hidden % 128 == 0 and dp == heads and dp % 4 == 0

    def chip_of(j):
        last = len(x_order) - 1
        return sum(((j // bit) % 2) << (last - place) for place, bit in enumerate(x_order))

    def swap_dp(values, bit):
        return lax.ppermute(values, "dp", [(j, j ^ bit) for j in range(dp)])

    def swap_fs(values):
        return lax.ppermute(values, "fsdp", [(j, 1 - j) for j in range(2)])

    def after(values, *others):
        return lax.optimization_barrier((values, *others))[0]

    def half_rows(values):
        return jnp.stack([lax.dynamic_slice_in_dim(w, core * half, half, axis=0) for w in values])

    def both_halves(sent):
        got = swap_fs(sent)
        return got, swap_dp(got, 1)

    def quarter(bit):
        return 2 * ((me // bit) % 2) + core

    def quarter_starts(bit):
        rows = [(1 - shard) * span + (quarter(bit) ^ more) * (half // 2) for more in (0, 2, 1, 3)]
        return jnp.stack([shard * span] + rows).astype(jnp.int32)

    def gather_rows(values):
        return [lax.all_gather(w, "fsdp", axis=0, tiled=True) for w in values]

    def both_tokens(values):
        if paired:
            return jnp.concatenate([values, swap_fs(values)], axis=0)
        return lax.all_gather(values, "fsdp", axis=0, tiled=True)

    def reduce_chips(kept, got, order=x_order, marks=()):
        total = kept.astype(F32) + got.astype(F32)
        for place, bit in enumerate(order[1:]):
            count = total.shape[0] // 2
            sent, total = total[count:].astype(BF16), total[:count]
            if place < len(marks):
                sent = after(sent, marks[place])
            total = total + swap_dp(sent, bit).astype(F32)
        return total.astype(BF16)

    x, g, e = inputs[:, 0], cotangent[:, 0], encoded[:, 0]

    low, offsets = [x], [0]
    for bit in reversed(chip_bits[1:]):
        low = low + [swap_dp(piece, bit) for piece in low]
        offsets = offsets + [offset | bit for offset in offsets]
    high = [swap_dp(piece, 2) for piece in low]
    near, far = jnp.stack(low), jnp.stack(high)
    offsets = [offset ^ more for more in (0, 2, 1, 3) for offset in offsets]
    source = me ^ jnp.array(offsets, jnp.int32)
    e_all = lax.all_gather(e, "dp", axis=0)

    gains = jnp.stack([gain_self, gain_cross, gain_dense])
    own_head = lambda w: lax.dynamic_slice_in_dim(w, head * 64, 64, axis=1)
    if paired:
        pad = jnp.pad(position_bias.reshape(1, -1), ((0, 0), (0, span - position_bias.size)))
        small = jnp.concatenate([gains, pad], axis=0)
        small_got = swap_fs(small)
        head_pack = jnp.concatenate([own_head(w) for w in (query_self, key_self, value_self)], 1)
        head_got = swap_fs(head_pack)
        first, second = (
            jnp.where(shard == which, mine, got)
            for which, mine, got in ((0, small, small_got), (1, small, small_got))
        )
        gains = jnp.concatenate([first[:3], second[:3]], axis=1)
        bias_all = jnp.concatenate(
            [piece[3, : position_bias.size].reshape(position_bias.shape) for piece in (first, second)]
        )
        other = (1 - shard) * span
        half_starts = jnp.stack([shard * span, other + core * half, other + (1 - core) * half])
        half_starts = half_starts.astype(jnp.int32)
        near_bit, dense_bit = chip_bits[0], chip_bits[1]
        starts = quarter_starts(near_bit)
        kv_own = (key_cross, value_cross)
        near_own = (output_self, query_cross, output_cross)
        near_sent, theirs = pack(
            jnp.stack([quarter(near_bit), quarter(dense_bit), 1 - shard]).astype(jnp.int32),
            kv_own + near_own,
            (dense_gate, dense_up),
            half // 2,
            hidden,
        )
        near_got = swap_fs(near_sent)
        near_far = swap_dp(near_got, near_bit)
        dense_got = swap_fs(after(theirs, near_got))
        dense_own = (dense_gate, dense_up)
        which = jnp.stack([shard, core]).astype(jnp.int32)
        dense_starts = jnp.concatenate([quarter_starts(dense_bit), which])
    else:
        gains = lax.all_gather(gains, "fsdp", axis=1, tiled=True)
        bias_all = lax.all_gather(position_bias, "fsdp", axis=0, tiled=True)
        kv_own, kv_more = gather_rows((key_cross, value_cross)), ()
        near_own, near_more = gather_rows((output_self, query_cross, output_cross)), ()
        first_own, first_more = gather_rows((query_self, key_self, value_self)), ()
        half_starts = jnp.zeros((1,), jnp.int32)
        head_whole = jnp.concatenate([own_head(w) for w in first_own], axis=1)
        dense_own = [
            lax.all_to_all(w, "fsdp", 1, 0, tiled=True) for w in (dense_gate, dense_up)
        ]
        dense_more = ()
        starts = jnp.zeros((1,), jnp.int32)
        dense_starts = jnp.zeros((3,), jnp.int32)
        g_group = both_tokens(g.reshape(tokens, width))
    gains, bias_all = gains.astype(F32), bias_all.astype(F32)
    marks = jnp.arange(bias_all.shape[0], dtype=jnp.int32)
    edges = jnp.sum((buckets[:, None] < marks[None, :]).astype(jnp.int32), axis=0)
    bias_values = lax.dynamic_slice_in_dim(bias_all, head, 1, axis=1)[:, 0]
    table = bias_table(edges, bias_values, length)
    x_groups = [near, far, swap_dp(near, 1), swap_dp(after(far, table), 1)]
    doc_row = jnp.broadcast_to(doc_ids[:, 0, :, None], (micro_count, dp, rows))
    doc_row = doc_row.reshape(micro_count, length)
    doc_col = doc_row[:, :, None]

    if paired:
        head_got = after(head_got, *x_groups[2:])
        head_whole = jnp.where(
            shard == 0,
            jnp.concatenate([head_pack, head_got]),
            jnp.concatenate([head_got, head_pack]),
        )
    head_w = jnp.concatenate(
        [head_whole[:, at : at + 64] for at in (0, 0, 64, 64, 128, 128)], axis=1
    )

    n_all, qkv, mixed = pl.pallas_call(
        functools.partial(self_forward_kernel, len(x_groups)),
        out_shape=[
            jax.ShapeDtypeStruct((dp, micro_count, rows, width), BF16),
            jax.ShapeDtypeStruct((length, 384), BF16),
            jax.ShapeDtypeStruct((length, 128), BF16),
        ],
        in_specs=[smem()] + [vmem()] * (len(x_groups) + 5),
        out_specs=[vmem()] * 3,
        compiler_params=params(),
        cost_estimate=cost(12),
        name="self_forward",
    )(source, *x_groups, gains[0:1], head_w, table, doc_row, doc_col)
    if paired:
        mixed = after(mixed, dense_got)
    o1_heads = lax.all_to_all(mixed.reshape(dp, rows, 128), "dp", 0, 0, tiled=True)[::copies]

    if paired:
        near_more = (near_got, near_far, swap_dp(near_got, 1), swap_dp(after(near_far, mixed), 1))
        kv_more = near_more
        dense_far = swap_dp(after(dense_got, mixed), dense_bit)
    ke, ve = cross_kv(starts, e_all, *kv_own, kv_more)

    row32 = jax.ShapeDtypeStruct((tokens, width), F32)
    row16 = jax.ShapeDtypeStruct((tokens, width), BF16)
    left, x1, q2, x2, n3, left_sent = pl.pallas_call(
        functools.partial(mid_forward_kernel, len(near_more)),
        grid=(1,),
        out_shape=[
            jax.ShapeDtypeStruct((3, tokens, width), BF16),
            row32,
            row16,
            row32,
            row16,
            jax.ShapeDtypeStruct((3, tokens, span), BF16),
        ],
        in_specs=[smem()] + [vmem()] * 8 + part_specs(near_more, 2, 1) + part_specs(near_more, 1, 4),
        out_specs=[vmem()] * 6,
        scratch_shapes=[pltpu.VMEM((tokens, width), BF16)] * 3,
        compiler_params=params(VMEM_MOST),
        cost_estimate=cost(12),
        name="mid_forward",
    )(starts, o1_heads, x, gains, ke, ve, *near_own, *near_more, *near_more)

    if paired:
        dense_more = (
            dense_got,
            dense_far,
            swap_dp(after(dense_got, ke), 1),
            swap_dp(after(dense_far, ke), 1),
        )
        g_rows = g.reshape(tokens, width)
        g_got = swap_fs(after(g_rows, dense_got))
        n_got = swap_fs(n3)
        back, y32, _, dn3, _ = dense_layer(
            dense_starts, n3, g_rows, *dense_own, dense_down, dense_more, tokens
        )
        back_mate = swap_dp(back, 1)
        back_got, _, y16, _, d16 = dense_layer(
            dense_starts,
            after(n_got, dn3),
            g_got,
            *dense_own,
            dense_down,
            dense_more,
            tokens,
        )
        back_got_mate = swap_dp(back_got, 1)
        dn3_more = swap_fs(after(d16, back_mate))
        left_got = swap_fs(after(left_sent, dn3_more))
    else:
        n_group = both_tokens(n3)
        back, _, y16, _, d16 = dense_layer(
            dense_starts, n_group, g_group, *dense_own, dense_down, dense_more, tokens
        )
        dn3 = jnp.zeros((tokens, width), F32)
        dn3_more = lax.psum_scatter(d16, "fsdp", scatter_dimension=0, tiled=True)
        dense_out = lax.psum_scatter(y16, "fsdp", scatter_dimension=0, tiled=True).astype(F32)
        outputs = (x2 + dense_out).astype(BF16)

    if chunked:
        where = jnp.stack([core, shard, me // 2]).astype(jnp.int32)
        masks = [
            [
                sum(((slot >> (len(order) - 1 - at)) & 1) * (bit // 2) for at, bit in enumerate(order))
                for slot in range(chips)
            ]
            for order in (x_order, z_order)
        ]
        own_kept, own_sent, down_kept, down_sent, far_kept, far_sent = chunk_weights(
            functools.partial(dense_weight_kernel, *masks),
            where,
            (after(n3, dn3_more), n_got, g_rows, g_got, back, back_got, back_mate, back_got_mate),
            (
                span // chips * hidden // 128,
                hidden // chips * width // 256,
                span // chips * hidden // 128,
            ),
            chips // 2,
            [
                pltpu.VMEM((max(hidden, half), max(hidden, width // 2)), F32),
                pltpu.VMEM((4 * tokens, width), BF16),
            ],
            7,
            "dense_weight",
        )
        dn3_more = after(dn3_more, own_sent)
        own_got, down_got = swap_dp(own_sent, z_order[0]), swap_dp(down_sent, x_order[0])

    straight = chunked
    if straight:
        slots = jnp.append(chip_of(me ^ (2 * jnp.arange(heads // 2))), core).astype(jnp.int32)
    else:
        slots = jnp.append(jnp.arange(heads // 2), 0).astype(jnp.int32)
    g_rows = g.reshape(tokens, width)
    right, gx2, dkv_kept, dkv_sent, dc_dense = pl.pallas_call(
        functools.partial(cross_backward_kernel, len(near_more)),
        grid=(1,),
        out_shape=[
            jax.ShapeDtypeStruct((tokens, 2 * width), BF16),
            row32,
            jax.ShapeDtypeStruct((heads // 2, dp, micro_count, part, 128), BF16),
            jax.ShapeDtypeStruct((heads // 2, dp, micro_count, part, 128), BF16),
            jax.ShapeDtypeStruct((1, width), F32),
        ],
        in_specs=[smem()] * 2 + [vmem()] * 9 + part_specs(near_more, 1, 4),
        out_specs=[vmem()] * 5,
        scratch_shapes=[pltpu.VMEM((tokens, width), F32), pltpu.VMEM((tokens, width), BF16)],
        compiler_params=params(),
        cost_estimate=cost(15),
        name="cross_backward",
    )(starts, slots, g_rows, dn3, dn3_more, x2, gains, q2, ke, ve, near_own[2], *near_more)
    if chunked:
        gx2 = after(gx2, own_got, down_got, left_got)
    gx1, last, do1_heads, dc_cross = pl.pallas_call(
        functools.partial(mid_backward_kernel, len(near_more)),
        grid=(1,),
        out_shape=[
            row32,
            row16,
            jax.ShapeDtypeStruct((heads, rows, 128), BF16),
            jax.ShapeDtypeStruct((1, width), F32),
        ],
        in_specs=[smem()] + [vmem()] * 6 + part_specs(near_more, 2, 1),
        out_specs=[vmem()] * 4,
        scratch_shapes=[pltpu.VMEM((tokens, width), F32)],
        compiler_params=params(),
        cost_estimate=cost(6),
        name="mid_backward",
    )(starts, right, gx2, x1, gains, *near_own[:2], *near_more)
    do1 = lax.all_to_all(
        jnp.repeat(do1_heads, copies, axis=0) if copies > 1 else do1_heads, "dp", 0, 0, tiled=True
    ).reshape(length, 128)

    if chunked:
        right_got, last_got = swap_fs(after(right, do1_heads)), swap_fs(last)
        far_got = swap_fs(after(far_sent, right_got, last_got))
        if straight:
            dkv_got = swap_dp(after(dkv_sent, do1_heads), 1)
            dkv_total = dkv_kept.astype(F32) + dkv_got.astype(F32)
            dkv_far = swap_dp(dkv_total[chips // 2 :].astype(BF16), x_order[0])
        token_left = after(left, do1)
        do1 = after(do1, dkv_got)

    dqkv, table_grad = pl.pallas_call(
        self_backward_kernel,
        out_shape=[
            jax.ShapeDtypeStruct((length, 384), BF16),
            jax.ShapeDtypeStruct((TILE, length), F32),
        ],
        in_specs=[vmem()] * 5,
        out_specs=[vmem()] * 2,
        scratch_shapes=[pltpu.VMEM((length, 128), F32), pltpu.VMEM((length, 128), F32)],
        compiler_params=params(),
        cost_estimate=cost(10),
        name="self_backward",
    )(qkv, do1, table, doc_row, doc_col)
    if chunked:
        dqkv = after(dqkv, right_got, last_got)
        far_x = swap_dp(after(far_got, table_grad, dkv_far), x_order[0])
        far_kept = swap_fs(after(far_kept, table_grad))
    if chunked:
        token_kept, token_sent = chunk_weights(
            functools.partial(token_weight_kernel, masks[1]),
            where,
            (token_left, left_got, right, right_got, last, last_got),
            (3 * half // chips * width // 128,),
            chips,
            [pltpu.VMEM((span, width), F32)],
            6,
            "token_weight",
        )
        token_got = swap_dp(token_sent, 1)
        dqkv = after(dqkv, token_kept)
    head_grad = pl.pallas_call(
        head_weight_kernel,
        out_shape=jax.ShapeDtypeStruct((fs, span * 3 // 2, 128), BF16),
        in_specs=[vmem()] * 2,
        out_specs=vmem(),
        compiler_params=params(),
        cost_estimate=cost(6),
        name="head_weight",
    )(n_all, dqkv)
    def sum_shards(values):
        if paired:
            kept = lax.dynamic_index_in_dim(values, shard, 0)
            sent = lax.dynamic_index_in_dim(values, 1 - shard, 0)
            return (kept.astype(F32) + swap_fs(sent).astype(F32)).astype(BF16)
        return lax.psum_scatter(values, "fsdp", scatter_dimension=0, tiled=True)

    head_sum = sum_shards(head_grad)

    if paired:
        first_own = (query_self, key_self, value_self)
        first_more = both_halves(after(half_rows(first_own), head_sum))
        y16 = swap_fs(after(y16, first_more[0]))
        outputs = (x2 + (y32 + y16.astype(F32))).astype(BF16)
    own_d = lax.all_to_all(dqkv.reshape(dp, rows, 384), "dp", 0, 0, tiled=True)[::copies]
    grad_inputs, dc_one = pl.pallas_call(
        functools.partial(input_grad_kernel, len(first_more)),
        out_shape=[row32, jax.ShapeDtypeStruct((1, width), F32)],
        in_specs=[smem()] + [vmem()] * (7 + len(first_more)),
        out_specs=[vmem()] * 2,
        scratch_shapes=[
            pltpu.VMEM((tokens, 3 * width), BF16),
            pltpu.VMEM((tokens, width), F32),
        ],
        compiler_params=params(),
        cost_estimate=cost(7),
        name="input_grad",
    )(half_starts, own_d, x, gains, gx1, *first_own, *first_more)

    if chunked:
        table_grad = after(table_grad, far_x)
    bucket_parts = bucket_sums(edges, table_grad, bias_all.shape[0])
    table_sums = jnp.sum(bucket_parts, axis=1)
    if straight:
        dkv = reduce_chips(dkv_total[: chips // 2], dkv_far).reshape(-1, 128)
        dkv = after(dkv, bucket_parts)
    else:
        dkv = jnp.stack([dkv_kept, dkv_sent], axis=1).reshape(heads * copies, -1, 128)
        dkv = lax.psum_scatter(dkv, "dp", scatter_dimension=0, tiled=True)[0]
        bit = 1
        while bit < copies:
            got = swap_dp(dkv, bit)
            dkv = jnp.where(
                (me // bit) % 2 == 0, jnp.concatenate([dkv, got]), jnp.concatenate([got, dkv])
            )
            bit *= 2
    cross_grad = pl.pallas_call(
        cross_head_weight_kernel,
        out_shape=jax.ShapeDtypeStruct((fs, span, 128), BF16),
        in_specs=[vmem()] * 2,
        out_specs=vmem(),
        compiler_params=params(),
        cost_estimate=cost(3),
        name="cross_head_weight",
    )(e_all, dkv)
    cross_sum = sum_shards(cross_grad)
    own_dkv = dkv.reshape(dp, micro_count * part, 128)
    own_dkv = lax.all_to_all(own_dkv, "dp", 0, 0, tiled=True)[::copies]
    grad_encoded = pl.pallas_call(
        functools.partial(encoder_grad_kernel, len(kv_more)),
        grid=(1,),
        out_shape=jax.ShapeDtypeStruct((micro_count * part, width), F32),
        in_specs=[smem()] + [vmem()] * 3 + part_specs(kv_more, 2, 0),
        out_specs=vmem(),
        scratch_shapes=[pltpu.VMEM((micro_count * part, width), BF16)] * 2,
        compiler_params=params(),
        cost_estimate=cost(4),
        name="encoder_grad",
    )(starts, own_dkv, *kv_own, *kv_more)

    if chunked:
        sums = (
            reduce_chips(own_kept, own_got, z_order, (do1, dkv_far)),
            reduce_chips(down_kept, down_got, x_order, (do1, dkv_far)),
            reduce_chips(far_kept, far_x, x_order, (dqkv, head_grad)),
            head_sum,
            reduce_chips(token_kept, token_got, [1] + z_order, (token_kept, dkv_far)),
            cross_sum,
        )
        pieces = lax.all_gather(jnp.concatenate(sums, axis=1), "dp", axis=0, tiled=True)
        square, wide = (span, width), (span, fs * hidden)
        (
            grad_dense_gate,
            grad_dense_up,
            grad_dense_down,
            grad_query_self,
            grad_key_self,
            grad_value_self,
            grad_output_cross,
            grad_query_cross,
            grad_output_self,
            grad_key_cross,
            grad_value_cross,
        ) = spread(
            where,
            pieces,
            [(wide, "core")] * 2
            + [((hidden, width), "chip")]
            + [(square, "head")] * 3
            + [(square, "core")] * 3
            + [(square, "head")] * 2,
        )
    else:

        def all_heads(values, kinds):
            pieces = lax.all_gather(values, "dp", axis=0, tiled=True)[::copies]
            return plain_head_spread(pieces, span, width, kinds)

        grad_query_self, grad_key_self, grad_value_self = all_heads(head_sum, 3)
        grad_key_cross, grad_value_cross = all_heads(cross_sum, 2)
        right = jnp.concatenate([right, last], axis=1)

        def over_dp(values):
            return lax.psum(values.astype(BF16), "dp").astype(F32)

        def over_all(a, b):
            made = t_dot(a, b).astype(BF16)
            return over_dp(lax.psum_scatter(made, "fsdp", scatter_dimension=0, tiled=True))

        grad_output_cross, grad_query_cross, grad_output_self = (
            over_all(left[kind], right[:, kind * width : (kind + 1) * width]) for kind in range(3)
        )
        grad_dense_gate, grad_dense_up = (
            over_dp(
                lax.all_to_all(
                    t_dot(n_group, back[:, kind * hidden : (kind + 1) * hidden]).astype(BF16),
                    "fsdp",
                    0,
                    1,
                    tiled=True,
                )
            )
            for kind in range(2)
        )
        grad_dense_down = over_dp(t_dot(back[:, 2 * hidden :], g_group))

    column = (jnp.arange(heads) == head) & (me % copies == 0)
    bias_row = jnp.where(column[None, :], table_sums[:, None], 0.0).reshape(1, -1)
    bias_row = jnp.pad(bias_row, ((0, 0), (0, width - bias_row.shape[1])))
    sums = jnp.concatenate([dc_one, dc_dense, dc_cross, bias_row], axis=0)
    if paired:
        sums = sums + swap_fs(sums)
        for bit in [1] + chip_bits:
            sums = sums + swap_dp(sums, bit)
    else:
        sums = lax.psum(sums, ("dp", "fsdp"))
    own = lax.dynamic_slice_in_dim(sums[:3], shard * span, span, axis=1)
    grad_bias = sums[3, : bias_all.size].reshape(bias_all.shape)
    grad_bias = lax.dynamic_slice_in_dim(
        grad_bias, shard * position_bias.shape[0], position_bias.shape[0], axis=0
    )
    shape = (micro_count, 1, rows, width)
    return (
        outputs.reshape(shape),
        grad_inputs.reshape(shape),
        grad_encoded.reshape(micro_count, 1, part, width),
        own[0],
        grad_query_self,
        grad_key_self,
        grad_value_self,
        grad_output_self,
        grad_bias,
        own[2],
        grad_query_cross,
        grad_key_cross,
        grad_value_cross,
        grad_output_cross,
        own[1],
        grad_dense_gate,
        grad_dense_up,
        grad_dense_down,
    )


def solution(mesh):
    matrix = P("fsdp", None)
    token = P(None, "fsdp", "dp", None)
    weights = (
        (P("fsdp"),)
        + (matrix,) * 5
        + (P("fsdp"),)
        + (matrix,) * 4
        + (P("fsdp"),)
        + (matrix,) * 3
    )
    return jax.shard_map(
        per_device,
        mesh=mesh,
        in_specs=(token,) * 3 + (P(None, "fsdp", None), P()) + weights,
        out_specs=(token,) * 3 + weights,
        check_vma=False,
    )
```
